32 devices in a mesh: seq: 8 (over z, y), doc: 4 (over x, core).
Axes of the slice: x: 2, y: 2, z: 4, core: 2. Of those that a mesh axis runs over, the one named last changes fastest.
Arguments:
- tokens: bfloat16 [4, 1024, 4096], P('doc', 'seq'), may hold values from -6 to 6
- norm_gain: float32 [4096], replicated, may hold values from 0.5 to 9
- w_query: bfloat16 [4096, 2048], P(None, 'doc'), may hold values from -0.09375 to 0.09375
- key_weight: bfloat16 [4096, 512], P(None, 'doc'), may hold values from -0.09375 to 0.09375
- value_weight: bfloat16 [4096, 512], P(None, 'doc'), may hold values from -0.09375 to 0.09375
- vertical_blocks: int32 [4, 4, 4], replicated, may hold values from 0 to 7, as said below
- slash_offsets: int32 [4, 4, 4], replicated, may hold values from 2 to 7, as said below
Outputs:
- attended: bfloat16 [4, 1024, 2048], P('doc', 'seq')
The draws below stay inside these ranges and needn't reach their ends.
Inputs may be any that keep to these rules, and one draw needn't show every extreme that they name: `vertical_blocks`: within one document and key-value head the 4 block indices are distinct. `slash_offsets`: within one document and key-value head the 4 offsets are distinct.
All inputs are finite; a program needn't handle non-finite values.
Results may differ from the reference program's by a relative error of at most 0.013.
The reference program's roundings to bfloat16 on the way count: a program that leaves them out, or rounds other values in their place, can miss the bound.
Values may be sent and summed in bfloat16 or wider, within the bound.
No kernel may reach another device: no remote copies, remote signals or barrier semaphores. Data moves between devices by JAX's collectives and lax.ppermute only.
A program may use at most 64 MiB of HBM per device.

```python
import jax
import jax.numpy as jnp
from jax import lax

MODEL_WIDTH = 4096
QUERY_HEADS = 16
KEY_VALUE_HEADS = 4
HEAD_WIDTH = 128
BLOCK_TOKENS = 128
VERTICAL_TOTAL = 4
SLASH_TOTAL = 4
DOCUMENT_COUNT = 4
LEN = 1024


def unique_rows(key, rows, width, low, high):
    span = high - low
    row_keys = jax.random.split(key, rows)
    common = jax.vmap(lambda row_key: jax.random.permutation(row_key, span)[:width])(row_keys) + low
    top_row = jnp.concatenate([jax.random.permutation(row_keys[0], span - 1)[:width - 1] + low, jnp.full((1,), high - 1, jnp.int32)])
    bottom_row = jnp.concatenate([jax.random.permutation(row_keys[1], span - 1)[:width - 1] + low + 1, jnp.full((1,), low, jnp.int32)])
    return common.astype(jnp.int32).at[0].set(top_row.astype(jnp.int32)).at[1].set(bottom_row.astype(jnp.int32))


def draw_vertical_blocks(key, part):
    block_list = LEN // BLOCK_TOKENS
    return unique_rows(jax.random.fold_in(key, 11), DOCUMENT_COUNT * KEY_VALUE_HEADS, VERTICAL_TOTAL, 0, block_list).reshape(DOCUMENT_COUNT, KEY_VALUE_HEADS, VERTICAL_TOTAL)


def draw_slash_offsets(key, part):
    block_list = LEN // BLOCK_TOKENS
    return unique_rows(jax.random.fold_in(key, 23), DOCUMENT_COUNT * KEY_VALUE_HEADS, SLASH_TOTAL, 2, block_list).reshape(DOCUMENT_COUNT, KEY_VALUE_HEADS, SLASH_TOTAL)


def draw_norm_gain(key, part):
    value_rows = jax.random.uniform(key, (MODEL_WIDTH,), jnp.float32, 0.5, 1.5)
    return value_rows


def block_levels(own_key, shape, cuts, smallest, high):
    loudness, own = 1.0, jax.random.fold_in(own_key, 6)
    for dim, shards_of in cuts:
        steps = jnp.exp(jax.random.uniform(jax.random.fold_in(own, dim), (shards_of,), jnp.float32, smallest / len(cuts), high / len(cuts)))
        loudness = loudness * jnp.repeat(steps, shape[dim] // shards_of).reshape([-1 if axis == dim else 1 for axis in range(len(shape))])
    return loudness


def bell_draw(stream_key, shape, deviation, reach, shards=(), held_as=jnp.bfloat16):
    level = block_levels(stream_key, shape, shards, -0.22, 0.18) if shards else 1.0
    array = jax.random.normal(stream_key, shape, jnp.float32) * deviation * level
    return jnp.minimum(jnp.maximum(array, -reach), reach).astype(held_as)


def setup_inputs(seed: int = 0) -> dict:
    streams_of = jax.random.split(jax.random.key(seed), 8)
    return {
        "tokens": bell_draw(streams_of[0], (DOCUMENT_COUNT, LEN, MODEL_WIDTH), 1.0, 6.0, ((0, 4), (1, 8))),
        "norm_gain": draw_norm_gain(jax.random.fold_in(streams_of[7], 71), 0),
        "w_query": bell_draw(streams_of[2], (MODEL_WIDTH, QUERY_HEADS * HEAD_WIDTH), MODEL_WIDTH ** -0.5, 0.09375, ((1, 4),)),
        "key_weight": bell_draw(streams_of[3], (MODEL_WIDTH, KEY_VALUE_HEADS * HEAD_WIDTH), MODEL_WIDTH ** -0.5, 0.09375, ((1, 4),)),
        "value_weight": bell_draw(streams_of[4], (MODEL_WIDTH, KEY_VALUE_HEADS * HEAD_WIDTH), MODEL_WIDTH ** -0.5, 0.09375, ((1, 4),)),
        "vertical_blocks": draw_vertical_blocks(jax.random.fold_in(streams_of[7], 71), 0),
        "slash_offsets": draw_slash_offsets(jax.random.fold_in(streams_of[7], 71), 0),
    }


def rope_table(positions, width):
    inverse = jnp.power(jnp.float32(500000.0), -jnp.arange(0, width, 2, dtype=jnp.float32) / width)
    angles = positions.astype(jnp.float32)[:, None] * inverse[None, :]
    return (jnp.cos(angles), jnp.sin(angles))

def apply_rotation(value_rows, cosine_table, sine_table):
    half = value_rows.shape[-1] // 2
    first = value_rows[..., :half]
    second = value_rows[..., half:]
    cosine_table = cosine_table[:, None, :]
    sine_table = sine_table[:, None, :]
    return jnp.concatenate([first * cosine_table - second * sine_table, second * cosine_table + first * sine_table], axis=-1)

def normalize(tokens, norm_gain):
    widened = tokens.astype(jnp.float32)
    scale = lax.rsqrt(lax.optimization_barrier(jnp.mean(widened * widened, axis=-1, keepdims=True)) + 1e-05)
    return (widened * scale * norm_gain).astype(jnp.bfloat16)

def slot_masks(rows, slots):
    query_index = jnp.arange(rows)[:, None, None]
    key_index = jnp.arange(rows)[None, None, :]
    slot_index = jnp.arange(slots)[None, :, None]
    return (slot_index > 0) | (key_index <= query_index)

def block_validity(place, vertical, offsets):
    slash_index = place - offsets
    repeated = jnp.any(vertical[..., :, None] == slash_index[..., None, :], axis=-1)
    own = jnp.ones(slash_index.shape[:-1] + (1,), dtype=jnp.bool_)
    previous = jnp.broadcast_to(place >= 1, own.shape)
    return jnp.concatenate([own, previous, slash_index >= 0, (vertical < place - 1) & ~repeated], axis=-1)

def reference(tokens, norm_gain, w_query, key_weight, value_weight, vertical_blocks, slash_offsets):
    document_list, sequence_length, width = tokens.shape
    query_group = QUERY_HEADS // KEY_VALUE_HEADS
    block_list = sequence_length // BLOCK_TOKENS
    normed_input = normalize(tokens, norm_gain).reshape(document_list * sequence_length, width)
    cosine_table, sine_table = rope_table(jnp.arange(sequence_length, dtype=jnp.int32), HEAD_WIDTH)
    query_rows = jnp.dot(normed_input, w_query, preferred_element_type=jnp.float32).reshape(document_list, sequence_length, QUERY_HEADS, HEAD_WIDTH)
    query_rows = apply_rotation(query_rows, cosine_table, sine_table).astype(jnp.bfloat16).reshape(document_list, sequence_length, KEY_VALUE_HEADS, query_group, HEAD_WIDTH)
    key_rows = jnp.dot(normed_input, key_weight, preferred_element_type=jnp.float32).reshape(document_list, sequence_length, KEY_VALUE_HEADS, HEAD_WIDTH)
    key_rows = apply_rotation(key_rows, cosine_table, sine_table).astype(jnp.bfloat16)
    value_rows = jnp.dot(normed_input, value_weight, preferred_element_type=jnp.float32).reshape(document_list, sequence_length, KEY_VALUE_HEADS, HEAD_WIDTH).astype(jnp.bfloat16)
    query_streams = jnp.transpose(query_rows, (0, 2, 1, 3, 4)).reshape(document_list * KEY_VALUE_HEADS, block_list, BLOCK_TOKENS, query_group, HEAD_WIDTH)
    key_streams = jnp.transpose(key_rows, (0, 2, 1, 3)).reshape(document_list * KEY_VALUE_HEADS, block_list, BLOCK_TOKENS, HEAD_WIDTH)
    value_streams = jnp.transpose(value_rows, (0, 2, 1, 3)).reshape(document_list * KEY_VALUE_HEADS, block_list, BLOCK_TOKENS, HEAD_WIDTH)
    masks = slot_masks(BLOCK_TOKENS, 2 + SLASH_TOTAL + VERTICAL_TOTAL)
    index = jnp.arange(block_list, dtype=jnp.int32)[:, None]

    def one_lane(items):
        query_lane, key_lane, value_lane, vertical, offsets = items
        chosen = jnp.concatenate([index, index - 1, index - offsets[None, :], jnp.broadcast_to(vertical[None, :], (block_list, vertical.shape[0]))], axis=1)
        chosen = jnp.clip(chosen, 0, block_list - 1).astype(jnp.int32)
        valid = block_validity(index, vertical, offsets)
        key_blocks = key_lane[chosen]
        value_blocks = value_lane[chosen]
        scores = jnp.einsum('bqgd,bskd->bgqsk', query_lane.astype(jnp.float32), key_blocks.astype(jnp.float32)) * HEAD_WIDTH ** (-0.5)
        mask = valid[:, None, None, :, None] & masks[None, None]
        scores = jnp.where(mask, scores, -jnp.inf)
        highest = lax.optimization_barrier(jnp.max(scores, axis=(3, 4), keepdims=True))
        raised = jnp.exp(scores - highest)
        total = lax.optimization_barrier(jnp.sum(raised, axis=(3, 4)))
        weights = raised.astype(jnp.bfloat16)
        mixed_output = jnp.einsum('bgqsk,bskd->bqgd', weights.astype(jnp.float32), value_blocks.astype(jnp.float32))
        mixed_output = mixed_output / jnp.transpose(total, (0, 2, 1))[..., None]
        return mixed_output.astype(jnp.bfloat16).reshape(sequence_length, query_group * HEAD_WIDTH)
    mixed_output = lax.map(one_lane, (query_streams, key_streams, value_streams, vertical_blocks.reshape(-1, VERTICAL_TOTAL), slash_offsets.reshape(-1, SLASH_TOTAL)))
    return jnp.transpose(mixed_output.reshape(document_list, KEY_VALUE_HEADS, sequence_length, query_group * HEAD_WIDTH), (0, 2, 1, 3)).reshape(document_list, sequence_length, QUERY_HEADS * HEAD_WIDTH)
```

```python
import functools

import jax
import jax.numpy as jnp
from jax import lax
from jax.experimental import pallas as pl
from jax.experimental.pallas import tpu as pltpu
from jax.sharding import PartitionSpec as P

HEAD_WIDTH = 128
QUERY_HEADS = 16
KEY_VALUE_HEADS = 4
QUERY_GROUP = QUERY_HEADS // KEY_VALUE_HEADS
EPSILON = 1e-05


def swap(value, axis, mask):
    count = lax.axis_size(axis)
    return lax.ppermute(value, axis, [(source, source ^ mask) for source in range(count)])


def rope_table(positions, width):
    inverse = jnp.power(jnp.float32(500000.0), -jnp.arange(0, width, 2, dtype=jnp.float32) / width)
    angles = positions.astype(jnp.float32)[:, None] * inverse[None, :]
    return (jnp.cos(angles), jnp.sin(angles))


def project_kernel(lanes, rows, steps, *refs):
    token_refs = refs[:lanes]
    gain_ref, wq_ref, wk_ref, wv_ref, table_ref, q_ref, kv_ref, normed, q_acc, kv_acc = refs[lanes:]
    step = pl.program_id(0)
    depth = wq_ref.shape[0]
    heads = wk_ref.shape[1] // HEAD_WIDTH

    @pl.when(step == 0)
    def _():
        for lane in range(lanes):
            wide = token_refs[lane][0].astype(jnp.float32)
            scale = lax.rsqrt(jnp.mean(wide * wide, axis=-1, keepdims=True) + EPSILON)
            done = (wide * scale * gain_ref[...]).astype(jnp.bfloat16)
            for piece in range(steps):
                normed[piece, lane * rows:(lane + 1) * rows, :] = done[:, piece * depth:(piece + 1) * depth]
        q_acc[...] = jnp.zeros_like(q_acc)
        kv_acc[...] = jnp.zeros_like(kv_acc)

    part = normed[step]
    cols = heads * HEAD_WIDTH
    q_acc[...] += jnp.dot(part, wq_ref[...], preferred_element_type=jnp.float32)
    kv_acc[:, :cols] += jnp.dot(part, wk_ref[...], preferred_element_type=jnp.float32)
    kv_acc[:, cols:] += jnp.dot(part, wv_ref[...], preferred_element_type=jnp.float32)

    @pl.when(step == steps - 1)
    def _():
        half = HEAD_WIDTH // 2
        table = table_ref[...]
        cosine = table[:, :HEAD_WIDTH]
        sine = table[:, HEAD_WIDTH:]

        def rotate(value):
            turned = jnp.concatenate([value[:, half:], value[:, :half]], axis=1)
            return (value * cosine + turned * sine).astype(jnp.bfloat16)

        for lane in range(lanes):
            band = pl.ds(lane * rows, rows)
            for head in range(heads * QUERY_GROUP):
                q_ref[lane, :, head * HEAD_WIDTH:(head + 1) * HEAD_WIDTH] = rotate(
                    q_acc[band, head * HEAD_WIDTH:(head + 1) * HEAD_WIDTH]
                )
            for head in range(heads):
                at = 2 * head * HEAD_WIDTH
                kv_ref[lane, :, at:at + HEAD_WIDTH] = rotate(
                    kv_acc[band, head * HEAD_WIDTH:(head + 1) * HEAD_WIDTH]
                )
                kv_ref[lane, :, at + HEAD_WIDTH:at + 2 * HEAD_WIDTH] = kv_acc[
                    band, cols + head * HEAD_WIDTH:cols + (head + 1) * HEAD_WIDTH
                ].astype(jnp.bfloat16)


def project(tokens, gain, w_query, key_weight, value_weight, table, steps=8):
    lanes = len(tokens)
    rows, width = tokens[0].shape[1:]
    depth = width // steps
    q_cols, k_cols = w_query.shape[1], key_weight.shape[1]
    total = lanes * rows
    whole = lambda shape: pl.BlockSpec(shape, lambda s: (0,) * len(shape))
    return pl.pallas_call(
        functools.partial(project_kernel, lanes, rows, steps),
        grid=(steps,),
        in_specs=[whole((1, rows, width))] * lanes
        + [
            whole((1, width)),
            pl.BlockSpec((depth, q_cols), lambda s: (s, 0)),
            pl.BlockSpec((depth, k_cols), lambda s: (s, 0)),
            pl.BlockSpec((depth, k_cols), lambda s: (s, 0)),
            whole((rows, 2 * HEAD_WIDTH)),
        ],
        out_specs=[whole((lanes, rows, q_cols)), whole((lanes, rows, 2 * k_cols))],
        out_shape=[
            jax.ShapeDtypeStruct((lanes, rows, q_cols), jnp.bfloat16),
            jax.ShapeDtypeStruct((lanes, rows, 2 * k_cols), jnp.bfloat16),
        ],
        scratch_shapes=[
            pltpu.VMEM((steps, total, depth), jnp.bfloat16),
            pltpu.VMEM((total, q_cols), jnp.float32),
            pltpu.VMEM((total, 2 * k_cols), jnp.float32),
        ],
        compiler_params=pltpu.CompilerParams(vmem_limit_bytes=40 * 1024 * 1024),
        cost_estimate=pl.CostEstimate(
            flops=2 * total * width * (q_cols + 2 * k_cols),
            bytes_accessed=2 * width * (q_cols + 2 * k_cols) + 2 * total * width,
            transcendentals=0,
        ),
        name="project",
    )(*tokens, gain, w_query, key_weight, value_weight, table)


def attend_kernel(lanes, chunk, chunks, place_ref, docs_ref, vertical_ref, offset_ref, q_ref, kv_ref, out_ref):
    rows = q_ref.shape[1]
    heads = kv_ref.shape[3] // (2 * HEAD_WIDTH)
    place = place_ref[0]
    group_place = place_ref[1]
    rank = QUERY_GROUP * rows
    span = chunk * rows
    factor = HEAD_WIDTH ** (-0.5)
    query_at = place * rows + lax.broadcasted_iota(jnp.int32, (rows, rows), 0)
    key_at = lax.broadcasted_iota(jnp.int32, (rows, rows), 1)

    def block_allowed(doc, group, block):
        slash = jnp.bool_(False)
        for s in range(offset_ref.shape[2]):
            slash = slash | (block == place - offset_ref[doc, group, s])
        vertical = jnp.bool_(False)
        for s in range(vertical_ref.shape[2]):
            vertical = vertical | (block == vertical_ref[doc, group, s])
        return (block == place) | (block == place - 1) | slash | (vertical & (block < place - 1))

    for lane in range(lanes):
        doc = docs_ref[lane]
        for head in range(heads):
            group = group_place * heads + head
            at = head * QUERY_GROUP * HEAD_WIDTH
            queries = jnp.concatenate(
                [
                    q_ref[lane, :, at + h * HEAD_WIDTH:at + (h + 1) * HEAD_WIDTH]
                    for h in range(QUERY_GROUP)
                ],
                axis=0,
            )

            def step(index, carry):
                highest, total, mixed = carry
                first = index * chunk
                kv = kv_ref[pl.ds(first, chunk), lane, :, 2 * head * HEAD_WIDTH:2 * (head + 1) * HEAD_WIDTH]
                keys = kv[:, :, :HEAD_WIDTH].reshape(span, HEAD_WIDTH)
                values = kv[:, :, HEAD_WIDTH:].reshape(span, HEAD_WIDTH)
                scores = lax.dot_general(
                    queries, keys, (((1,), (1,)), ((), ())), preferred_element_type=jnp.float32
                ) * factor
                bias = jnp.concatenate(
                    [
                        jnp.where(
                            (key_at + (first + j) * rows <= query_at)
                            & block_allowed(doc, group, first + j),
                            jnp.float32(0),
                            -jnp.inf,
                        )
                        for j in range(chunk)
                    ],
                    axis=1,
                )
                scores = (scores.reshape(QUERY_GROUP, rows, span) + bias[None]).reshape(rank, span)
                top = jnp.max(scores, axis=1, keepdims=True)
                if chunks > 1:
                    fresh = jnp.maximum(highest, top)
                    safe = jnp.where(fresh == -jnp.inf, jnp.float32(0), fresh)
                    fade = jnp.exp(highest - safe)
                else:
                    fresh = safe = top
                raised = jnp.exp(scores - safe)
                part = jnp.sum(raised, axis=1, keepdims=True)
                product = jnp.dot(
                    raised.astype(jnp.bfloat16), values, preferred_element_type=jnp.float32
                )
                if chunks > 1:
                    return fresh, total * fade + part, mixed * fade + product
                return fresh, part, product

            initial = (
                jnp.full((rank, 1), -jnp.inf, jnp.float32),
                jnp.zeros((rank, 1), jnp.float32),
                jnp.zeros((rank, HEAD_WIDTH), jnp.float32),
            )
            if chunks > 1:
                _, total, mixed = lax.fori_loop(0, chunks, step, initial)
            else:
                _, total, mixed = step(0, initial)
            result = (mixed / total).astype(jnp.bfloat16)
            for h in range(QUERY_GROUP):
                out_ref[lane, :, at + h * HEAD_WIDTH:at + (h + 1) * HEAD_WIDTH] = result[
                    h * rows:(h + 1) * rows
                ]


def attend(place, docs, vertical, offsets, queries, keys_values):
    lanes, rows, q_cols = queries.shape
    blocks = keys_values.shape[0]
    chunk = 8 if blocks % 8 == 0 else 1
    smem = pl.BlockSpec(memory_space=pltpu.SMEM)
    vmem = pl.BlockSpec(memory_space=pltpu.VMEM)
    return pl.pallas_call(
        functools.partial(attend_kernel, lanes, chunk, blocks // chunk),
        in_specs=[smem] * 4 + [vmem] * 2,
        out_specs=vmem,
        out_shape=jax.ShapeDtypeStruct(queries.shape, jnp.bfloat16),
        compiler_params=pltpu.CompilerParams(vmem_limit_bytes=48 * 1024 * 1024),
        cost_estimate=pl.CostEstimate(
            flops=4 * lanes * rows * q_cols * blocks * rows,
            bytes_accessed=2 * keys_values.size + 4 * queries.size,
            transcendentals=lanes * rows * blocks * rows * q_cols // HEAD_WIDTH,
        ),
        name="attend",
    )(place, docs, vertical, offsets, queries, keys_values)


def assemble_kernel(place_ref, *refs):
    out_ref = refs[-1]
    cols = refs[0].shape[1]
    for mask, piece in enumerate(refs[:-1]):
        at = pl.multiple_of((place_ref[1] ^ mask) * cols, cols)
        out_ref[0, :, pl.ds(at, cols)] = piece[...]


def assemble(place, pieces):
    rows, cols = pieces[0].shape
    smem = pl.BlockSpec(memory_space=pltpu.SMEM)
    vmem = pl.BlockSpec(memory_space=pltpu.VMEM)
    return pl.pallas_call(
        assemble_kernel,
        in_specs=[smem] + [vmem] * len(pieces),
        out_specs=vmem,
        out_shape=jax.ShapeDtypeStruct((1, rows, cols * len(pieces)), jnp.bfloat16),
        compiler_params=pltpu.CompilerParams(vmem_limit_bytes=16 * 1024 * 1024),
        name="assemble",
    )(place, *pieces)


def local(tokens, norm_gain, w_query, key_weight, value_weight, vertical_blocks, slash_offsets):
    _, rows, width = tokens.shape
    doc_count = lax.axis_size("doc")
    place = lax.axis_index("seq")
    doc_place = lax.axis_index("doc")
    places = jnp.stack([place, doc_place]).astype(jnp.int32)
    cosine, sine = rope_table(place * rows + jnp.arange(rows, dtype=jnp.int32), HEAD_WIDTH)
    table = jnp.concatenate([cosine, cosine, -sine, sine], axis=1)
    gain = norm_gain.reshape(1, width)

    held = {0: tokens}
    half = doc_count // 2
    if half > 1:
        held[half] = swap(tokens, "doc", half)
    bit = 1
    while bit < max(half, 2) and bit < doc_count:
        for mask in list(held):
            if mask & bit == 0 and (mask | bit) not in held:
                held[mask | bit] = swap(held[mask], "doc", bit)
        bit *= 2
    order = sorted(held)
    groups = [order[:half], order[half:]] if half else [order]

    pieces = {}
    for masks in groups:
        queries, kv = project([held[m] for m in masks], gain, w_query, key_weight, value_weight, table)
        gathered = lax.all_gather(kv, "seq", axis=0)
        docs = jnp.stack([doc_place ^ m for m in masks]).astype(jnp.int32)
        mixed = attend(places, docs, vertical_blocks, slash_offsets, queries, gathered)
        for lane, mask in enumerate(masks):
            pieces[mask] = mixed[lane] if mask == 0 else swap(mixed[lane], "doc", mask)
    return assemble(places, [pieces[m] for m in order])


def solution(mesh):
    return jax.shard_map(
        local,
        mesh=mesh,
        in_specs=(
            P("doc", "seq", None),
            P(),
            P(None, "doc"),
            P(None, "doc"),
            P(None, "doc"),
            P(),
            P(),
        ),
        out_specs=P("doc", "seq", None),
        check_vma=False,
    )
```

```python
import functools

import jax
import jax.numpy as jnp
from jax import lax
from jax.experimental import pallas as pl
from jax.experimental.pallas import tpu as pltpu
from jax.sharding import PartitionSpec as P

HEAD_WIDTH = 128
QUERY_HEADS = 16
KEY_VALUE_HEADS = 4
QUERY_GROUP = QUERY_HEADS // KEY_VALUE_HEADS
EPSILON = 1e-05


def swap(value, axis, mask):
    count = lax.axis_size(axis)
    return lax.ppermute(value, axis, [(source, source ^ mask) for source in range(count)])


def rope_table(positions, width):
    inverse = jnp.power(jnp.float32(500000.0), -jnp.arange(0, width, 2, dtype=jnp.float32) / width)
    angles = positions.astype(jnp.float32)[:, None] * inverse[None, :]
    return (jnp.cos(angles), jnp.sin(angles))


def project_kernel(lanes, *refs):
    token_refs = refs[:lanes]
    gain_ref, wq_ref, wk_ref, wv_ref, table_ref, q_ref, kv_ref, normed = refs[lanes:]
    rows, width = token_refs[0].shape[1:]
    heads = wk_ref.shape[1] // HEAD_WIDTH
    band = 16
    deep = min(1024, width)

    for lane in range(lanes):

        def norm_band(index, carry):
            at = pl.ds(pl.multiple_of(index * band, band), band)
            wide = token_refs[lane][0, at, :].astype(jnp.float32)
            scale = lax.rsqrt(jnp.mean(wide * wide, axis=-1, keepdims=True) + EPSILON)
            normed[pl.ds(pl.multiple_of(lane * rows + index * band, band), band), :] = (
                wide * scale * gain_ref[...]
            ).astype(jnp.bfloat16)
            return carry

        lax.fori_loop(0, rows // band, norm_band, 0, unroll=2)

    half = HEAD_WIDTH // 2
    cosine = table_ref[:, :HEAD_WIDTH]
    sine = table_ref[:, HEAD_WIDTH:]

    def rotate(value):
        turned = jnp.concatenate([value[:, half:], value[:, :half]], axis=1)
        return (value * cosine + turned * sine).astype(jnp.bfloat16)

    def multiply(weight_of):
        total = None
        for start in range(0, width, deep):
            part = jnp.dot(
                normed[:, start:start + deep],
                weight_of(slice(start, start + deep)),
                preferred_element_type=jnp.float32,
            )
            total = part if total is None else total + part
        return total

    for head in range(heads):
        at = slice(head * HEAD_WIDTH, (head + 1) * HEAD_WIDTH)
        both = multiply(lambda k: jnp.concatenate([wk_ref[k, at], wv_ref[k, at]], axis=1))
        for lane in range(lanes):
            mine = both[lane * rows:(lane + 1) * rows]
            out = 2 * head * HEAD_WIDTH
            kv_ref[lane, :, out:out + HEAD_WIDTH] = rotate(mine[:, :HEAD_WIDTH])
            kv_ref[lane, :, out + HEAD_WIDTH:out + 2 * HEAD_WIDTH] = mine[:, HEAD_WIDTH:].astype(
                jnp.bfloat16
            )
    pair = 2 * HEAD_WIDTH
    for start in range(0, wq_ref.shape[1], pair):
        both = multiply(lambda k: wq_ref[k, start:start + pair])
        for lane in range(lanes):
            for at in (0, HEAD_WIDTH):
                q_ref[lane, :, start + at:start + at + HEAD_WIDTH] = rotate(
                    both[lane * rows:(lane + 1) * rows, at:at + HEAD_WIDTH]
                )


def project(tokens, gain, w_query, key_weight, value_weight, table):
    lanes = len(tokens)
    rows, width = tokens[0].shape[1:]
    q_cols, k_cols = w_query.shape[1], key_weight.shape[1]
    total = lanes * rows
    vmem = pl.BlockSpec(memory_space=pltpu.VMEM)
    return pl.pallas_call(
        functools.partial(project_kernel, lanes),
        in_specs=[vmem] * (lanes + 5),
        out_specs=[vmem] * 2,
        out_shape=[
            jax.ShapeDtypeStruct((lanes, rows, q_cols), jnp.bfloat16),
            jax.ShapeDtypeStruct((lanes, rows, 2 * k_cols), jnp.bfloat16),
        ],
        scratch_shapes=[pltpu.VMEM((total, width), jnp.bfloat16)],
        compiler_params=pltpu.CompilerParams(vmem_limit_bytes=28 * 1024 * 1024),
        cost_estimate=pl.CostEstimate(
            flops=2 * total * width * (q_cols + 2 * k_cols),
            bytes_accessed=2 * width * (q_cols + 2 * k_cols) + 2 * total * width,
            transcendentals=0,
        ),
        name="project",
    )(*tokens, gain, w_query, key_weight, value_weight, table)


def attend_kernel(lanes, pieces, chunks, place_ref, docs_ref, vertical_ref, offset_ref, q_ref, *refs):
    kv_refs, out_ref = refs[:-1], refs[-1]
    rows = q_ref.shape[1]
    heads = kv_refs[0].shape[2] // (2 * HEAD_WIDTH)
    place = place_ref[0]
    group_place = place_ref[1]
    rank = QUERY_GROUP * rows
    span = len(pieces) * rows
    factor = HEAD_WIDTH ** (-0.5)
    query_at = place * rows + lax.broadcasted_iota(jnp.int32, (rows, rows), 0)
    key_at = lax.broadcasted_iota(jnp.int32, (rows, rows), 1)

    def block_allowed(doc, group, block):
        found = (block == place) | (block == place - 1)
        for s in range(offset_ref.shape[2]):
            found = found | (block == place - offset_ref[doc, group, s])
        for s in range(vertical_ref.shape[2]):
            found = found | ((block == vertical_ref[doc, group, s]) & (block < place - 1))
        return found & (block >= 0)

    for lane in range(lanes):
        doc = docs_ref[lane]
        for head in range(heads):
            group = group_place * heads + head
            at = head * QUERY_GROUP * HEAD_WIDTH
            queries = jnp.concatenate(
                [
                    q_ref[lane, :, at + h * HEAD_WIDTH:at + (h + 1) * HEAD_WIDTH]
                    for h in range(QUERY_GROUP)
                ],
                axis=0,
            )
            key_cols = pl.ds(2 * head * HEAD_WIDTH, HEAD_WIDTH)
            value_cols = pl.ds((2 * head + 1) * HEAD_WIDTH, HEAD_WIDTH)

            def step(index, carry):
                highest, total, mixed = carry
                found = [piece(place, index, lanes) for piece in pieces]
                keys = jnp.concatenate([kv_refs[r][i + lane, :, key_cols] for r, i, _ in found], axis=0)
                values = jnp.concatenate([kv_refs[r][i + lane, :, value_cols] for r, i, _ in found], axis=0)
                scores = lax.dot_general(
                    queries, keys, (((1,), (1,)), ((), ())), preferred_element_type=jnp.float32
                ) * factor
                bias = jnp.concatenate(
                    [
                        jnp.where(
                            (key_at + block * rows <= query_at) & block_allowed(doc, group, block),
                            jnp.float32(0),
                            -jnp.inf,
                        )
                        for _, _, block in found
                    ],
                    axis=1,
                )
                scores = (scores.reshape(QUERY_GROUP, rows, span) + bias[None]).reshape(rank, span)
                top = jnp.max(scores, axis=1, keepdims=True)
                if chunks > 1:
                    fresh = jnp.maximum(highest, top)
                    safe = jnp.where(fresh == -jnp.inf, jnp.float32(0), fresh)
                    fade = jnp.exp(highest - safe)
                else:
                    fresh = safe = top
                raised = jnp.exp(scores - safe)
                part = jnp.sum(raised, axis=1, keepdims=True)
                product = jnp.dot(
                    raised.astype(jnp.bfloat16), values, preferred_element_type=jnp.float32
                )
                if chunks > 1:
                    return fresh, total * fade + part, mixed * fade + product
                return fresh, part, product

            initial = (
                jnp.full((rank, 1), -jnp.inf, jnp.float32),
                jnp.zeros((rank, 1), jnp.float32),
                jnp.zeros((rank, HEAD_WIDTH), jnp.float32),
            )
            if chunks > 1:
                _, total, mixed = lax.fori_loop(0, chunks, step, initial)
            else:
                _, total, mixed = step(0, initial)
            result = (mixed / total).astype(jnp.bfloat16)
            for h in range(QUERY_GROUP):
                out_ref[lane, :, at + h * HEAD_WIDTH:at + (h + 1) * HEAD_WIDTH] = result[
                    h * rows:(h + 1) * rows
                ]


def attend(place, docs, vertical, offsets, queries, spread):
    arrays, pieces, chunks = spread
    lanes, rows, q_cols = queries.shape
    span = len(pieces) * chunks * rows
    smem = pl.BlockSpec(memory_space=pltpu.SMEM)
    vmem = pl.BlockSpec(memory_space=pltpu.VMEM)
    return pl.pallas_call(
        functools.partial(attend_kernel, lanes, pieces, chunks),
        in_specs=[smem] * 4 + [vmem] * (1 + len(arrays)),
        out_specs=vmem,
        out_shape=jax.ShapeDtypeStruct(queries.shape, jnp.bfloat16),
        compiler_params=pltpu.CompilerParams(vmem_limit_bytes=28 * 1024 * 1024),
        cost_estimate=pl.CostEstimate(
            flops=4 * lanes * rows * q_cols * span,
            bytes_accessed=2 * sum(a.size for a in arrays) + 4 * queries.size,
            transcendentals=lanes * rows * span * q_cols // HEAD_WIDTH,
        ),
        name="attend",
    )(place, docs, vertical, offsets, queries, *arrays)


def spread_blocks(kv):
    count = lax.axis_size("seq")
    if count > 8 or count % 2:
        chunk = 8 if count % 8 == 0 else 1
        lanes = kv.shape[0]
        gathered = lax.all_gather(kv, "seq", axis=0, tiled=True)

        def inside(j):
            return lambda place, index, lanes: (
                0,
                (index * chunk + j) * lanes,
                index * chunk + j,
            )

        return [gathered], [inside(j) for j in range(chunk)], count // chunk

    def apart(r, flip, back):
        return lambda place, index, lanes: (r, 0, (place ^ flip) - back)

    arrays, pieces = [], []
    held = kv
    for back in range(0, count, 2):
        if back:
            held = lax.ppermute(held, "seq", [(s, s + 2) for s in range(back - 2, count - 2)])
        pairs = [(s, s ^ 1) for s in range(back, count) if back or s % 2 == 0]
        other = lax.ppermute(held, "seq", pairs)
        for flip, value in ((0, held), (1, other)):
            pieces.append(apart(len(arrays), flip, back))
            arrays.append(value)
    return arrays, pieces, 1


def assemble_kernel(place_ref, *refs):
    out_ref = refs[-1]
    cols = refs[0].shape[1]
    for mask, piece in enumerate(refs[:-1]):
        at = pl.multiple_of((place_ref[1] ^ mask) * cols, cols)
        out_ref[0, :, pl.ds(at, cols)] = piece[...]


def assemble(place, pieces):
    rows, cols = pieces[0].shape
    smem = pl.BlockSpec(memory_space=pltpu.SMEM)
    vmem = pl.BlockSpec(memory_space=pltpu.VMEM)
    return pl.pallas_call(
        assemble_kernel,
        in_specs=[smem] + [vmem] * len(pieces),
        out_specs=vmem,
        out_shape=jax.ShapeDtypeStruct((1, rows, cols * len(pieces)), jnp.bfloat16),
        compiler_params=pltpu.CompilerParams(vmem_limit_bytes=16 * 1024 * 1024),
        name="assemble",
    )(place, *pieces)


def local(tokens, norm_gain, w_query, key_weight, value_weight, vertical_blocks, slash_offsets):
    _, rows, width = tokens.shape
    doc_count = lax.axis_size("doc")
    place = lax.axis_index("seq")
    doc_place = lax.axis_index("doc")
    places = jnp.stack([place, doc_place]).astype(jnp.int32)
    cosine, sine = rope_table(place * rows + jnp.arange(rows, dtype=jnp.int32), HEAD_WIDTH)
    table = jnp.concatenate([cosine, cosine, -sine, sine], axis=1)
    gain = norm_gain.reshape(1, width)

    held = {0: tokens}
    half = doc_count // 2
    if half > 1:
        held[half] = swap(tokens, "doc", half)
    bit = 1
    while bit < max(half, 2) and bit < doc_count:
        for mask in list(held):
            if mask & bit == 0 and (mask | bit) not in held:
                held[mask | bit] = swap(held[mask], "doc", bit)
        bit *= 2
    order = sorted(held)
    groups = [order[:half], order[half:]] if half else [order]

    pieces = {}
    for masks in groups:
        queries, kv = project([held[m] for m in masks], gain, w_query, key_weight, value_weight, table)
        spread = spread_blocks(kv)
        docs = jnp.stack([doc_place ^ m for m in masks]).astype(jnp.int32)
        mixed = attend(places, docs, vertical_blocks, slash_offsets, queries, spread)
        for lane, mask in enumerate(masks):
            pieces[mask] = mixed[lane] if mask == 0 else swap(mixed[lane], "doc", mask)
    return assemble(places, [pieces[m] for m in order])


def solution(mesh):
    return jax.shard_map(
        local,
        mesh=mesh,
        in_specs=(
            P("doc", "seq", None),
            P(),
            P(None, "doc"),
            P(None, "doc"),
            P(None, "doc"),
            P(),
            P(),
        ),
        out_specs=P("doc", "seq", None),
        check_vma=False,
    )
```

```python
import functools

import jax
import jax.numpy as jnp
from jax import lax
from jax.experimental import pallas as pl
from jax.experimental.pallas import tpu as pltpu
from jax.sharding import PartitionSpec as P

HEAD_WIDTH = 128
QUERY_HEADS = 16
KEY_VALUE_HEADS = 4
QUERY_GROUP = QUERY_HEADS // KEY_VALUE_HEADS
EPSILON = 1e-05
BAND = 16
MIB = 1024 * 1024

SMEM = pl.BlockSpec(memory_space=pltpu.SMEM)
VMEM = pl.BlockSpec(memory_space=pltpu.VMEM)
ANYWHERE = pl.BlockSpec(memory_space=pl.ANY)
HBM = pl.BlockSpec(memory_space=pltpu.HBM)


def swap(value, axis, mask):
    count = lax.axis_size(axis)
    return lax.ppermute(value, axis, [(source, source ^ mask) for source in range(count)])


def after(value, *others):
    return lax.optimization_barrier((value,) + others)[0]


def rope_table(positions, width):
    inverse = jnp.power(jnp.float32(500000.0), -jnp.arange(0, width, 2, dtype=jnp.float32) / width)
    angles = positions.astype(jnp.float32)[:, None] * inverse[None, :]
    return (jnp.cos(angles), jnp.sin(angles))


def project_kernel(places, table_rows, early, core_ref, *refs):
    token_refs = refs[:len(places)]
    refs = refs[len(places):]
    gain_ref, wq_ref, wk_ref, wv_ref, table_ref, q_ref, kv_ref, normed = refs[:8]
    core = core_ref[0]
    width = gain_ref.shape[1]
    heads = wk_ref.shape[1] // HEAD_WIDTH
    deep = min(1024, width)
    copies = []
    if early:
        sources = (wk_ref, wv_ref, wq_ref)
        wk_ref, wv_ref, wq_ref, sems = refs[8:]
        for at, (source, target) in enumerate(zip(sources, (wk_ref, wv_ref, wq_ref))):
            copies.append(pltpu.make_async_copy(source, target, sems.at[at]))
            copies[-1].start()

    for piece, place in enumerate(places):
        first = place(core)
        ref = token_refs[piece]

        def norm_band(index, carry, ref=ref, first=first):
            at = pl.ds(pl.multiple_of(index * BAND, BAND), BAND)
            wide = ref[at, :].astype(jnp.float32)
            scale = lax.rsqrt(jnp.mean(wide * wide, axis=-1, keepdims=True) + EPSILON)
            normed[pl.ds(pl.multiple_of(first + index * BAND, BAND), BAND), :] = (
                wide * scale * gain_ref[...]
            ).astype(jnp.bfloat16)
            return carry

        lax.fori_loop(0, ref.shape[0] // BAND, norm_band, 0, unroll=2)

    half = HEAD_WIDTH // 2

    def rotate(value, rows):
        cosine = table_ref[rows, :HEAD_WIDTH]
        sine = table_ref[rows, HEAD_WIDTH:]
        turned = jnp.concatenate([value[:, half:], value[:, :half]], axis=1)
        return (value * cosine + turned * sine).astype(jnp.bfloat16)

    def multiply(weight_of):
        total = None
        for start in range(0, width, deep):
            part = jnp.dot(
                normed[:, start:start + deep],
                weight_of(slice(start, start + deep)),
                preferred_element_type=jnp.float32,
            )
            total = part if total is None else total + part
        return total

    if early:
        copies[0].wait()
        copies[1].wait()
    for head in range(heads):
        at = slice(head * HEAD_WIDTH, (head + 1) * HEAD_WIDTH)
        both = multiply(lambda k: jnp.concatenate([wk_ref[k, at], wv_ref[k, at]], axis=1))
        out = 2 * head * HEAD_WIDTH
        row = 0
        for begin, count in table_rows:
            mine = both[row:row + count]
            kv_ref[row:row + count, out:out + HEAD_WIDTH] = rotate(
                mine[:, :HEAD_WIDTH], slice(begin, begin + count)
            )
            kv_ref[row:row + count, out + HEAD_WIDTH:out + 2 * HEAD_WIDTH] = mine[
                :, HEAD_WIDTH:
            ].astype(jnp.bfloat16)
            row += count
    if early:
        copies[2].wait()
    pair = 2 * HEAD_WIDTH
    for start in range(0, wq_ref.shape[1], pair):
        both = multiply(lambda k: wq_ref[k, start:start + pair])
        row = 0
        for begin, count in table_rows:
            for at in (0, HEAD_WIDTH):
                q_ref[row:row + count, start + at:start + at + HEAD_WIDTH] = rotate(
                    both[row:row + count, at:at + HEAD_WIDTH], slice(begin, begin + count)
                )
            row += count


def project(core, pieces, places, table_rows, gain, w_query, key_weight, value_weight, table, early):
    width = gain.shape[1]
    q_cols, k_cols = w_query.shape[1], key_weight.shape[1]
    total = sum(count for _, count in table_rows)
    scratch = [pltpu.VMEM((total, width), jnp.bfloat16)]
    if early:
        scratch += [pltpu.VMEM((width, cols), jnp.bfloat16) for cols in (k_cols, k_cols, q_cols)]
        scratch.append(pltpu.SemaphoreType.DMA((3,)))
    weights = HBM if early else VMEM
    return pl.pallas_call(
        functools.partial(project_kernel, places, table_rows, early),
        in_specs=[SMEM] + [VMEM] * (len(pieces) + 1) + [weights] * 3 + [VMEM],
        out_specs=[VMEM] * 2,
        out_shape=[
            jax.ShapeDtypeStruct((total, q_cols), jnp.bfloat16),
            jax.ShapeDtypeStruct((total, 2 * k_cols), jnp.bfloat16),
        ],
        scratch_shapes=scratch,
        compiler_params=pltpu.CompilerParams(vmem_limit_bytes=28 * MIB),
        cost_estimate=pl.CostEstimate(
            flops=2 * total * width * (q_cols + 2 * k_cols),
            bytes_accessed=2 * width * (q_cols + 2 * k_cols) + 2 * total * width,
            transcendentals=0,
        ),
        name="project",
    )(core, *pieces, gain, w_query, key_weight, value_weight, table)


def pick_kernel(begin, core_ref, own_ref, twin_ref, first_ref, second_ref, sems):
    count = first_ref.shape[0]
    for core in range(2):

        @pl.when(core_ref[0] == core)
        def _(core=core):
            rows = pl.ds(begin + core * count, count)
            mine = pltpu.make_async_copy(own_ref.at[rows], (first_ref, second_ref)[core], sems.at[0])
            other = pltpu.make_async_copy(
                twin_ref.at[rows], (second_ref, first_ref)[core], sems.at[1]
            )
            mine.start()
            other.start()
            mine.wait()
            other.wait()


def pick(core, own, twin, begin):
    rows, width = own.shape
    shape = jax.ShapeDtypeStruct(((rows - begin) // 2, width), own.dtype)
    return pl.pallas_call(
        functools.partial(pick_kernel, begin),
        in_specs=[SMEM, ANYWHERE, ANYWHERE],
        out_specs=[VMEM] * 2,
        out_shape=[shape] * 2,
        scratch_shapes=[pltpu.SemaphoreType.DMA((2,))],
        compiler_params=pltpu.CompilerParams(vmem_limit_bytes=16 * MIB),
        name="pick",
    )(core, own, twin)


def spread_blocks(kv):
    count = lax.axis_size("seq")
    total = kv.shape[0]
    if count > 8 or count % 2:
        chunk = 8 if count % 8 == 0 else 1
        gathered = lax.all_gather(kv, "seq", axis=0, tiled=True)

        def inside(j):
            return lambda place, index: (
                0,
                pl.multiple_of((index * chunk + j) * total, BAND),
                index * chunk + j,
            )

        return [gathered], [inside(j) for j in range(chunk)], count // chunk

    def apart(r, flip, back):
        return lambda place, index: (r, 0, (place ^ flip) - back)

    arrays, slots = [], []
    held = kv
    for back in range(0, count, 2):
        ahead = None
        if back + 2 < count:
            ahead = lax.ppermute(held, "seq", [(s, (s + 2) % count) for s in range(count)])
        for flip, value in ((0, held), (1, swap(held, "seq", 1))):
            slots.append(apart(len(arrays), flip, back))
            arrays.append(value)
        held = ahead
    return arrays, slots, 1


def attend_kernel(lanes, spreads, q_count, place_ref, docs_ref, vertical_ref, offset_ref, *refs):
    q_refs = refs[:q_count]
    kv_refs, at = [], q_count
    for arrays, _, _ in spreads:
        kv_refs.append(refs[at:at + arrays])
        at += arrays
    out_refs = refs[at:]
    slots, chunks = spreads[0][1], spreads[0][2]
    heads = kv_refs[0][0].shape[1] // (2 * HEAD_WIDTH)
    rows = out_refs[0].shape[0]
    place = place_ref[0]
    group_place = place_ref[1]
    rank = QUERY_GROUP * rows
    span = len(slots) * rows
    factor = HEAD_WIDTH ** (-0.5)
    query_at = place * rows + lax.broadcasted_iota(jnp.int32, (rows, rows), 0)
    key_at = lax.broadcasted_iota(jnp.int32, (rows, rows), 1)

    def block_allowed(doc, group, block):
        found = (block == place) | (block == place - 1)
        for s in range(offset_ref.shape[2]):
            found = found | (block == place - offset_ref[doc, group, s])
        for s in range(vertical_ref.shape[2]):
            found = found | ((block == vertical_ref[doc, group, s]) & (block < place - 1))
        return found & (block >= 0)

    for lane, segments in enumerate(lanes):
        doc = docs_ref[lane]
        for head in range(heads):
            group = group_place * heads + head
            queries = jnp.concatenate(
                [
                    q_refs[source][
                        start:start + count,
                        (head * QUERY_GROUP + h) * HEAD_WIDTH:(head * QUERY_GROUP + h + 1) * HEAD_WIDTH,
                    ]
                    for h in range(QUERY_GROUP)
                    for source, start, count in segments
                ],
                axis=0,
            )

            def column(index, at):
                cols = slice(at * HEAD_WIDTH, (at + 1) * HEAD_WIDTH)
                parts = []
                for number in range(len(slots)):
                    for source, start, count in segments:
                        r, first, _ = spreads[source][1][number](place, index)
                        if isinstance(first, int):
                            where = slice(first + start, first + start + count)
                        else:
                            where = pl.ds(pl.multiple_of(first + start, BAND), count)
                        parts.append(kv_refs[source][r][where, cols])
                return jnp.concatenate(parts, axis=0)

            def step(index, carry):
                highest, total, mixed = carry
                keys, values = column(index, 2 * head), column(index, 2 * head + 1)
                scores = lax.dot_general(
                    queries, keys, (((1,), (1,)), ((), ())), preferred_element_type=jnp.float32
                ) * factor
                bias = []
                for slot in slots:
                    block = slot(place, index)[2]
                    bias.append(
                        jnp.where(
                            (key_at + block * rows <= query_at) & block_allowed(doc, group, block),
                            jnp.float32(0),
                            -jnp.inf,
                        )
                    )
                bias = jnp.concatenate(bias, axis=1)
                scores = (scores.reshape(QUERY_GROUP, rows, span) + bias[None]).reshape(rank, span)
                top = jnp.max(scores, axis=1, keepdims=True)
                if chunks > 1:
                    fresh = jnp.maximum(highest, top)
                    safe = jnp.where(fresh == -jnp.inf, jnp.float32(0), fresh)
                    fade = jnp.exp(highest - safe)
                else:
                    fresh = safe = top
                raised = jnp.exp(scores - safe)
                part = jnp.sum(raised, axis=1, keepdims=True)
                product = jnp.dot(
                    raised.astype(jnp.bfloat16), values, preferred_element_type=jnp.float32
                )
                if chunks > 1:
                    return fresh, total * fade + part, mixed * fade + product
                return fresh, part, product

            initial = (
                jnp.full((rank, 1), -jnp.inf, jnp.float32),
                jnp.zeros((rank, 1), jnp.float32),
                jnp.zeros((rank, HEAD_WIDTH), jnp.float32),
            )
            if chunks > 1:
                _, total, mixed = lax.fori_loop(0, chunks, step, initial)
            else:
                _, total, mixed = step(0, initial)
            result = (mixed / total).astype(jnp.bfloat16)
            for h in range(QUERY_GROUP):
                cols = slice(
                    (head * QUERY_GROUP + h) * HEAD_WIDTH, (head * QUERY_GROUP + h + 1) * HEAD_WIDTH
                )
                out_refs[lane][:, cols] = result[h * rows:(h + 1) * rows]


def attend(place, docs, vertical, offsets, lanes, queries, spreads):
    q_cols = queries[0].shape[1]
    rows = sum(count for _, _, count in lanes[0])
    slots, chunks = spreads[0][1:]
    span = len(slots) * chunks * rows
    arrays = [array for spread in spreads for array in spread[0]]
    layout = [(len(spread[0]), spread[1], spread[2]) for spread in spreads]
    return pl.pallas_call(
        functools.partial(attend_kernel, lanes, layout, len(queries)),
        in_specs=[SMEM] * 4 + [VMEM] * (len(queries) + len(arrays)),
        out_specs=[VMEM] * len(lanes),
        out_shape=[jax.ShapeDtypeStruct((rows, q_cols), jnp.bfloat16)] * len(lanes),
        compiler_params=pltpu.CompilerParams(vmem_limit_bytes=28 * MIB),
        cost_estimate=pl.CostEstimate(
            flops=4 * len(lanes) * rows * q_cols * span,
            bytes_accessed=2 * sum(a.size for a in arrays) + 4 * len(lanes) * rows * q_cols,
            transcendentals=len(lanes) * rows * span * q_cols // HEAD_WIDTH,
        ),
        name="attend",
    )(place, docs, vertical, offsets, *queries, *arrays)


def assemble_kernel(place_ref, own_ref, twin_ref, straight0, crossed0, straight1, crossed1, out_ref):
    me = place_ref[1]
    cols = own_ref.shape[1]

    def put(mask, ref):
        out_ref[0, :, pl.ds(pl.multiple_of((me ^ mask) * cols, cols), cols)] = ref[...]

    put(0, own_ref)
    put(1, twin_ref)

    @pl.when(me % 2 == 0)
    def _():
        put(2, straight0)
        put(3, crossed0)

    @pl.when(me % 2 == 1)
    def _():
        put(2, straight1)
        put(3, crossed1)


def assemble(place, *pieces):
    rows, cols = pieces[0].shape
    return pl.pallas_call(
        assemble_kernel,
        in_specs=[SMEM] + [VMEM] * len(pieces),
        out_specs=VMEM,
        out_shape=jax.ShapeDtypeStruct((1, rows, 4 * cols), jnp.bfloat16),
        compiler_params=pltpu.CompilerParams(vmem_limit_bytes=16 * MIB),
        name="assemble",
    )(place, *pieces)


def local(tokens, norm_gain, w_query, key_weight, value_weight, vertical_blocks, slash_offsets):
    _, rows, width = tokens.shape
    doc_count = lax.axis_size("doc")
    assert doc_count == 4
    place = lax.axis_index("seq")
    doc_place = lax.axis_index("doc")
    core = (doc_place % 2).astype(jnp.int32)[None]
    places = jnp.stack([place, doc_place]).astype(jnp.int32)
    cosine, sine = rope_table(place * rows + jnp.arange(rows, dtype=jnp.int32), HEAD_WIDTH)
    table = jnp.concatenate([cosine, cosine, -sine, sine], axis=1)
    own = tokens[0]
    params = (norm_gain.reshape(1, width), w_query, key_weight, value_weight, table)
    head = rows // 4 // BAND * BAND
    rest = (rows - head) // 2
    remote = doc_place ^ 2

    def documents(*docs):
        return jnp.stack(docs).astype(jnp.int32)

    twin = swap(own, "doc", 1)
    lead = swap(own[:head], "doc", 2)
    q_near, kv_near = project(
        core,
        [own, twin],
        [lambda c: 0, lambda c: rows],
        [(0, rows), (0, rows)],
        *params,
        early=True,
    )
    near = spread_blocks(kv_near)

    send_first, send_second = pick(core, own, twin, head)
    got_first = swap(after(send_first, lead), "doc", 2)
    lead_twin = swap(lead, "doc", 1)

    got_second = swap(after(send_second, got_first), "doc", 2)
    got_first_twin = swap(got_first, "doc", 1)
    q_first, kv_first = project(
        core,
        [lead, lead_twin, got_first, got_first_twin],
        [
            lambda c: c * rows,
            lambda c: (1 - c) * rows,
            lambda c: head + c * rest,
            lambda c: head + (1 - c) * rest,
        ],
        [(0, rows), (0, head)],
        *params,
        early=False,
    )
    first = spread_blocks(kv_first)
    mixed_own, mixed_twin = attend(
        places,
        documents(doc_place, doc_place ^ 1),
        vertical_blocks,
        slash_offsets,
        [[(0, 0, rows)], [(0, rows, rows)]],
        [q_near],
        [near],
    )
    out_twin = swap(mixed_twin, "doc", 1)

    got_second_twin = swap(got_second, "doc", 1)
    q_second, kv_second = project(
        core,
        [got_second, got_second_twin],
        [lambda c: c * rest, lambda c: (1 - c) * rest],
        [(head, rows - head)],
        *params,
        early=False,
    )
    second = spread_blocks(kv_second)
    (mixed_first,) = attend(
        places,
        documents(remote & ~1),
        vertical_blocks,
        slash_offsets,
        [[(0, 0, rows)]],
        [q_first],
        [first],
    )
    (mixed_second,) = attend(
        places,
        documents(remote | 1),
        vertical_blocks,
        slash_offsets,
        [[(0, rows, head), (1, 0, rows - head)]],
        [q_first, q_second],
        [first, second],
    )

    def home(mixed, target):
        straight = lax.ppermute(mixed, "doc", [(target ^ 2, target), (target, target ^ 2)])
        crossed = lax.ppermute(mixed, "doc", [(target ^ 3, target), (target ^ 1, target ^ 2)])
        return straight, crossed

    return assemble(
        places, mixed_own, out_twin, *home(mixed_first, 0), *home(mixed_second, 1)
    )


def solution(mesh):
    return jax.shard_map(
        local,
        mesh=mesh,
        in_specs=(
            P("doc", "seq", None),
            P(),
            P(None, "doc"),
            P(None, "doc"),
            P(None, "doc"),
            P(),
            P(),
        ),
        out_specs=P("doc", "seq", None),
        check_vma=False,
    )
```

```python
import functools

import jax
import jax.numpy as jnp
from jax import lax
from jax.experimental import pallas as pl
from jax.experimental.pallas import tpu as pltpu
from jax.sharding import PartitionSpec as P

HEAD_WIDTH = 128
QUERY_HEADS = 16
KEY_VALUE_HEADS = 4
QUERY_GROUP = QUERY_HEADS // KEY_VALUE_HEADS
EPSILON = 1e-05
BAND = 16
MIB = 1024 * 1024

SMEM = pl.BlockSpec(memory_space=pltpu.SMEM)
VMEM = pl.BlockSpec(memory_space=pltpu.VMEM)
ANYWHERE = pl.BlockSpec(memory_space=pl.ANY)
HBM = pl.BlockSpec(memory_space=pltpu.HBM)


def swap(value, axis, mask):
    count = lax.axis_size(axis)
    return lax.ppermute(value, axis, [(source, source ^ mask) for source in range(count)])


def after(value, *others):
    return lax.optimization_barrier((value,) + others)[0]


def in_hbm(array):
    return pltpu.with_memory_space_constraint(array, pltpu.HBM)


def rope_table(positions, width):
    inverse = jnp.power(jnp.float32(500000.0), -jnp.arange(0, width, 2, dtype=jnp.float32) / width)
    angles = positions.astype(jnp.float32)[:, None] * inverse[None, :]
    return (jnp.cos(angles), jnp.sin(angles))


def project_kernel(places, table_rows, early, info_ref, *refs):
    token_refs = list(refs[:len(places)])
    refs = refs[len(places):]
    gain_ref, wq_ref, wk_ref, wv_ref, table_ref, q_ref, kv_ref, normed = refs[:8]
    core = info_ref[1] % 2
    width = gain_ref.shape[1]
    heads = wk_ref.shape[1] // HEAD_WIDTH
    deep = min(1024, width)
    copies = []
    if early:
        sources = (gain_ref, token_refs[0], wk_ref, wv_ref, wq_ref)
        held, sems = refs[8:13], refs[13]
        gain_ref, token_refs[0], wk_ref, wv_ref, wq_ref = held
        for at, (source, target) in enumerate(zip(sources, held)):
            copies.append(pltpu.make_async_copy(source, target, sems.at[at]))
            copies[-1].start()
        copies[0].wait()
        copies[1].wait()

    for piece, place in enumerate(places):
        first = place(core)
        ref = token_refs[piece]

        def norm_band(index, carry, ref=ref, first=first):
            at = pl.ds(pl.multiple_of(index * BAND, BAND), BAND)
            wide = ref[at, :].astype(jnp.float32)
            scale = lax.rsqrt(jnp.mean(wide * wide, axis=-1, keepdims=True) + EPSILON)
            normed[pl.ds(pl.multiple_of(first + index * BAND, BAND), BAND), :] = (
                wide * scale * gain_ref[...]
            ).astype(jnp.bfloat16)
            return carry

        lax.fori_loop(0, ref.shape[0] // BAND, norm_band, 0, unroll=2)

    half = HEAD_WIDTH // 2

    def rotate(value, rows):
        cosine = table_ref[rows, :HEAD_WIDTH]
        sine = table_ref[rows, HEAD_WIDTH:]
        turned = jnp.concatenate([value[:, half:], value[:, :half]], axis=1)
        return (value * cosine + turned * sine).astype(jnp.bfloat16)

    def multiply(weight_of):
        total = None
        for start in range(0, width, deep):
            part = jnp.dot(
                normed[:, start:start + deep],
                weight_of(slice(start, start + deep)),
                preferred_element_type=jnp.float32,
            )
            total = part if total is None else total + part
        return total

    if early:
        copies[2].wait()
        copies[3].wait()
    for head in range(heads):
        at = slice(head * HEAD_WIDTH, (head + 1) * HEAD_WIDTH)
        both = multiply(lambda k: jnp.concatenate([wk_ref[k, at], wv_ref[k, at]], axis=1))
        out = 2 * head * HEAD_WIDTH
        row = 0
        for begin, count in table_rows:
            mine = both[row:row + count]
            kv_ref[row:row + count, out:out + HEAD_WIDTH] = rotate(
                mine[:, :HEAD_WIDTH], slice(begin, begin + count)
            )
            kv_ref[row:row + count, out + HEAD_WIDTH:out + 2 * HEAD_WIDTH] = mine[
                :, HEAD_WIDTH:
            ].astype(jnp.bfloat16)
            row += count
    if early:
        copies[4].wait()
    pair = 2 * HEAD_WIDTH
    for start in range(0, wq_ref.shape[1], pair):
        both = multiply(lambda k: wq_ref[k, start:start + pair])
        row = 0
        for begin, count in table_rows:
            for at in (0, HEAD_WIDTH):
                q_ref[row:row + count, start + at:start + at + HEAD_WIDTH] = rotate(
                    both[row:row + count, at:at + HEAD_WIDTH], slice(begin, begin + count)
                )
            row += count


def project(info, pieces, places, table_rows, gain, w_query, key_weight, value_weight, table, early):
    width = gain.shape[1]
    q_cols, k_cols = w_query.shape[1], key_weight.shape[1]
    total = sum(count for _, count in table_rows)
    params = (gain, w_query, key_weight, value_weight)
    scratch = [pltpu.VMEM((total, width), jnp.bfloat16)]
    kind = [VMEM] * (len(pieces) + len(params))
    if early:
        held = (gain, pieces[0], key_weight, value_weight, w_query)
        scratch += [pltpu.VMEM(array.shape, array.dtype) for array in held]
        scratch.append(pltpu.SemaphoreType.DMA((len(held),)))
        params = tuple(in_hbm(array) for array in params)
        pieces = [in_hbm(pieces[0])] + list(pieces[1:])
        kind = [HBM] + [VMEM] * (len(pieces) - 1) + [HBM] * len(params)
    return pl.pallas_call(
        functools.partial(project_kernel, places, table_rows, early),
        in_specs=[SMEM] + kind + [VMEM],
        out_specs=[VMEM] * 2,
        out_shape=[
            jax.ShapeDtypeStruct((total, q_cols), jnp.bfloat16),
            jax.ShapeDtypeStruct((total, 2 * k_cols), jnp.bfloat16),
        ],
        scratch_shapes=scratch,
        compiler_params=pltpu.CompilerParams(vmem_limit_bytes=28 * MIB),
        cost_estimate=pl.CostEstimate(
            flops=2 * total * width * (q_cols + 2 * k_cols),
            bytes_accessed=2 * width * (q_cols + 2 * k_cols) + 2 * total * width,
            transcendentals=0,
        ),
        name="project",
    )(info, *pieces, *params, table)


def pick_kernel(begin, info_ref, own_ref, twin_ref, first_ref, second_ref, sems):
    count = first_ref.shape[0]
    for core in range(2):

        @pl.when(info_ref[1] % 2 == core)
        def _(core=core):
            rows = pl.ds(begin + core * count, count)
            mine = pltpu.make_async_copy(own_ref.at[rows], (first_ref, second_ref)[core], sems.at[0])
            other = pltpu.make_async_copy(
                twin_ref.at[rows], (second_ref, first_ref)[core], sems.at[1]
            )
            mine.start()
            other.start()
            mine.wait()
            other.wait()


def pick(info, own, twin, begin):
    rows, width = own.shape
    shape = jax.ShapeDtypeStruct(((rows - begin) // 2, width), own.dtype)
    return pl.pallas_call(
        functools.partial(pick_kernel, begin),
        in_specs=[SMEM, HBM, VMEM],
        out_specs=[VMEM] * 2,
        out_shape=[shape] * 2,
        scratch_shapes=[pltpu.SemaphoreType.DMA((2,))],
        compiler_params=pltpu.CompilerParams(vmem_limit_bytes=16 * MIB),
        name="pick",
    )(info, in_hbm(own), twin)


def spread_blocks(kv):
    count = lax.axis_size("seq")
    total = kv.shape[0]
    if count > 8 or count % 2:
        chunk = 8 if count % 8 == 0 else 1
        gathered = lax.all_gather(kv, "seq", axis=0, tiled=True)

        def inside(j):
            return lambda place, index: (
                0,
                pl.multiple_of((index * chunk + j) * total, BAND),
                index * chunk + j,
            )

        return [gathered], [inside(j) for j in range(chunk)], count // chunk

    def apart(r, flip, back):
        return lambda place, index: (r, 0, (place ^ flip) - back)

    arrays, slots = [], []
    held = kv
    for back in range(0, count, 2):
        ahead = None
        if back + 2 < count:
            ahead = lax.ppermute(held, "seq", [(s, (s + 2) % count) for s in range(count)])
        for flip, value in ((0, held), (1, swap(held, "seq", 1))):
            slots.append(apart(len(arrays), flip, back))
            arrays.append(value)
        held = ahead
    return arrays, slots, 1


def attend_kernel(lanes, spreads, q_count, counts, info_ref, *refs):
    q_refs = refs[:q_count]
    kv_refs, at = [], q_count
    for arrays, _, _ in spreads:
        kv_refs.append(refs[at:at + arrays])
        at += arrays
    out_refs = refs[at:]
    slots, chunks = spreads[0][1], spreads[0][2]
    heads = kv_refs[0][0].shape[1] // (2 * HEAD_WIDTH)
    rows = out_refs[0].shape[0]
    place = info_ref[0]
    group_place = info_ref[1]
    groups, verticals, slashes = counts
    rank = QUERY_GROUP * rows
    span = len(slots) * rows
    factor = HEAD_WIDTH ** (-0.5)
    query_at = place * rows + lax.broadcasted_iota(jnp.int32, (rows, rows), 0)
    key_at = lax.broadcasted_iota(jnp.int32, (rows, rows), 1)
    slash_at = 2 + (info_ref.shape[0] - 2) * verticals // (verticals + slashes)

    def block_allowed(doc, group, block):
        found = (block == place) | (block == place - 1)
        pair = doc * groups + group
        for s in range(slashes):
            found = found | (block == place - info_ref[slash_at + pair * slashes + s])
        for s in range(verticals):
            found = found | ((block == info_ref[2 + pair * verticals + s]) & (block < place - 1))
        return found & (block >= 0)

    for lane, (doc_of, segments) in enumerate(lanes):
        doc = doc_of(info_ref[1])
        for head in range(heads):
            group = group_place * heads + head
            queries = jnp.concatenate(
                [
                    q_refs[source][
                        start:start + count,
                        (head * QUERY_GROUP + h) * HEAD_WIDTH:(head * QUERY_GROUP + h + 1) * HEAD_WIDTH,
                    ]
                    for h in range(QUERY_GROUP)
                    for source, start, count in segments
                ],
                axis=0,
            )

            def column(index, at):
                cols = slice(at * HEAD_WIDTH, (at + 1) * HEAD_WIDTH)
                parts = []
                for number in range(len(slots)):
                    for source, start, count in segments:
                        r, first, _ = spreads[source][1][number](place, index)
                        if isinstance(first, int):
                            where = slice(first + start, first + start + count)
                        else:
                            where = pl.ds(pl.multiple_of(first + start, BAND), count)
                        parts.append(kv_refs[source][r][where, cols])
                return jnp.concatenate(parts, axis=0)

            def step(index, carry):
                highest, total, mixed = carry
                keys, values = column(index, 2 * head), column(index, 2 * head + 1)
                scores = lax.dot_general(
                    queries, keys, (((1,), (1,)), ((), ())), preferred_element_type=jnp.float32
                ) * factor
                bias = []
                for slot in slots:
                    block = slot(place, index)[2]
                    bias.append(
                        jnp.where(
                            (key_at + block * rows <= query_at) & block_allowed(doc, group, block),
                            jnp.float32(0),
                            -jnp.inf,
                        )
                    )
                bias = jnp.concatenate(bias, axis=1)
                scores = (scores.reshape(QUERY_GROUP, rows, span) + bias[None]).reshape(rank, span)
                top = jnp.max(scores, axis=1, keepdims=True)
                if chunks > 1:
                    fresh = jnp.maximum(highest, top)
                    safe = jnp.where(fresh == -jnp.inf, jnp.float32(0), fresh)
                    fade = jnp.exp(highest - safe)
                else:
                    fresh = safe = top
                raised = jnp.exp(scores - safe)
                part = jnp.sum(raised, axis=1, keepdims=True)
                product = jnp.dot(
                    raised.astype(jnp.bfloat16), values, preferred_element_type=jnp.float32
                )
                if chunks > 1:
                    return fresh, total * fade + part, mixed * fade + product
                return fresh, part, product

            initial = (
                jnp.full((rank, 1), -jnp.inf, jnp.float32),
                jnp.zeros((rank, 1), jnp.float32),
                jnp.zeros((rank, HEAD_WIDTH), jnp.float32),
            )
            if chunks > 1:
                _, total, mixed = lax.fori_loop(0, chunks, step, initial)
            else:
                _, total, mixed = step(0, initial)
            result = (mixed / total).astype(jnp.bfloat16)
            for h in range(QUERY_GROUP):
                cols = slice(
                    (head * QUERY_GROUP + h) * HEAD_WIDTH, (head * QUERY_GROUP + h + 1) * HEAD_WIDTH
                )
                out_refs[lane][:, cols] = result[h * rows:(h + 1) * rows]


def attend(info, counts, lanes, queries, spreads):
    q_cols = queries[0].shape[1]
    rows = sum(count for _, _, count in lanes[0][1])
    slots, chunks = spreads[0][1:]
    span = len(slots) * chunks * rows
    arrays = [array for spread in spreads for array in spread[0]]
    layout = [(len(spread[0]), spread[1], spread[2]) for spread in spreads]
    return pl.pallas_call(
        functools.partial(attend_kernel, lanes, layout, len(queries), counts),
        in_specs=[SMEM] + [VMEM] * (len(queries) + len(arrays)),
        out_specs=[VMEM] * len(lanes),
        out_shape=[jax.ShapeDtypeStruct((rows, q_cols), jnp.bfloat16)] * len(lanes),
        compiler_params=pltpu.CompilerParams(vmem_limit_bytes=28 * MIB),
        cost_estimate=pl.CostEstimate(
            flops=4 * len(lanes) * rows * q_cols * span,
            bytes_accessed=2 * sum(a.size for a in arrays) + 4 * len(lanes) * rows * q_cols,
            transcendentals=len(lanes) * rows * span * q_cols // HEAD_WIDTH,
        ),
        name="attend",
    )(info, *queries, *arrays)


def assemble_kernel(info_ref, own_ref, twin_ref, near0, far0, near1, far1, out_ref):
    me = info_ref[1]
    cols = own_ref.shape[1]

    def put(mask, ref):
        out_ref[0, :, pl.ds(pl.multiple_of((me ^ mask) * cols, cols), cols)] = ref[...]

    put(0, own_ref)
    put(1, twin_ref)

    @pl.when(me % 2 == 0)
    def _():
        put(2, near0)
        put(3, far0)

    @pl.when(me % 2 == 1)
    def _():
        put(2, near1)
        put(3, far1)


def assemble(info, *pieces):
    rows, cols = pieces[0].shape
    return pl.pallas_call(
        assemble_kernel,
        in_specs=[SMEM] + [VMEM] * len(pieces),
        out_specs=VMEM,
        out_shape=jax.ShapeDtypeStruct((1, rows, 4 * cols), jnp.bfloat16),
        compiler_params=pltpu.CompilerParams(vmem_limit_bytes=16 * MIB),
        name="assemble",
    )(info, *pieces)


def local(tokens, norm_gain, w_query, key_weight, value_weight, vertical_blocks, slash_offsets):
    _, rows, width = tokens.shape
    assert lax.axis_size("doc") == 4
    place = lax.axis_index("seq")
    doc_place = lax.axis_index("doc")
    counts = (vertical_blocks.shape[1], vertical_blocks.shape[2], slash_offsets.shape[2])
    info = jnp.concatenate(
        [
            jnp.stack([place, doc_place]).astype(jnp.int32),
            vertical_blocks.reshape(-1),
            slash_offsets.reshape(-1),
        ]
    )
    cosine, sine = rope_table(place * rows + jnp.arange(rows, dtype=jnp.int32), HEAD_WIDTH)
    table = jnp.concatenate([cosine, cosine, -sine, sine], axis=1)
    own = tokens[0]
    params = (norm_gain.reshape(1, width), w_query, key_weight, value_weight, table)
    head = rows // 4 // BAND * BAND
    rest = (rows - head) // 2

    twin = swap(own, "doc", 1)
    lead = swap(own[:head], "doc", 2)
    q_near, kv_near = project(
        info,
        [own, twin],
        [lambda c: 0, lambda c: rows],
        [(0, rows), (0, rows)],
        *params,
        early=True,
    )
    near = spread_blocks(kv_near)
    send_first, send_second = pick(info, own, twin, head)

    lead = after(lead, kv_near)
    got_first = swap(after(send_first, lead), "doc", 2)
    lead_twin = swap(lead, "doc", 1)

    got_second = swap(after(send_second, got_first, near[0][min(4, len(near[0]) - 1)]), "doc", 2)
    got_first_twin = swap(got_first, "doc", 1)
    q_first, kv_first = project(
        info,
        [lead, lead_twin, got_first, got_first_twin],
        [
            lambda c: c * rows,
            lambda c: (1 - c) * rows,
            lambda c: head + c * rest,
            lambda c: head + (1 - c) * rest,
        ],
        [(0, rows), (0, head)],
        *params,
        early=False,
    )
    first = spread_blocks(kv_first)
    mixed_own, mixed_twin = attend(
        info,
        counts,
        [(lambda d: d, [(0, 0, rows)]), (lambda d: d ^ 1, [(0, rows, rows)])],
        [q_near],
        [near],
    )
    out_twin = swap(mixed_twin, "doc", 1)

    got_second = after(got_second, mixed_twin)
    got_second_twin = swap(got_second, "doc", 1)
    q_second, kv_second = project(
        info,
        [got_second, got_second_twin],
        [lambda c: c * rest, lambda c: (1 - c) * rest],
        [(head, rows - head)],
        *params,
        early=False,
    )
    second = spread_blocks(kv_second)
    (mixed_first,) = attend(
        info, counts, [(lambda d: 2 - d // 2 * 2, [(0, 0, rows)])], [q_first], [first]
    )
    (mixed_second,) = attend(
        info,
        counts,
        [(lambda d: 3 - d // 2 * 2, [(0, rows, head), (1, 0, rows - head)])],
        [q_first, q_second],
        [first, second],
    )
    home = [mixed_own, out_twin]
    for mixed in (mixed_first, mixed_second):
        near_part = swap(mixed, "doc", 2)
        home += [near_part, swap(near_part, "doc", 1)]
    return assemble(info, *home)


def solution(mesh):
    return jax.shard_map(
        local,
        mesh=mesh,
        in_specs=(
            P("doc", "seq", None),
            P(),
            P(None, "doc"),
            P(None, "doc"),
            P(None, "doc"),
            P(),
            P(),
        ),
        out_specs=P("doc", "seq", None),
        check_vma=False,
    )
```

```python
import functools

import jax
import jax.numpy as jnp
from jax import lax
from jax.experimental import pallas as pl
from jax.experimental.pallas import tpu as pltpu
from jax.sharding import PartitionSpec as P

HEAD_WIDTH = 128
QUERY_HEADS = 16
KEY_VALUE_HEADS = 4
QUERY_GROUP = QUERY_HEADS // KEY_VALUE_HEADS
EPSILON = 1e-05
BAND = 16
MIB = 1024 * 1024

SMEM = pl.BlockSpec(memory_space=pltpu.SMEM)
VMEM = pl.BlockSpec(memory_space=pltpu.VMEM)
ANYWHERE = pl.BlockSpec(memory_space=pl.ANY)
HBM = pl.BlockSpec(memory_space=pltpu.HBM)


def swap(value, axis, mask):
    count = lax.axis_size(axis)
    return lax.ppermute(value, axis, [(source, source ^ mask) for source in range(count)])


def after(value, *others):
    return lax.optimization_barrier((value,) + others)[0]


def in_hbm(array):
    return pltpu.with_memory_space_constraint(array, pltpu.HBM)


def rope_table(positions, width):
    inverse = jnp.power(jnp.float32(500000.0), -jnp.arange(0, width, 2, dtype=jnp.float32) / width)
    angles = positions.astype(jnp.float32)[:, None] * inverse[None, :]
    return (jnp.cos(angles), jnp.sin(angles))


def project_kernel(places, table_rows, early, info_ref, *refs):
    token_refs = list(refs[:len(places)])
    refs = list(refs[len(places):])
    gain_ref, wq_ref, wk_ref, wv_ref, table_ref, q_ref, kv_ref = refs[:7]
    refs = refs[7:]
    core = info_ref[1] % 2
    copies = []
    if early is not None:
        send_refs, refs = refs[:2], refs[2:]
        sources = (gain_ref, token_refs[0], wk_ref, wv_ref, wq_ref)
        held, refs = refs[:1] + refs[5:6] + refs[1:4], refs[4:5] + refs[6:]
        sems = refs[1]
        gain_ref, token_refs[0], wk_ref, wv_ref, wq_ref = held
        for at, (source, target) in enumerate(zip(sources, held)):
            copies.append(pltpu.make_async_copy(source, target, sems.at[at]))
            copies[-1].start()
        copies[0].wait()
    normed = refs[0]
    width = gain_ref.shape[1]
    heads = wk_ref.shape[1] // HEAD_WIDTH
    deep = min(1024, width)

    for piece, place in reversed(list(enumerate(places))):
        if piece == 0 and early is not None:
            copies[1].wait()
        first = place(core)
        ref = token_refs[piece]

        def norm_band(index, carry, ref=ref, first=first):
            at = pl.ds(pl.multiple_of(index * BAND, BAND), BAND)
            wide = ref[at, :].astype(jnp.float32)
            scale = lax.rsqrt(jnp.mean(wide * wide, axis=-1, keepdims=True) + EPSILON)
            normed[pl.ds(pl.multiple_of(first + index * BAND, BAND), BAND), :] = (
                wide * scale * gain_ref[...]
            ).astype(jnp.bfloat16)
            return carry

        lax.fori_loop(0, ref.shape[0] // BAND, norm_band, 0, unroll=2)

    if early is not None:
        count = send_refs[0].shape[0]
        for side in range(2):

            @pl.when(core == side)
            def _(side=side):
                rows = slice(early + side * count, early + (side + 1) * count)
                send_refs[side][...] = token_refs[0][rows, :]
                send_refs[1 - side][...] = token_refs[1][rows, :]

    half = HEAD_WIDTH // 2

    def rotate(value, rows):
        cosine = table_ref[rows, :HEAD_WIDTH]
        sine = table_ref[rows, HEAD_WIDTH:]
        turned = jnp.concatenate([value[:, half:], value[:, :half]], axis=1)
        return (value * cosine + turned * sine).astype(jnp.bfloat16)

    def multiply(weight_of):
        total = None
        for start in range(0, width, deep):
            part = jnp.dot(
                normed[:, start:start + deep],
                weight_of(slice(start, start + deep)),
                preferred_element_type=jnp.float32,
            )
            total = part if total is None else total + part
        return total

    if early is not None:
        copies[2].wait()
        copies[3].wait()
    for head in range(heads):
        at = slice(head * HEAD_WIDTH, (head + 1) * HEAD_WIDTH)
        both = multiply(lambda k: jnp.concatenate([wk_ref[k, at], wv_ref[k, at]], axis=1))
        out = 2 * head * HEAD_WIDTH
        row = 0
        for begin, count in table_rows:
            mine = both[row:row + count]
            kv_ref[row:row + count, out:out + HEAD_WIDTH] = rotate(
                mine[:, :HEAD_WIDTH], slice(begin, begin + count)
            )
            kv_ref[row:row + count, out + HEAD_WIDTH:out + 2 * HEAD_WIDTH] = mine[
                :, HEAD_WIDTH:
            ].astype(jnp.bfloat16)
            row += count
    if early is not None:
        copies[4].wait()
    pair = 2 * HEAD_WIDTH
    for start in range(0, wq_ref.shape[1], pair):
        both = multiply(lambda k: wq_ref[k, start:start + pair])
        row = 0
        for begin, count in table_rows:
            for at in (0, HEAD_WIDTH):
                q_ref[row:row + count, start + at:start + at + HEAD_WIDTH] = rotate(
                    both[row:row + count, at:at + HEAD_WIDTH], slice(begin, begin + count)
                )
            row += count


def project(info, pieces, places, table_rows, gain, w_query, key_weight, value_weight, table, early=None):
    width = gain.shape[1]
    q_cols, k_cols = w_query.shape[1], key_weight.shape[1]
    total = sum(count for _, count in table_rows)
    params = (gain, w_query, key_weight, value_weight)
    scratch = [pltpu.VMEM((total, width), jnp.bfloat16)]
    kind = [VMEM] * (len(pieces) + len(params))
    shapes = [
        jax.ShapeDtypeStruct((total, q_cols), jnp.bfloat16),
        jax.ShapeDtypeStruct((total, 2 * k_cols), jnp.bfloat16),
    ]
    if early is not None:
        scratch.append(pltpu.VMEM(pieces[0].shape, pieces[0].dtype))
        scratch.append(pltpu.SemaphoreType.DMA((5,)))
        params = tuple(in_hbm(array) for array in params)
        shapes += [jax.ShapeDtypeStruct(((pieces[0].shape[0] - early) // 2, width), jnp.bfloat16)] * 2
        shapes += [
            jax.ShapeDtypeStruct(array.shape, array.dtype)
            for array in (gain, key_weight, value_weight, w_query)
        ]
        pieces = [in_hbm(pieces[0])] + list(pieces[1:])
        kind = [HBM] + [VMEM] * (len(pieces) - 1) + [HBM] * len(params)
    return pl.pallas_call(
        functools.partial(project_kernel, places, table_rows, early),
        in_specs=[SMEM] + kind + [VMEM],
        out_specs=[VMEM] * len(shapes),
        out_shape=shapes,
        scratch_shapes=scratch,
        compiler_params=pltpu.CompilerParams(vmem_limit_bytes=28 * MIB),
        cost_estimate=pl.CostEstimate(
            flops=2 * total * width * (q_cols + 2 * k_cols),
            bytes_accessed=2 * width * (q_cols + 2 * k_cols) + 2 * total * width,
            transcendentals=0,
        ),
        name="project",
    )(info, *pieces, *params, table)


def cut_kernel(source, target, sem):
    copy = pltpu.make_async_copy(source.at[pl.ds(0, target.shape[0])], target, sem)
    copy.start()
    copy.wait()


def cut(array, rows):
    return pl.pallas_call(
        cut_kernel,
        in_specs=[HBM],
        out_specs=VMEM,
        out_shape=jax.ShapeDtypeStruct((rows,) + array.shape[1:], array.dtype),
        scratch_shapes=[pltpu.SemaphoreType.DMA],
        compiler_params=pltpu.CompilerParams(vmem_limit_bytes=16 * MIB),
        name="cut",
    )(in_hbm(array))


class Spread:
    def __init__(self, kv):
        count = lax.axis_size("seq")
        total = kv.shape[0]
        self.count, self.chunks, self.stages = count, 1, 0
        self.arrays, self.slots = [], []
        self.held, self.last, self.stage = None, (), 0
        if count > 8 or count % 2:
            chunk = 8 if count % 8 == 0 else 1
            self.chunks = count // chunk
            self.arrays.append(lax.all_gather(kv, "seq", axis=0, tiled=True))
            for j in range(chunk):
                self.slots.append(
                    lambda place, index, j=j: (
                        0,
                        pl.multiple_of((index * chunk + j) * total, BAND),
                        index * chunk + j,
                    )
                )
        else:
            self.stages = count // 2
            self.held = kv

    def advance(self, *others):
        if not self.stages:
            return
        stage, deep = self.stage, self.count // 2
        value = after(self.held, *self.last, *others)
        ahead = None
        if stage + 1 < deep:
            step = [(z + 1 if z + 1 < deep else stage) if z >= stage else z for z in range(deep)]
            ahead = lax.ppermute(
                value, "seq", [(2 * z + y, 2 * step[z] + y) for z in range(deep) for y in range(2)]
            )
        other = swap(value, "seq", 1)
        for flip, array in ((0, value), (1, other)):
            self.slots.append(
                lambda place, index, r=len(self.arrays), flip=flip: (r, 0, (place ^ flip) - 2 * stage)
            )
            self.arrays.append(array)
        self.held, self.last, self.stage = ahead, (other,), stage + 1
        self.stages -= 1

    def done(self):
        if self.chunks > 1 or self.held is None:
            return tuple(self.arrays)
        return (self.held,) + self.last


def attend_kernel(lanes, spreads, q_count, info_ref, vertical_ref, slash_ref, *refs):
    q_refs = refs[:q_count]
    kv_refs, at = [], q_count
    for arrays, _, _ in spreads:
        kv_refs.append(refs[at:at + arrays])
        at += arrays
    out_refs = refs[at:]
    slots, chunks = spreads[0][1], spreads[0][2]
    heads = kv_refs[0][0].shape[1] // (2 * HEAD_WIDTH)
    rows = out_refs[0].shape[0]
    place = info_ref[0]
    group_place = info_ref[1]
    rank = QUERY_GROUP * rows
    span = len(slots) * rows
    factor = HEAD_WIDTH ** (-0.5)
    query_at = place * rows + lax.broadcasted_iota(jnp.int32, (rows, rows), 0)
    key_at = lax.broadcasted_iota(jnp.int32, (rows, rows), 1)

    def block_allowed(doc, group, block):
        found = (block == place) | (block == place - 1)
        for s in range(slash_ref.shape[2]):
            found = found | (block == place - slash_ref[doc, group, s])
        for s in range(vertical_ref.shape[2]):
            found = found | ((block == vertical_ref[doc, group, s]) & (block < place - 1))
        return found & (block >= 0)

    for lane, (doc_of, segments) in enumerate(lanes):
        doc = doc_of(info_ref[1])
        for head in range(heads):
            group = group_place * heads + head
            queries = jnp.concatenate(
                [
                    q_refs[source][
                        start:start + count,
                        (head * QUERY_GROUP + h) * HEAD_WIDTH:(head * QUERY_GROUP + h + 1) * HEAD_WIDTH,
                    ]
                    for h in range(QUERY_GROUP)
                    for source, start, count in segments
                ],
                axis=0,
            )

            def column(index, at):
                cols = slice(at * HEAD_WIDTH, (at + 1) * HEAD_WIDTH)
                parts = []
                for number in range(len(slots)):
                    for source, start, count in segments:
                        r, first, _ = spreads[source][1][number](place, index)
                        if isinstance(first, int):
                            where = slice(first + start, first + start + count)
                        else:
                            where = pl.ds(pl.multiple_of(first + start, BAND), count)
                        parts.append(kv_refs[source][r][where, cols])
                return jnp.concatenate(parts, axis=0)

            def step(index, carry):
                highest, total, mixed = carry
                keys, values = column(index, 2 * head), column(index, 2 * head + 1)
                scores = lax.dot_general(
                    queries, keys, (((1,), (1,)), ((), ())), preferred_element_type=jnp.float32
                ) * factor
                bias = []
                for slot in slots:
                    block = slot(place, index)[2]
                    bias.append(
                        jnp.where(
                            (key_at + block * rows <= query_at) & block_allowed(doc, group, block),
                            jnp.float32(0),
                            -jnp.inf,
                        )
                    )
                bias = jnp.concatenate(bias, axis=1)
                scores = (scores.reshape(QUERY_GROUP, rows, span) + bias[None]).reshape(rank, span)
                top = jnp.max(scores, axis=1, keepdims=True)
                if chunks > 1:
                    fresh = jnp.maximum(highest, top)
                    safe = jnp.where(fresh == -jnp.inf, jnp.float32(0), fresh)
                    fade = jnp.exp(highest - safe)
                else:
                    fresh = safe = top
                raised = jnp.exp(scores - safe)
                part = jnp.sum(raised, axis=1, keepdims=True)
                product = jnp.dot(
                    raised.astype(jnp.bfloat16), values, preferred_element_type=jnp.float32
                )
                if chunks > 1:
                    return fresh, total * fade + part, mixed * fade + product
                return fresh, part, product

            initial = (
                jnp.full((rank, 1), -jnp.inf, jnp.float32),
                jnp.zeros((rank, 1), jnp.float32),
                jnp.zeros((rank, HEAD_WIDTH), jnp.float32),
            )
            if chunks > 1:
                _, total, mixed = lax.fori_loop(0, chunks, step, initial)
            else:
                _, total, mixed = step(0, initial)
            result = (mixed / total).astype(jnp.bfloat16)
            for h in range(QUERY_GROUP):
                cols = slice(
                    (head * QUERY_GROUP + h) * HEAD_WIDTH, (head * QUERY_GROUP + h + 1) * HEAD_WIDTH
                )
                out_refs[lane][:, cols] = result[h * rows:(h + 1) * rows]


def attend(info, vertical, slash, lanes, queries, spreads):
    q_cols = queries[0].shape[1]
    rows = sum(count for _, _, count in lanes[0][1])
    span = len(spreads[0].slots) * spreads[0].chunks * rows
    arrays = [array for spread in spreads for array in spread.arrays]
    layout = [(len(spread.arrays), spread.slots, spread.chunks) for spread in spreads]
    return pl.pallas_call(
        functools.partial(attend_kernel, lanes, layout, len(queries)),
        in_specs=[SMEM] * 3 + [VMEM] * (len(queries) + len(arrays)),
        out_specs=[VMEM] * len(lanes),
        out_shape=[jax.ShapeDtypeStruct((rows, q_cols), jnp.bfloat16)] * len(lanes),
        compiler_params=pltpu.CompilerParams(vmem_limit_bytes=28 * MIB),
        cost_estimate=pl.CostEstimate(
            flops=4 * len(lanes) * rows * q_cols * span,
            bytes_accessed=2 * sum(a.size for a in arrays) + 4 * len(lanes) * rows * q_cols,
            transcendentals=len(lanes) * rows * span * q_cols // HEAD_WIDTH,
        ),
        name="attend",
    )(info, vertical, slash, *queries, *arrays)


def assemble_kernel(info_ref, own_ref, twin_ref, near0, far0, near1, far1, out_ref):
    me = info_ref[1]
    cols = own_ref.shape[1]

    def put(mask, ref):
        out_ref[0, :, pl.ds(pl.multiple_of((me ^ mask) * cols, cols), cols)] = ref[...]

    put(0, own_ref)
    put(1, twin_ref)

    @pl.when(me % 2 == 0)
    def _():
        put(2, near0)
        put(3, far0)

    @pl.when(me % 2 == 1)
    def _():
        put(2, near1)
        put(3, far1)


def assemble(info, *pieces):
    rows, cols = pieces[0].shape
    return pl.pallas_call(
        assemble_kernel,
        in_specs=[SMEM] + [VMEM] * len(pieces),
        out_specs=VMEM,
        out_shape=jax.ShapeDtypeStruct((1, rows, 4 * cols), jnp.bfloat16),
        compiler_params=pltpu.CompilerParams(vmem_limit_bytes=16 * MIB),
        name="assemble",
    )(info, *pieces)


def local(tokens, norm_gain, w_query, key_weight, value_weight, vertical_blocks, slash_offsets):
    _, rows, width = tokens.shape
    assert lax.axis_size("doc") == 4
    place = lax.axis_index("seq")
    doc_place = lax.axis_index("doc")
    info = jnp.stack([place, doc_place]).astype(jnp.int32)
    cosine, sine = rope_table(place * rows + jnp.arange(rows, dtype=jnp.int32), HEAD_WIDTH)
    table = jnp.concatenate([cosine, cosine, -sine, sine], axis=1)
    own = tokens[0]
    gain = norm_gain.reshape(1, width)
    weights = (w_query, key_weight, value_weight)
    pattern = (info, vertical_blocks, slash_offsets)
    head = rows // 4 // BAND * BAND
    rest = (rows - head) // 2

    twin = swap(own, "doc", 1)
    lead = swap(cut(own, head), "doc", 2)
    q_near, kv_near, send_first, send_second, gain_in, wk_in, wv_in, wq_in = project(
        info,
        [own, twin],
        [lambda c: 0, lambda c: rows],
        [(0, rows), (0, rows)],
        gain,
        *weights,
        table,
        early=head,
    )
    near = Spread(kv_near)
    near.advance()
    lead = after(lead, kv_near)
    got_first = swap(after(send_first, lead), "doc", 2)
    lead_twin = swap(lead, "doc", 1)
    near.advance(lead_twin)

    got_first = after(got_first, *near.done())
    near.advance()
    got_second = swap(after(send_second, got_first), "doc", 2)
    got_first_twin = swap(got_first, "doc", 1)
    near.advance()
    params = (gain_in, wq_in, wk_in, wv_in, table)
    q_first, kv_first = project(
        info,
        [lead, lead_twin, got_first, got_first_twin],
        [
            lambda c: c * rows,
            lambda c: (1 - c) * rows,
            lambda c: head + c * rest,
            lambda c: head + (1 - c) * rest,
        ],
        [(0, rows), (0, head)],
        *params,
    )
    first = Spread(kv_first)
    first.advance()
    begun = first.done()
    first.advance()
    mixed_own, mixed_twin = attend(
        *pattern,
        [(lambda d: d, [(0, 0, rows)]), (lambda d: d ^ 1, [(0, rows, rows)])],
        [after(q_near, *begun)],
        [near],
    )
    out_twin = swap(mixed_twin, "doc", 1)

    got_second = after(got_second, out_twin, *first.done())
    got_second_twin = swap(got_second, "doc", 1)
    first.advance()
    ahead = first.done()
    first.advance()
    q_second, kv_second = project(
        info,
        [got_second, got_second_twin],
        [lambda c: c * rest, lambda c: (1 - c) * rest],
        [(head, rows - head)],
        *params,
    )
    second = Spread(kv_second)
    second.advance()
    second.advance(*ahead)
    begun = second.done()
    second.advance(*first.last)
    (mixed_first,) = attend(
        *pattern,
        [(lambda d: 2 - d // 2 * 2, [(0, 0, rows)])],
        [after(q_first, *begun)],
        [first],
    )
    second.advance(mixed_first)
    (mixed_second,) = attend(
        *pattern,
        [(lambda d: 3 - d // 2 * 2, [(0, rows, head), (1, 0, rows - head)])],
        [q_first, q_second],
        [first, second],
    )
    home = [mixed_own, out_twin]
    for mixed in (mixed_first, mixed_second):
        near_part = swap(mixed, "doc", 2)
        home += [near_part, swap(near_part, "doc", 1)]
    return assemble(info, *home)


def solution(mesh):
    return jax.shard_map(
        local,
        mesh=mesh,
        in_specs=(
            P("doc", "seq", None),
            P(),
            P(None, "doc"),
            P(None, "doc"),
            P(None, "doc"),
            P(),
            P(),
        ),
        out_specs=P("doc", "seq", None),
        check_vma=False,
    )
```

```python
import functools

import jax
import jax.numpy as jnp
from jax import lax
from jax.experimental import pallas as pl
from jax.experimental.pallas import tpu as pltpu
from jax.sharding import PartitionSpec as P

HEAD_WIDTH = 128
QUERY_HEADS = 16
KEY_VALUE_HEADS = 4
QUERY_GROUP = QUERY_HEADS // KEY_VALUE_HEADS
EPSILON = 1e-05
BAND = 16
MIB = 1024 * 1024

SMEM = pl.BlockSpec(memory_space=pltpu.SMEM)
VMEM = pl.BlockSpec(memory_space=pltpu.VMEM)
ANYWHERE = pl.BlockSpec(memory_space=pl.ANY)
HBM = pl.BlockSpec(memory_space=pltpu.HBM)


def swap(value, axis, mask):
    count = lax.axis_size(axis)
    return lax.ppermute(value, axis, [(source, source ^ mask) for source in range(count)])


def after(value, *others):
    return lax.optimization_barrier((value,) + others)[0]


def in_hbm(array):
    return pltpu.with_memory_space_constraint(array, pltpu.HBM)


def rope_table(positions, width):
    inverse = jnp.power(jnp.float32(500000.0), -jnp.arange(0, width, 2, dtype=jnp.float32) / width)
    angles = positions.astype(jnp.float32)[:, None] * inverse[None, :]
    return (jnp.cos(angles), jnp.sin(angles))


def project_kernel(places, table_rows, early, info_ref, *refs):
    token_refs = list(refs[:len(places)])
    refs = list(refs[len(places):])
    gain_ref, wq_ref, wk_ref, wv_ref, table_ref, q_ref, kv_ref = refs[:7]
    refs = refs[7:]
    core = info_ref[1] % 2
    copies = []
    if early:
        sources = (gain_ref, token_refs[0], wk_ref, wv_ref, wq_ref)
        held, refs = refs[:1] + refs[5:6] + refs[1:4], refs[4:5] + refs[6:]
        sems = refs[1]
        gain_ref, token_refs[0], wk_ref, wv_ref, wq_ref = held
        for at, (source, target) in enumerate(zip(sources, held)):
            copies.append(pltpu.make_async_copy(source, target, sems.at[at]))
            copies[-1].start()
        copies[0].wait()
    normed = refs[0]
    width = gain_ref.shape[1]
    heads = wk_ref.shape[1] // HEAD_WIDTH
    deep = min(1024, width)

    for piece, place in reversed(list(enumerate(places))):
        if piece == 0 and early:
            copies[1].wait()
        first = place(core)
        ref = token_refs[piece]

        def norm_band(index, carry, ref=ref, first=first):
            at = pl.ds(pl.multiple_of(index * BAND, BAND), BAND)
            wide = ref[at, :].astype(jnp.float32)
            scale = lax.rsqrt(jnp.mean(wide * wide, axis=-1, keepdims=True) + EPSILON)
            normed[pl.ds(pl.multiple_of(first + index * BAND, BAND), BAND), :] = (
                wide * scale * gain_ref[...]
            ).astype(jnp.bfloat16)
            return carry

        lax.fori_loop(0, ref.shape[0] // BAND, norm_band, 0, unroll=2)

    half = HEAD_WIDTH // 2

    def rotate(value, rows):
        cosine = table_ref[rows, :HEAD_WIDTH]
        sine = table_ref[rows, HEAD_WIDTH:]
        turned = jnp.concatenate([value[:, half:], value[:, :half]], axis=1)
        return (value * cosine + turned * sine).astype(jnp.bfloat16)

    def multiply(weight_of):
        total = None
        for start in range(0, width, deep):
            part = jnp.dot(
                normed[:, start:start + deep],
                weight_of(slice(start, start + deep)),
                preferred_element_type=jnp.float32,
            )
            total = part if total is None else total + part
        return total

    if early:
        copies[2].wait()
        copies[3].wait()
    for head in range(heads):
        at = slice(head * HEAD_WIDTH, (head + 1) * HEAD_WIDTH)
        both = multiply(lambda k: jnp.concatenate([wk_ref[k, at], wv_ref[k, at]], axis=1))
        out = 2 * head * HEAD_WIDTH
        row = 0
        for begin, count in table_rows:
            mine = both[row:row + count]
            kv_ref[row:row + count, out:out + HEAD_WIDTH] = rotate(
                mine[:, :HEAD_WIDTH], slice(begin, begin + count)
            )
            kv_ref[row:row + count, out + HEAD_WIDTH:out + 2 * HEAD_WIDTH] = mine[
                :, HEAD_WIDTH:
            ].astype(jnp.bfloat16)
            row += count
    if early:
        copies[4].wait()
    pair = 2 * HEAD_WIDTH
    for start in range(0, wq_ref.shape[1], pair):
        both = multiply(lambda k: wq_ref[k, start:start + pair])
        row = 0
        for begin, count in table_rows:
            for at in (0, HEAD_WIDTH):
                q_ref[row:row + count, start + at:start + at + HEAD_WIDTH] = rotate(
                    both[row:row + count, at:at + HEAD_WIDTH], slice(begin, begin + count)
                )
            row += count


def project(info, pieces, places, table_rows, gain, w_query, key_weight, value_weight, table, early=False):
    width = gain.shape[1]
    q_cols, k_cols = w_query.shape[1], key_weight.shape[1]
    total = sum(count for _, count in table_rows)
    params = (gain, w_query, key_weight, value_weight)
    scratch = [pltpu.VMEM((total, width), jnp.bfloat16)]
    kind = [VMEM] * (len(pieces) + len(params))
    shapes = [
        jax.ShapeDtypeStruct((total, q_cols), jnp.bfloat16),
        jax.ShapeDtypeStruct((total, 2 * k_cols), jnp.bfloat16),
    ]
    if early:
        scratch.append(pltpu.VMEM(pieces[0].shape, pieces[0].dtype))
        scratch.append(pltpu.SemaphoreType.DMA((5,)))
        params = tuple(in_hbm(array) for array in params)
        shapes += [
            jax.ShapeDtypeStruct(array.shape, array.dtype)
            for array in (gain, key_weight, value_weight, w_query)
        ]
        pieces = [in_hbm(pieces[0])] + list(pieces[1:])
        kind = [HBM] + [VMEM] * (len(pieces) - 1) + [HBM] * len(params)
    return pl.pallas_call(
        functools.partial(project_kernel, places, table_rows, early),
        in_specs=[SMEM] + kind + [VMEM],
        out_specs=[VMEM] * len(shapes),
        out_shape=shapes,
        scratch_shapes=scratch,
        compiler_params=pltpu.CompilerParams(vmem_limit_bytes=28 * MIB),
        cost_estimate=pl.CostEstimate(
            flops=2 * total * width * (q_cols + 2 * k_cols),
            bytes_accessed=2 * width * (q_cols + 2 * k_cols) + 2 * total * width,
            transcendentals=0,
        ),
        name="project",
    )(info, *pieces, *params, table)


def cut_kernel(source, *refs):
    sems = refs[-1]
    copies, first = [], 0
    for at, target in enumerate(refs[:-1]):
        count = target.shape[0]
        copies.append(pltpu.make_async_copy(source.at[pl.ds(first, count)], target, sems.at[at]))
        copies[-1].start()
        first += count
    for copy in copies:
        copy.wait()


def cut(array, counts):
    return pl.pallas_call(
        cut_kernel,
        in_specs=[HBM],
        out_specs=[VMEM] * len(counts),
        out_shape=[jax.ShapeDtypeStruct((rows,) + array.shape[1:], array.dtype) for rows in counts],
        scratch_shapes=[pltpu.SemaphoreType.DMA((len(counts),))],
        compiler_params=pltpu.CompilerParams(vmem_limit_bytes=16 * MIB),
        name="cut",
    )(in_hbm(array))


class Ring:
    def __init__(self, kv):
        count = lax.axis_size("seq")
        total = kv.shape[0]
        self.count, self.chunks, self.stage = count, 1, 0
        self.arrays, self.slots, self.latest = [], [], ()
        if count > 8 or count % 2:
            chunk = 8 if count % 8 == 0 else 1
            self.chunks = count // chunk
            self.arrays.append(lax.all_gather(kv, "seq", axis=0, tiled=True))
            for j in range(chunk):
                self.slots.append(
                    lambda place, index, j=j: (
                        0,
                        pl.multiple_of((index * chunk + j) * total, BAND),
                        index * chunk + j,
                    )
                )
        else:
            self.order = list(range(0, count, 2)) + list(range(count - 1, 0, -2))
            self.front = {1: kv, -1: kv}
            self.hold(kv, 0)

    def hold(self, array, steps):
        count, half = self.count, self.count // 2

        def slot(place, index, r=len(self.arrays)):
            z, y = place // 2, place % 2
            at = jnp.where(y == 0, z, count - 1 - z) + count - steps
            at = at % count
            return r, 0, jnp.where(at < half, 2 * at, 2 * (count - 1 - at) + 1)

        self.slots.append(slot)
        self.arrays.append(array)

    def advance(self, *others):
        if self.chunks > 1 or self.stage >= self.count // 2:
            return
        self.stage += 1
        ways = (1, -1) if 2 * self.stage < self.count else (1,)
        fresh = []
        for way in ways:
            value = after(self.front[way], *others) if others else self.front[way]
            pairs = [
                (source, self.order[(at + way) % self.count]) for at, source in enumerate(self.order)
            ]
            self.front[way] = lax.ppermute(value, "seq", pairs)
            fresh.append(self.front[way])
            self.hold(self.front[way], way * self.stage)
        self.latest = tuple(fresh)


def attend_kernel(lanes, spreads, q_count, info_ref, vertical_ref, slash_ref, *refs):
    q_refs = refs[:q_count]
    kv_refs, at = [], q_count
    for arrays, _, _ in spreads:
        kv_refs.append(refs[at:at + arrays])
        at += arrays
    out_refs = refs[at:]
    slots, chunks = spreads[0][1], spreads[0][2]
    heads = kv_refs[0][0].shape[1] // (2 * HEAD_WIDTH)
    rows = out_refs[0].shape[0]
    place = info_ref[0]
    group_place = info_ref[1]
    rank = QUERY_GROUP * rows
    span = len(slots) * rows
    factor = HEAD_WIDTH ** (-0.5)
    query_at = place * rows + lax.broadcasted_iota(jnp.int32, (rows, rows), 0)
    key_at = lax.broadcasted_iota(jnp.int32, (rows, rows), 1)

    def block_allowed(doc, group, block):
        found = (block == place) | (block == place - 1)
        for s in range(slash_ref.shape[2]):
            found = found | (block == place - slash_ref[doc, group, s])
        for s in range(vertical_ref.shape[2]):
            found = found | ((block == vertical_ref[doc, group, s]) & (block < place - 1))
        return found & (block >= 0)

    for lane, (doc_of, segments) in enumerate(lanes):
        doc = doc_of(info_ref[1])
        for head in range(heads):
            group = group_place * heads + head
            queries = jnp.concatenate(
                [
                    q_refs[source][
                        start:start + count,
                        (head * QUERY_GROUP + h) * HEAD_WIDTH:(head * QUERY_GROUP + h + 1) * HEAD_WIDTH,
                    ]
                    for h in range(QUERY_GROUP)
                    for source, start, count in segments
                ],
                axis=0,
            )

            def column(index, at):
                cols = slice(at * HEAD_WIDTH, (at + 1) * HEAD_WIDTH)
                parts = []
                for number in range(len(slots)):
                    for source, start, count in segments:
                        r, first, _ = spreads[source][1][number](place, index)
                        if isinstance(first, int):
                            where = slice(first + start, first + start + count)
                        else:
                            where = pl.ds(pl.multiple_of(first + start, BAND), count)
                        parts.append(kv_refs[source][r][where, cols])
                return jnp.concatenate(parts, axis=0)

            def step(index, carry):
                highest, total, mixed = carry
                keys, values = column(index, 2 * head), column(index, 2 * head + 1)
                scores = lax.dot_general(
                    queries, keys, (((1,), (1,)), ((), ())), preferred_element_type=jnp.float32
                ) * factor
                bias = []
                for slot in slots:
                    block = slot(place, index)[2]
                    bias.append(
                        jnp.where(
                            (key_at + block * rows <= query_at) & block_allowed(doc, group, block),
                            jnp.float32(0),
                            -jnp.inf,
                        )
                    )
                bias = jnp.concatenate(bias, axis=1)
                scores = (scores.reshape(QUERY_GROUP, rows, span) + bias[None]).reshape(rank, span)
                top = jnp.max(scores, axis=1, keepdims=True)
                if chunks > 1:
                    fresh = jnp.maximum(highest, top)
                    safe = jnp.where(fresh == -jnp.inf, jnp.float32(0), fresh)
                    fade = jnp.exp(highest - safe)
                else:
                    fresh = safe = top
                raised = jnp.exp(scores - safe)
                part = jnp.sum(raised, axis=1, keepdims=True)
                product = jnp.dot(
                    raised.astype(jnp.bfloat16), values, preferred_element_type=jnp.float32
                )
                if chunks > 1:
                    return fresh, total * fade + part, mixed * fade + product
                return fresh, part, product

            initial = (
                jnp.full((rank, 1), -jnp.inf, jnp.float32),
                jnp.zeros((rank, 1), jnp.float32),
                jnp.zeros((rank, HEAD_WIDTH), jnp.float32),
            )
            if chunks > 1:
                _, total, mixed = lax.fori_loop(0, chunks, step, initial)
            else:
                _, total, mixed = step(0, initial)
            result = (mixed / total).astype(jnp.bfloat16)
            for h in range(QUERY_GROUP):
                cols = slice(
                    (head * QUERY_GROUP + h) * HEAD_WIDTH, (head * QUERY_GROUP + h + 1) * HEAD_WIDTH
                )
                out_refs[lane][:, cols] = result[h * rows:(h + 1) * rows]


def attend(info, vertical, slash, lanes, queries, spreads):
    q_cols = queries[0].shape[1]
    rows = sum(count for _, _, count in lanes[0][1])
    span = len(spreads[0].slots) * spreads[0].chunks * rows
    arrays = [array for spread in spreads for array in spread.arrays]
    layout = [(len(spread.arrays), spread.slots, spread.chunks) for spread in spreads]
    return pl.pallas_call(
        functools.partial(attend_kernel, lanes, layout, len(queries)),
        in_specs=[SMEM] * 3 + [VMEM] * (len(queries) + len(arrays)),
        out_specs=[VMEM] * len(lanes),
        out_shape=[jax.ShapeDtypeStruct((rows, q_cols), jnp.bfloat16)] * len(lanes),
        compiler_params=pltpu.CompilerParams(vmem_limit_bytes=28 * MIB),
        cost_estimate=pl.CostEstimate(
            flops=4 * len(lanes) * rows * q_cols * span,
            bytes_accessed=2 * sum(a.size for a in arrays) + 4 * len(lanes) * rows * q_cols,
            transcendentals=len(lanes) * rows * span * q_cols // HEAD_WIDTH,
        ),
        name="attend",
    )(info, vertical, slash, *queries, *arrays)


def assemble_kernel(info_ref, *refs):
    out_ref = refs[-1]
    cols = refs[0].shape[1]
    for mask, ref in enumerate(refs[:-1]):
        at = pl.multiple_of((info_ref[1] ^ mask) * cols, cols)
        out_ref[0, :, pl.ds(at, cols)] = ref[...]


def assemble(info, *pieces):
    rows, cols = pieces[0].shape
    return pl.pallas_call(
        assemble_kernel,
        in_specs=[SMEM] + [VMEM] * len(pieces),
        out_specs=VMEM,
        out_shape=jax.ShapeDtypeStruct((1, rows, len(pieces) * cols), jnp.bfloat16),
        compiler_params=pltpu.CompilerParams(vmem_limit_bytes=16 * MIB),
        name="assemble",
    )(info, *pieces)


def local(tokens, norm_gain, w_query, key_weight, value_weight, vertical_blocks, slash_offsets):
    _, rows, width = tokens.shape
    assert lax.axis_size("doc") == 4
    place = lax.axis_index("seq")
    doc_place = lax.axis_index("doc")
    info = jnp.stack([place, doc_place]).astype(jnp.int32)
    cosine, sine = rope_table(place * rows + jnp.arange(rows, dtype=jnp.int32), HEAD_WIDTH)
    table = jnp.concatenate([cosine, cosine, -sine, sine], axis=1)
    own = tokens[0]
    gain = norm_gain.reshape(1, width)
    weights = (w_query, key_weight, value_weight)
    pattern = (info, vertical_blocks, slash_offsets)
    head = rows * 3 // 4 // BAND * BAND
    tail = rows - head

    twin = swap(own, "doc", 1)
    send_head, send_tail = cut(own, (head, tail))
    got_head = swap(send_head, "doc", 2)
    q_near, kv_near, gain_in, wk_in, wv_in, wq_in = project(
        info,
        [own, twin],
        [lambda c: 0, lambda c: rows],
        [(0, rows), (0, rows)],
        gain,
        *weights,
        table,
        early=True,
    )
    params = (gain_in, wq_in, wk_in, wv_in, table)
    near = Ring(kv_near)
    near.advance()
    near.advance()
    got_head = after(got_head, *near.latest)

    got_tail = swap(after(send_tail, got_head), "doc", 2)
    head_twin = swap(got_head, "doc", 1)
    near.advance()
    q_head, kv_head = project(
        info,
        [got_head, head_twin],
        [lambda c: 0, lambda c: head],
        [(0, head), (0, head)],
        *params,
    )
    ring_head = Ring(kv_head)
    ring_head.advance()

    got_tail = after(got_tail, *near.latest, *ring_head.latest)
    near.advance()
    tail_twin = swap(got_tail, "doc", 1)
    ring_head.advance()
    q_tail, kv_tail = project(
        info,
        [got_tail, tail_twin],
        [lambda c: 0, lambda c: tail],
        [(head, tail), (head, tail)],
        *params,
    )
    ring_tail = Ring(kv_tail)
    ring_tail.advance()
    mixed_own, mixed_twin = attend(
        *pattern,
        [(lambda d: d, [(0, 0, rows)]), (lambda d: d ^ 1, [(0, rows, rows)])],
        [after(q_near, *ring_tail.latest)],
        [near],
    )
    out_twin = swap(mixed_twin, "doc", 1)
    ring_head.advance()
    ring_tail.advance(mixed_twin)
    ring_head.advance()
    ring_tail.advance()
    ring_tail.advance()
    mixed = attend(
        *pattern,
        [
            (lambda d: d ^ 2, [(0, 0, head), (1, 0, tail)]),
            (lambda d: d ^ 3, [(0, head, head), (1, tail, tail)]),
        ],
        [after(q_head, out_twin), q_tail],
        [ring_head, ring_tail],
    )
    return assemble(info, mixed_own, out_twin, swap(mixed[0], "doc", 2), swap(mixed[1], "doc", 3))


def solution(mesh):
    return jax.shard_map(
        local,
        mesh=mesh,
        in_specs=(
            P("doc", "seq", None),
            P(),
            P(None, "doc"),
            P(None, "doc"),
            P(None, "doc"),
            P(),
            P(),
        ),
        out_specs=P("doc", "seq", None),
        check_vma=False,
    )
```

```python
import functools

import jax
import jax.numpy as jnp
from jax import lax
from jax.experimental import pallas as pl
from jax.experimental.pallas import tpu as pltpu
from jax.sharding import PartitionSpec as P

HEAD_WIDTH = 128
QUERY_HEADS = 16
KEY_VALUE_HEADS = 4
QUERY_GROUP = QUERY_HEADS // KEY_VALUE_HEADS
EPSILON = 1e-05
BAND = 16
MIB = 1024 * 1024

SMEM = pl.BlockSpec(memory_space=pltpu.SMEM)
VMEM = pl.BlockSpec(memory_space=pltpu.VMEM)
ANYWHERE = pl.BlockSpec(memory_space=pl.ANY)
HBM = pl.BlockSpec(memory_space=pltpu.HBM)


def swap(value, axis, mask):
    count = lax.axis_size(axis)
    return lax.ppermute(value, axis, [(source, source ^ mask) for source in range(count)])


def after(value, *others):
    return lax.optimization_barrier((value,) + others)[0]


def in_hbm(array):
    return pltpu.with_memory_space_constraint(array, pltpu.HBM)


def rope_table(positions, width):
    inverse = jnp.power(jnp.float32(500000.0), -jnp.arange(0, width, 2, dtype=jnp.float32) / width)
    angles = positions.astype(jnp.float32)[:, None] * inverse[None, :]
    return (jnp.cos(angles), jnp.sin(angles))


def project_kernel(places, table_rows, early, info_ref, *refs):
    token_refs = list(refs[:len(places)])
    refs = list(refs[len(places):])
    gain_ref, wq_ref, wk_ref, wv_ref, table_ref, q_ref, kv_ref = refs[:7]
    refs = refs[7:]
    core = info_ref[1] % 2
    copies = []
    if early:
        sources = (gain_ref, token_refs[0], wk_ref, wv_ref, wq_ref)
        held, refs = refs[:1] + refs[5:6] + refs[1:4], refs[4:5] + refs[6:]
        sems = refs[1]
        gain_ref, token_refs[0], wk_ref, wv_ref, wq_ref = held
        for at, (source, target) in enumerate(zip(sources, held)):
            copies.append(pltpu.make_async_copy(source, target, sems.at[at]))
            copies[-1].start()
        copies[0].wait()
    normed = refs[0]
    width = gain_ref.shape[1]
    heads = wk_ref.shape[1] // HEAD_WIDTH
    deep = min(1024, width)

    for piece, place in reversed(list(enumerate(places))):
        if piece == 0 and early:
            copies[1].wait()
        first = place(core)
        ref = token_refs[piece]

        def norm_band(index, carry, ref=ref, first=first):
            at = pl.ds(pl.multiple_of(index * BAND, BAND), BAND)
            wide = ref[at, :].astype(jnp.float32)
            scale = lax.rsqrt(jnp.mean(wide * wide, axis=-1, keepdims=True) + EPSILON)
            normed[pl.ds(pl.multiple_of(first + index * BAND, BAND), BAND), :] = (
                wide * scale * gain_ref[...]
            ).astype(jnp.bfloat16)
            return carry

        lax.fori_loop(0, ref.shape[0] // BAND, norm_band, 0, unroll=2)

    half = HEAD_WIDTH // 2

    def rotate(value, rows):
        cosine = table_ref[rows, :HEAD_WIDTH]
        sine = table_ref[rows, HEAD_WIDTH:]
        turned = jnp.concatenate([value[:, half:], value[:, :half]], axis=1)
        return (value * cosine + turned * sine).astype(jnp.bfloat16)

    def multiply(weight_of):
        total = None
        for start in range(0, width, deep):
            part = jnp.dot(
                normed[:, start:start + deep],
                weight_of(slice(start, start + deep)),
                preferred_element_type=jnp.float32,
            )
            total = part if total is None else total + part
        return total

    if early:
        copies[2].wait()
        copies[3].wait()
    for head in range(heads):
        at = slice(head * HEAD_WIDTH, (head + 1) * HEAD_WIDTH)
        both = multiply(lambda k: jnp.concatenate([wk_ref[k, at], wv_ref[k, at]], axis=1))
        out = 2 * head * HEAD_WIDTH
        row = 0
        for begin, count in table_rows:
            mine = both[row:row + count]
            kv_ref[row:row + count, out:out + HEAD_WIDTH] = rotate(
                mine[:, :HEAD_WIDTH], slice(begin, begin + count)
            )
            kv_ref[row:row + count, out + HEAD_WIDTH:out + 2 * HEAD_WIDTH] = mine[
                :, HEAD_WIDTH:
            ].astype(jnp.bfloat16)
            row += count
    if early:
        copies[4].wait()
    pair = 2 * HEAD_WIDTH
    for start in range(0, wq_ref.shape[1], pair):
        both = multiply(lambda k: wq_ref[k, start:start + pair])
        row = 0
        for begin, count in table_rows:
            for at in (0, HEAD_WIDTH):
                q_ref[row:row + count, start + at:start + at + HEAD_WIDTH] = rotate(
                    both[row:row + count, at:at + HEAD_WIDTH], slice(begin, begin + count)
                )
            row += count


def project(info, pieces, places, table_rows, gain, w_query, key_weight, value_weight, table, early=False):
    width = gain.shape[1]
    q_cols, k_cols = w_query.shape[1], key_weight.shape[1]
    total = sum(count for _, count in table_rows)
    params = (gain, w_query, key_weight, value_weight)
    scratch = [pltpu.VMEM((total, width), jnp.bfloat16)]
    kind = [VMEM] * (len(pieces) + len(params))
    shapes = [
        jax.ShapeDtypeStruct((total, q_cols), jnp.bfloat16),
        jax.ShapeDtypeStruct((total, 2 * k_cols), jnp.bfloat16),
    ]
    if early:
        scratch.append(pltpu.VMEM(pieces[0].shape, pieces[0].dtype))
        scratch.append(pltpu.SemaphoreType.DMA((5,)))
        params = tuple(in_hbm(array) for array in params)
        shapes += [
            jax.ShapeDtypeStruct(array.shape, array.dtype)
            for array in (gain, key_weight, value_weight, w_query)
        ]
        pieces = [in_hbm(pieces[0])] + list(pieces[1:])
        kind = [HBM] + [VMEM] * (len(pieces) - 1) + [HBM] * len(params)
    return pl.pallas_call(
        functools.partial(project_kernel, places, table_rows, early),
        in_specs=[SMEM] + kind + [VMEM],
        out_specs=[VMEM] * len(shapes),
        out_shape=shapes,
        scratch_shapes=scratch,
        compiler_params=pltpu.CompilerParams(vmem_limit_bytes=28 * MIB),
        cost_estimate=pl.CostEstimate(
            flops=2 * total * width * (q_cols + 2 * k_cols),
            bytes_accessed=2 * width * (q_cols + 2 * k_cols) + 2 * total * width,
            transcendentals=0,
        ),
        name="project",
    )(info, *pieces, *params, table)


def cut_kernel(source, *refs):
    sems = refs[-1]
    copies, first = [], 0
    for at, target in enumerate(refs[:-1]):
        count = target.shape[0]
        copies.append(pltpu.make_async_copy(source.at[pl.ds(first, count)], target, sems.at[at]))
        copies[-1].start()
        first += count
    for copy in copies:
        copy.wait()


def cut(array, counts):
    return pl.pallas_call(
        cut_kernel,
        in_specs=[HBM],
        out_specs=[VMEM] * len(counts),
        out_shape=[jax.ShapeDtypeStruct((rows,) + array.shape[1:], array.dtype) for rows in counts],
        scratch_shapes=[pltpu.SemaphoreType.DMA((len(counts),))],
        compiler_params=pltpu.CompilerParams(vmem_limit_bytes=16 * MIB),
        name="cut",
    )(in_hbm(array))


def ring_order(count):
    return list(range(0, count, 2)) + list(range(count - 1, 0, -2))


def ring_place(place, count):
    return jnp.where(place % 2 == 0, place // 2, count - 1 - place // 2)


def ring_block(at, count):
    at = (at + count) % count
    return jnp.where(at < count // 2, 2 * at, 2 * (count - 1 - at) + 1)


class Gathered:
    def __init__(self, kv):
        count = lax.axis_size("seq")
        total = kv.shape[0]
        chunk = 8 if count % 8 == 0 else 1
        self.chunks, self.latest = count // chunk, ()
        self.arrays = [lax.all_gather(kv, "seq", axis=0, tiled=True)]
        self.slots = [
            lambda place, index, j=j: (
                0,
                pl.multiple_of((index * chunk + j) * total, BAND),
                index * chunk + j,
            )
            for j in range(chunk)
        ]

    def advance(self, *others):
        pass


class Ring:
    def __init__(self, kv):
        self.count, self.chunks, self.stage = lax.axis_size("seq"), 1, 0
        self.order = ring_order(self.count)
        self.arrays, self.slots, self.latest = [], [], ()
        self.front = {1: kv, -1: kv}
        self.hold(kv, 0)

    def hold(self, array, steps):
        count = self.count
        self.slots.append(
            lambda place, index, r=len(self.arrays): (
                r,
                0,
                ring_block(ring_place(place, count) - steps, count),
            )
        )
        self.arrays.append(array)

    def advance(self, *others):
        if self.stage >= self.count // 2:
            return
        self.stage += 1
        fresh = []
        for way in (1, -1) if 2 * self.stage < self.count else (1,):
            value = after(self.front[way], *others) if others else self.front[way]
            pairs = [
                (source, self.order[(at + way) % self.count]) for at, source in enumerate(self.order)
            ]
            self.front[way] = lax.ppermute(value, "seq", pairs)
            fresh.append(self.front[way])
            self.hold(self.front[way], way * self.stage)
        self.latest = tuple(fresh)


class Pairs:
    def __init__(self, kv):
        self.count, self.chunks, self.step = lax.axis_size("seq"), 1, 0
        self.order = ring_order(self.count)
        self.total, self.front, self.latest = kv.shape[0], kv, ()
        self.arrays, self.slots = [kv], []
        self.hold(0, 0, lambda at: at)

    def hold(self, r, first, block_at):
        count = self.count
        self.slots.append(
            lambda place, index: (r, first, ring_block(block_at(ring_place(place, count)), count))
        )

    def beside(self, at, step):
        up = 1 - 2 * (at % 2)
        return (at + (up if step % 2 == 1 else -up) + self.count) % self.count

    def source(self, at, step):
        for back in range(step, 1, -1):
            at = self.beside(at, back)
        return at if step > 1 else self.beside(at, 1)

    def advance(self, *others):
        if self.step >= self.count // 2:
            return
        self.step += 1
        step = self.step
        value = after(self.front, *others) if others else self.front
        pairs = [(source, self.order[self.beside(at, step)]) for at, source in enumerate(self.order)]
        got = lax.ppermute(value, "seq", pairs)
        r = len(self.arrays)
        self.arrays.append(got)
        self.hold(r, 0, lambda at: self.source(at, step))
        if step == 1:
            self.front = jnp.concatenate([self.front, got], axis=0)
        else:
            self.front = got
            self.hold(r, self.total, lambda at: self.beside(self.source(at, step), 1))
        self.latest = (got,)


def attend_kernel(lanes, slots, chunks, q_count, kv_count, begin, end, info_ref, vertical_ref, slash_ref, *refs):
    q_refs, kv_refs, refs = refs[:q_count], refs[q_count:q_count + kv_count], refs[q_count + kv_count:]
    state_refs = refs[:0 if begin else 3 * len(lanes)]
    out_refs = refs[len(state_refs):]
    heads = kv_refs[0].shape[1] // (2 * HEAD_WIDTH)
    place = info_ref[0]
    factor = HEAD_WIDTH ** (-0.5)

    def block_allowed(doc, group, block):
        found = (block == place) | (block == place - 1)
        for s in range(slash_ref.shape[2]):
            found = found | (block == place - slash_ref[doc, group, s])
        for s in range(vertical_ref.shape[2]):
            found = found | ((block == vertical_ref[doc, group, s]) & (block < place - 1))
        return found & (block >= 0)

    for lane, (doc_of, segments, (kv_first, keys_in, base)) in enumerate(lanes):
        doc = doc_of(info_ref[1])
        rows = sum(count for _, _, count in segments)
        rank = QUERY_GROUP * rows
        span = len(slots) * keys_in
        query_at = place * rows + lax.broadcasted_iota(jnp.int32, (rows, span), 0)
        column_at = lax.broadcasted_iota(jnp.int32, (1, span), 1)
        for head in range(heads):
            group = info_ref[1] * heads + head
            queries = jnp.concatenate(
                [
                    q_refs[source][
                        start:start + count,
                        (head * QUERY_GROUP + h) * HEAD_WIDTH:(head * QUERY_GROUP + h + 1) * HEAD_WIDTH,
                    ]
                    for h in range(QUERY_GROUP)
                    for source, start, count in segments
                ],
                axis=0,
            )

            def step(index, carry):
                found = [slot(place, index) for slot in slots]

                def column(at):
                    cols = slice(at * HEAD_WIDTH, (at + 1) * HEAD_WIDTH)
                    parts = []
                    for r, first, _ in found:
                        if isinstance(first, int):
                            where = slice(first + kv_first, first + kv_first + keys_in)
                        else:
                            where = pl.ds(pl.multiple_of(first + kv_first, BAND), keys_in)
                        parts.append(kv_refs[r][where, cols])
                    return jnp.concatenate(parts, axis=0)

                keys, values = column(2 * head), column(2 * head + 1)
                scores = lax.dot_general(
                    queries, keys, (((1,), (1,)), ((), ())), preferred_element_type=jnp.float32
                ) * factor
                key_at = jnp.zeros((1, span), jnp.int32)
                for j, (_, _, block) in enumerate(found):
                    shift = jnp.where(
                        block_allowed(doc, group, block), block * rows + base - j * keys_in, 1 << 30
                    )
                    inside = (column_at >= j * keys_in) & (column_at < (j + 1) * keys_in)
                    key_at = jnp.where(inside, column_at + shift, key_at)
                bias = jnp.where(key_at <= query_at, jnp.float32(0), -jnp.inf)
                scores = (scores.reshape(QUERY_GROUP, rows, span) + bias[None]).reshape(rank, span)
                top = jnp.max(scores, axis=1, keepdims=True)
                if carry is None:
                    raised = jnp.exp(scores - top)
                    return (
                        top,
                        jnp.sum(raised, axis=1, keepdims=True),
                        jnp.dot(
                            raised.astype(jnp.bfloat16), values, preferred_element_type=jnp.float32
                        ),
                    )
                highest, total, mixed = carry
                fresh = jnp.maximum(highest, top)
                safe = jnp.where(fresh == -jnp.inf, jnp.float32(0), fresh)
                fade = jnp.exp(highest - safe)
                raised = jnp.exp(scores - safe)
                part = jnp.sum(raised, axis=1, keepdims=True)
                product = jnp.dot(
                    raised.astype(jnp.bfloat16), values, preferred_element_type=jnp.float32
                )
                return fresh, total * fade + part, mixed * fade + product

            band = slice(head * rank, (head + 1) * rank)
            carry = None
            if not begin:
                top_ref, total_ref, mixed_ref = state_refs[3 * lane:3 * lane + 3]
                carry = (top_ref[band, :1], total_ref[band, :1], mixed_ref[band, :])
            elif chunks > 1:
                carry = (
                    jnp.full((rank, 1), -jnp.inf, jnp.float32),
                    jnp.zeros((rank, 1), jnp.float32),
                    jnp.zeros((rank, HEAD_WIDTH), jnp.float32),
                )
            if chunks > 1:
                carry = lax.fori_loop(0, chunks, step, carry)
            else:
                carry = step(0, carry)
            top, total, mixed = carry
            if not end:
                top_ref, total_ref, mixed_ref = out_refs[3 * lane:3 * lane + 3]
                top_ref[band, :] = jnp.broadcast_to(top, (rank, HEAD_WIDTH))
                total_ref[band, :] = jnp.broadcast_to(total, (rank, HEAD_WIDTH))
                mixed_ref[band, :] = mixed
                continue
            result = (mixed / total).astype(jnp.bfloat16)
            for h in range(QUERY_GROUP):
                cols = slice(
                    (head * QUERY_GROUP + h) * HEAD_WIDTH, (head * QUERY_GROUP + h + 1) * HEAD_WIDTH
                )
                out_refs[lane][:, cols] = result[h * rows:(h + 1) * rows]


def attend(info, vertical, slash, lanes, queries, spread, states=None, end=True):
    q_cols = queries[0].shape[1]
    rows = sum(count for _, _, count in lanes[0][1])
    span = len(spread.slots) * spread.chunks * lanes[0][2][1]
    arrays = spread.arrays
    held = [array for state in states for array in state] if states else []
    if end:
        shapes = [jax.ShapeDtypeStruct((rows, q_cols), jnp.bfloat16)] * len(lanes)
    else:
        shape = (rows * q_cols // HEAD_WIDTH, HEAD_WIDTH)
        shapes = [jax.ShapeDtypeStruct(shape, jnp.float32)] * (3 * len(lanes))
    kernel = functools.partial(
        attend_kernel, lanes, spread.slots, spread.chunks, len(queries), len(arrays), not states, end
    )
    return pl.pallas_call(
        kernel,
        in_specs=[SMEM] * 3 + [VMEM] * (len(queries) + len(arrays) + len(held)),
        out_specs=[VMEM] * len(shapes),
        out_shape=shapes,
        compiler_params=pltpu.CompilerParams(vmem_limit_bytes=28 * MIB),
        cost_estimate=pl.CostEstimate(
            flops=4 * len(lanes) * rows * q_cols * span,
            bytes_accessed=2 * sum(a.size for a in arrays) + 4 * len(lanes) * rows * q_cols,
            transcendentals=len(lanes) * rows * span * q_cols // HEAD_WIDTH,
        ),
        name="attend",
    )(info, vertical, slash, *queries, *arrays, *held)


def deliver_kernel(masks, info_ref, *refs):
    pieces, (out_ref, sems) = refs[:len(masks)], refs[-2:]
    cols = pieces[0].shape[1]
    copies = []
    for at, (mask, piece) in enumerate(zip(masks, pieces)):
        where = pl.ds(pl.multiple_of((info_ref[1] ^ mask) * cols, cols), cols)
        copies.append(pltpu.make_async_copy(piece, out_ref.at[0, :, where], sems.at[at]))
        copies[-1].start()
    for copy in copies:
        copy.wait()


def deliver(info, masks, pieces, count, before=None):
    rows, cols = pieces[0].shape
    begun = () if before is None else (before,)
    return pl.pallas_call(
        functools.partial(deliver_kernel, masks),
        in_specs=[SMEM] + [VMEM] * len(pieces) + [HBM] * len(begun),
        out_specs=HBM,
        out_shape=jax.ShapeDtypeStruct((1, rows, count * cols), jnp.bfloat16),
        input_output_aliases={1 + len(pieces): 0} if begun else {},
        scratch_shapes=[pltpu.SemaphoreType.DMA((len(pieces),))],
        compiler_params=pltpu.CompilerParams(vmem_limit_bytes=16 * MIB),
        name="deliver",
    )(info, *pieces, *begun)


def local(tokens, norm_gain, w_query, key_weight, value_weight, vertical_blocks, slash_offsets):
    _, rows, width = tokens.shape
    assert lax.axis_size("doc") == 4
    place = lax.axis_index("seq")
    doc_place = lax.axis_index("doc")
    info = jnp.stack([place, doc_place]).astype(jnp.int32)
    cosine, sine = rope_table(place * rows + jnp.arange(rows, dtype=jnp.int32), HEAD_WIDTH)
    table = jnp.concatenate([cosine, cosine, -sine, sine], axis=1)
    own = tokens[0]
    gain = norm_gain.reshape(1, width)
    weights = (w_query, key_weight, value_weight)
    pattern = (info, vertical_blocks, slash_offsets)
    head = rows * 3 // 4 // BAND * BAND
    tail = rows - head

    twin = swap(own, "doc", 1)
    send_head, send_tail = cut(own, (head, tail))
    got_head = swap(send_head, "doc", 2)
    q_near, kv_near, gain_in, wk_in, wv_in, wq_in = project(
        info,
        [own, twin],
        [lambda c: 0, lambda c: rows],
        [(0, rows), (0, rows)],
        gain,
        *weights,
        table,
        early=True,
    )
    params = (gain_in, wq_in, wk_in, wv_in, table)
    long = lax.axis_size("seq") > 8 or lax.axis_size("seq") % 2 == 1
    ring, pairs = (Gathered, Gathered) if long else (Ring, Pairs)
    near = ring(kv_near)
    near.advance()
    near.advance()
    got_head = after(got_head, *near.latest)

    got_tail = swap(after(send_tail, got_head), "doc", 2)
    head_twin = swap(got_head, "doc", 1)
    near.advance()
    q_head, kv_head = project(
        info,
        [got_head, head_twin],
        [lambda c: 0, lambda c: head],
        [(0, head), (0, head)],
        *params,
    )
    early = ring(kv_head)
    early.advance()

    got_tail = after(got_tail, *near.latest, *early.latest)
    near.advance()
    tail_twin = swap(got_tail, "doc", 1)
    early.advance()
    q_tail, kv_tail = project(
        info,
        [got_tail, tail_twin],
        [lambda c: 0, lambda c: tail],
        [(head, tail), (head, tail)],
        *params,
    )
    late = pairs(kv_tail)
    late.advance()
    mixed_own, mixed_twin = attend(
        *pattern,
        [
            (lambda d: d, [(0, 0, rows)], (0, rows, 0)),
            (lambda d: d ^ 1, [(0, rows, rows)], (rows, rows, 0)),
        ],
        [after(q_near, kv_tail)],
        near,
    )
    out_twin = swap(mixed_twin, "doc", 1)
    early.advance()
    late.advance(mixed_twin)
    early.advance()
    late.advance()
    late.advance()
    remote = [
        (lambda d: d ^ 2, [(0, 0, head), (1, 0, tail)]),
        (lambda d: d ^ 3, [(0, head, head), (1, tail, tail)]),
    ]
    queries = [after(q_head, out_twin), q_tail]
    states = attend(
        *pattern,
        [lane + ((at * head, head, 0),) for at, lane in enumerate(remote)],
        queries,
        early,
        end=False,
    )
    home = []
    for at, lane in enumerate(remote):
        state = states[3 * at:3 * at + 3]
        (mixed,) = attend(
            *pattern, [lane + ((at * tail, tail, head),)], queries, late, states=[state]
        )
        home.append(swap(mixed, "doc", 2 + at))
    count = lax.axis_size("doc")
    result = deliver(info, (0, 1), [mixed_own, out_twin], count)
    return deliver(info, (2, 3), home, count, before=result)


def solution(mesh):
    return jax.shard_map(
        local,
        mesh=mesh,
        in_specs=(
            P("doc", "seq", None),
            P(),
            P(None, "doc"),
            P(None, "doc"),
            P(None, "doc"),
            P(),
            P(),
        ),
        out_specs=P("doc", "seq", None),
        check_vma=False,
    )
```

```python
import functools

import jax
import jax.numpy as jnp
from jax import lax
from jax.experimental import pallas as pl
from jax.experimental.pallas import tpu as pltpu
from jax.sharding import PartitionSpec as P

HEAD_WIDTH = 128
QUERY_HEADS = 16
KEY_VALUE_HEADS = 4
QUERY_GROUP = QUERY_HEADS // KEY_VALUE_HEADS
EPSILON = 1e-05
BAND = 16
MIB = 1024 * 1024
OUT_OF_REACH = 1 << 30

SMEM = pl.BlockSpec(memory_space=pltpu.SMEM)
VMEM = pl.BlockSpec(memory_space=pltpu.VMEM)
ANYWHERE = pl.BlockSpec(memory_space=pl.ANY)
HBM = pl.BlockSpec(memory_space=pltpu.HBM)


def swap(value, axis, mask):
    count = lax.axis_size(axis)
    return lax.ppermute(value, axis, [(source, source ^ mask) for source in range(count)])


def after(value, *others):
    return lax.optimization_barrier((value,) + others)[0]


def in_hbm(array):
    return pltpu.with_memory_space_constraint(array, pltpu.HBM)


def rope_table(positions, width):
    inverse = jnp.power(jnp.float32(500000.0), -jnp.arange(0, width, 2, dtype=jnp.float32) / width)
    angles = positions.astype(jnp.float32)[:, None] * inverse[None, :]
    return (jnp.cos(angles), jnp.sin(angles))


def project_kernel(places, table_rows, early, info_ref, *refs):
    token_refs = list(refs[:len(places)])
    refs = list(refs[len(places):])
    gain_ref, wq_ref, wk_ref, wv_ref, table_ref, q_ref, kv_ref = refs[:7]
    refs = refs[7:]
    core = info_ref[1] % 2
    copies = []
    if early:
        sources = (gain_ref, token_refs[0], wk_ref, wv_ref, wq_ref)
        held, refs = refs[:1] + refs[5:6] + refs[1:4], refs[4:5] + refs[6:]
        sems = refs[1]
        gain_ref, token_refs[0], wk_ref, wv_ref, wq_ref = held
        for at, (source, target) in enumerate(zip(sources, held)):
            copies.append(pltpu.make_async_copy(source, target, sems.at[at]))
            copies[-1].start()
        copies[0].wait()
    normed = refs[0]
    width = gain_ref.shape[1]
    heads = wk_ref.shape[1] // HEAD_WIDTH
    deep = min(1024, width)

    for piece, place in reversed(list(enumerate(places))):
        if piece == 0 and early:
            copies[1].wait()
        first = place(core)
        ref = token_refs[piece]

        def norm_band(index, carry, ref=ref, first=first):
            at = pl.ds(pl.multiple_of(index * BAND, BAND), BAND)
            wide = ref[at, :].astype(jnp.float32)
            scale = lax.rsqrt(jnp.mean(wide * wide, axis=-1, keepdims=True) + EPSILON)
            normed[pl.ds(pl.multiple_of(first + index * BAND, BAND), BAND), :] = (
                wide * scale * gain_ref[...]
            ).astype(jnp.bfloat16)
            return carry

        lax.fori_loop(0, ref.shape[0] // BAND, norm_band, 0, unroll=2)

    half = HEAD_WIDTH // 2

    def rotate(value, rows):
        cosine = table_ref[rows, :HEAD_WIDTH]
        sine = table_ref[rows, HEAD_WIDTH:]
        turned = jnp.concatenate([value[:, half:], value[:, :half]], axis=1)
        return (value * cosine + turned * sine).astype(jnp.bfloat16)

    def multiply(weight_of):
        total = None
        for start in range(0, width, deep):
            part = jnp.dot(
                normed[:, start:start + deep],
                weight_of(slice(start, start + deep)),
                preferred_element_type=jnp.float32,
            )
            total = part if total is None else total + part
        return total

    if early:
        copies[2].wait()
        copies[3].wait()
    for head in range(heads):
        at = slice(head * HEAD_WIDTH, (head + 1) * HEAD_WIDTH)
        both = multiply(lambda k: jnp.concatenate([wk_ref[k, at], wv_ref[k, at]], axis=1))
        out = 2 * head * HEAD_WIDTH
        row = 0
        for begin, count in table_rows:
            mine = both[row:row + count]
            kv_ref[row:row + count, out:out + HEAD_WIDTH] = rotate(
                mine[:, :HEAD_WIDTH], slice(begin, begin + count)
            )
            kv_ref[row:row + count, out + HEAD_WIDTH:out + 2 * HEAD_WIDTH] = mine[
                :, HEAD_WIDTH:
            ].astype(jnp.bfloat16)
            row += count
    if early:
        copies[4].wait()
    pair = 2 * HEAD_WIDTH
    for start in range(0, wq_ref.shape[1], pair):
        both = multiply(lambda k: wq_ref[k, start:start + pair])
        row = 0
        for begin, count in table_rows:
            for at in (0, HEAD_WIDTH):
                q_ref[row:row + count, start + at:start + at + HEAD_WIDTH] = rotate(
                    both[row:row + count, at:at + HEAD_WIDTH], slice(begin, begin + count)
                )
            row += count


def project(info, pieces, places, table_rows, gain, w_query, key_weight, value_weight, table, early=False):
    width = gain.shape[1]
    q_cols, k_cols = w_query.shape[1], key_weight.shape[1]
    total = sum(count for _, count in table_rows)
    params = (gain, w_query, key_weight, value_weight)
    scratch = [pltpu.VMEM((total, width), jnp.bfloat16)]
    kind = [VMEM] * (len(pieces) + len(params))
    shapes = [
        jax.ShapeDtypeStruct((total, q_cols), jnp.bfloat16),
        jax.ShapeDtypeStruct((total, 2 * k_cols), jnp.bfloat16),
    ]
    if early:
        scratch.append(pltpu.VMEM(pieces[0].shape, pieces[0].dtype))
        scratch.append(pltpu.SemaphoreType.DMA((5,)))
        params = tuple(in_hbm(array) for array in params)
        shapes += [
            jax.ShapeDtypeStruct(array.shape, array.dtype)
            for array in (gain, key_weight, value_weight, w_query)
        ]
        pieces = [in_hbm(pieces[0])] + list(pieces[1:])
        kind = [HBM] + [VMEM] * (len(pieces) - 1) + [HBM] * len(params)
    return pl.pallas_call(
        functools.partial(project_kernel, places, table_rows, early),
        in_specs=[SMEM] + kind + [VMEM],
        out_specs=[VMEM] * len(shapes),
        out_shape=shapes,
        scratch_shapes=scratch,
        compiler_params=pltpu.CompilerParams(vmem_limit_bytes=28 * MIB),
        cost_estimate=pl.CostEstimate(
            flops=2 * total * width * (q_cols + 2 * k_cols),
            bytes_accessed=2 * width * (q_cols + 2 * k_cols) + 2 * total * width,
            transcendentals=0,
        ),
        name="project",
    )(info, *pieces, *params, table)


def cut_kernel(source, *refs):
    sems = refs[-1]
    copies, first = [], 0
    for at, target in enumerate(refs[:-1]):
        count = target.shape[0]
        copies.append(pltpu.make_async_copy(source.at[pl.ds(first, count)], target, sems.at[at]))
        copies[-1].start()
        first += count
    for copy in copies:
        copy.wait()


def cut(array, counts):
    return pl.pallas_call(
        cut_kernel,
        in_specs=[HBM],
        out_specs=[VMEM] * len(counts),
        out_shape=[jax.ShapeDtypeStruct((rows,) + array.shape[1:], array.dtype) for rows in counts],
        scratch_shapes=[pltpu.SemaphoreType.DMA((len(counts),))],
        compiler_params=pltpu.CompilerParams(vmem_limit_bytes=16 * MIB),
        name="cut",
    )(in_hbm(array))


def ring_order(count):
    return list(range(0, count, 2)) + list(range(count - 1, 0, -2))


class Gathered:
    kind = 0

    def __init__(self, kv):
        count = lax.axis_size("seq")
        total = kv.shape[0]
        chunk = 8 if count % 8 == 0 else 1
        self.chunks, self.latest = count // chunk, ()
        self.arrays = [lax.all_gather(kv, "seq", axis=0, tiled=True)]
        self.slots = [
            lambda index, j=j: (0, pl.multiple_of((index * chunk + j) * total, BAND))
            for j in range(chunk)
        ]

    def advance(self, *others):
        pass


class Ring:
    kind = 0

    def __init__(self, kv):
        self.count, self.chunks, self.stage = lax.axis_size("seq"), 1, 0
        self.order = ring_order(self.count)
        self.arrays, self.slots, self.latest = [], [], ()
        self.front = {1: kv, -1: kv}
        self.hold(kv)

    @staticmethod
    def sources(at, count):
        steps = [0]
        for stage in range(1, count // 2 + 1):
            steps += [stage, -stage] if 2 * stage < count else [stage]
        return [(at - step) % count for step in steps]

    def hold(self, array):
        self.slots.append(lambda index, r=len(self.arrays): (r, 0))
        self.arrays.append(array)

    def advance(self, *others):
        if self.stage >= self.count // 2:
            return
        self.stage += 1
        fresh = []
        for way in (1, -1) if 2 * self.stage < self.count else (1,):
            value = after(self.front[way], *others) if others else self.front[way]
            pairs = [
                (source, self.order[(at + way) % self.count]) for at, source in enumerate(self.order)
            ]
            self.front[way] = lax.ppermute(value, "seq", pairs)
            fresh.append(self.front[way])
            self.hold(self.front[way])
        self.latest = tuple(fresh)


class Pairs:
    kind = 1

    def __init__(self, kv):
        self.count, self.chunks, self.step = lax.axis_size("seq"), 1, 0
        self.order = ring_order(self.count)
        self.total, self.front, self.latest = kv.shape[0], kv, ()
        self.arrays, self.slots = [kv], [lambda index: (0, 0)]

    @staticmethod
    def beside(at, step, count):
        return (at + (1 if (at + step) % 2 == 1 else -1)) % count

    @staticmethod
    def sources(at, count):
        def first(at, step):
            if step == 1:
                return Pairs.beside(at, 1, count)
            for back in range(step, 1, -1):
                at = Pairs.beside(at, back, count)
            return at

        found = [at, first(at, 1)]
        for step in range(2, count // 2 + 1):
            found += [first(at, step), Pairs.beside(first(at, step), 1, count)]
        return found

    def advance(self, *others):
        if self.step >= self.count // 2:
            return
        self.step += 1
        step = self.step
        value = after(self.front, *others) if others else self.front
        pairs = [
            (source, self.order[self.beside(at, step, self.count)])
            for at, source in enumerate(self.order)
        ]
        got = lax.ppermute(value, "seq", pairs)
        r = len(self.arrays)
        self.arrays.append(got)
        self.slots.append(lambda index: (r, 0))
        if step == 1:
            self.front = jnp.concatenate([self.front, got], axis=0)
        else:
            self.front = got
            self.slots.append(lambda index: (r, self.total))
        self.latest = (got,)


def plan_kernel(kinds, lanes, heads, count, rows, info_ref, vertical_ref, slash_ref, plan_ref):
    place, me = info_ref[0], info_ref[1]
    plan_ref[0] = place

    def enter(number, kind, block):
        for lane in range(lanes):
            doc = me ^ lane
            for head in range(heads):
                group = me * heads + head
                found = (block == place) | (block == place - 1)
                for s in range(slash_ref.shape[2]):
                    found = found | (block == place - slash_ref[doc, group, s])
                for s in range(vertical_ref.shape[2]):
                    found = found | ((block == vertical_ref[doc, group, s]) & (block < place - 1))
                at = 1 + ((kind * lanes + lane) * heads + head) * count + number
                plan_ref[at] = jnp.where(found & (block >= 0), block * rows, OUT_OF_REACH)

    if kinds:
        order = ring_order(count)
        for kind, maker in enumerate(kinds):
            lists = {order[at]: [order[r] for r in maker.sources(at, count)] for at in range(count)}
            for number in range(count):
                block = jnp.int32(0)
                for here, blocks in lists.items():
                    block = jnp.where(place == here, blocks[number], block)
                enter(number, kind, block)
    else:

        def one(number, carry):
            enter(number, 0, number)
            return carry

        lax.fori_loop(0, count, one, 0)


def plan(info, vertical, slash, kinds, rows):
    count, lanes = lax.axis_size("seq"), lax.axis_size("doc")
    heads = vertical.shape[1] // lanes
    length = 1 + max(len(kinds), 1) * lanes * heads * count
    return pl.pallas_call(
        functools.partial(plan_kernel, kinds, lanes, heads, count, rows),
        in_specs=[SMEM] * 3,
        out_specs=SMEM,
        out_shape=jax.ShapeDtypeStruct((length,), jnp.int32),
        compiler_params=pltpu.CompilerParams(vmem_limit_bytes=16 * MIB),
        name="plan",
    )(info, vertical, slash)


def attend_kernel(lanes, documents, kind, slots, chunks, q_count, kv_count, begin, end, plan_ref, *refs):
    q_refs, kv_refs, refs = refs[:q_count], refs[q_count:q_count + kv_count], refs[q_count + kv_count:]
    state_refs = refs[:0 if begin else 3 * len(lanes)]
    out_refs = refs[len(state_refs):]
    heads = kv_refs[0].shape[1] // (2 * HEAD_WIDTH)
    place = plan_ref[0]
    factor = HEAD_WIDTH ** (-0.5)

    for lane, (mask, segments, (kv_first, keys_in, base)) in enumerate(lanes):
        rows = sum(count for _, _, count in segments)
        rank = QUERY_GROUP * rows
        span = len(slots) * keys_in
        query_at = place * rows + lax.broadcasted_iota(jnp.int32, (rows, span), 0)
        column_at = lax.broadcasted_iota(jnp.int32, (1, span), 1)
        for head in range(heads):
            table = 1 + ((kind * documents + mask) * heads + head) * len(slots) * chunks
            queries = jnp.concatenate(
                [
                    q_refs[source][
                        start:start + count,
                        (head * QUERY_GROUP + h) * HEAD_WIDTH:(head * QUERY_GROUP + h + 1) * HEAD_WIDTH,
                    ]
                    for h in range(QUERY_GROUP)
                    for source, start, count in segments
                ],
                axis=0,
            )

            def step(index, carry):
                found = [slot(index) for slot in slots]

                def column(at):
                    cols = slice(at * HEAD_WIDTH, (at + 1) * HEAD_WIDTH)
                    parts = []
                    for r, first in found:
                        if isinstance(first, int):
                            where = slice(first + kv_first, first + kv_first + keys_in)
                        else:
                            where = pl.ds(pl.multiple_of(first + kv_first, BAND), keys_in)
                        parts.append(kv_refs[r][where, cols])
                    return jnp.concatenate(parts, axis=0)

                keys, values = column(2 * head), column(2 * head + 1)
                scores = lax.dot_general(
                    queries, keys, (((1,), (1,)), ((), ())), preferred_element_type=jnp.float32
                ) * factor
                key_at = jnp.zeros((1, span), jnp.int32)
                for j in range(len(slots)):
                    shift = plan_ref[table + index * len(slots) + j] + (base - j * keys_in)
                    inside = (column_at >= j * keys_in) & (column_at < (j + 1) * keys_in)
                    key_at = jnp.where(inside, column_at + shift, key_at)
                bias = jnp.where(key_at <= query_at, jnp.float32(0), -jnp.inf)
                scores = (scores.reshape(QUERY_GROUP, rows, span) + bias[None]).reshape(rank, span)
                top = jnp.max(scores, axis=1, keepdims=True)
                if carry is None:
                    raised = jnp.exp(scores - top)
                    return (
                        top,
                        jnp.sum(raised, axis=1, keepdims=True),
                        jnp.dot(
                            raised.astype(jnp.bfloat16), values, preferred_element_type=jnp.float32
                        ),
                    )
                highest, total, mixed = carry
                fresh = jnp.maximum(highest, top)
                safe = jnp.where(fresh == -jnp.inf, jnp.float32(0), fresh)
                fade = jnp.exp(highest - safe)
                raised = jnp.exp(scores - safe)
                part = jnp.sum(raised, axis=1, keepdims=True)
                product = jnp.dot(
                    raised.astype(jnp.bfloat16), values, preferred_element_type=jnp.float32
                )
                return fresh, total * fade + part, mixed * fade + product

            band = slice(head * rank, (head + 1) * rank)
            carry = None
            if not begin:
                top_ref, total_ref, mixed_ref = state_refs[3 * lane:3 * lane + 3]
                carry = (top_ref[band, :1], total_ref[band, :1], mixed_ref[band, :])
            elif chunks > 1:
                carry = (
                    jnp.full((rank, 1), -jnp.inf, jnp.float32),
                    jnp.zeros((rank, 1), jnp.float32),
                    jnp.zeros((rank, HEAD_WIDTH), jnp.float32),
                )
            if chunks > 1:
                carry = lax.fori_loop(0, chunks, step, carry)
            else:
                carry = step(0, carry)
            top, total, mixed = carry
            if not end:
                top_ref, total_ref, mixed_ref = out_refs[3 * lane:3 * lane + 3]
                top_ref[band, :] = jnp.broadcast_to(top, (rank, HEAD_WIDTH))
                total_ref[band, :] = jnp.broadcast_to(total, (rank, HEAD_WIDTH))
                mixed_ref[band, :] = mixed
                continue
            result = (mixed / total).astype(jnp.bfloat16)
            for h in range(QUERY_GROUP):
                cols = slice(
                    (head * QUERY_GROUP + h) * HEAD_WIDTH, (head * QUERY_GROUP + h + 1) * HEAD_WIDTH
                )
                out_refs[lane][:, cols] = result[h * rows:(h + 1) * rows]


def attend(table, lanes, queries, spread, states=None, end=True):
    q_cols = queries[0].shape[1]
    rows = sum(count for _, _, count in lanes[0][1])
    span = len(spread.slots) * spread.chunks * lanes[0][2][1]
    arrays = spread.arrays
    held = [array for state in states for array in state] if states else []
    if end:
        shapes = [jax.ShapeDtypeStruct((rows, q_cols), jnp.bfloat16)] * len(lanes)
    else:
        shape = (rows * q_cols // HEAD_WIDTH, HEAD_WIDTH)
        shapes = [jax.ShapeDtypeStruct(shape, jnp.float32)] * (3 * len(lanes))
    kernel = functools.partial(
        attend_kernel,
        lanes,
        lax.axis_size("doc"),
        spread.kind,
        spread.slots,
        spread.chunks,
        len(queries),
        len(arrays),
        not states,
        end,
    )
    return pl.pallas_call(
        kernel,
        in_specs=[SMEM] + [VMEM] * (len(queries) + len(arrays) + len(held)),
        out_specs=[VMEM] * len(shapes),
        out_shape=shapes,
        compiler_params=pltpu.CompilerParams(vmem_limit_bytes=28 * MIB),
        cost_estimate=pl.CostEstimate(
            flops=4 * len(lanes) * rows * q_cols * span,
            bytes_accessed=2 * sum(a.size for a in arrays) + 4 * len(lanes) * rows * q_cols,
            transcendentals=len(lanes) * rows * span * q_cols // HEAD_WIDTH,
        ),
        name="attend",
    )(table, *queries, *arrays, *held)


def deliver_kernel(masks, info_ref, *refs):
    pieces, (out_ref, sems) = refs[:len(masks)], refs[-2:]
    cols = pieces[0].shape[1]
    copies = []
    for at, (mask, piece) in enumerate(zip(masks, pieces)):
        where = pl.ds(pl.multiple_of((info_ref[1] ^ mask) * cols, cols), cols)
        copies.append(pltpu.make_async_copy(piece, out_ref.at[0, :, where], sems.at[at]))
        copies[-1].start()
    for copy in copies:
        copy.wait()


def deliver(info, masks, pieces, count, before=None):
    rows, cols = pieces[0].shape
    begun = () if before is None else (before,)
    return pl.pallas_call(
        functools.partial(deliver_kernel, masks),
        in_specs=[SMEM] + [VMEM] * len(pieces) + [HBM] * len(begun),
        out_specs=HBM,
        out_shape=jax.ShapeDtypeStruct((1, rows, count * cols), jnp.bfloat16),
        input_output_aliases={1 + len(pieces): 0} if begun else {},
        scratch_shapes=[pltpu.SemaphoreType.DMA((len(pieces),))],
        compiler_params=pltpu.CompilerParams(vmem_limit_bytes=16 * MIB),
        name="deliver",
    )(info, *pieces, *begun)


def local(tokens, norm_gain, w_query, key_weight, value_weight, vertical_blocks, slash_offsets):
    _, rows, width = tokens.shape
    assert lax.axis_size("doc") == 4
    place = lax.axis_index("seq")
    doc_place = lax.axis_index("doc")
    info = jnp.stack([place, doc_place]).astype(jnp.int32)
    cosine, sine = rope_table(place * rows + jnp.arange(rows, dtype=jnp.int32), HEAD_WIDTH)
    table = jnp.concatenate([cosine, cosine, -sine, sine], axis=1)
    own = tokens[0]
    gain = norm_gain.reshape(1, width)
    weights = (w_query, key_weight, value_weight)
    long = lax.axis_size("seq") > 8 or lax.axis_size("seq") % 2 == 1
    ring, pairs = (Gathered, Gathered) if long else (Ring, Pairs)
    pattern = plan(info, vertical_blocks, slash_offsets, () if long else (Ring, Pairs), rows)
    head = rows * 3 // 4 // BAND * BAND
    tail = rows - head

    twin = swap(own, "doc", 1)
    send_head, send_tail = cut(own, (head, tail))
    got_head = swap(send_head, "doc", 2)
    q_near, kv_near, gain_in, wk_in, wv_in, wq_in = project(
        info,
        [own, twin],
        [lambda c: 0, lambda c: rows],
        [(0, rows), (0, rows)],
        gain,
        *weights,
        table,
        early=True,
    )
    params = (gain_in, wq_in, wk_in, wv_in, table)
    near = ring(kv_near)
    near.advance()
    near.advance(pattern)
    got_head = after(got_head, *near.latest)

    got_tail = swap(after(send_tail, got_head), "doc", 2)
    head_twin = swap(got_head, "doc", 1)
    near.advance()
    q_head, kv_head = project(
        info,
        [got_head, head_twin],
        [lambda c: 0, lambda c: head],
        [(0, head), (0, head)],
        *params,
    )
    early = ring(kv_head)
    early.advance()

    got_tail = after(got_tail, *near.latest, *early.latest)
    near.advance()
    tail_twin = swap(got_tail, "doc", 1)
    early.advance()
    q_tail, kv_tail = project(
        info,
        [got_tail, tail_twin],
        [lambda c: 0, lambda c: tail],
        [(head, tail), (head, tail)],
        *params,
    )
    late = pairs(kv_tail)
    late.advance()
    mixed_own, mixed_twin = attend(
        pattern,
        [(0, [(0, 0, rows)], (0, rows, 0)), (1, [(0, rows, rows)], (rows, rows, 0))],
        [after(q_near, kv_tail)],
        near,
    )
    out_twin = swap(mixed_twin, "doc", 1)
    early.advance(kv_tail)
    late.advance(mixed_twin)
    early.advance()
    late.advance()
    late.advance()
    remote = [
        (2, [(0, 0, head), (1, 0, tail)]),
        (3, [(0, head, head), (1, tail, tail)]),
    ]
    queries = [after(q_head, out_twin), q_tail]
    states = attend(
        pattern,
        [lane + ((at * head, head, 0),) for at, lane in enumerate(remote)],
        queries,
        early,
        end=False,
    )
    home = []
    for at, lane in enumerate(remote):
        state = states[3 * at:3 * at + 3]
        (mixed,) = attend(
            pattern, [lane + ((at * tail, tail, head),)], queries, late, states=[state]
        )
        home.append(swap(mixed, "doc", 2 + at))
    count = lax.axis_size("doc")
    result = deliver(info, (0, 1), [mixed_own, out_twin], count)
    return deliver(info, (2, 3), home, count, before=result)


def solution(mesh):
    return jax.shard_map(
        local,
        mesh=mesh,
        in_specs=(
            P("doc", "seq", None),
            P(),
            P(None, "doc"),
            P(None, "doc"),
            P(None, "doc"),
            P(),
            P(),
        ),
        out_specs=P("doc", "seq", None),
        check_vma=False,
    )
```

```python
import functools
import math

import jax
import jax.numpy as jnp
from jax import lax
from jax.experimental import pallas as pl
from jax.experimental.pallas import tpu as pltpu
from jax.sharding import PartitionSpec as P

HEAD_WIDTH = 128
QUERY_HEADS = 16
KEY_VALUE_HEADS = 4
QUERY_GROUP = QUERY_HEADS // KEY_VALUE_HEADS
EPSILON = 1e-05
BAND = 16
MIB = 1024 * 1024
OUT_OF_REACH = 1 << 30

SMEM = pl.BlockSpec(memory_space=pltpu.SMEM)
VMEM = pl.BlockSpec(memory_space=pltpu.VMEM)
ANYWHERE = pl.BlockSpec(memory_space=pl.ANY)
HBM = pl.BlockSpec(memory_space=pltpu.HBM)


def swap(value, axis, mask):
    count = lax.axis_size(axis)
    return lax.ppermute(value, axis, [(source, source ^ mask) for source in range(count)])


def after(value, *others):
    return lax.optimization_barrier((value,) + others)[0]


def in_hbm(array):
    return pltpu.with_memory_space_constraint(array, pltpu.HBM)


def rope_table(positions, width):
    inverse = jnp.power(jnp.float32(500000.0), -jnp.arange(0, width, 2, dtype=jnp.float32) / width)
    angles = positions.astype(jnp.float32)[:, None] * inverse[None, :]
    return (jnp.cos(angles), jnp.sin(angles))


def project_kernel(places, table_rows, early, ready, info_ref, *refs):
    token_refs = list(refs[:len(places)])
    refs = list(refs[len(places):])
    gain_ref, wq_ref, wk_ref, wv_ref, table_ref, q_ref, kv_ref = refs[:7]
    refs = refs[7:]
    core = info_ref[1] % 2
    copies = []
    if early:
        sources = (gain_ref, token_refs[0], wk_ref, wv_ref, wq_ref)
        send_ref, refs = refs[0], refs[1:]
        held, refs = refs[:1] + refs[5:6] + refs[1:4], refs[4:5] + refs[6:]
        sems = refs[1]
        gain_ref, token_refs[0], wk_ref, wv_ref, wq_ref = held
        for at, (source, target) in enumerate(zip(sources, held)):
            copies.append(pltpu.make_async_copy(source, target, sems.at[at]))
            copies[-1].start()
        copies[0].wait()
    normed = refs[0]
    width = gain_ref.shape[1]
    heads = wk_ref.shape[1] // HEAD_WIDTH
    deep = min(1024, width)

    for piece, place in reversed(list(enumerate(places))):
        if piece == 0 and early:
            copies[1].wait()
        first = place(core)
        ref = token_refs[piece]
        if ready:
            normed[pl.ds(pl.multiple_of(first, BAND), ref.shape[0]), :] = ref[...]
            continue

        def norm_band(index, carry, ref=ref, first=first):
            at = pl.ds(pl.multiple_of(index * BAND, BAND), BAND)
            wide = ref[at, :].astype(jnp.float32)
            scale = lax.rsqrt(jnp.mean(wide * wide, axis=-1, keepdims=True) + EPSILON)
            normed[pl.ds(pl.multiple_of(first + index * BAND, BAND), BAND), :] = (
                wide * scale * gain_ref[...]
            ).astype(jnp.bfloat16)
            return carry

        lax.fori_loop(0, ref.shape[0] // BAND, norm_band, 0, unroll=2)

    if early:
        send_ref[...] = normed[early:token_refs[0].shape[0], :]
    half = HEAD_WIDTH // 2

    def rotate(value, rows):
        cosine = table_ref[rows, :HEAD_WIDTH]
        sine = table_ref[rows, HEAD_WIDTH:]
        turned = jnp.concatenate([value[:, half:], value[:, :half]], axis=1)
        return (value * cosine + turned * sine).astype(jnp.bfloat16)

    def multiply(weight_of):
        total = None
        for start in range(0, width, deep):
            part = jnp.dot(
                normed[:, start:start + deep],
                weight_of(slice(start, start + deep)),
                preferred_element_type=jnp.float32,
            )
            total = part if total is None else total + part
        return total

    if early:
        copies[2].wait()
        copies[3].wait()
    for head in range(heads):
        at = slice(head * HEAD_WIDTH, (head + 1) * HEAD_WIDTH)
        both = multiply(lambda k: jnp.concatenate([wk_ref[k, at], wv_ref[k, at]], axis=1))
        out = 2 * head * HEAD_WIDTH
        row = 0
        for begin, count in table_rows:
            mine = both[row:row + count]
            kv_ref[row:row + count, out:out + HEAD_WIDTH] = rotate(
                mine[:, :HEAD_WIDTH], slice(begin, begin + count)
            )
            kv_ref[row:row + count, out + HEAD_WIDTH:out + 2 * HEAD_WIDTH] = mine[
                :, HEAD_WIDTH:
            ].astype(jnp.bfloat16)
            row += count
    if early:
        copies[4].wait()
    pair = 2 * HEAD_WIDTH
    for start in range(0, wq_ref.shape[1], pair):
        both = multiply(lambda k: wq_ref[k, start:start + pair])
        row = 0
        for begin, count in table_rows:
            for at in (0, HEAD_WIDTH):
                q_ref[row:row + count, start + at:start + at + HEAD_WIDTH] = rotate(
                    both[row:row + count, at:at + HEAD_WIDTH], slice(begin, begin + count)
                )
            row += count


def project(info, pieces, places, table_rows, gain, w_query, key_weight, value_weight, table, early=0, ready=False):
    width = gain.shape[1]
    q_cols, k_cols = w_query.shape[1], key_weight.shape[1]
    total = sum(count for _, count in table_rows)
    params = (gain, w_query, key_weight, value_weight)
    scratch = [pltpu.VMEM((total, width), jnp.bfloat16)]
    kind = [VMEM] * (len(pieces) + len(params))
    shapes = [
        jax.ShapeDtypeStruct((total, q_cols), jnp.bfloat16),
        jax.ShapeDtypeStruct((total, 2 * k_cols), jnp.bfloat16),
    ]
    if early:
        scratch.append(pltpu.VMEM(pieces[0].shape, pieces[0].dtype))
        scratch.append(pltpu.SemaphoreType.DMA((5,)))
        params = tuple(in_hbm(array) for array in params)
        shapes.append(jax.ShapeDtypeStruct((pieces[0].shape[0] - early, width), jnp.bfloat16))
        shapes += [
            jax.ShapeDtypeStruct(array.shape, array.dtype)
            for array in (gain, key_weight, value_weight, w_query)
        ]
        pieces = [in_hbm(pieces[0])] + list(pieces[1:])
        kind = [HBM] + [VMEM] * (len(pieces) - 1) + [HBM] * len(params)
    return pl.pallas_call(
        functools.partial(project_kernel, places, table_rows, early, ready),
        in_specs=[SMEM] + kind + [VMEM],
        out_specs=[VMEM] * len(shapes),
        out_shape=shapes,
        scratch_shapes=scratch,
        compiler_params=pltpu.CompilerParams(vmem_limit_bytes=28 * MIB),
        cost_estimate=pl.CostEstimate(
            flops=2 * total * width * (q_cols + 2 * k_cols),
            bytes_accessed=2 * width * (q_cols + 2 * k_cols) + 2 * total * width,
            transcendentals=0,
        ),
        name="project",
    )(info, *pieces, *params, table)


def cut_kernel(source, target, sem):
    copy = pltpu.make_async_copy(source.at[pl.ds(0, target.shape[0])], target, sem)
    copy.start()
    copy.wait()


def cut(array, rows):
    return pl.pallas_call(
        cut_kernel,
        in_specs=[HBM],
        out_specs=VMEM,
        out_shape=jax.ShapeDtypeStruct((rows,) + array.shape[1:], array.dtype),
        scratch_shapes=[pltpu.SemaphoreType.DMA],
        compiler_params=pltpu.CompilerParams(vmem_limit_bytes=16 * MIB),
        name="cut",
    )(in_hbm(array))


def ring_order(count):
    return list(range(0, count, 2)) + list(range(count - 1, 0, -2))


class Gathered:
    kind = 0

    def __init__(self, kv):
        count = lax.axis_size("seq")
        total = kv.shape[0]
        chunk = 8 if count % 8 == 0 else 1
        self.chunks, self.latest = count // chunk, ()
        self.arrays = [lax.all_gather(kv, "seq", axis=0, tiled=True)]
        self.slots = [
            lambda index, j=j: (0, pl.multiple_of((index * chunk + j) * total, BAND))
            for j in range(chunk)
        ]

    def advance(self, *others):
        pass


class Ring:
    kind = 0

    def __init__(self, kv):
        self.count, self.chunks, self.stage = lax.axis_size("seq"), 1, 0
        self.order = ring_order(self.count)
        self.arrays, self.slots, self.latest = [], [], ()
        self.front = {1: kv, -1: kv}
        self.hold(kv)

    @staticmethod
    def sources(at, count):
        steps = [0]
        for stage in range(1, count // 2 + 1):
            steps += [stage, -stage] if 2 * stage < count else [stage]
        return [(at - step) % count for step in steps]

    def hold(self, array):
        self.slots.append(lambda index, r=len(self.arrays): (r, 0))
        self.arrays.append(array)

    def advance(self, *others):
        if self.stage >= self.count // 2:
            return
        self.stage += 1
        fresh = []
        for way in (1, -1) if 2 * self.stage < self.count else (1,):
            value = after(self.front[way], *others) if others else self.front[way]
            pairs = [
                (source, self.order[(at + way) % self.count]) for at, source in enumerate(self.order)
            ]
            self.front[way] = lax.ppermute(value, "seq", pairs)
            fresh.append(self.front[way])
            self.hold(self.front[way])
        self.latest = tuple(fresh)


class Pairs:
    kind = 1

    def __init__(self, kv):
        self.count, self.chunks, self.step = lax.axis_size("seq"), 1, 0
        self.order = ring_order(self.count)
        self.total, self.front, self.latest = kv.shape[0], kv, ()
        self.arrays, self.slots = [kv], [lambda index: (0, 0)]

    @staticmethod
    def beside(at, step, count):
        return (at + (1 if (at + step) % 2 == 1 else -1)) % count

    @staticmethod
    def sources(at, count):
        def first(at, step):
            if step == 1:
                return Pairs.beside(at, 1, count)
            for back in range(step, 1, -1):
                at = Pairs.beside(at, back, count)
            return at

        found = [at, first(at, 1)]
        for step in range(2, count // 2 + 1):
            found += [first(at, step), Pairs.beside(first(at, step), 1, count)]
        return found

    def advance(self, *others):
        if self.step >= self.count // 2:
            return
        self.step += 1
        step = self.step
        value = after(self.front, *others) if others else self.front
        pairs = [
            (source, self.order[self.beside(at, step, self.count)])
            for at, source in enumerate(self.order)
        ]
        got = lax.ppermute(value, "seq", pairs)
        r = len(self.arrays)
        self.arrays.append(got)
        self.slots.append(lambda index: (r, 0))
        if step == 1:
            self.front = jnp.concatenate([self.front, got], axis=0)
        else:
            self.front = got
            self.slots.append(lambda index: (r, self.total))
        self.latest = (got,)


def plan_kernel(kinds, lanes, heads, count, rows, info_ref, vertical_ref, slash_ref, plan_ref):
    place, me = info_ref[0], info_ref[1]
    plan_ref[0] = place

    def enter(number, kind, block):
        for lane in range(lanes):
            doc = me ^ lane
            for head in range(heads):
                group = me * heads + head
                found = (block == place) | (block == place - 1)
                for s in range(slash_ref.shape[2]):
                    found = found | (block == place - slash_ref[doc, group, s])
                for s in range(vertical_ref.shape[2]):
                    found = found | ((block == vertical_ref[doc, group, s]) & (block < place - 1))
                at = 1 + ((kind * lanes + lane) * heads + head) * count + number
                plan_ref[at] = jnp.where(found & (block >= 0), block * rows, OUT_OF_REACH)

    if kinds:
        order = ring_order(count)
        for kind, maker in enumerate(kinds):
            lists = {order[at]: [order[r] for r in maker.sources(at, count)] for at in range(count)}
            for number in range(count):
                block = jnp.int32(0)
                for here, blocks in lists.items():
                    block = jnp.where(place == here, blocks[number], block)
                enter(number, kind, block)
    else:

        def one(number, carry):
            enter(number, 0, number)
            return carry

        lax.fori_loop(0, count, one, 0)


def plan(info, vertical, slash, kinds, rows):
    count, lanes = lax.axis_size("seq"), lax.axis_size("doc")
    heads = vertical.shape[1] // lanes
    length = 1 + max(len(kinds), 1) * lanes * heads * count
    return pl.pallas_call(
        functools.partial(plan_kernel, kinds, lanes, heads, count, rows),
        in_specs=[SMEM] * 3,
        out_specs=SMEM,
        out_shape=jax.ShapeDtypeStruct((length,), jnp.int32),
        compiler_params=pltpu.CompilerParams(vmem_limit_bytes=16 * MIB),
        name="plan",
    )(info, vertical, slash)


def attend_kernel(lanes, documents, kind, slots, chunks, q_count, kv_count, begin, end, plan_ref, *refs):
    q_refs, kv_refs, refs = refs[:q_count], refs[q_count:q_count + kv_count], refs[q_count + kv_count:]
    state_refs = refs[:0 if begin else 3 * len(lanes)]
    out_refs = refs[len(state_refs):]
    heads = kv_refs[0].shape[1] // (2 * HEAD_WIDTH)
    place = plan_ref[0]
    factor = HEAD_WIDTH ** (-0.5) * math.log2(math.e)

    for lane, (mask, segments, (kv_first, keys_in, base)) in enumerate(lanes):
        rows = sum(count for _, _, count in segments)
        rank = QUERY_GROUP * rows
        row_at = place * rows + lax.broadcasted_iota(jnp.int32, (1, rows), 1)
        query_at = jnp.concatenate([row_at] * QUERY_GROUP, axis=1)
        key_at = base + lax.broadcasted_iota(jnp.int32, (keys_in, rank), 0)
        for head in range(heads):
            table = 1 + ((kind * documents + mask) * heads + head) * len(slots) * chunks
            queries = jnp.concatenate(
                [
                    q_refs[source][
                        start:start + count,
                        (head * QUERY_GROUP + h) * HEAD_WIDTH:(head * QUERY_GROUP + h + 1) * HEAD_WIDTH,
                    ]
                    for h in range(QUERY_GROUP)
                    for source, start, count in segments
                ],
                axis=0,
            )

            def step(index, carry):
                found = [slot(index) for slot in slots]

                def column(at):
                    cols = slice(at * HEAD_WIDTH, (at + 1) * HEAD_WIDTH)
                    parts = []
                    for r, first in found:
                        if isinstance(first, int):
                            where = slice(first + kv_first, first + kv_first + keys_in)
                        else:
                            where = pl.ds(pl.multiple_of(first + kv_first, BAND), keys_in)
                        parts.append(kv_refs[r][where, cols])
                    return jnp.concatenate(parts, axis=0)

                keys, values = column(2 * head), column(2 * head + 1)
                scores = lax.dot_general(
                    keys, queries, (((1,), (1,)), ((), ())), preferred_element_type=jnp.float32
                )
                parts = []
                for j in range(len(slots)):
                    shift = plan_ref[table + index * len(slots) + j]
                    parts.append(
                        jnp.where(
                            key_at <= query_at - shift,
                            scores[j * keys_in:(j + 1) * keys_in],
                            -jnp.inf,
                        )
                    )
                scores = jnp.concatenate(parts, axis=0)
                top = jnp.max(scores, axis=0, keepdims=True)
                if carry is None:
                    fresh = safe = top
                else:
                    fresh = jnp.maximum(carry[0], top)
                    safe = jnp.where(fresh == -jnp.inf, jnp.float32(0), fresh)
                raised = jnp.exp2((scores - safe) * factor)
                total = jnp.sum(raised, axis=0, keepdims=True)
                mixed = lax.dot_general(
                    values,
                    raised.astype(jnp.bfloat16),
                    (((0,), (0,)), ((), ())),
                    preferred_element_type=jnp.float32,
                )
                if carry is not None:
                    fade = jnp.exp2((carry[0] - safe) * factor)
                    total, mixed = carry[1] * fade + total, carry[2] * fade + mixed
                return fresh, total, mixed

            carry = None
            if not begin:
                carry = tuple(ref[head] for ref in state_refs[3 * lane:3 * lane + 3])
            elif chunks > 1:
                carry = (
                    jnp.full((1, rank), -jnp.inf, jnp.float32),
                    jnp.zeros((1, rank), jnp.float32),
                    jnp.zeros((HEAD_WIDTH, rank), jnp.float32),
                )
            if chunks > 1:
                carry = lax.fori_loop(0, chunks, step, carry)
            else:
                carry = step(0, carry)
            if not end:
                for ref, value in zip(out_refs[3 * lane:3 * lane + 3], carry):
                    ref[head] = value
                continue
            result = carry[2] / carry[1]
            for h in range(QUERY_GROUP):
                cols = slice(
                    (head * QUERY_GROUP + h) * HEAD_WIDTH, (head * QUERY_GROUP + h + 1) * HEAD_WIDTH
                )
                out_refs[lane][:, cols] = result[:, h * rows:(h + 1) * rows].T.astype(jnp.bfloat16)


def attend(table, lanes, queries, spread, states=None, end=True):
    q_cols = queries[0].shape[1]
    rows = sum(count for _, _, count in lanes[0][1])
    span = len(spread.slots) * spread.chunks * lanes[0][2][1]
    arrays = spread.arrays
    held = [array for state in states for array in state] if states else []
    if end:
        shapes = [jax.ShapeDtypeStruct((rows, q_cols), jnp.bfloat16)] * len(lanes)
    else:
        heads = q_cols // (QUERY_GROUP * HEAD_WIDTH)
        shapes = [
            jax.ShapeDtypeStruct((heads, deep, QUERY_GROUP * rows), jnp.float32)
            for deep in (1, 1, HEAD_WIDTH)
        ] * len(lanes)
    kernel = functools.partial(
        attend_kernel,
        lanes,
        lax.axis_size("doc"),
        spread.kind,
        spread.slots,
        spread.chunks,
        len(queries),
        len(arrays),
        not states,
        end,
    )
    return pl.pallas_call(
        kernel,
        in_specs=[SMEM] + [VMEM] * (len(queries) + len(arrays) + len(held)),
        out_specs=[VMEM] * len(shapes),
        out_shape=shapes,
        compiler_params=pltpu.CompilerParams(vmem_limit_bytes=28 * MIB),
        cost_estimate=pl.CostEstimate(
            flops=4 * len(lanes) * rows * q_cols * span,
            bytes_accessed=2 * sum(a.size for a in arrays) + 4 * len(lanes) * rows * q_cols,
            transcendentals=len(lanes) * rows * span * q_cols // HEAD_WIDTH,
        ),
        name="attend",
    )(table, *queries, *arrays, *held)


def deliver_kernel(masks, info_ref, *refs):
    pieces, (out_ref, sems) = refs[:len(masks)], refs[-2:]
    cols = pieces[0].shape[1]
    copies = []
    for at, (mask, piece) in enumerate(zip(masks, pieces)):
        where = pl.ds(pl.multiple_of((info_ref[1] ^ mask) * cols, cols), cols)
        copies.append(pltpu.make_async_copy(piece, out_ref.at[0, :, where], sems.at[at]))
        copies[-1].start()
    for copy in copies:
        copy.wait()


def deliver(info, masks, pieces, count, before=None):
    rows, cols = pieces[0].shape
    begun = () if before is None else (before,)
    return pl.pallas_call(
        functools.partial(deliver_kernel, masks),
        in_specs=[SMEM] + [VMEM] * len(pieces) + [HBM] * len(begun),
        out_specs=HBM,
        out_shape=jax.ShapeDtypeStruct((1, rows, count * cols), jnp.bfloat16),
        input_output_aliases={1 + len(pieces): 0} if begun else {},
        scratch_shapes=[pltpu.SemaphoreType.DMA((len(pieces),))],
        compiler_params=pltpu.CompilerParams(vmem_limit_bytes=16 * MIB),
        name="deliver",
    )(info, *pieces, *begun)


def local(tokens, norm_gain, w_query, key_weight, value_weight, vertical_blocks, slash_offsets):
    _, rows, width = tokens.shape
    assert lax.axis_size("doc") == 4
    place = lax.axis_index("seq")
    doc_place = lax.axis_index("doc")
    info = jnp.stack([place, doc_place]).astype(jnp.int32)
    cosine, sine = rope_table(place * rows + jnp.arange(rows, dtype=jnp.int32), HEAD_WIDTH)
    table = jnp.concatenate([cosine, cosine, -sine, sine], axis=1)
    own = tokens[0]
    gain = norm_gain.reshape(1, width)
    weights = (w_query, key_weight, value_weight)
    long = lax.axis_size("seq") > 8 or lax.axis_size("seq") % 2 == 1
    ring, pairs = (Gathered, Gathered) if long else (Ring, Pairs)
    pattern = plan(info, vertical_blocks, slash_offsets, () if long else (Ring, Pairs), rows)
    head = rows * 3 // 4 // BAND * BAND
    tail = rows - head

    twin = swap(own, "doc", 1)
    got_head = swap(cut(own, head), "doc", 2)
    q_near, kv_near, send_tail, gain_in, wk_in, wv_in, wq_in = project(
        info,
        [own, twin],
        [lambda c: 0, lambda c: rows],
        [(0, rows), (0, rows)],
        gain,
        *weights,
        table,
        early=head,
    )
    params = (gain_in, wq_in, wk_in, wv_in, table)
    near = ring(kv_near)
    near.advance()
    near.advance(pattern)
    got_head = after(got_head, *near.latest)

    got_tail = swap(after(send_tail, got_head), "doc", 2)
    head_twin = swap(got_head, "doc", 1)
    near.advance()
    q_head, kv_head = project(
        info,
        [got_head, head_twin],
        [lambda c: 0, lambda c: head],
        [(0, head), (0, head)],
        *params,
    )
    early = ring(kv_head)
    early.advance()

    got_tail = after(got_tail, *near.latest, *early.latest)
    near.advance()
    tail_twin = swap(got_tail, "doc", 1)
    early.advance()
    q_tail, kv_tail = project(
        info,
        [got_tail, tail_twin],
        [lambda c: 0, lambda c: tail],
        [(head, tail), (head, tail)],
        *params,
        ready=True,
    )
    late = pairs(kv_tail)
    late.advance()
    mixed_own, mixed_twin = attend(
        pattern,
        [(0, [(0, 0, rows)], (0, rows, 0)), (1, [(0, rows, rows)], (rows, rows, 0))],
        [after(q_near, kv_tail)],
        near,
    )
    out_twin = swap(mixed_twin, "doc", 1)
    early.advance(mixed_twin)
    late.advance(mixed_twin)
    early.advance()
    late.advance()
    late.advance()
    remote = [
        (2, [(0, 0, head), (1, 0, tail)]),
        (3, [(0, head, head), (1, tail, tail)]),
    ]
    queries = [after(q_head, out_twin), q_tail]
    states = attend(
        pattern,
        [lane + ((at * head, head, 0),) for at, lane in enumerate(remote)],
        queries,
        early,
        end=False,
    )
    home = []
    for at, lane in enumerate(remote):
        state = states[3 * at:3 * at + 3]
        (mixed,) = attend(
            pattern, [lane + ((at * tail, tail, head),)], queries, late, states=[state]
        )
        home.append(swap(mixed, "doc", 2 + at))
    count = lax.axis_size("doc")
    result = deliver(info, (0, 1), [mixed_own, out_twin], count)
    return deliver(info, (2, 3), home, count, before=result)


def solution(mesh):
    return jax.shard_map(
        local,
        mesh=mesh,
        in_specs=(
            P("doc", "seq", None),
            P(),
            P(None, "doc"),
            P(None, "doc"),
            P(None, "doc"),
            P(),
            P(),
        ),
        out_specs=P("doc", "seq", None),
        check_vma=False,
    )
```

```python
import functools
import math

import jax
import jax.numpy as jnp
from jax import lax
from jax.experimental import pallas as pl
from jax.experimental.pallas import tpu as pltpu
from jax.sharding import PartitionSpec as P

HEAD_WIDTH = 128
QUERY_HEADS = 16
KEY_VALUE_HEADS = 4
QUERY_GROUP = QUERY_HEADS // KEY_VALUE_HEADS
EPSILON = 1e-05
BAND = 16
MIB = 1024 * 1024
OUT_OF_REACH = 1 << 30

SMEM = pl.BlockSpec(memory_space=pltpu.SMEM)
VMEM = pl.BlockSpec(memory_space=pltpu.VMEM)
ANYWHERE = pl.BlockSpec(memory_space=pl.ANY)
HBM = pl.BlockSpec(memory_space=pltpu.HBM)


def swap(value, axis, mask):
    count = lax.axis_size(axis)
    return lax.ppermute(value, axis, [(source, source ^ mask) for source in range(count)])


def after(value, *others):
    return lax.optimization_barrier((value,) + others)[0]


def in_hbm(array):
    return pltpu.with_memory_space_constraint(array, pltpu.HBM)


def rope_table(positions, width):
    inverse = jnp.power(jnp.float32(500000.0), -jnp.arange(0, width, 2, dtype=jnp.float32) / width)
    angles = positions.astype(jnp.float32)[:, None] * inverse[None, :]
    return (jnp.cos(angles), jnp.sin(angles))


def project_kernel(places, table_rows, early, ready, info_ref, *refs):
    token_refs = list(refs[:len(places)])
    refs = list(refs[len(places):])
    gain_ref, wq_ref, wk_ref, wv_ref, table_ref, q_ref, kv_ref = refs[:7]
    refs = refs[7:]
    core = info_ref[1] % 2
    copies = []
    if early:
        sources = (gain_ref, token_refs[0], wk_ref, wv_ref, wq_ref)
        send_ref, refs = refs[0], refs[1:]
        held, refs = refs[:1] + refs[5:6] + refs[1:4], refs[4:5] + refs[6:]
        sems = refs[1]
        gain_ref, token_refs[0], wk_ref, wv_ref, wq_ref = held
        for at, (source, target) in enumerate(zip(sources, held)):
            copies.append(pltpu.make_async_copy(source, target, sems.at[at]))
            copies[-1].start()
        copies[0].wait()
    normed = refs[0]
    width = gain_ref.shape[1]
    heads = wk_ref.shape[1] // HEAD_WIDTH
    deep = min(1024, width)

    for piece, place in reversed(list(enumerate(places))):
        if piece == 0 and early:
            copies[1].wait()
        first = place(core)
        ref = token_refs[piece]
        if ready:
            normed[pl.ds(pl.multiple_of(first, BAND), ref.shape[0]), :] = ref[...]
            continue

        def norm_band(index, carry, ref=ref, first=first):
            at = pl.ds(pl.multiple_of(index * BAND, BAND), BAND)
            wide = ref[at, :].astype(jnp.float32)
            scale = lax.rsqrt(jnp.mean(wide * wide, axis=-1, keepdims=True) + EPSILON)
            normed[pl.ds(pl.multiple_of(first + index * BAND, BAND), BAND), :] = (
                wide * scale * gain_ref[...]
            ).astype(jnp.bfloat16)
            return carry

        lax.fori_loop(0, ref.shape[0] // BAND, norm_band, 0, unroll=2)

    if early:
        send_ref[...] = normed[early:token_refs[0].shape[0], :]
    half = HEAD_WIDTH // 2

    def rotate(value, rows):
        cosine = table_ref[rows, :HEAD_WIDTH]
        sine = table_ref[rows, HEAD_WIDTH:]
        turned = jnp.concatenate([value[:, half:], value[:, :half]], axis=1)
        return (value * cosine + turned * sine).astype(jnp.bfloat16)

    def multiply(weight_of):
        total = None
        for start in range(0, width, deep):
            part = jnp.dot(
                normed[:, start:start + deep],
                weight_of(slice(start, start + deep)),
                preferred_element_type=jnp.float32,
            )
            total = part if total is None else total + part
        return total

    if early:
        copies[2].wait()
        copies[3].wait()
    for head in range(heads):
        at = slice(head * HEAD_WIDTH, (head + 1) * HEAD_WIDTH)
        both = multiply(lambda k: jnp.concatenate([wk_ref[k, at], wv_ref[k, at]], axis=1))
        out = 2 * head * HEAD_WIDTH
        row = 0
        for begin, count in table_rows:
            mine = both[row:row + count]
            kv_ref[row:row + count, out:out + HEAD_WIDTH] = rotate(
                mine[:, :HEAD_WIDTH], slice(begin, begin + count)
            )
            kv_ref[row:row + count, out + HEAD_WIDTH:out + 2 * HEAD_WIDTH] = mine[
                :, HEAD_WIDTH:
            ].astype(jnp.bfloat16)
            row += count
    if early:
        copies[4].wait()
    pair = 2 * HEAD_WIDTH
    for start in range(0, wq_ref.shape[1], pair):
        both = multiply(lambda k: wq_ref[k, start:start + pair])
        row = 0
        for begin, count in table_rows:
            for at in (0, HEAD_WIDTH):
                q_ref[row:row + count, start + at:start + at + HEAD_WIDTH] = rotate(
                    both[row:row + count, at:at + HEAD_WIDTH], slice(begin, begin + count)
                )
            row += count


def project(info, pieces, places, table_rows, gain, w_query, key_weight, value_weight, table, early=0, ready=False):
    width = gain.shape[1]
    q_cols, k_cols = w_query.shape[1], key_weight.shape[1]
    total = sum(count for _, count in table_rows)
    params = (gain, w_query, key_weight, value_weight)
    scratch = [pltpu.VMEM((total, width), jnp.bfloat16)]
    kind = [VMEM] * (len(pieces) + len(params))
    shapes = [
        jax.ShapeDtypeStruct((total, q_cols), jnp.bfloat16),
        jax.ShapeDtypeStruct((total, 2 * k_cols), jnp.bfloat16),
    ]
    if early:
        scratch.append(pltpu.VMEM(pieces[0].shape, pieces[0].dtype))
        scratch.append(pltpu.SemaphoreType.DMA((5,)))
        params = tuple(in_hbm(array) for array in params)
        shapes.append(jax.ShapeDtypeStruct((pieces[0].shape[0] - early, width), jnp.bfloat16))
        shapes += [
            jax.ShapeDtypeStruct(array.shape, array.dtype)
            for array in (gain, key_weight, value_weight, w_query)
        ]
        pieces = [in_hbm(pieces[0])] + list(pieces[1:])
        kind = [HBM] + [VMEM] * (len(pieces) - 1) + [HBM] * len(params)
    return pl.pallas_call(
        functools.partial(project_kernel, places, table_rows, early, ready),
        in_specs=[SMEM] + kind + [VMEM],
        out_specs=[VMEM] * len(shapes),
        out_shape=shapes,
        scratch_shapes=scratch,
        compiler_params=pltpu.CompilerParams(vmem_limit_bytes=28 * MIB),
        cost_estimate=pl.CostEstimate(
            flops=2 * total * width * (q_cols + 2 * k_cols),
            bytes_accessed=2 * width * (q_cols + 2 * k_cols) + 2 * total * width,
            transcendentals=0,
        ),
        name="project",
    )(info, *pieces, *params, table)


def cut_kernel(source, target, sem):
    copy = pltpu.make_async_copy(source.at[pl.ds(0, target.shape[0])], target, sem)
    copy.start()
    copy.wait()


def cut(array, rows):
    return pl.pallas_call(
        cut_kernel,
        in_specs=[HBM],
        out_specs=VMEM,
        out_shape=jax.ShapeDtypeStruct((rows,) + array.shape[1:], array.dtype),
        scratch_shapes=[pltpu.SemaphoreType.DMA],
        compiler_params=pltpu.CompilerParams(vmem_limit_bytes=16 * MIB),
        name="cut",
    )(in_hbm(array))


def ring_order(count):
    return list(range(0, count, 2)) + list(range(count - 1, 0, -2))


class Gathered:
    kind = 0

    def __init__(self, kv):
        count = lax.axis_size("seq")
        total = kv.shape[0]
        chunk = 8 if count % 8 == 0 else 1
        self.chunks, self.latest = count // chunk, ()
        self.arrays = [lax.all_gather(kv, "seq", axis=0, tiled=True)]
        self.slots = [
            lambda index, j=j: (0, pl.multiple_of((index * chunk + j) * total, BAND))
            for j in range(chunk)
        ]

    def advance(self, *others):
        pass


class Ring:
    kind = 0

    def __init__(self, kv):
        self.count, self.chunks, self.stage = lax.axis_size("seq"), 1, 0
        self.order = ring_order(self.count)
        self.arrays, self.slots, self.latest = [], [], ()
        self.front = {1: kv, -1: kv}
        self.hold(kv)

    @staticmethod
    def sources(at, count):
        steps = [0]
        for stage in range(1, count // 2 + 1):
            steps += [stage, -stage] if 2 * stage < count else [stage]
        return [(at - step) % count for step in steps]

    def hold(self, array):
        self.slots.append(lambda index, r=len(self.arrays): (r, 0))
        self.arrays.append(array)

    def advance(self, *others):
        if self.stage >= self.count // 2:
            return
        self.stage += 1
        fresh = []
        for way in (1, -1) if 2 * self.stage < self.count else (1,):
            value = after(self.front[way], *others) if others else self.front[way]
            pairs = [
                (source, self.order[(at + way) % self.count]) for at, source in enumerate(self.order)
            ]
            self.front[way] = lax.ppermute(value, "seq", pairs)
            fresh.append(self.front[way])
            self.hold(self.front[way])
        self.latest = tuple(fresh)


class Pairs:
    kind = 1

    def __init__(self, kv):
        self.count, self.chunks, self.step = lax.axis_size("seq"), 1, 0
        self.order = ring_order(self.count)
        self.total, self.front, self.latest = kv.shape[0], kv, ()
        self.arrays, self.slots = [kv], [lambda index: (0, 0)]

    @staticmethod
    def beside(at, step, count):
        return (at + (1 if (at + step) % 2 == 1 else -1)) % count

    @staticmethod
    def sources(at, count):
        def first(at, step):
            if step == 1:
                return Pairs.beside(at, 1, count)
            for back in range(step, 1, -1):
                at = Pairs.beside(at, back, count)
            return at

        found = [at, first(at, 1)]
        for step in range(2, count // 2 + 1):
            found += [first(at, step), Pairs.beside(first(at, step), 1, count)]
        return found

    def advance(self, *others):
        if self.step >= self.count // 2:
            return
        self.step += 1
        step = self.step
        value = after(self.front, *others) if others else self.front
        pairs = [
            (source, self.order[self.beside(at, step, self.count)])
            for at, source in enumerate(self.order)
        ]
        got = lax.ppermute(value, "seq", pairs)
        r = len(self.arrays)
        self.arrays.append(got)
        self.slots.append(lambda index: (r, 0))
        if step == 1:
            self.front = jnp.concatenate([self.front, got], axis=0)
        else:
            self.front = got
            self.slots.append(lambda index: (r, self.total))
        self.latest = (got,)


def plan_kernel(kinds, lanes, heads, count, rows, info_ref, vertical_ref, slash_ref, plan_ref):
    place, me = info_ref[0], info_ref[1]
    plan_ref[0] = place

    def enter(number, kind, block):
        for lane in range(lanes):
            doc = me ^ lane
            for head in range(heads):
                group = me * heads + head
                found = (block == place) | (block == place - 1)
                for s in range(slash_ref.shape[2]):
                    found = found | (block == place - slash_ref[doc, group, s])
                for s in range(vertical_ref.shape[2]):
                    found = found | ((block == vertical_ref[doc, group, s]) & (block < place - 1))
                at = 1 + ((kind * lanes + lane) * heads + head) * count + number
                plan_ref[at] = jnp.where(found & (block >= 0), block * rows, OUT_OF_REACH)

    if kinds:
        order = ring_order(count)
        for kind, maker in enumerate(kinds):
            lists = {order[at]: [order[r] for r in maker.sources(at, count)] for at in range(count)}
            for number in range(count):
                block = jnp.int32(0)
                for here, blocks in lists.items():
                    block = jnp.where(place == here, blocks[number], block)
                enter(number, kind, block)
    else:

        def one(number, carry):
            enter(number, 0, number)
            return carry

        lax.fori_loop(0, count, one, 0)


def plan(info, vertical, slash, kinds, rows):
    count, lanes = lax.axis_size("seq"), lax.axis_size("doc")
    heads = vertical.shape[1] // lanes
    length = 1 + max(len(kinds), 1) * lanes * heads * count
    return pl.pallas_call(
        functools.partial(plan_kernel, kinds, lanes, heads, count, rows),
        in_specs=[SMEM] * 3,
        out_specs=SMEM,
        out_shape=jax.ShapeDtypeStruct((length,), jnp.int32),
        compiler_params=pltpu.CompilerParams(vmem_limit_bytes=16 * MIB),
        name="plan",
    )(info, vertical, slash)


def attend_kernel(lanes, documents, kind, slots, chunks, q_count, kv_count, begin, end, plan_ref, *refs):
    q_refs, kv_refs, refs = refs[:q_count], refs[q_count:q_count + kv_count], refs[q_count + kv_count:]
    state_refs = refs[:0 if begin else 3 * len(lanes)]
    out_refs = refs[len(state_refs):]
    heads = kv_refs[0].shape[1] // (2 * HEAD_WIDTH)
    place = plan_ref[0]
    factor = HEAD_WIDTH ** (-0.5) * math.log2(math.e)

    for lane, (mask, segments, (kv_first, keys_in, base)) in enumerate(lanes):
        rows = sum(count for _, _, count in segments)
        rank = QUERY_GROUP * rows
        row_at = place * rows + lax.broadcasted_iota(jnp.int32, (1, rows), 1)
        query_at = jnp.concatenate([row_at] * QUERY_GROUP, axis=1)
        key_at = base + lax.broadcasted_iota(jnp.int32, (keys_in, rank), 0)
        for head in range(heads):
            table = 1 + ((kind * documents + mask) * heads + head) * len(slots) * chunks
            queries = jnp.concatenate(
                [
                    q_refs[source][
                        start:start + count,
                        (head * QUERY_GROUP + h) * HEAD_WIDTH:(head * QUERY_GROUP + h + 1) * HEAD_WIDTH,
                    ]
                    for h in range(QUERY_GROUP)
                    for source, start, count in segments
                ],
                axis=0,
            )

            def step(index, carry):
                found = [slot(index) for slot in slots]

                def column(at):
                    cols = slice(at * HEAD_WIDTH, (at + 1) * HEAD_WIDTH)
                    parts = []
                    for r, first in found:
                        if isinstance(first, int):
                            where = slice(first + kv_first, first + kv_first + keys_in)
                        else:
                            where = pl.ds(pl.multiple_of(first + kv_first, BAND), keys_in)
                        parts.append(kv_refs[r][where, cols])
                    return jnp.concatenate(parts, axis=0)

                keys, values = column(2 * head), column(2 * head + 1)
                scores = lax.dot_general(
                    keys, queries, (((1,), (1,)), ((), ())), preferred_element_type=jnp.float32
                )
                parts = []
                for j in range(len(slots)):
                    shift = plan_ref[table + index * len(slots) + j]
                    parts.append(
                        jnp.where(
                            key_at <= query_at - shift,
                            scores[j * keys_in:(j + 1) * keys_in],
                            -jnp.inf,
                        )
                    )
                scores = jnp.concatenate(parts, axis=0)
                top = jnp.max(scores, axis=0, keepdims=True)
                if carry is None:
                    fresh = safe = top
                else:
                    fresh = jnp.maximum(carry[0], top)
                    safe = jnp.where(fresh == -jnp.inf, jnp.float32(0), fresh)
                raised = jnp.exp2((scores - safe) * factor)
                total = jnp.sum(raised, axis=0, keepdims=True)
                mixed = lax.dot_general(
                    values,
                    raised.astype(jnp.bfloat16),
                    (((0,), (0,)), ((), ())),
                    preferred_element_type=jnp.float32,
                )
                if carry is not None:
                    fade = jnp.exp2((carry[0] - safe) * factor)
                    total, mixed = carry[1] * fade + total, carry[2] * fade + mixed
                return fresh, total, mixed

            carry = None
            if not begin:
                carry = tuple(ref[head] for ref in state_refs[3 * lane:3 * lane + 3])
            elif chunks > 1:
                carry = (
                    jnp.full((1, rank), -jnp.inf, jnp.float32),
                    jnp.zeros((1, rank), jnp.float32),
                    jnp.zeros((HEAD_WIDTH, rank), jnp.float32),
                )
            if chunks > 1:
                carry = lax.fori_loop(0, chunks, step, carry)
            else:
                carry = step(0, carry)
            if not end:
                for ref, value in zip(out_refs[3 * lane:3 * lane + 3], carry):
                    ref[head] = value
                continue
            result = carry[2] / carry[1]
            for h in range(QUERY_GROUP):
                cols = slice(
                    (head * QUERY_GROUP + h) * HEAD_WIDTH, (head * QUERY_GROUP + h + 1) * HEAD_WIDTH
                )
                out_refs[lane][:, cols] = result[:, h * rows:(h + 1) * rows].T.astype(jnp.bfloat16)


def attend(table, lanes, queries, spread, states=None, end=True):
    q_cols = queries[0].shape[1]
    rows = sum(count for _, _, count in lanes[0][1])
    span = len(spread.slots) * spread.chunks * lanes[0][2][1]
    arrays = spread.arrays
    held = [array for state in states for array in state] if states else []
    if end:
        shapes = [jax.ShapeDtypeStruct((rows, q_cols), jnp.bfloat16)] * len(lanes)
    else:
        heads = q_cols // (QUERY_GROUP * HEAD_WIDTH)
        shapes = [
            jax.ShapeDtypeStruct((heads, deep, QUERY_GROUP * rows), jnp.float32)
            for deep in (1, 1, HEAD_WIDTH)
        ] * len(lanes)
    kernel = functools.partial(
        attend_kernel,
        lanes,
        lax.axis_size("doc"),
        spread.kind,
        spread.slots,
        spread.chunks,
        len(queries),
        len(arrays),
        not states,
        end,
    )
    return pl.pallas_call(
        kernel,
        in_specs=[SMEM] + [VMEM] * (len(queries) + len(arrays) + len(held)),
        out_specs=[VMEM] * len(shapes),
        out_shape=shapes,
        compiler_params=pltpu.CompilerParams(vmem_limit_bytes=28 * MIB),
        cost_estimate=pl.CostEstimate(
            flops=4 * len(lanes) * rows * q_cols * span,
            bytes_accessed=2 * sum(a.size for a in arrays) + 4 * len(lanes) * rows * q_cols,
            transcendentals=len(lanes) * rows * span * q_cols // HEAD_WIDTH,
        ),
        name="attend",
    )(table, *queries, *arrays, *held)


def deliver_kernel(masks, info_ref, *refs):
    pieces, (out_ref, sems) = refs[:len(masks)], refs[-2:]
    cols = pieces[0].shape[1]
    copies = []
    for at, (mask, piece) in enumerate(zip(masks, pieces)):
        where = pl.ds(pl.multiple_of((info_ref[1] ^ mask) * cols, cols), cols)
        copies.append(pltpu.make_async_copy(piece, out_ref.at[0, :, where], sems.at[at]))
        copies[-1].start()
    for copy in copies:
        copy.wait()


def deliver(info, masks, pieces, count, before=None):
    rows, cols = pieces[0].shape
    begun = () if before is None else (before,)
    return pl.pallas_call(
        functools.partial(deliver_kernel, masks),
        in_specs=[SMEM] + [VMEM] * len(pieces) + [HBM] * len(begun),
        out_specs=HBM,
        out_shape=jax.ShapeDtypeStruct((1, rows, count * cols), jnp.bfloat16),
        input_output_aliases={1 + len(pieces): 0} if begun else {},
        scratch_shapes=[pltpu.SemaphoreType.DMA((len(pieces),))],
        compiler_params=pltpu.CompilerParams(vmem_limit_bytes=16 * MIB),
        name="deliver",
    )(info, *pieces, *begun)


def local(tokens, norm_gain, w_query, key_weight, value_weight, vertical_blocks, slash_offsets):
    _, rows, width = tokens.shape
    assert lax.axis_size("doc") == 4
    place = lax.axis_index("seq")
    doc_place = lax.axis_index("doc")
    info = jnp.stack([place, doc_place]).astype(jnp.int32)
    cosine, sine = rope_table(place * rows + jnp.arange(rows, dtype=jnp.int32), HEAD_WIDTH)
    table = jnp.concatenate([cosine, cosine, -sine, sine], axis=1)
    own = tokens[0]
    gain = norm_gain.reshape(1, width)
    weights = (w_query, key_weight, value_weight)
    long = lax.axis_size("seq") > 8 or lax.axis_size("seq") % 2 == 1
    ring, pairs = (Gathered, Gathered) if long else (Ring, Pairs)
    pattern = plan(info, vertical_blocks, slash_offsets, () if long else (Ring, Pairs), rows)
    head = rows * 3 // 4 // BAND * BAND
    tail = rows - head

    twin = swap(own, "doc", 1)
    got_head = swap(cut(own, head), "doc", 2)
    q_near, kv_near, send_tail, gain_in, wk_in, wv_in, wq_in = project(
        info,
        [own, twin],
        [lambda c: 0, lambda c: rows],
        [(0, rows), (0, rows)],
        gain,
        *weights,
        table,
        early=head,
    )
    params = (gain_in, wq_in, wk_in, wv_in, table)
    near = ring(kv_near)
    near.advance()
    near.advance(pattern)
    got_head = after(got_head, *near.latest)

    got_tail = swap(after(send_tail, got_head), "doc", 2)
    head_twin = swap(got_head, "doc", 1)
    near.advance()
    q_head, kv_head = project(
        info,
        [got_head, head_twin],
        [lambda c: 0, lambda c: head],
        [(0, head), (0, head)],
        *params,
    )
    early = ring(kv_head)
    early.advance()

    got_tail = after(got_tail, *near.latest, kv_head)
    near.advance()
    tail_twin = swap(got_tail, "doc", 1)
    q_tail, kv_tail = project(
        info,
        [got_tail, tail_twin],
        [lambda c: 0, lambda c: tail],
        [(head, tail), (head, tail)],
        *params,
        ready=True,
    )
    early.advance(kv_tail)
    late = pairs(kv_tail)
    late.advance()
    mixed_own, mixed_twin = attend(
        pattern,
        [(0, [(0, 0, rows)], (0, rows, 0)), (1, [(0, rows, rows)], (rows, rows, 0))],
        [after(q_near, kv_tail)],
        near,
    )
    out_twin = swap(mixed_twin, "doc", 1)
    early.advance(mixed_twin)
    late.advance(mixed_twin)
    early.advance()
    late.advance()
    late.advance()
    remote = [
        (2, [(0, 0, head), (1, 0, tail)]),
        (3, [(0, head, head), (1, tail, tail)]),
    ]
    queries = [after(q_head, out_twin), q_tail]
    states = attend(
        pattern,
        [lane + ((at * head, head, 0),) for at, lane in enumerate(remote)],
        queries,
        early,
        end=False,
    )
    home = []
    for at, lane in enumerate(remote):
        state = states[3 * at:3 * at + 3]
        (mixed,) = attend(
            pattern, [lane + ((at * tail, tail, head),)], queries, late, states=[state]
        )
        home.append(swap(mixed, "doc", 2 + at))
    count = lax.axis_size("doc")
    result = deliver(info, (0, 1), [mixed_own, out_twin], count)
    return deliver(info, (2, 3), home, count, before=result)


def solution(mesh):
    return jax.shard_map(
        local,
        mesh=mesh,
        in_specs=(
            P("doc", "seq", None),
            P(),
            P(None, "doc"),
            P(None, "doc"),
            P(None, "doc"),
            P(),
            P(),
        ),
        out_specs=P("doc", "seq", None),
        check_vma=False,
    )
```

```python
import functools
import math

import jax
import jax.numpy as jnp
from jax import lax
from jax.experimental import pallas as pl
from jax.experimental.pallas import tpu as pltpu
from jax.sharding import PartitionSpec as P

HEAD_WIDTH = 128
QUERY_HEADS = 16
KEY_VALUE_HEADS = 4
QUERY_GROUP = QUERY_HEADS // KEY_VALUE_HEADS
EPSILON = 1e-05
BAND = 16
MIB = 1024 * 1024
OUT_OF_REACH = 1 << 30

SMEM = pl.BlockSpec(memory_space=pltpu.SMEM)
VMEM = pl.BlockSpec(memory_space=pltpu.VMEM)
ANYWHERE = pl.BlockSpec(memory_space=pl.ANY)
HBM = pl.BlockSpec(memory_space=pltpu.HBM)


def swap(value, axis, mask):
    count = lax.axis_size(axis)
    return lax.ppermute(value, axis, [(source, source ^ mask) for source in range(count)])


def after(value, *others):
    return lax.optimization_barrier((value,) + others)[0]


def in_hbm(array):
    return pltpu.with_memory_space_constraint(array, pltpu.HBM)


def rope_table(positions, width):
    inverse = jnp.power(jnp.float32(500000.0), -jnp.arange(0, width, 2, dtype=jnp.float32) / width)
    angles = positions.astype(jnp.float32)[:, None] * inverse[None, :]
    return (jnp.cos(angles), jnp.sin(angles))


def project_kernel(places, table_rows, early, ready, info_ref, *refs):
    token_refs = list(refs[:len(places)])
    refs = list(refs[len(places):])
    gain_ref, wq_ref, wk_ref, wv_ref, table_ref, q_ref, kv_ref = refs[:7]
    refs = refs[7:]
    core = info_ref[1] % 2
    copies = []
    if early:
        sources = (gain_ref, token_refs[0], wk_ref, wv_ref, wq_ref)
        send_ref, refs = refs[0], refs[1:]
        held, refs = refs[:1] + refs[5:6] + refs[1:4], refs[4:5] + refs[6:]
        sems = refs[1]
        gain_ref, token_refs[0], wk_ref, wv_ref, wq_ref = held
        for at, (source, target) in enumerate(zip(sources, held)):
            copies.append(pltpu.make_async_copy(source, target, sems.at[at]))
            copies[-1].start()
        copies[0].wait()
    normed = refs[0]
    width = gain_ref.shape[1]
    heads = wk_ref.shape[1] // HEAD_WIDTH
    deep = min(1024, width)

    for piece, place in reversed(list(enumerate(places))):
        if piece == 0 and early:
            copies[1].wait()
        first = place(core)
        ref = token_refs[piece]
        if ready:
            normed[pl.ds(pl.multiple_of(first, BAND), ref.shape[0]), :] = ref[...]
            continue

        def norm_band(index, carry, ref=ref, first=first):
            at = pl.ds(pl.multiple_of(index * BAND, BAND), BAND)
            wide = ref[at, :].astype(jnp.float32)
            scale = lax.rsqrt(jnp.mean(wide * wide, axis=-1, keepdims=True) + EPSILON)
            normed[pl.ds(pl.multiple_of(first + index * BAND, BAND), BAND), :] = (
                wide * scale * gain_ref[...]
            ).astype(jnp.bfloat16)
            return carry

        lax.fori_loop(0, ref.shape[0] // BAND, norm_band, 0, unroll=2)

    if early:
        send_ref[...] = normed[early:token_refs[0].shape[0], :]
    half = HEAD_WIDTH // 2

    def rotate(value, rows):
        cosine = table_ref[rows, :HEAD_WIDTH]
        sine = table_ref[rows, HEAD_WIDTH:]
        turned = jnp.concatenate([value[:, half:], value[:, :half]], axis=1)
        return (value * cosine + turned * sine).astype(jnp.bfloat16)

    def multiply(weight_of):
        total = None
        for start in range(0, width, deep):
            part = jnp.dot(
                normed[:, start:start + deep],
                weight_of(slice(start, start + deep)),
                preferred_element_type=jnp.float32,
            )
            total = part if total is None else total + part
        return total

    if early:
        copies[2].wait()
        copies[3].wait()
    for head in range(heads):
        at = slice(head * HEAD_WIDTH, (head + 1) * HEAD_WIDTH)
        both = multiply(lambda k: jnp.concatenate([wk_ref[k, at], wv_ref[k, at]], axis=1))
        out = 2 * head * HEAD_WIDTH
        row = 0
        for begin, count in table_rows:
            mine = both[row:row + count]
            kv_ref[row:row + count, out:out + HEAD_WIDTH] = rotate(
                mine[:, :HEAD_WIDTH], slice(begin, begin + count)
            )
            kv_ref[row:row + count, out + HEAD_WIDTH:out + 2 * HEAD_WIDTH] = mine[
                :, HEAD_WIDTH:
            ].astype(jnp.bfloat16)
            row += count
    if early:
        copies[4].wait()
    pair = 2 * HEAD_WIDTH
    for start in range(0, wq_ref.shape[1], pair):
        both = multiply(lambda k: wq_ref[k, start:start + pair])
        row = 0
        for begin, count in table_rows:
            for at in (0, HEAD_WIDTH):
                q_ref[row:row + count, start + at:start + at + HEAD_WIDTH] = rotate(
                    both[row:row + count, at:at + HEAD_WIDTH], slice(begin, begin + count)
                )
            row += count


def project(info, pieces, places, table_rows, gain, w_query, key_weight, value_weight, table, early=0, ready=False):
    width = gain.shape[1]
    q_cols, k_cols = w_query.shape[1], key_weight.shape[1]
    total = sum(count for _, count in table_rows)
    params = (gain, w_query, key_weight, value_weight)
    scratch = [pltpu.VMEM((total, width), jnp.bfloat16)]
    kind = [VMEM] * (len(pieces) + len(params))
    shapes = [
        jax.ShapeDtypeStruct((total, q_cols), jnp.bfloat16),
        jax.ShapeDtypeStruct((total, 2 * k_cols), jnp.bfloat16),
    ]
    if early:
        scratch.append(pltpu.VMEM(pieces[0].shape, pieces[0].dtype))
        scratch.append(pltpu.SemaphoreType.DMA((5,)))
        params = tuple(in_hbm(array) for array in params)
        shapes.append(jax.ShapeDtypeStruct((pieces[0].shape[0] - early, width), jnp.bfloat16))
        shapes += [
            jax.ShapeDtypeStruct(array.shape, array.dtype)
            for array in (gain, key_weight, value_weight, w_query)
        ]
        pieces = [in_hbm(pieces[0])] + list(pieces[1:])
        kind = [HBM] + [VMEM] * (len(pieces) - 1) + [HBM] * len(params)
    return pl.pallas_call(
        functools.partial(project_kernel, places, table_rows, early, ready),
        in_specs=[SMEM] + kind + [VMEM],
        out_specs=[VMEM] * len(shapes),
        out_shape=shapes,
        scratch_shapes=scratch,
        compiler_params=pltpu.CompilerParams(vmem_limit_bytes=28 * MIB),
        cost_estimate=pl.CostEstimate(
            flops=2 * total * width * (q_cols + 2 * k_cols),
            bytes_accessed=2 * width * (q_cols + 2 * k_cols) + 2 * total * width,
            transcendentals=0,
        ),
        name="project",
    )(info, *pieces, *params, table)


def cut_kernel(source, target, sem):
    copy = pltpu.make_async_copy(source.at[pl.ds(0, target.shape[0])], target, sem)
    copy.start()
    copy.wait()


def cut(array, rows):
    return pl.pallas_call(
        cut_kernel,
        in_specs=[HBM],
        out_specs=VMEM,
        out_shape=jax.ShapeDtypeStruct((rows,) + array.shape[1:], array.dtype),
        scratch_shapes=[pltpu.SemaphoreType.DMA],
        compiler_params=pltpu.CompilerParams(vmem_limit_bytes=16 * MIB),
        name="cut",
    )(in_hbm(array))


def ring_order(count):
    return list(range(0, count, 2)) + list(range(count - 1, 0, -2))


class Gathered:
    kind = 0

    def __init__(self, kv):
        count = lax.axis_size("seq")
        total = kv.shape[0]
        chunk = 8 if count % 8 == 0 else 1
        self.chunks, self.latest = count // chunk, ()
        self.arrays = [lax.all_gather(kv, "seq", axis=0, tiled=True)]
        self.slots = [
            lambda index, j=j: (0, pl.multiple_of((index * chunk + j) * total, BAND))
            for j in range(chunk)
        ]

    def advance(self, *others):
        pass


class Ring:
    kind = 0

    def __init__(self, kv):
        self.count, self.chunks, self.stage = lax.axis_size("seq"), 1, 0
        self.order = ring_order(self.count)
        self.arrays, self.slots, self.latest = [], [], ()
        self.front = {1: kv, -1: kv}
        self.hold(kv)

    @staticmethod
    def sources(at, count):
        steps = [0]
        for stage in range(1, count // 2 + 1):
            steps += [stage, -stage] if 2 * stage < count else [stage]
        return [(at - step) % count for step in steps]

    def hold(self, array):
        self.slots.append(lambda index, r=len(self.arrays): (r, 0))
        self.arrays.append(array)

    def advance(self, *others):
        if self.stage >= self.count // 2:
            return
        self.stage += 1
        fresh = []
        for way in (1, -1) if 2 * self.stage < self.count else (1,):
            value = after(self.front[way], *others) if others else self.front[way]
            pairs = [
                (source, self.order[(at + way) % self.count]) for at, source in enumerate(self.order)
            ]
            self.front[way] = lax.ppermute(value, "seq", pairs)
            fresh.append(self.front[way])
            self.hold(self.front[way])
        self.latest = tuple(fresh)


class Direct:
    kind = 1

    @staticmethod
    def moves(count):
        return [(up, over) for up in reversed(range(count // 2)) for over in (1, 0) if up or over]

    @staticmethod
    def sources(at, count):
        order = ring_order(count)
        z, y = order[at] // 2, order[at] % 2
        places = [order[at]]
        for up, over in Direct.moves(count):
            places.append(2 * ((z - up) % (count // 2)) + (y ^ over))
        return [order.index(place) for place in places]

    def __init__(self, kv, *others):
        count, self.chunks = lax.axis_size("seq"), 1
        self.arrays, deep = [kv], count // 2
        for up, over in self.moves(count):
            pairs = [(s, 2 * ((s // 2 + up) % deep) + (s % 2 ^ over)) for s in range(count)]
            self.arrays.append(lax.ppermute(kv, "seq", pairs))
        self.slots = [lambda index, r=r: (r, 0) for r in range(count)]
        self.latest = tuple(self.arrays[1:])


def plan_kernel(kinds, lanes, heads, count, rows, info_ref, vertical_ref, slash_ref, plan_ref):
    place, me = info_ref[0], info_ref[1]
    plan_ref[0] = place

    def enter(number, kind, block):
        for lane in range(lanes):
            doc = me ^ lane
            for head in range(heads):
                group = me * heads + head
                found = (block == place) | (block == place - 1)
                for s in range(slash_ref.shape[2]):
                    found = found | (block == place - slash_ref[doc, group, s])
                for s in range(vertical_ref.shape[2]):
                    found = found | ((block == vertical_ref[doc, group, s]) & (block < place - 1))
                at = 1 + ((kind * lanes + lane) * heads + head) * count + number
                plan_ref[at] = jnp.where(found & (block >= 0), block * rows, OUT_OF_REACH)

    if kinds:
        order = ring_order(count)
        for kind, maker in enumerate(kinds):
            lists = {order[at]: [order[r] for r in maker.sources(at, count)] for at in range(count)}
            for number in range(count):
                block = jnp.int32(0)
                for here, blocks in lists.items():
                    block = jnp.where(place == here, blocks[number], block)
                enter(number, kind, block)
    else:

        def one(number, carry):
            enter(number, 0, number)
            return carry

        lax.fori_loop(0, count, one, 0)


def plan(info, vertical, slash, kinds, rows):
    count, lanes = lax.axis_size("seq"), lax.axis_size("doc")
    heads = vertical.shape[1] // lanes
    length = 1 + max(len(kinds), 1) * lanes * heads * count
    return pl.pallas_call(
        functools.partial(plan_kernel, kinds, lanes, heads, count, rows),
        in_specs=[SMEM] * 3,
        out_specs=SMEM,
        out_shape=jax.ShapeDtypeStruct((length,), jnp.int32),
        compiler_params=pltpu.CompilerParams(vmem_limit_bytes=16 * MIB),
        name="plan",
    )(info, vertical, slash)


def attend_kernel(lanes, documents, kind, slots, chunks, q_count, kv_count, begin, end, plan_ref, *refs):
    q_refs, kv_refs, refs = refs[:q_count], refs[q_count:q_count + kv_count], refs[q_count + kv_count:]
    state_refs = refs[:0 if begin else 3 * len(lanes)]
    out_refs = refs[len(state_refs):]
    heads = kv_refs[0].shape[1] // (2 * HEAD_WIDTH)
    place = plan_ref[0]
    factor = HEAD_WIDTH ** (-0.5) * math.log2(math.e)

    for lane, (mask, segments, (kv_first, keys_in, base)) in enumerate(lanes):
        rows = sum(count for _, _, count in segments)
        rank = QUERY_GROUP * rows
        row_at = place * rows + lax.broadcasted_iota(jnp.int32, (1, rows), 1)
        query_at = jnp.concatenate([row_at] * QUERY_GROUP, axis=1)
        key_at = base + lax.broadcasted_iota(jnp.int32, (keys_in, rank), 0)
        for head in range(heads):
            table = 1 + ((kind * documents + mask) * heads + head) * len(slots) * chunks
            queries = jnp.concatenate(
                [
                    q_refs[source][
                        start:start + count,
                        (head * QUERY_GROUP + h) * HEAD_WIDTH:(head * QUERY_GROUP + h + 1) * HEAD_WIDTH,
                    ]
                    for h in range(QUERY_GROUP)
                    for source, start, count in segments
                ],
                axis=0,
            )

            def step(index, carry):
                found = [slot(index) for slot in slots]

                def column(at):
                    cols = slice(at * HEAD_WIDTH, (at + 1) * HEAD_WIDTH)
                    parts = []
                    for r, first in found:
                        if isinstance(first, int):
                            where = slice(first + kv_first, first + kv_first + keys_in)
                        else:
                            where = pl.ds(pl.multiple_of(first + kv_first, BAND), keys_in)
                        parts.append(kv_refs[r][where, cols])
                    return jnp.concatenate(parts, axis=0)

                keys, values = column(2 * head), column(2 * head + 1)
                scores = lax.dot_general(
                    keys, queries, (((1,), (1,)), ((), ())), preferred_element_type=jnp.float32
                )
                parts = []
                for j in range(len(slots)):
                    shift = plan_ref[table + index * len(slots) + j]
                    parts.append(
                        jnp.where(
                            key_at <= query_at - shift,
                            scores[j * keys_in:(j + 1) * keys_in],
                            -jnp.inf,
                        )
                    )
                scores = jnp.concatenate(parts, axis=0)
                top = jnp.max(scores, axis=0, keepdims=True)
                if carry is None:
                    fresh = safe = top
                else:
                    fresh = jnp.maximum(carry[0], top)
                    safe = jnp.where(fresh == -jnp.inf, jnp.float32(0), fresh)
                raised = jnp.exp2((scores - safe) * factor)
                total = jnp.sum(raised, axis=0, keepdims=True)
                mixed = lax.dot_general(
                    values,
                    raised.astype(jnp.bfloat16),
                    (((0,), (0,)), ((), ())),
                    preferred_element_type=jnp.float32,
                )
                if carry is not None:
                    fade = jnp.exp2((carry[0] - safe) * factor)
                    total, mixed = carry[1] * fade + total, carry[2] * fade + mixed
                return fresh, total, mixed

            carry = None
            if not begin:
                carry = tuple(ref[head] for ref in state_refs[3 * lane:3 * lane + 3])
            elif chunks > 1:
                carry = (
                    jnp.full((1, rank), -jnp.inf, jnp.float32),
                    jnp.zeros((1, rank), jnp.float32),
                    jnp.zeros((HEAD_WIDTH, rank), jnp.float32),
                )
            if chunks > 1:
                carry = lax.fori_loop(0, chunks, step, carry)
            else:
                carry = step(0, carry)
            if not end:
                for ref, value in zip(out_refs[3 * lane:3 * lane + 3], carry):
                    ref[head] = value
                continue
            result = carry[2] / carry[1]
            for h in range(QUERY_GROUP):
                cols = slice(
                    (head * QUERY_GROUP + h) * HEAD_WIDTH, (head * QUERY_GROUP + h + 1) * HEAD_WIDTH
                )
                out_refs[lane][:, cols] = result[:, h * rows:(h + 1) * rows].T.astype(jnp.bfloat16)


def attend(table, lanes, queries, spread, states=None, end=True):
    q_cols = queries[0].shape[1]
    rows = sum(count for _, _, count in lanes[0][1])
    span = len(spread.slots) * spread.chunks * lanes[0][2][1]
    arrays = spread.arrays
    held = [array for state in states for array in state] if states else []
    if end:
        shapes = [jax.ShapeDtypeStruct((rows, q_cols), jnp.bfloat16)] * len(lanes)
    else:
        heads = q_cols // (QUERY_GROUP * HEAD_WIDTH)
        shapes = [
            jax.ShapeDtypeStruct((heads, deep, QUERY_GROUP * rows), jnp.float32)
            for deep in (1, 1, HEAD_WIDTH)
        ] * len(lanes)
    kernel = functools.partial(
        attend_kernel,
        lanes,
        lax.axis_size("doc"),
        spread.kind,
        spread.slots,
        spread.chunks,
        len(queries),
        len(arrays),
        not states,
        end,
    )
    return pl.pallas_call(
        kernel,
        in_specs=[SMEM] + [VMEM] * (len(queries) + len(arrays) + len(held)),
        out_specs=[VMEM] * len(shapes),
        out_shape=shapes,
        compiler_params=pltpu.CompilerParams(vmem_limit_bytes=28 * MIB),
        cost_estimate=pl.CostEstimate(
            flops=4 * len(lanes) * rows * q_cols * span,
            bytes_accessed=2 * sum(a.size for a in arrays) + 4 * len(lanes) * rows * q_cols,
            transcendentals=len(lanes) * rows * span * q_cols // HEAD_WIDTH,
        ),
        name="attend",
    )(table, *queries, *arrays, *held)


def deliver_kernel(masks, info_ref, *refs):
    pieces, (out_ref, sems) = refs[:len(masks)], refs[-2:]
    cols = pieces[0].shape[1]
    copies = []
    for at, (mask, piece) in enumerate(zip(masks, pieces)):
        where = pl.ds(pl.multiple_of((info_ref[1] ^ mask) * cols, cols), cols)
        copies.append(pltpu.make_async_copy(piece, out_ref.at[0, :, where], sems.at[at]))
        copies[-1].start()
    for copy in copies:
        copy.wait()


def deliver(info, masks, pieces, count, before=None):
    rows, cols = pieces[0].shape
    begun = () if before is None else (before,)
    return pl.pallas_call(
        functools.partial(deliver_kernel, masks),
        in_specs=[SMEM] + [VMEM] * len(pieces) + [HBM] * len(begun),
        out_specs=HBM,
        out_shape=jax.ShapeDtypeStruct((1, rows, count * cols), jnp.bfloat16),
        input_output_aliases={1 + len(pieces): 0} if begun else {},
        scratch_shapes=[pltpu.SemaphoreType.DMA((len(pieces),))],
        compiler_params=pltpu.CompilerParams(vmem_limit_bytes=16 * MIB),
        name="deliver",
    )(info, *pieces, *begun)


def local(tokens, norm_gain, w_query, key_weight, value_weight, vertical_blocks, slash_offsets):
    _, rows, width = tokens.shape
    assert lax.axis_size("doc") == 4
    place = lax.axis_index("seq")
    doc_place = lax.axis_index("doc")
    info = jnp.stack([place, doc_place]).astype(jnp.int32)
    cosine, sine = rope_table(place * rows + jnp.arange(rows, dtype=jnp.int32), HEAD_WIDTH)
    table = jnp.concatenate([cosine, cosine, -sine, sine], axis=1)
    own = tokens[0]
    gain = norm_gain.reshape(1, width)
    weights = (w_query, key_weight, value_weight)
    long = lax.axis_size("seq") > 8 or lax.axis_size("seq") % 2 == 1
    ring, direct = (Gathered, Gathered) if long else (Ring, Direct)
    pattern = plan(info, vertical_blocks, slash_offsets, () if long else (Ring, Direct), rows)
    head = rows * 3 // 4 // BAND * BAND
    tail = rows - head

    twin = swap(own, "doc", 1)
    got_head = swap(cut(own, head), "doc", 2)
    q_near, kv_near, send_tail, gain_in, wk_in, wv_in, wq_in = project(
        info,
        [own, twin],
        [lambda c: 0, lambda c: rows],
        [(0, rows), (0, rows)],
        gain,
        *weights,
        table,
        early=head,
    )
    params = (gain_in, wq_in, wk_in, wv_in, table)
    near = ring(kv_near)
    near.advance()
    near.advance(pattern)
    got_head = after(got_head, *near.latest)

    got_tail = swap(after(send_tail, got_head), "doc", 2)
    head_twin = swap(got_head, "doc", 1)
    near.advance()
    q_head, kv_head = project(
        info,
        [got_head, head_twin],
        [lambda c: 0, lambda c: head],
        [(0, head), (0, head)],
        *params,
    )
    early = ring(kv_head)
    early.advance()

    got_tail = after(got_tail, *near.latest, kv_head)
    near.advance()
    tail_twin = swap(got_tail, "doc", 1)
    q_tail, kv_tail = project(
        info,
        [got_tail, tail_twin],
        [lambda c: 0, lambda c: tail],
        [(head, tail), (head, tail)],
        *params,
        ready=True,
    )
    early.advance(kv_tail)
    late = direct(kv_tail)
    mixed_own, mixed_twin = attend(
        pattern,
        [(0, [(0, 0, rows)], (0, rows, 0)), (1, [(0, rows, rows)], (rows, rows, 0))],
        [after(q_near, kv_tail)],
        near,
    )
    out_twin = swap(mixed_twin, "doc", 1)
    early.advance(mixed_twin)
    early.advance(*late.latest)
    remote = [
        (2, [(0, 0, head), (1, 0, tail)]),
        (3, [(0, head, head), (1, tail, tail)]),
    ]
    queries = [after(q_head, out_twin), q_tail]
    states = attend(
        pattern,
        [lane + ((at * head, head, 0),) for at, lane in enumerate(remote)],
        queries,
        early,
        end=False,
    )
    home = []
    for at, lane in enumerate(remote):
        state = states[3 * at:3 * at + 3]
        (mixed,) = attend(
            pattern, [lane + ((at * tail, tail, head),)], queries, late, states=[state]
        )
        home.append(swap(mixed, "doc", 2 + at))
    count = lax.axis_size("doc")
    result = deliver(info, (0, 1), [mixed_own, out_twin], count)
    return deliver(info, (2, 3), home, count, before=result)


def solution(mesh):
    return jax.shard_map(
        local,
        mesh=mesh,
        in_specs=(
            P("doc", "seq", None),
            P(),
            P(None, "doc"),
            P(None, "doc"),
            P(None, "doc"),
            P(),
            P(),
        ),
        out_specs=P("doc", "seq", None),
        check_vma=False,
    )
```

```python
import functools
import math

import jax
import jax.numpy as jnp
from jax import lax
from jax.experimental import pallas as pl
from jax.experimental.pallas import tpu as pltpu
from jax.sharding import PartitionSpec as P

HEAD_WIDTH = 128
QUERY_HEADS = 16
KEY_VALUE_HEADS = 4
QUERY_GROUP = QUERY_HEADS // KEY_VALUE_HEADS
EPSILON = 1e-05
BAND = 16
MIB = 1024 * 1024
OUT_OF_REACH = 1 << 30

SMEM = pl.BlockSpec(memory_space=pltpu.SMEM)
VMEM = pl.BlockSpec(memory_space=pltpu.VMEM)
ANYWHERE = pl.BlockSpec(memory_space=pl.ANY)
HBM = pl.BlockSpec(memory_space=pltpu.HBM)


def swap(value, axis, mask):
    count = lax.axis_size(axis)
    return lax.ppermute(value, axis, [(source, source ^ mask) for source in range(count)])


def after(value, *others):
    return lax.optimization_barrier((value,) + others)[0]


def in_hbm(array):
    return pltpu.with_memory_space_constraint(array, pltpu.HBM)


def rope_table(positions, width):
    inverse = jnp.power(jnp.float32(500000.0), -jnp.arange(0, width, 2, dtype=jnp.float32) / width)
    angles = positions.astype(jnp.float32)[:, None] * inverse[None, :]
    return (jnp.cos(angles), jnp.sin(angles))


def project_kernel(pieces, early, before, *refs):
    token_refs, refs = list(refs[:pieces]), list(refs[pieces:])
    ahead = 0
    if before:
        before_ref, refs = refs[0], refs[1:]
        ahead = before_ref.shape[0]
    gain_ref, wq_ref, wk_ref, wv_ref, table_ref, q_ref, kv_ref = refs[:7]
    refs = refs[7:]
    if before:
        kv_ref[:ahead, :] = before_ref[...]
    copies = []
    if early:
        sources = (gain_ref, token_refs[0], wk_ref, wv_ref, wq_ref)
        held, refs = refs[:1] + refs[5:6] + refs[1:4], refs[4:5] + refs[6:]
        sems = refs[1]
        gain_ref, token_refs[0], wk_ref, wv_ref, wq_ref = held
        for at, (source, target) in enumerate(zip(sources, held)):
            copies.append(pltpu.make_async_copy(source, target, sems.at[at]))
            copies[-1].start()
        copies[0].wait()
    normed = refs[0]
    width = gain_ref.shape[1]
    heads = wk_ref.shape[1] // HEAD_WIDTH
    deep = min(1024, width)

    rows = token_refs[0].shape[0]
    for piece in reversed(range(pieces)):
        if piece == 0 and early:
            copies[1].wait()
        ref, first = token_refs[piece], piece * rows

        def norm_band(index, carry, ref=ref, first=first):
            at = pl.ds(pl.multiple_of(index * BAND, BAND), BAND)
            wide = ref[at, :].astype(jnp.float32)
            scale = lax.rsqrt(jnp.mean(wide * wide, axis=-1, keepdims=True) + EPSILON)
            normed[pl.ds(pl.multiple_of(first + index * BAND, BAND), BAND), :] = (
                wide * scale * gain_ref[...]
            ).astype(jnp.bfloat16)
            return carry

        lax.fori_loop(0, rows // BAND, norm_band, 0, unroll=2)

    half = HEAD_WIDTH // 2

    def rotate(value):
        turned = jnp.concatenate([value[:, half:], value[:, :half]], axis=1)
        return (
            value * table_ref[:, :HEAD_WIDTH] + turned * table_ref[:, HEAD_WIDTH:]
        ).astype(jnp.bfloat16)

    def multiply(weight_of):
        total = None
        for start in range(0, width, deep):
            part = jnp.dot(
                normed[:, start:start + deep],
                weight_of(slice(start, start + deep)),
                preferred_element_type=jnp.float32,
            )
            total = part if total is None else total + part
        return total

    if early:
        copies[2].wait()
        copies[3].wait()
    for head in range(heads):
        at = slice(head * HEAD_WIDTH, (head + 1) * HEAD_WIDTH)
        both = multiply(lambda k: jnp.concatenate([wk_ref[k, at], wv_ref[k, at]], axis=1))
        out = 2 * head * HEAD_WIDTH
        for piece in range(pieces):
            mine = both[piece * rows:(piece + 1) * rows]
            band = slice(ahead + piece * rows, ahead + (piece + 1) * rows)
            kv_ref[band, out:out + HEAD_WIDTH] = rotate(mine[:, :HEAD_WIDTH])
            kv_ref[band, out + HEAD_WIDTH:out + 2 * HEAD_WIDTH] = mine[:, HEAD_WIDTH:].astype(
                jnp.bfloat16
            )
    if early:
        copies[4].wait()
    pair = 2 * HEAD_WIDTH
    for start in range(0, wq_ref.shape[1], pair):
        both = multiply(lambda k: wq_ref[k, start:start + pair])
        for piece in range(pieces):
            band = slice(piece * rows, (piece + 1) * rows)
            for at in (0, HEAD_WIDTH):
                q_ref[band, start + at:start + at + HEAD_WIDTH] = rotate(
                    both[band, at:at + HEAD_WIDTH]
                )


def project(pieces, gain, w_query, key_weight, value_weight, table, early=False, before=None):
    width = gain.shape[1]
    q_cols, k_cols = w_query.shape[1], key_weight.shape[1]
    total = len(pieces) * pieces[0].shape[0]
    params = (gain, w_query, key_weight, value_weight)
    held = () if before is None else (before,)
    scratch = [pltpu.VMEM((total, width), jnp.bfloat16)]
    kind = [VMEM] * (len(pieces) + len(held) + len(params))
    shapes = [
        jax.ShapeDtypeStruct((total, q_cols), jnp.bfloat16),
        jax.ShapeDtypeStruct((total + sum(a.shape[0] for a in held), 2 * k_cols), jnp.bfloat16),
    ]
    if early:
        scratch.append(pltpu.VMEM(pieces[0].shape, pieces[0].dtype))
        scratch.append(pltpu.SemaphoreType.DMA((5,)))
        params = tuple(in_hbm(array) for array in params)
        shapes += [
            jax.ShapeDtypeStruct(array.shape, array.dtype)
            for array in (gain, key_weight, value_weight, w_query)
        ]
        pieces = [in_hbm(pieces[0])] + list(pieces[1:])
        kind = [HBM] + [VMEM] * (len(pieces) - 1) + [HBM] * len(params)
    return pl.pallas_call(
        functools.partial(project_kernel, len(pieces), early, before is not None),
        in_specs=kind + [VMEM],
        out_specs=[VMEM] * len(shapes),
        out_shape=shapes,
        scratch_shapes=scratch,
        compiler_params=pltpu.CompilerParams(vmem_limit_bytes=28 * MIB),
        cost_estimate=pl.CostEstimate(
            flops=2 * total * width * (q_cols + 2 * k_cols),
            bytes_accessed=2 * width * (q_cols + 2 * k_cols) + 2 * total * width,
            transcendentals=0,
        ),
        name="project",
    )(*pieces, *held, *params, table)


def ring_order(count):
    return list(range(0, count, 2)) + list(range(count - 1, 0, -2))


class Gathered:
    def __init__(self, kv):
        count = lax.axis_size("seq")
        total = kv.shape[0]
        chunk = 8 if count % 8 == 0 else 1
        self.chunks, self.latest = count // chunk, ()
        self.arrays = [lax.all_gather(kv, "seq", axis=0, tiled=True)]
        self.slots = [
            lambda index, j=j: (0, pl.multiple_of((index * chunk + j) * total, BAND))
            for j in range(chunk)
        ]

    def advance(self, *others):
        pass


class Ring:
    def __init__(self, kv):
        self.count, self.chunks, self.stage = lax.axis_size("seq"), 1, 0
        self.order = ring_order(self.count)
        self.arrays, self.slots, self.latest = [], [], ()
        self.front = {1: kv, -1: kv}
        self.hold(kv)

    @staticmethod
    def sources(at, count):
        steps = [0]
        for stage in range(1, count // 2 + 1):
            steps += [stage, -stage] if 2 * stage < count else [stage]
        return [(at - step) % count for step in steps]

    def hold(self, array):
        self.slots.append(lambda index, r=len(self.arrays): (r, 0))
        self.arrays.append(array)

    def advance(self, *others):
        if self.stage >= self.count // 2:
            return
        self.stage += 1
        fresh = []
        for way in (1, -1) if 2 * self.stage < self.count else (1,):
            value = after(self.front[way], *others) if others else self.front[way]
            pairs = [
                (source, self.order[(at + way) % self.count]) for at, source in enumerate(self.order)
            ]
            self.front[way] = lax.ppermute(value, "seq", pairs)
            fresh.append(self.front[way])
            self.hold(self.front[way])
        self.latest = tuple(fresh)


def plan_kernel(ring, lanes, heads, count, rows, info_ref, vertical_ref, slash_ref, plan_ref):
    place, me = info_ref[0], info_ref[1]
    plan_ref[0] = place

    def enter(number, block):
        for lane in range(lanes):
            doc = me ^ lane
            for head in range(heads):
                group = me * heads + head
                found = (block == place) | (block == place - 1)
                for s in range(slash_ref.shape[2]):
                    found = found | (block == place - slash_ref[doc, group, s])
                for s in range(vertical_ref.shape[2]):
                    found = found | ((block == vertical_ref[doc, group, s]) & (block < place - 1))
                at = 1 + (lane * heads + head) * count + number
                plan_ref[at] = jnp.where(found & (block >= 0), block * rows, OUT_OF_REACH)

    if ring:
        order = ring_order(count)
        lists = {order[at]: [order[r] for r in Ring.sources(at, count)] for at in range(count)}
        for number in range(count):
            block = jnp.int32(0)
            for here, blocks in lists.items():
                block = jnp.where(place == here, blocks[number], block)
            enter(number, block)
    else:

        def one(number, carry):
            enter(number, number)
            return carry

        lax.fori_loop(0, count, one, 0)


def plan(info, vertical, slash, ring, rows):
    count, lanes = lax.axis_size("seq"), lax.axis_size("doc")
    heads = vertical.shape[1] // lanes
    length = 1 + lanes * heads * count
    return pl.pallas_call(
        functools.partial(plan_kernel, ring, lanes, heads, count, rows),
        in_specs=[SMEM] * 3,
        out_specs=SMEM,
        out_shape=jax.ShapeDtypeStruct((length,), jnp.int32),
        compiler_params=pltpu.CompilerParams(vmem_limit_bytes=16 * MIB),
        name="plan",
    )(info, vertical, slash)


def attend_kernel(lanes, stride, slot_at, slots, chunks, q_count, kv_count, begin, end, plan_ref, *refs):
    q_refs, kv_refs, refs = refs[:q_count], refs[q_count:q_count + kv_count], refs[q_count + kv_count:]
    state_refs = refs[:0 if begin else 3 * len(lanes)]
    out_refs = refs[len(state_refs):]
    heads = kv_refs[0].shape[1] // (2 * HEAD_WIDTH)
    place = plan_ref[0]
    factor = HEAD_WIDTH ** (-0.5) * math.log2(math.e)

    for lane, (mask, q_at, kv_first, rows) in enumerate(lanes):
        rank = QUERY_GROUP * rows
        row_at = place * rows + lax.broadcasted_iota(jnp.int32, (1, rows), 1)
        query_at = jnp.concatenate([row_at] * QUERY_GROUP, axis=1)
        key_at = lax.broadcasted_iota(jnp.int32, (rows, rank), 0)
        for head in range(heads):
            table = 1 + (mask * heads + head) * stride + slot_at
            queries = jnp.concatenate(
                [
                    q_refs[q_at[0]][
                        q_at[1]:q_at[1] + rows,
                        (head * QUERY_GROUP + h) * HEAD_WIDTH:(head * QUERY_GROUP + h + 1) * HEAD_WIDTH,
                    ]
                    for h in range(QUERY_GROUP)
                ],
                axis=0,
            )

            def step(index, carry):
                found = [slot(index) for slot in slots]

                def column(at):
                    cols = slice(at * HEAD_WIDTH, (at + 1) * HEAD_WIDTH)
                    parts = []
                    for r, first in found:
                        if isinstance(first, int):
                            where = slice(first + kv_first, first + kv_first + rows)
                        else:
                            where = pl.ds(pl.multiple_of(first + kv_first, BAND), rows)
                        parts.append(kv_refs[r][where, cols])
                    return jnp.concatenate(parts, axis=0)

                keys, values = column(2 * head), column(2 * head + 1)
                scores = lax.dot_general(
                    keys, queries, (((1,), (1,)), ((), ())), preferred_element_type=jnp.float32
                )
                parts = []
                for j in range(len(slots)):
                    shift = plan_ref[table + index * len(slots) + j]
                    parts.append(
                        jnp.where(
                            key_at <= query_at - shift,
                            scores[j * rows:(j + 1) * rows],
                            -jnp.inf,
                        )
                    )
                scores = jnp.concatenate(parts, axis=0)
                top = jnp.max(scores, axis=0, keepdims=True)
                if carry is None:
                    fresh = safe = top
                else:
                    fresh = jnp.maximum(carry[0], top)
                    safe = jnp.where(fresh == -jnp.inf, jnp.float32(0), fresh)
                raised = jnp.exp2((scores - safe) * factor)
                total = jnp.sum(raised, axis=0, keepdims=True)
                mixed = lax.dot_general(
                    values,
                    raised.astype(jnp.bfloat16),
                    (((0,), (0,)), ((), ())),
                    preferred_element_type=jnp.float32,
                )
                if carry is not None:
                    fade = jnp.exp2((carry[0] - safe) * factor)
                    total, mixed = carry[1] * fade + total, carry[2] * fade + mixed
                return fresh, total, mixed

            carry = None
            if not begin:
                carry = tuple(ref[head] for ref in state_refs[3 * lane:3 * lane + 3])
            elif chunks > 1:
                carry = (
                    jnp.full((1, rank), -jnp.inf, jnp.float32),
                    jnp.zeros((1, rank), jnp.float32),
                    jnp.zeros((HEAD_WIDTH, rank), jnp.float32),
                )
            if chunks > 1:
                carry = lax.fori_loop(0, chunks, step, carry)
            else:
                carry = step(0, carry)
            if not end:
                for ref, value in zip(out_refs[3 * lane:3 * lane + 3], carry):
                    ref[head] = value
                continue
            result = carry[2] / carry[1]
            for h in range(QUERY_GROUP):
                cols = slice(
                    (head * QUERY_GROUP + h) * HEAD_WIDTH, (head * QUERY_GROUP + h + 1) * HEAD_WIDTH
                )
                out_refs[lane][:, cols] = result[:, h * rows:(h + 1) * rows].T.astype(jnp.bfloat16)


def attend(table, lanes, queries, spread, span=None, states=None, end=True):
    first, last = span or (0, len(spread.slots))
    q_cols = queries[0].shape[1]
    rows = lanes[0][3]
    arrays, slots = spread.arrays, spread.slots[first:last]
    if span:
        arrays, slots = arrays[first:last], spread.slots[:last - first]
    held = [array for state in states for array in state] if states else []
    if end:
        shapes = [jax.ShapeDtypeStruct((rows, q_cols), jnp.bfloat16)] * len(lanes)
    else:
        heads = q_cols // (QUERY_GROUP * HEAD_WIDTH)
        shapes = [
            jax.ShapeDtypeStruct((heads, deep, QUERY_GROUP * rows), jnp.float32)
            for deep in (1, 1, HEAD_WIDTH)
        ] * len(lanes)
    kernel = functools.partial(
        attend_kernel,
        lanes,
        lax.axis_size("seq"),
        first,
        slots,
        spread.chunks,
        len(queries),
        len(arrays),
        not states,
        end,
    )
    return pl.pallas_call(
        kernel,
        in_specs=[SMEM] + [VMEM] * (len(queries) + len(arrays) + len(held)),
        out_specs=[VMEM] * len(shapes),
        out_shape=shapes,
        compiler_params=pltpu.CompilerParams(vmem_limit_bytes=28 * MIB),
        cost_estimate=pl.CostEstimate(
            flops=4 * len(lanes) * rows * q_cols * len(slots) * spread.chunks * rows,
            bytes_accessed=2 * sum(a.size for a in arrays) + 4 * len(lanes) * rows * q_cols,
            transcendentals=len(lanes) * rows * len(slots) * spread.chunks * rows * QUERY_GROUP,
        ),
        name="attend",
    )(table, *queries, *arrays, *held)


def deliver_kernel(masks, info_ref, *refs):
    pieces, (out_ref, sems) = refs[:len(masks)], refs[-2:]
    cols = pieces[0].shape[1]
    copies = []
    for at, (mask, piece) in enumerate(zip(masks, pieces)):
        where = pl.ds(pl.multiple_of((info_ref[1] ^ mask) * cols, cols), cols)
        copies.append(pltpu.make_async_copy(piece, out_ref.at[0, :, where], sems.at[at]))
        copies[-1].start()
    for copy in copies:
        copy.wait()


def deliver(info, masks, pieces, count, before=None):
    rows, cols = pieces[0].shape
    begun = () if before is None else (before,)
    return pl.pallas_call(
        functools.partial(deliver_kernel, masks),
        in_specs=[SMEM] + [VMEM] * len(pieces) + [HBM] * len(begun),
        out_specs=HBM,
        out_shape=jax.ShapeDtypeStruct((1, rows, count * cols), jnp.bfloat16),
        input_output_aliases={1 + len(pieces): 0} if begun else {},
        scratch_shapes=[pltpu.SemaphoreType.DMA((len(pieces),))],
        compiler_params=pltpu.CompilerParams(vmem_limit_bytes=16 * MIB),
        name="deliver",
    )(info, *pieces, *begun)


def local(tokens, norm_gain, w_query, key_weight, value_weight, vertical_blocks, slash_offsets):
    _, rows, width = tokens.shape
    assert lax.axis_size("doc") == 4
    place = lax.axis_index("seq")
    doc_place = lax.axis_index("doc")
    info = jnp.stack([place, doc_place]).astype(jnp.int32)
    cosine, sine = rope_table(place * rows + jnp.arange(rows, dtype=jnp.int32), HEAD_WIDTH)
    table = jnp.concatenate([cosine, cosine, -sine, sine], axis=1)
    own = tokens[0]
    gain = norm_gain.reshape(1, width)
    long = lax.axis_size("seq") > 8 or lax.axis_size("seq") % 2 == 1
    ring = Gathered if long else Ring
    table_of = plan(info, vertical_blocks, slash_offsets, not long, rows)

    twin = swap(own, "doc", 1)
    across = swap(own, "doc", 2)
    q_near, kv_near, gain_in, wk_in, wv_in, wq_in = project(
        [own, twin], gain, w_query, key_weight, value_weight, table, early=True
    )
    params = (gain_in, wq_in, wk_in, wv_in, table)
    near = ring(kv_near)
    near.advance()
    near.advance(table_of)
    near.advance()

    across = after(across, *near.latest)
    near.advance()
    crossed = swap(across, "doc", 1)
    q_across, kv_across = project([across], *params)
    q_crossed, kv_far = project([crossed], *params, before=kv_across)
    far = ring(kv_far)
    far.advance()
    mixed_own, mixed_twin = attend(
        table_of,
        [(0, (0, 0), 0, rows), (1, (0, rows), rows, rows)],
        [after(q_near, kv_far)],
        near,
    )
    out_twin = swap(mixed_twin, "doc", 1)
    far.advance(mixed_twin)
    far.advance()
    remote = [(2, (0, 0), 0, rows), (3, (1, 0), rows, rows)]
    queries = [after(q_across, out_twin), q_crossed]
    home = []
    if long:
        for at, mixed in enumerate(attend(table_of, remote, queries, far)):
            home.append(swap(mixed, "doc", 2 + at))
    else:
        far.advance()
        last = len(far.slots) - 1
        states = attend(table_of, remote, queries, far, span=(0, last), end=False)
        for at, lane in enumerate(remote):
            state = states[3 * at:3 * at + 3]
            (mixed,) = attend(
                table_of, [lane], queries, far, span=(last, last + 1), states=[state]
            )
            home.append(swap(mixed, "doc", 2 + at))
    count = lax.axis_size("doc")
    result = deliver(info, (0, 1), [mixed_own, out_twin], count)
    return deliver(info, (2, 3), home, count, before=result)


def solution(mesh):
    return jax.shard_map(
        local,
        mesh=mesh,
        in_specs=(
            P("doc", "seq", None),
            P(),
            P(None, "doc"),
            P(None, "doc"),
            P(None, "doc"),
            P(),
            P(),
        ),
        out_specs=P("doc", "seq", None),
        check_vma=False,
    )
```

```python
import functools
import math

import jax
import jax.numpy as jnp
from jax import lax
from jax.experimental import pallas as pl
from jax.experimental.pallas import tpu as pltpu
from jax.sharding import PartitionSpec as P

HEAD_WIDTH = 128
QUERY_HEADS = 16
KEY_VALUE_HEADS = 4
QUERY_GROUP = QUERY_HEADS // KEY_VALUE_HEADS
EPSILON = 1e-05
BAND = 16
MIB = 1024 * 1024
OUT_OF_REACH = 1 << 30

SMEM = pl.BlockSpec(memory_space=pltpu.SMEM)
VMEM = pl.BlockSpec(memory_space=pltpu.VMEM)
ANYWHERE = pl.BlockSpec(memory_space=pl.ANY)
HBM = pl.BlockSpec(memory_space=pltpu.HBM)


def swap(value, axis, mask):
    count = lax.axis_size(axis)
    return lax.ppermute(value, axis, [(source, source ^ mask) for source in range(count)])


def after(value, *others):
    return lax.optimization_barrier((value,) + others)[0]


def in_hbm(array):
    return pltpu.with_memory_space_constraint(array, pltpu.HBM)


def rope_table(positions, width):
    inverse = jnp.power(jnp.float32(500000.0), -jnp.arange(0, width, 2, dtype=jnp.float32) / width)
    angles = positions.astype(jnp.float32)[:, None] * inverse[None, :]
    return (jnp.cos(angles), jnp.sin(angles))


def project_kernel(pieces, early, before, *refs):
    token_refs, refs = list(refs[:pieces]), list(refs[pieces:])
    ahead = 0
    if before:
        before_ref, refs = refs[0], refs[1:]
        ahead = before_ref.shape[0]
    gain_ref, wq_ref, wk_ref, wv_ref, table_ref, q_ref, kv_ref = refs[:7]
    refs = refs[7:]
    if before:
        kv_ref[:ahead, :] = before_ref[...]
    copies = []
    if early:
        sources = (gain_ref, token_refs[0], wk_ref, wv_ref, wq_ref)
        held, refs = refs[:1] + refs[5:6] + refs[1:4], refs[4:5] + refs[6:]
        sems = refs[1]
        gain_ref, token_refs[0], wk_ref, wv_ref, wq_ref = held
        for at, (source, target) in enumerate(zip(sources, held)):
            copies.append(pltpu.make_async_copy(source, target, sems.at[at]))
            copies[-1].start()
        copies[0].wait()
    normed = refs[0]
    width = gain_ref.shape[1]
    heads = wk_ref.shape[1] // HEAD_WIDTH
    deep = min(1024, width)

    rows = token_refs[0].shape[0]
    for piece in reversed(range(pieces)):
        if piece == 0 and early:
            copies[1].wait()
        ref, first = token_refs[piece], piece * rows

        def norm_band(index, carry, ref=ref, first=first):
            at = pl.ds(pl.multiple_of(index * BAND, BAND), BAND)
            wide = ref[at, :].astype(jnp.float32)
            scale = lax.rsqrt(jnp.mean(wide * wide, axis=-1, keepdims=True) + EPSILON)
            normed[pl.ds(pl.multiple_of(first + index * BAND, BAND), BAND), :] = (
                wide * scale * gain_ref[...]
            ).astype(jnp.bfloat16)
            return carry

        lax.fori_loop(0, rows // BAND, norm_band, 0, unroll=2)

    half = HEAD_WIDTH // 2

    def rotate(value):
        turned = jnp.concatenate([value[:, half:], value[:, :half]], axis=1)
        return (
            value * table_ref[:, :HEAD_WIDTH] + turned * table_ref[:, HEAD_WIDTH:]
        ).astype(jnp.bfloat16)

    def multiply(weight_of):
        total = None
        for start in range(0, width, deep):
            part = jnp.dot(
                normed[:, start:start + deep],
                weight_of(slice(start, start + deep)),
                preferred_element_type=jnp.float32,
            )
            total = part if total is None else total + part
        return total

    if early:
        copies[2].wait()
        copies[3].wait()
    for head in range(heads):
        at = slice(head * HEAD_WIDTH, (head + 1) * HEAD_WIDTH)
        both = multiply(lambda k: jnp.concatenate([wk_ref[k, at], wv_ref[k, at]], axis=1))
        out = 2 * head * HEAD_WIDTH
        for piece in range(pieces):
            mine = both[piece * rows:(piece + 1) * rows]
            band = slice(ahead + piece * rows, ahead + (piece + 1) * rows)
            kv_ref[band, out:out + HEAD_WIDTH] = rotate(mine[:, :HEAD_WIDTH])
            kv_ref[band, out + HEAD_WIDTH:out + 2 * HEAD_WIDTH] = mine[:, HEAD_WIDTH:].astype(
                jnp.bfloat16
            )
    if early:
        copies[4].wait()
    pair = 2 * HEAD_WIDTH
    for start in range(0, wq_ref.shape[1], pair):
        both = multiply(lambda k: wq_ref[k, start:start + pair])
        for piece in range(pieces):
            band = slice(piece * rows, (piece + 1) * rows)
            for at in (0, HEAD_WIDTH):
                q_ref[band, start + at:start + at + HEAD_WIDTH] = rotate(
                    both[band, at:at + HEAD_WIDTH]
                )


def project(pieces, gain, w_query, key_weight, value_weight, table, early=False, before=None):
    width = gain.shape[1]
    q_cols, k_cols = w_query.shape[1], key_weight.shape[1]
    total = len(pieces) * pieces[0].shape[0]
    params = (gain, w_query, key_weight, value_weight)
    held = () if before is None else (before,)
    scratch = [pltpu.VMEM((total, width), jnp.bfloat16)]
    kind = [VMEM] * (len(pieces) + len(held) + len(params))
    shapes = [
        jax.ShapeDtypeStruct((total, q_cols), jnp.bfloat16),
        jax.ShapeDtypeStruct((total + sum(a.shape[0] for a in held), 2 * k_cols), jnp.bfloat16),
    ]
    if early:
        scratch.append(pltpu.VMEM(pieces[0].shape, pieces[0].dtype))
        scratch.append(pltpu.SemaphoreType.DMA((5,)))
        params = tuple(in_hbm(array) for array in params)
        shapes += [
            jax.ShapeDtypeStruct(array.shape, array.dtype)
            for array in (gain, key_weight, value_weight, w_query)
        ]
        pieces = [in_hbm(pieces[0])] + list(pieces[1:])
        kind = [HBM] + [VMEM] * (len(pieces) - 1) + [HBM] * len(params)
    return pl.pallas_call(
        functools.partial(project_kernel, len(pieces), early, before is not None),
        in_specs=kind + [VMEM],
        out_specs=[VMEM] * len(shapes),
        out_shape=shapes,
        scratch_shapes=scratch,
        compiler_params=pltpu.CompilerParams(vmem_limit_bytes=20 * MIB),
        cost_estimate=pl.CostEstimate(
            flops=2 * total * width * (q_cols + 2 * k_cols),
            bytes_accessed=2 * width * (q_cols + 2 * k_cols) + 2 * total * width,
            transcendentals=0,
        ),
        name="project",
    )(*pieces, *held, *params, table)


def ring_order(count):
    return list(range(0, count, 2)) + list(range(count - 1, 0, -2))


class Gathered:
    def __init__(self, kv):
        count = lax.axis_size("seq")
        total = kv.shape[0]
        chunk = 8 if count % 8 == 0 else 1
        self.chunks, self.latest = count // chunk, ()
        self.arrays = [lax.all_gather(kv, "seq", axis=0, tiled=True)]
        self.slots = [
            lambda index, j=j: (0, pl.multiple_of((index * chunk + j) * total, BAND))
            for j in range(chunk)
        ]

    def advance(self, *others):
        pass


class Ring:
    def __init__(self, kv):
        self.count, self.chunks, self.stage = lax.axis_size("seq"), 1, 0
        self.order = ring_order(self.count)
        self.arrays, self.slots, self.latest = [], [], ()
        self.front = {1: kv, -1: kv}
        self.hold(kv)

    @staticmethod
    def sources(at, count):
        steps = [0]
        for stage in range(1, count // 2 + 1):
            steps += [stage, -stage] if 2 * stage < count else [stage]
        return [(at - step) % count for step in steps]

    def hold(self, array):
        self.slots.append(lambda index, r=len(self.arrays): (r, 0))
        self.arrays.append(array)

    def advance(self, *others):
        if self.stage >= self.count // 2:
            return
        self.stage += 1
        fresh = []
        for way in (1, -1) if 2 * self.stage < self.count else (1,):
            value = after(self.front[way], *others) if others else self.front[way]
            pairs = [
                (source, self.order[(at + way) % self.count]) for at, source in enumerate(self.order)
            ]
            self.front[way] = lax.ppermute(value, "seq", pairs)
            fresh.append(self.front[way])
            self.hold(self.front[way])
        self.latest = tuple(fresh)


def plan_kernel(ring, lanes, heads, count, rows, info_ref, vertical_ref, slash_ref, plan_ref):
    place, me = info_ref[0], info_ref[1]
    plan_ref[0] = place

    def enter(number, block):
        for lane in range(lanes):
            doc = me ^ lane
            for head in range(heads):
                group = me * heads + head
                found = (block == place) | (block == place - 1)
                for s in range(slash_ref.shape[2]):
                    found = found | (block == place - slash_ref[doc, group, s])
                for s in range(vertical_ref.shape[2]):
                    found = found | ((block == vertical_ref[doc, group, s]) & (block < place - 1))
                at = 1 + (lane * heads + head) * count + number
                plan_ref[at] = jnp.where(found & (block >= 0), block * rows, OUT_OF_REACH)

    if ring:
        order = ring_order(count)
        lists = {order[at]: [order[r] for r in Ring.sources(at, count)] for at in range(count)}
        for number in range(count):
            block = jnp.int32(0)
            for here, blocks in lists.items():
                block = jnp.where(place == here, blocks[number], block)
            enter(number, block)
    else:

        def one(number, carry):
            enter(number, number)
            return carry

        lax.fori_loop(0, count, one, 0)


def plan(info, vertical, slash, ring, rows):
    count, lanes = lax.axis_size("seq"), lax.axis_size("doc")
    heads = vertical.shape[1] // lanes
    length = 1 + lanes * heads * count
    return pl.pallas_call(
        functools.partial(plan_kernel, ring, lanes, heads, count, rows),
        in_specs=[SMEM] * 3,
        out_specs=SMEM,
        out_shape=jax.ShapeDtypeStruct((length,), jnp.int32),
        compiler_params=pltpu.CompilerParams(vmem_limit_bytes=4 * MIB),
        name="plan",
    )(info, vertical, slash)


def attend_kernel(lanes, stride, slot_at, slots, chunks, q_count, kv_count, begin, end, plan_ref, *refs):
    q_refs, kv_refs, refs = refs[:q_count], refs[q_count:q_count + kv_count], refs[q_count + kv_count:]
    state_refs = refs[:0 if begin else 3 * len(lanes)]
    out_refs = refs[len(state_refs):]
    heads = kv_refs[0].shape[1] // (2 * HEAD_WIDTH)
    place = plan_ref[0]
    factor = HEAD_WIDTH ** (-0.5) * math.log2(math.e)

    for lane, (mask, q_at, kv_first, rows) in enumerate(lanes):
        rank = QUERY_GROUP * rows
        row_at = place * rows + lax.broadcasted_iota(jnp.int32, (1, rows), 1)
        query_at = jnp.concatenate([row_at] * QUERY_GROUP, axis=1)
        key_at = lax.broadcasted_iota(jnp.int32, (rows, rank), 0)
        for head in range(heads):
            table = 1 + (mask * heads + head) * stride + slot_at
            queries = jnp.concatenate(
                [
                    q_refs[q_at[0]][
                        q_at[1]:q_at[1] + rows,
                        (head * QUERY_GROUP + h) * HEAD_WIDTH:(head * QUERY_GROUP + h + 1) * HEAD_WIDTH,
                    ]
                    for h in range(QUERY_GROUP)
                ],
                axis=0,
            )

            def step(index, carry):
                found = [slot(index) for slot in slots]

                def column(at):
                    cols = slice(at * HEAD_WIDTH, (at + 1) * HEAD_WIDTH)
                    parts = []
                    for r, first in found:
                        if isinstance(first, int):
                            where = slice(first + kv_first, first + kv_first + rows)
                        else:
                            where = pl.ds(pl.multiple_of(first + kv_first, BAND), rows)
                        parts.append(kv_refs[r][where, cols])
                    return jnp.concatenate(parts, axis=0)

                keys, values = column(2 * head), column(2 * head + 1)
                scores = lax.dot_general(
                    keys, queries, (((1,), (1,)), ((), ())), preferred_element_type=jnp.float32
                )
                parts = []
                for j in range(len(slots)):
                    shift = plan_ref[table + index * len(slots) + j]
                    parts.append(
                        jnp.where(
                            key_at <= query_at - shift,
                            scores[j * rows:(j + 1) * rows],
                            -jnp.inf,
                        )
                    )
                scores = jnp.concatenate(parts, axis=0)
                top = jnp.max(scores, axis=0, keepdims=True)
                if carry is None:
                    fresh = safe = top
                else:
                    fresh = jnp.maximum(carry[0], top)
                    safe = jnp.where(fresh == -jnp.inf, jnp.float32(0), fresh)
                raised = jnp.exp2((scores - safe) * factor)
                total = jnp.sum(raised, axis=0, keepdims=True)
                mixed = lax.dot_general(
                    values,
                    raised.astype(jnp.bfloat16),
                    (((0,), (0,)), ((), ())),
                    preferred_element_type=jnp.float32,
                )
                if carry is not None:
                    fade = jnp.exp2((carry[0] - safe) * factor)
                    total, mixed = carry[1] * fade + total, carry[2] * fade + mixed
                return fresh, total, mixed

            carry = None
            if not begin:
                carry = tuple(ref[head] for ref in state_refs[3 * lane:3 * lane + 3])
            elif chunks > 1:
                carry = (
                    jnp.full((1, rank), -jnp.inf, jnp.float32),
                    jnp.zeros((1, rank), jnp.float32),
                    jnp.zeros((HEAD_WIDTH, rank), jnp.float32),
                )
            if chunks > 1:
                carry = lax.fori_loop(0, chunks, step, carry)
            else:
                carry = step(0, carry)
            if not end:
                for ref, value in zip(out_refs[3 * lane:3 * lane + 3], carry):
                    ref[head] = value
                continue
            result = carry[2] / carry[1]
            for h in range(QUERY_GROUP):
                cols = slice(
                    (head * QUERY_GROUP + h) * HEAD_WIDTH, (head * QUERY_GROUP + h + 1) * HEAD_WIDTH
                )
                out_refs[lane][:, cols] = result[:, h * rows:(h + 1) * rows].T.astype(jnp.bfloat16)


def attend(table, lanes, queries, spread, span=None, states=None, end=True):
    first, last = span or (0, len(spread.slots))
    q_cols = queries[0].shape[1]
    rows = lanes[0][3]
    arrays, slots = spread.arrays, spread.slots[first:last]
    if span:
        arrays, slots = arrays[first:last], spread.slots[:last - first]
    held = [array for state in states for array in state] if states else []
    if end:
        shapes = [jax.ShapeDtypeStruct((rows, q_cols), jnp.bfloat16)] * len(lanes)
    else:
        heads = q_cols // (QUERY_GROUP * HEAD_WIDTH)
        shapes = [
            jax.ShapeDtypeStruct((heads, deep, QUERY_GROUP * rows), jnp.float32)
            for deep in (1, 1, HEAD_WIDTH)
        ] * len(lanes)
    kernel = functools.partial(
        attend_kernel,
        lanes,
        lax.axis_size("seq"),
        first,
        slots,
        spread.chunks,
        len(queries),
        len(arrays),
        not states,
        end,
    )
    return pl.pallas_call(
        kernel,
        in_specs=[SMEM] + [VMEM] * (len(queries) + len(arrays) + len(held)),
        out_specs=[VMEM] * len(shapes),
        out_shape=shapes,
        compiler_params=pltpu.CompilerParams(
            vmem_limit_bytes=10 * MIB + 4 * sum(a.size for a in (*queries, *arrays))
        ),
        cost_estimate=pl.CostEstimate(
            flops=4 * len(lanes) * rows * q_cols * len(slots) * spread.chunks * rows,
            bytes_accessed=2 * sum(a.size for a in arrays) + 4 * len(lanes) * rows * q_cols,
            transcendentals=len(lanes) * rows * len(slots) * spread.chunks * rows * QUERY_GROUP,
        ),
        name="attend",
    )(table, *queries, *arrays, *held)


def deliver_kernel(masks, info_ref, *refs):
    pieces, (out_ref, sems) = refs[:len(masks)], refs[-2:]
    cols = pieces[0].shape[1]
    copies = []
    for at, (mask, piece) in enumerate(zip(masks, pieces)):
        where = pl.ds(pl.multiple_of((info_ref[1] ^ mask) * cols, cols), cols)
        copies.append(pltpu.make_async_copy(piece, out_ref.at[0, :, where], sems.at[at]))
        copies[-1].start()
    for copy in copies:
        copy.wait()


def deliver(info, masks, pieces, count, before=None):
    rows, cols = pieces[0].shape
    begun = () if before is None else (before,)
    return pl.pallas_call(
        functools.partial(deliver_kernel, masks),
        in_specs=[SMEM] + [VMEM] * len(pieces) + [HBM] * len(begun),
        out_specs=HBM,
        out_shape=jax.ShapeDtypeStruct((1, rows, count * cols), jnp.bfloat16),
        input_output_aliases={1 + len(pieces): 0} if begun else {},
        scratch_shapes=[pltpu.SemaphoreType.DMA((len(pieces),))],
        compiler_params=pltpu.CompilerParams(vmem_limit_bytes=4 * MIB),
        name="deliver",
    )(info, *pieces, *begun)


def local(tokens, norm_gain, w_query, key_weight, value_weight, vertical_blocks, slash_offsets):
    _, rows, width = tokens.shape
    assert lax.axis_size("doc") == 4
    place = lax.axis_index("seq")
    doc_place = lax.axis_index("doc")
    info = jnp.stack([place, doc_place]).astype(jnp.int32)
    cosine, sine = rope_table(place * rows + jnp.arange(rows, dtype=jnp.int32), HEAD_WIDTH)
    table = jnp.concatenate([cosine, cosine, -sine, sine], axis=1)
    own = tokens[0]
    gain = norm_gain.reshape(1, width)
    long = lax.axis_size("seq") > 8 or lax.axis_size("seq") % 2 == 1
    ring = Gathered if long else Ring
    table_of = plan(info, vertical_blocks, slash_offsets, not long, rows)

    twin = swap(own, "doc", 1)
    across = swap(own, "doc", 2)
    q_near, kv_near, gain_in, wk_in, wv_in, wq_in = project(
        [own, twin], gain, w_query, key_weight, value_weight, table, early=True
    )
    params = (gain_in, wq_in, wk_in, wv_in, table)
    near = ring(kv_near)
    near.advance()
    near.advance(table_of)
    near.advance()

    across = after(across, *near.latest)
    near.advance()
    crossed = swap(across, "doc", 1)
    q_across, kv_across = project([across], *params)
    q_crossed, kv_far = project([crossed], *params, before=kv_across)
    far = ring(kv_far)
    far.advance()
    mixed_own, mixed_twin = attend(
        table_of,
        [(0, (0, 0), 0, rows), (1, (0, rows), rows, rows)],
        [after(q_near, kv_far)],
        near,
    )
    out_twin = swap(mixed_twin, "doc", 1)
    far.advance(mixed_twin)
    far.advance()
    remote = [(2, (0, 0), 0, rows), (3, (1, 0), rows, rows)]
    queries = [after(q_across, out_twin), q_crossed]
    home = []
    if long:
        for at, mixed in enumerate(attend(table_of, remote, queries, far)):
            home.append(swap(mixed, "doc", 2 + at))
    else:
        far.advance()
        last = len(far.slots) - 1
        states = attend(table_of, remote, queries, far, span=(0, last), end=False)
        for at, lane in enumerate(remote):
            state = states[3 * at:3 * at + 3]
            (mixed,) = attend(
                table_of, [lane], queries, far, span=(last, last + 1), states=[state]
            )
            home.append(swap(mixed, "doc", 2 + at))
    count = lax.axis_size("doc")
    result = deliver(info, (0, 1), [mixed_own, out_twin], count)
    return deliver(info, (2, 3), home, count, before=result)


def solution(mesh):
    return jax.shard_map(
        local,
        mesh=mesh,
        in_specs=(
            P("doc", "seq", None),
            P(),
            P(None, "doc"),
            P(None, "doc"),
            P(None, "doc"),
            P(),
            P(),
        ),
        out_specs=P("doc", "seq", None),
        check_vma=False,
    )
```

```python
import functools
import math

import jax
import jax.numpy as jnp
from jax import lax
from jax.experimental import pallas as pl
from jax.experimental.pallas import tpu as pltpu
from jax.sharding import PartitionSpec as P

HEAD_WIDTH = 128
QUERY_HEADS = 16
KEY_VALUE_HEADS = 4
QUERY_GROUP = QUERY_HEADS // KEY_VALUE_HEADS
EPSILON = 1e-05
BAND = 16
MIB = 1024 * 1024
OUT_OF_REACH = 1 << 30

SMEM = pl.BlockSpec(memory_space=pltpu.SMEM)
VMEM = pl.BlockSpec(memory_space=pltpu.VMEM)
ANYWHERE = pl.BlockSpec(memory_space=pl.ANY)
HBM = pl.BlockSpec(memory_space=pltpu.HBM)


def swap(value, axis, mask):
    count = lax.axis_size(axis)
    return lax.ppermute(value, axis, [(source, source ^ mask) for source in range(count)])


def after(value, *others):
    return lax.optimization_barrier((value,) + others)[0]


def in_hbm(array):
    return pltpu.with_memory_space_constraint(array, pltpu.HBM)


def rope_table(positions, width):
    inverse = jnp.power(jnp.float32(500000.0), -jnp.arange(0, width, 2, dtype=jnp.float32) / width)
    angles = positions.astype(jnp.float32)[:, None] * inverse[None, :]
    return (jnp.cos(angles), jnp.sin(angles))


def project_kernel(pieces, early, before, *refs):
    token_refs, refs = list(refs[:pieces]), list(refs[pieces:])
    ahead = 0
    if before:
        before_ref, refs = refs[0], refs[1:]
        ahead = before_ref.shape[0]
    gain_ref, wq_ref, wk_ref, wv_ref, table_ref, q_ref, kv_ref = refs[:7]
    refs = refs[7:]
    if before:
        kv_ref[:ahead, :] = before_ref[...]
    copies = []
    if early:
        sources = (gain_ref, token_refs[0], wk_ref, wv_ref, wq_ref)
        held, refs = refs[:1] + refs[5:6] + refs[1:4], refs[4:5] + refs[6:]
        sems = refs[1]
        gain_ref, token_refs[0], wk_ref, wv_ref, wq_ref = held
        for at, (source, target) in enumerate(zip(sources, held)):
            copies.append(pltpu.make_async_copy(source, target, sems.at[at]))
            copies[-1].start()
        copies[0].wait()
    normed = refs[0]
    width = gain_ref.shape[1]
    heads = wk_ref.shape[1] // HEAD_WIDTH
    deep = min(1024, width)

    rows = token_refs[0].shape[0]
    for piece in reversed(range(pieces)):
        if piece == 0 and early:
            copies[1].wait()
        ref, first = token_refs[piece], piece * rows

        def norm_band(index, carry, ref=ref, first=first):
            at = pl.ds(pl.multiple_of(index * BAND, BAND), BAND)
            wide = ref[at, :].astype(jnp.float32)
            scale = lax.rsqrt(jnp.mean(wide * wide, axis=-1, keepdims=True) + EPSILON)
            normed[pl.ds(pl.multiple_of(first + index * BAND, BAND), BAND), :] = (
                wide * scale * gain_ref[...]
            ).astype(jnp.bfloat16)
            return carry

        lax.fori_loop(0, rows // BAND, norm_band, 0, unroll=2)

    half = HEAD_WIDTH // 2

    def rotate(value):
        turned = jnp.concatenate([value[:, half:], value[:, :half]], axis=1)
        return (
            value * table_ref[:, :HEAD_WIDTH] + turned * table_ref[:, HEAD_WIDTH:]
        ).astype(jnp.bfloat16)

    def multiply(weight_of):
        total = None
        for start in range(0, width, deep):
            part = jnp.dot(
                normed[:, start:start + deep],
                weight_of(slice(start, start + deep)),
                preferred_element_type=jnp.float32,
            )
            total = part if total is None else total + part
        return total

    if early:
        copies[2].wait()
        copies[3].wait()
    for head in range(heads):
        at = slice(head * HEAD_WIDTH, (head + 1) * HEAD_WIDTH)
        both = multiply(lambda k: jnp.concatenate([wk_ref[k, at], wv_ref[k, at]], axis=1))
        out = 2 * head * HEAD_WIDTH
        for piece in range(pieces):
            mine = both[piece * rows:(piece + 1) * rows]
            band = slice(ahead + piece * rows, ahead + (piece + 1) * rows)
            kv_ref[band, out:out + HEAD_WIDTH] = rotate(mine[:, :HEAD_WIDTH])
            kv_ref[band, out + HEAD_WIDTH:out + 2 * HEAD_WIDTH] = mine[:, HEAD_WIDTH:].astype(
                jnp.bfloat16
            )
    if early:
        copies[4].wait()
    pair = 2 * HEAD_WIDTH
    for start in range(0, wq_ref.shape[1], pair):
        both = multiply(lambda k: wq_ref[k, start:start + pair])
        for piece in range(pieces):
            band = slice(piece * rows, (piece + 1) * rows)
            for at in (0, HEAD_WIDTH):
                q_ref[band, start + at:start + at + HEAD_WIDTH] = rotate(
                    both[band, at:at + HEAD_WIDTH]
                )


def project(pieces, gain, w_query, key_weight, value_weight, table, early=False, before=None):
    width = gain.shape[1]
    q_cols, k_cols = w_query.shape[1], key_weight.shape[1]
    total = len(pieces) * pieces[0].shape[0]
    params = (gain, w_query, key_weight, value_weight)
    held = () if before is None else (before,)
    scratch = [pltpu.VMEM((total, width), jnp.bfloat16)]
    kind = [VMEM] * (len(pieces) + len(held) + len(params))
    shapes = [
        jax.ShapeDtypeStruct((total, q_cols), jnp.bfloat16),
        jax.ShapeDtypeStruct((total + sum(a.shape[0] for a in held), 2 * k_cols), jnp.bfloat16),
    ]
    if early:
        scratch.append(pltpu.VMEM(pieces[0].shape, pieces[0].dtype))
        scratch.append(pltpu.SemaphoreType.DMA((5,)))
        params = tuple(in_hbm(array) for array in params)
        shapes += [
            jax.ShapeDtypeStruct(array.shape, array.dtype)
            for array in (gain, key_weight, value_weight, w_query)
        ]
        pieces = [in_hbm(pieces[0])] + list(pieces[1:])
        kind = [HBM] + [VMEM] * (len(pieces) - 1) + [HBM] * len(params)
    return pl.pallas_call(
        functools.partial(project_kernel, len(pieces), early, before is not None),
        in_specs=kind + [VMEM],
        out_specs=[VMEM] * len(shapes),
        out_shape=shapes,
        scratch_shapes=scratch,
        compiler_params=pltpu.CompilerParams(vmem_limit_bytes=20 * MIB),
        cost_estimate=pl.CostEstimate(
            flops=2 * total * width * (q_cols + 2 * k_cols),
            bytes_accessed=2 * width * (q_cols + 2 * k_cols) + 2 * total * width,
            transcendentals=0,
        ),
        name="project",
    )(*pieces, *held, *params, table)


def ring_order(count):
    return list(range(0, count, 2)) + list(range(count - 1, 0, -2))


class Gathered:
    def __init__(self, kv):
        count = lax.axis_size("seq")
        total = kv.shape[0]
        chunk = 8 if count % 8 == 0 else 1
        self.chunks, self.latest = count // chunk, ()
        self.arrays = [lax.all_gather(kv, "seq", axis=0, tiled=True)]
        self.slots = [
            lambda index, j=j: (0, pl.multiple_of((index * chunk + j) * total, BAND))
            for j in range(chunk)
        ]

    def advance(self, *others):
        pass


class Ring:
    def __init__(self, kv):
        self.count, self.chunks, self.stage = lax.axis_size("seq"), 1, 0
        self.order = ring_order(self.count)
        self.arrays, self.slots, self.latest = [], [], ()
        self.front = {1: kv, -1: kv}
        self.hold(kv)

    @staticmethod
    def sources(at, count):
        steps = [0]
        for stage in range(1, count // 2 + 1):
            steps += [stage, -stage] if 2 * stage < count else [stage]
        return [(at - step) % count for step in steps]

    def hold(self, array):
        self.slots.append(lambda index, r=len(self.arrays): (r, 0))
        self.arrays.append(array)

    def advance(self, *others):
        if self.stage >= self.count // 2:
            return
        self.stage += 1
        fresh = []
        for way in (1, -1) if 2 * self.stage < self.count else (1,):
            value = after(self.front[way], *others) if others else self.front[way]
            pairs = [
                (source, self.order[(at + way) % self.count]) for at, source in enumerate(self.order)
            ]
            self.front[way] = lax.ppermute(value, "seq", pairs)
            fresh.append(self.front[way])
            self.hold(self.front[way])
        self.latest = tuple(fresh)


def plan_kernel(ring, lanes, heads, count, rows, info_ref, vertical_ref, slash_ref, plan_ref):
    place, me = info_ref[0], info_ref[1]
    plan_ref[0] = place

    def enter(number, block):
        for lane in range(lanes):
            doc = me ^ lane
            for head in range(heads):
                group = me * heads + head
                found = (block == place) | (block == place - 1)
                for s in range(slash_ref.shape[2]):
                    found = found | (block == place - slash_ref[doc, group, s])
                for s in range(vertical_ref.shape[2]):
                    found = found | ((block == vertical_ref[doc, group, s]) & (block < place - 1))
                at = 1 + (lane * heads + head) * count + number
                plan_ref[at] = jnp.where(found & (block >= 0), block * rows, OUT_OF_REACH)

    if ring:
        order = ring_order(count)
        lists = {order[at]: [order[r] for r in Ring.sources(at, count)] for at in range(count)}
        for number in range(count):
            block = jnp.int32(0)
            for here, blocks in lists.items():
                block = jnp.where(place == here, blocks[number], block)
            enter(number, block)
    else:

        def one(number, carry):
            enter(number, number)
            return carry

        lax.fori_loop(0, count, one, 0)


def plan(info, vertical, slash, ring, rows):
    count, lanes = lax.axis_size("seq"), lax.axis_size("doc")
    heads = vertical.shape[1] // lanes
    length = 1 + lanes * heads * count
    return pl.pallas_call(
        functools.partial(plan_kernel, ring, lanes, heads, count, rows),
        in_specs=[SMEM] * 3,
        out_specs=SMEM,
        out_shape=jax.ShapeDtypeStruct((length,), jnp.int32),
        compiler_params=pltpu.CompilerParams(vmem_limit_bytes=4 * MIB),
        name="plan",
    )(info, vertical, slash)


def attend_kernel(lanes, stride, slot_at, slots, chunks, q_count, kv_count, begin, end, plan_ref, *refs):
    q_refs, kv_refs, refs = refs[:q_count], refs[q_count:q_count + kv_count], refs[q_count + kv_count:]
    state_refs = refs[:0 if begin else 3 * len(lanes)]
    out_refs = refs[len(state_refs):]
    heads = kv_refs[0].shape[1] // (2 * HEAD_WIDTH)
    place = plan_ref[0]
    factor = HEAD_WIDTH ** (-0.5) * math.log2(math.e)

    for lane, (mask, q_at, kv_first, rows) in enumerate(lanes):
        rank = QUERY_GROUP * rows
        row_at = place * rows + lax.broadcasted_iota(jnp.int32, (1, rows), 1)
        query_at = jnp.concatenate([row_at] * QUERY_GROUP, axis=1)
        key_at = lax.broadcasted_iota(jnp.int32, (rows, rank), 0)
        for head in range(heads):
            table = 1 + (mask * heads + head) * stride + slot_at
            queries = jnp.concatenate(
                [
                    q_refs[q_at[0]][
                        q_at[1]:q_at[1] + rows,
                        (head * QUERY_GROUP + h) * HEAD_WIDTH:(head * QUERY_GROUP + h + 1) * HEAD_WIDTH,
                    ]
                    for h in range(QUERY_GROUP)
                ],
                axis=0,
            )

            def step(index, carry):
                found = [slot(index) for slot in slots]

                def column(at):
                    cols = slice(at * HEAD_WIDTH, (at + 1) * HEAD_WIDTH)
                    parts = []
                    for r, first in found:
                        if isinstance(first, int):
                            where = slice(first + kv_first, first + kv_first + rows)
                        else:
                            where = pl.ds(pl.multiple_of(first + kv_first, BAND), rows)
                        parts.append(kv_refs[r][where, cols])
                    return jnp.concatenate(parts, axis=0)

                keys, values = column(2 * head), column(2 * head + 1)
                scores = lax.dot_general(
                    keys, queries, (((1,), (1,)), ((), ())), preferred_element_type=jnp.float32
                )
                parts = []
                for j in range(len(slots)):
                    shift = plan_ref[table + index * len(slots) + j]
                    parts.append(
                        jnp.where(
                            key_at <= query_at - shift,
                            scores[j * rows:(j + 1) * rows],
                            -jnp.inf,
                        )
                    )
                scores = jnp.concatenate(parts, axis=0)
                top = jnp.max(scores, axis=0, keepdims=True)
                if carry is None:
                    fresh = safe = top
                else:
                    fresh = jnp.maximum(carry[0], top)
                    safe = jnp.where(fresh == -jnp.inf, jnp.float32(0), fresh)
                raised = jnp.exp2((scores - safe) * factor)
                total = jnp.sum(raised, axis=0, keepdims=True)
                mixed = lax.dot_general(
                    values,
                    raised.astype(jnp.bfloat16),
                    (((0,), (0,)), ((), ())),
                    preferred_element_type=jnp.float32,
                )
                if carry is not None:
                    fade = jnp.exp2((carry[0] - safe) * factor)
                    total, mixed = carry[1] * fade + total, carry[2] * fade + mixed
                return fresh, total, mixed

            carry = None
            if not begin:
                carry = tuple(ref[head] for ref in state_refs[3 * lane:3 * lane + 3])
            elif chunks > 1:
                carry = (
                    jnp.full((1, rank), -jnp.inf, jnp.float32),
                    jnp.zeros((1, rank), jnp.float32),
                    jnp.zeros((HEAD_WIDTH, rank), jnp.float32),
                )
            if chunks > 1:
                carry = lax.fori_loop(0, chunks, step, carry)
            else:
                carry = step(0, carry)
            if not end:
                for ref, value in zip(out_refs[3 * lane:3 * lane + 3], carry):
                    ref[head] = value
                continue
            result = carry[2] / carry[1]
            for h in range(QUERY_GROUP):
                cols = slice(
                    (head * QUERY_GROUP + h) * HEAD_WIDTH, (head * QUERY_GROUP + h + 1) * HEAD_WIDTH
                )
                out_refs[lane][:, cols] = result[:, h * rows:(h + 1) * rows].T.astype(jnp.bfloat16)


def attend(table, lanes, queries, spread, span=None, states=None, end=True):
    first, last = span or (0, len(spread.slots))
    q_cols = queries[0].shape[1]
    rows = lanes[0][3]
    arrays, slots = spread.arrays, spread.slots[first:last]
    if span:
        arrays, slots = arrays[first:last], spread.slots[:last - first]
    held = [array for state in states for array in state] if states else []
    if end:
        shapes = [jax.ShapeDtypeStruct((rows, q_cols), jnp.bfloat16)] * len(lanes)
    else:
        heads = q_cols // (QUERY_GROUP * HEAD_WIDTH)
        shapes = [
            jax.ShapeDtypeStruct((heads, deep, QUERY_GROUP * rows), jnp.float32)
            for deep in (1, 1, HEAD_WIDTH)
        ] * len(lanes)
    kernel = functools.partial(
        attend_kernel,
        lanes,
        lax.axis_size("seq"),
        first,
        slots,
        spread.chunks,
        len(queries),
        len(arrays),
        not states,
        end,
    )
    return pl.pallas_call(
        kernel,
        in_specs=[SMEM] + [VMEM] * (len(queries) + len(arrays) + len(held)),
        out_specs=[VMEM] * len(shapes),
        out_shape=shapes,
        compiler_params=pltpu.CompilerParams(
            vmem_limit_bytes=10 * MIB + 4 * sum(a.size for a in (*queries, *arrays))
        ),
        cost_estimate=pl.CostEstimate(
            flops=4 * len(lanes) * rows * q_cols * len(slots) * spread.chunks * rows,
            bytes_accessed=2 * sum(a.size for a in arrays) + 4 * len(lanes) * rows * q_cols,
            transcendentals=len(lanes) * rows * len(slots) * spread.chunks * rows * QUERY_GROUP,
        ),
        name="attend",
    )(table, *queries, *arrays, *held)


def deliver_kernel(masks, info_ref, *refs):
    pieces, (out_ref, sems) = refs[:len(masks)], refs[-2:]
    cols = pieces[0].shape[1]
    copies = []
    for at, (mask, piece) in enumerate(zip(masks, pieces)):
        where = pl.ds(pl.multiple_of((info_ref[1] ^ mask) * cols, cols), cols)
        copies.append(pltpu.make_async_copy(piece, out_ref.at[0, :, where], sems.at[at]))
        copies[-1].start()
    for copy in copies:
        copy.wait()


def deliver(info, masks, pieces, count, before=None):
    rows, cols = pieces[0].shape
    begun = () if before is None else (before,)
    return pl.pallas_call(
        functools.partial(deliver_kernel, masks),
        in_specs=[SMEM] + [VMEM] * len(pieces) + [HBM] * len(begun),
        out_specs=HBM,
        out_shape=jax.ShapeDtypeStruct((1, rows, count * cols), jnp.bfloat16),
        input_output_aliases={1 + len(pieces): 0} if begun else {},
        scratch_shapes=[pltpu.SemaphoreType.DMA((len(pieces),))],
        compiler_params=pltpu.CompilerParams(vmem_limit_bytes=4 * MIB),
        name="deliver",
    )(info, *pieces, *begun)


def local(tokens, norm_gain, w_query, key_weight, value_weight, vertical_blocks, slash_offsets):
    _, rows, width = tokens.shape
    assert lax.axis_size("doc") == 4
    place = lax.axis_index("seq")
    doc_place = lax.axis_index("doc")
    info = after(jnp.stack([place, doc_place, place * rows]).astype(jnp.int32))
    cosine, sine = rope_table(info[2:] + jnp.arange(rows, dtype=jnp.int32), HEAD_WIDTH)
    table = jnp.concatenate([cosine, cosine, -sine, sine], axis=1)
    own = after(tokens, info)[0]
    gain = norm_gain.reshape(1, width)
    long = lax.axis_size("seq") > 8 or lax.axis_size("seq") % 2 == 1
    ring = Gathered if long else Ring
    table_of = plan(info, vertical_blocks, slash_offsets, not long, rows)

    twin = swap(own, "doc", 1)
    across = swap(own, "doc", 2)
    q_near, kv_near, gain_in, wk_in, wv_in, wq_in = project(
        [own, twin], gain, w_query, key_weight, value_weight, table, early=True
    )
    params = (gain_in, wq_in, wk_in, wv_in, table)
    near = ring(kv_near)
    near.advance()
    near.advance(table_of)
    near.advance()

    across = after(across, *near.latest)
    near.advance()
    crossed = swap(across, "doc", 1)
    q_across, kv_across = project([across], *params)
    q_crossed, kv_far = project([crossed], *params, before=kv_across)
    far = ring(kv_far)
    far.advance()
    mixed_own, mixed_twin = attend(
        table_of,
        [(0, (0, 0), 0, rows), (1, (0, rows), rows, rows)],
        [after(q_near, kv_far)],
        near,
    )
    out_twin = swap(mixed_twin, "doc", 1)
    far.advance(mixed_twin)
    far.advance()
    remote = [(2, (0, 0), 0, rows), (3, (1, 0), rows, rows)]
    queries = [after(q_across, out_twin), q_crossed]
    home = []
    if long:
        for at, mixed in enumerate(attend(table_of, remote, queries, far)):
            home.append(swap(mixed, "doc", 2 + at))
    else:
        far.advance()
        last = len(far.slots) - 1
        states = attend(table_of, remote, queries, far, span=(0, last), end=False)
        for at, lane in enumerate(remote):
            state = states[3 * at:3 * at + 3]
            (mixed,) = attend(
                table_of, [lane], queries, far, span=(last, last + 1), states=[state]
            )
            home.append(swap(mixed, "doc", 2 + at))
    count = lax.axis_size("doc")
    result = deliver(info, (0, 1), [mixed_own, out_twin], count)
    return deliver(info, (2, 3), home, count, before=result)


def solution(mesh):
    return jax.shard_map(
        local,
        mesh=mesh,
        in_specs=(
            P("doc", "seq", None),
            P(),
            P(None, "doc"),
            P(None, "doc"),
            P(None, "doc"),
            P(),
            P(),
        ),
        out_specs=P("doc", "seq", None),
        check_vma=False,
    )
```

```python
import functools
import math

import jax
import jax.numpy as jnp
from jax import lax
from jax.experimental import pallas as pl
from jax.experimental.pallas import tpu as pltpu
from jax.sharding import PartitionSpec as P

HEAD_WIDTH = 128
QUERY_HEADS = 16
KEY_VALUE_HEADS = 4
QUERY_GROUP = QUERY_HEADS // KEY_VALUE_HEADS
EPSILON = 1e-05
BAND = 16
MIB = 1024 * 1024
OUT_OF_REACH = 1 << 30

SMEM = pl.BlockSpec(memory_space=pltpu.SMEM)
VMEM = pl.BlockSpec(memory_space=pltpu.VMEM)
ANYWHERE = pl.BlockSpec(memory_space=pl.ANY)
HBM = pl.BlockSpec(memory_space=pltpu.HBM)


def swap(value, axis, mask):
    count = lax.axis_size(axis)
    return lax.ppermute(value, axis, [(source, source ^ mask) for source in range(count)])


def after(value, *others):
    return lax.optimization_barrier((value,) + others)[0]


def in_hbm(array):
    return pltpu.with_memory_space_constraint(array, pltpu.HBM)


def rope_table(positions, width):
    inverse = jnp.power(jnp.float32(500000.0), -jnp.arange(0, width, 2, dtype=jnp.float32) / width)
    angles = positions.astype(jnp.float32)[:, None] * inverse[None, :]
    return (jnp.cos(angles), jnp.sin(angles))


def normalize(token_ref, gain_ref, normed_ref, first):
    def norm_band(index, carry):
        at = pl.ds(pl.multiple_of(index * BAND, BAND), BAND)
        wide = token_ref[at, :].astype(jnp.float32)
        scale = lax.rsqrt(jnp.mean(wide * wide, axis=-1, keepdims=True) + EPSILON)
        normed_ref[pl.ds(pl.multiple_of(first + index * BAND, BAND), BAND), :] = (
            wide * scale * gain_ref[...]
        ).astype(jnp.bfloat16)
        return carry

    lax.fori_loop(0, token_ref.shape[0] // BAND, norm_band, 0, unroll=2)


def rotate(value, table_ref):
    half = HEAD_WIDTH // 2
    turned = jnp.concatenate([value[:, half:], value[:, :half]], axis=1)
    return (value * table_ref[:, :HEAD_WIDTH] + turned * table_ref[:, HEAD_WIDTH:]).astype(
        jnp.bfloat16
    )


def multiply(normed_ref, weight_of):
    width = normed_ref.shape[1]
    deep = min(1024, width)
    total = None
    for start in range(0, width, deep):
        part = jnp.dot(
            normed_ref[:, start:start + deep],
            weight_of(slice(start, start + deep)),
            preferred_element_type=jnp.float32,
        )
        total = part if total is None else total + part
    return total


def write_keys_values(normed_ref, wk_ref, wv_ref, table_ref, kv_ref, ahead):
    rows = table_ref.shape[0]
    for head in range(wk_ref.shape[1] // HEAD_WIDTH):
        at = slice(head * HEAD_WIDTH, (head + 1) * HEAD_WIDTH)
        both = multiply(
            normed_ref, lambda k: jnp.concatenate([wk_ref[k, at], wv_ref[k, at]], axis=1)
        )
        out = 2 * head * HEAD_WIDTH
        for first in range(0, normed_ref.shape[0], rows):
            mine = both[first:first + rows]
            band = slice(ahead + first, ahead + first + rows)
            kv_ref[band, out:out + HEAD_WIDTH] = rotate(mine[:, :HEAD_WIDTH], table_ref)
            kv_ref[band, out + HEAD_WIDTH:out + 2 * HEAD_WIDTH] = mine[:, HEAD_WIDTH:].astype(
                jnp.bfloat16
            )


def write_queries(normed_ref, wq_ref, table_ref, q_ref, ahead):
    rows, pair = table_ref.shape[0], 2 * HEAD_WIDTH
    for start in range(0, wq_ref.shape[1], pair):
        both = multiply(normed_ref, lambda k: wq_ref[k, start:start + pair])
        for first in range(0, normed_ref.shape[0], rows):
            band = slice(ahead + first, ahead + first + rows)
            for at in (0, HEAD_WIDTH):
                q_ref[band, start + at:start + at + HEAD_WIDTH] = rotate(
                    both[first:first + rows, at:at + HEAD_WIDTH], table_ref
                )


def near_kernel(
    own_hbm, twin_ref, gain_hbm, wq_hbm, wk_hbm, wv_hbm, table_ref,
    q_ref, kv_ref, gain_ref, wq_ref, wk_ref, wv_ref, own_ref, normed_ref, sems,
):
    copies = []
    for source, target in (
        (gain_hbm, gain_ref), (own_hbm, own_ref), (wk_hbm, wk_ref), (wv_hbm, wv_ref), (wq_hbm, wq_ref)
    ):
        copies.append(pltpu.make_async_copy(source, target, sems.at[len(copies)]))
        copies[-1].start()
    copies[0].wait()
    normalize(twin_ref, gain_ref, normed_ref, own_ref.shape[0])
    copies[1].wait()
    normalize(own_ref, gain_ref, normed_ref, 0)
    copies[2].wait()
    copies[3].wait()
    write_keys_values(normed_ref, wk_ref, wv_ref, table_ref, kv_ref, 0)
    copies[4].wait()
    write_queries(normed_ref, wq_ref, table_ref, q_ref, 0)


def keys_values_kernel(before, token_ref, gain_ref, wk_ref, wv_ref, table_ref, *refs):
    kv_ref, normed_ref = refs[-2:]
    ahead = 0
    if before:
        ahead = refs[0].shape[0]
        kv_ref[:ahead, :] = refs[0][...]
    normalize(token_ref, gain_ref, normed_ref, 0)
    write_keys_values(normed_ref, wk_ref, wv_ref, table_ref, kv_ref, ahead)


def queries_kernel(pieces, wq_ref, table_ref, *refs):
    for at, normed_ref in enumerate(refs[:pieces]):
        write_queries(normed_ref, wq_ref, table_ref, refs[pieces], at * normed_ref.shape[0])


def project_call(kernel, name, operands, kinds, shapes, scratch, rows, columns):
    width = max(array.shape[0] for array in operands)
    return pl.pallas_call(
        kernel,
        in_specs=kinds,
        out_specs=[VMEM] * len(shapes),
        out_shape=[jax.ShapeDtypeStruct(shape, dtype) for shape, dtype in shapes],
        scratch_shapes=scratch,
        compiler_params=pltpu.CompilerParams(vmem_limit_bytes=20 * MIB),
        cost_estimate=pl.CostEstimate(
            flops=2 * rows * width * columns,
            bytes_accessed=2 * width * (columns + rows),
            transcendentals=0,
        ),
        name=name,
    )(*operands)


def project_near(own, twin, gain, w_query, key_weight, value_weight, table):
    rows, width = own.shape
    q_cols, k_cols = w_query.shape[1], key_weight.shape[1]
    params = (gain, w_query, key_weight, value_weight)
    shapes = [((2 * rows, q_cols), jnp.bfloat16), ((2 * rows, 2 * k_cols), jnp.bfloat16)]
    shapes += [(array.shape, array.dtype) for array in params]
    return project_call(
        near_kernel,
        "project_near",
        (in_hbm(own), twin, *(in_hbm(array) for array in params), table),
        [HBM, VMEM] + [HBM] * 4 + [VMEM],
        shapes,
        [
            pltpu.VMEM(own.shape, own.dtype),
            pltpu.VMEM((2 * rows, width), jnp.bfloat16),
            pltpu.SemaphoreType.DMA((5,)),
        ],
        2 * rows,
        q_cols + 2 * k_cols,
    )


def project_keys_values(tokens, gain, key_weight, value_weight, table, before=None):
    held = () if before is None else (before,)
    rows, cols = tokens.shape[0], 2 * key_weight.shape[1]
    total = rows + sum(array.shape[0] for array in held)
    operands = (tokens, gain, key_weight, value_weight, table, *held)
    return project_call(
        functools.partial(keys_values_kernel, len(held)),
        "project_keys_values",
        operands,
        [VMEM] * len(operands),
        [((total, cols), jnp.bfloat16), (tokens.shape, jnp.bfloat16)],
        [],
        rows,
        cols,
    )


def project_queries(normed, w_query, table):
    operands = (w_query, table, *normed)
    rows = sum(array.shape[0] for array in normed)
    (queries,) = project_call(
        functools.partial(queries_kernel, len(normed)),
        "project_queries",
        operands,
        [VMEM] * len(operands),
        [((rows, w_query.shape[1]), jnp.bfloat16)],
        [],
        rows,
        w_query.shape[1],
    )
    return queries


def ring_order(count):
    return list(range(0, count, 2)) + list(range(count - 1, 0, -2))


class Gathered:
    def __init__(self, kv):
        count = lax.axis_size("seq")
        total = kv.shape[0]
        chunk = 8 if count % 8 == 0 else 1
        self.chunks, self.latest = count // chunk, ()
        self.arrays = [lax.all_gather(kv, "seq", axis=0, tiled=True)]
        self.slots = [
            lambda index, j=j: (0, pl.multiple_of((index * chunk + j) * total, BAND))
            for j in range(chunk)
        ]

    def advance(self, *others):
        pass


class Ring:
    def __init__(self, kv):
        self.count, self.chunks, self.stage = lax.axis_size("seq"), 1, 0
        self.order = ring_order(self.count)
        self.arrays, self.slots, self.latest = [], [], ()
        self.front = {1: kv, -1: kv}
        self.hold(kv)

    @staticmethod
    def sources(at, count):
        steps = [0]
        for stage in range(1, count // 2 + 1):
            steps += [stage, -stage] if 2 * stage < count else [stage]
        return [(at - step) % count for step in steps]

    def hold(self, array):
        self.slots.append(lambda index, r=len(self.arrays): (r, 0))
        self.arrays.append(array)

    def last(self, array):
        pairs = [(s, self.order[(at + 1) % self.count]) for at, s in enumerate(self.order)]
        return lax.ppermute(array, "seq", pairs)

    def advance(self, *others):
        if self.stage >= self.count // 2:
            return
        self.stage += 1
        fresh = []
        for way in (1, -1) if 2 * self.stage < self.count else (1,):
            value = after(self.front[way], *others) if others else self.front[way]
            pairs = [
                (source, self.order[(at + way) % self.count]) for at, source in enumerate(self.order)
            ]
            self.front[way] = lax.ppermute(value, "seq", pairs)
            fresh.append(self.front[way])
            self.hold(self.front[way])
        self.latest = tuple(fresh)


def plan_kernel(ring, lanes, heads, count, rows, info_ref, vertical_ref, slash_ref, plan_ref):
    place, me = info_ref[0], info_ref[1]
    plan_ref[0] = place

    def enter(number, block):
        for lane in range(lanes):
            doc = me ^ lane
            for head in range(heads):
                group = me * heads + head
                found = (block == place) | (block == place - 1)
                for s in range(slash_ref.shape[2]):
                    found = found | (block == place - slash_ref[doc, group, s])
                for s in range(vertical_ref.shape[2]):
                    found = found | ((block == vertical_ref[doc, group, s]) & (block < place - 1))
                at = 1 + (lane * heads + head) * count + number
                plan_ref[at] = jnp.where(found & (block >= 0), block * rows, OUT_OF_REACH)

    if ring:
        order = ring_order(count)
        lists = {order[at]: [order[r] for r in Ring.sources(at, count)] for at in range(count)}
        for number in range(count):
            block = jnp.int32(0)
            for here, blocks in lists.items():
                block = jnp.where(place == here, blocks[number], block)
            enter(number, block)
    else:

        def one(number, carry):
            enter(number, number)
            return carry

        lax.fori_loop(0, count, one, 0)


def plan(info, vertical, slash, ring, rows):
    count, lanes = lax.axis_size("seq"), lax.axis_size("doc")
    heads = vertical.shape[1] // lanes
    length = 1 + lanes * heads * count
    return pl.pallas_call(
        functools.partial(plan_kernel, ring, lanes, heads, count, rows),
        in_specs=[SMEM] * 3,
        out_specs=SMEM,
        out_shape=jax.ShapeDtypeStruct((length,), jnp.int32),
        compiler_params=pltpu.CompilerParams(vmem_limit_bytes=4 * MIB),
        name="plan",
    )(info, vertical, slash)


def attend_kernel(lanes, stride, slot_at, slots, chunks, q_count, kv_count, begin, end, plan_ref, *refs):
    q_refs, kv_refs, refs = refs[:q_count], refs[q_count:q_count + kv_count], refs[q_count + kv_count:]
    state_refs = refs[:0 if begin else 3 * len(lanes)]
    out_refs = refs[len(state_refs):]
    heads = kv_refs[0].shape[1] // (2 * HEAD_WIDTH)
    place = plan_ref[0]
    factor = HEAD_WIDTH ** (-0.5) * math.log2(math.e)

    for lane, (mask, q_at, kv_first, rows) in enumerate(lanes):
        rank = QUERY_GROUP * rows
        row_at = place * rows + lax.broadcasted_iota(jnp.int32, (1, rows), 1)
        query_at = jnp.concatenate([row_at] * QUERY_GROUP, axis=1)
        key_at = lax.broadcasted_iota(jnp.int32, (rows, rank), 0)
        for head in range(heads):
            table = 1 + (mask * heads + head) * stride + slot_at
            queries = jnp.concatenate(
                [
                    q_refs[q_at[0]][
                        q_at[1]:q_at[1] + rows,
                        (head * QUERY_GROUP + h) * HEAD_WIDTH:(head * QUERY_GROUP + h + 1) * HEAD_WIDTH,
                    ]
                    for h in range(QUERY_GROUP)
                ],
                axis=0,
            )

            def step(index, carry):
                found = [slot(index) for slot in slots]

                def column(at):
                    cols = slice(at * HEAD_WIDTH, (at + 1) * HEAD_WIDTH)
                    parts = []
                    for r, first in found:
                        if isinstance(first, int):
                            where = slice(first + kv_first, first + kv_first + rows)
                        else:
                            where = pl.ds(pl.multiple_of(first + kv_first, BAND), rows)
                        parts.append(kv_refs[r][where, cols])
                    return jnp.concatenate(parts, axis=0)

                keys, values = column(2 * head), column(2 * head + 1)
                scores = lax.dot_general(
                    keys, queries, (((1,), (1,)), ((), ())), preferred_element_type=jnp.float32
                )
                parts = []
                for j in range(len(slots)):
                    shift = plan_ref[table + index * len(slots) + j]
                    parts.append(
                        jnp.where(
                            key_at <= query_at - shift,
                            scores[j * rows:(j + 1) * rows],
                            -jnp.inf,
                        )
                    )
                scores = jnp.concatenate(parts, axis=0)
                top = jnp.max(scores, axis=0, keepdims=True)
                if carry is None:
                    fresh = safe = top
                else:
                    fresh = jnp.maximum(carry[0], top)
                    safe = jnp.where(fresh == -jnp.inf, jnp.float32(0), fresh)
                raised = jnp.exp2((scores - safe) * factor)
                total = jnp.sum(raised, axis=0, keepdims=True)
                mixed = lax.dot_general(
                    values,
                    raised.astype(jnp.bfloat16),
                    (((0,), (0,)), ((), ())),
                    preferred_element_type=jnp.float32,
                )
                if carry is not None:
                    fade = jnp.exp2((carry[0] - safe) * factor)
                    total, mixed = carry[1] * fade + total, carry[2] * fade + mixed
                return fresh, total, mixed

            carry = None
            if not begin:
                carry = tuple(ref[head] for ref in state_refs[3 * lane:3 * lane + 3])
            elif chunks > 1:
                carry = (
                    jnp.full((1, rank), -jnp.inf, jnp.float32),
                    jnp.zeros((1, rank), jnp.float32),
                    jnp.zeros((HEAD_WIDTH, rank), jnp.float32),
                )
            if chunks > 1:
                carry = lax.fori_loop(0, chunks, step, carry)
            else:
                carry = step(0, carry)
            if not end:
                for ref, value in zip(out_refs[3 * lane:3 * lane + 3], carry):
                    ref[head] = value
                continue
            result = carry[2] / carry[1]
            for h in range(QUERY_GROUP):
                cols = slice(
                    (head * QUERY_GROUP + h) * HEAD_WIDTH, (head * QUERY_GROUP + h + 1) * HEAD_WIDTH
                )
                out_refs[lane][:, cols] = result[:, h * rows:(h + 1) * rows].T.astype(jnp.bfloat16)


def attend(table, lanes, queries, arrays, slots, chunks=1, first=0, states=None, end=True):
    q_cols = queries[0].shape[1]
    rows = lanes[0][3]
    held = [array for state in states for array in state] if states else []
    if end:
        shapes = [jax.ShapeDtypeStruct((rows, q_cols), jnp.bfloat16)] * len(lanes)
    else:
        heads = q_cols // (QUERY_GROUP * HEAD_WIDTH)
        shapes = [
            jax.ShapeDtypeStruct((heads, deep, QUERY_GROUP * rows), jnp.float32)
            for deep in (1, 1, HEAD_WIDTH)
        ] * len(lanes)
    kernel = functools.partial(
        attend_kernel,
        lanes,
        lax.axis_size("seq"),
        first,
        slots,
        chunks,
        len(queries),
        len(arrays),
        not states,
        end,
    )
    return pl.pallas_call(
        kernel,
        in_specs=[SMEM] + [VMEM] * (len(queries) + len(arrays) + len(held)),
        out_specs=[VMEM] * len(shapes),
        out_shape=shapes,
        compiler_params=pltpu.CompilerParams(
            vmem_limit_bytes=10 * MIB + 4 * sum(a.size for a in (*queries, *arrays))
        ),
        cost_estimate=pl.CostEstimate(
            flops=4 * len(lanes) * rows * q_cols * len(slots) * chunks * rows,
            bytes_accessed=2 * sum(a.size for a in arrays) + 4 * len(lanes) * rows * q_cols,
            transcendentals=len(lanes) * rows * len(slots) * chunks * rows * QUERY_GROUP,
        ),
        name="attend",
    )(table, *queries, *arrays, *held)


def deliver_kernel(masks, info_ref, *refs):
    pieces, (out_ref, sems) = refs[:len(masks)], refs[-2:]
    cols = pieces[0].shape[1]
    copies = []
    for at, (mask, piece) in enumerate(zip(masks, pieces)):
        where = pl.ds(pl.multiple_of((info_ref[1] ^ mask) * cols, cols), cols)
        copies.append(pltpu.make_async_copy(piece, out_ref.at[0, :, where], sems.at[at]))
        copies[-1].start()
    for copy in copies:
        copy.wait()


def deliver(info, masks, pieces, count, before=None):
    rows, cols = pieces[0].shape
    begun = () if before is None else (before,)
    return pl.pallas_call(
        functools.partial(deliver_kernel, masks),
        in_specs=[SMEM] + [VMEM] * len(pieces) + [HBM] * len(begun),
        out_specs=HBM,
        out_shape=jax.ShapeDtypeStruct((1, rows, count * cols), jnp.bfloat16),
        input_output_aliases={1 + len(pieces): 0} if begun else {},
        scratch_shapes=[pltpu.SemaphoreType.DMA((len(pieces),))],
        compiler_params=pltpu.CompilerParams(vmem_limit_bytes=4 * MIB),
        name="deliver",
    )(info, *pieces, *begun)


def local(tokens, norm_gain, w_query, key_weight, value_weight, vertical_blocks, slash_offsets):
    _, rows, width = tokens.shape
    assert lax.axis_size("doc") == 4
    place = lax.axis_index("seq")
    doc_place = lax.axis_index("doc")
    info = after(jnp.stack([place, doc_place, place * rows]).astype(jnp.int32))
    cosine, sine = rope_table(info[2:] + jnp.arange(rows, dtype=jnp.int32), HEAD_WIDTH)
    table = jnp.concatenate([cosine, cosine, -sine, sine], axis=1)
    own = after(tokens, info)[0]
    gain = norm_gain.reshape(1, width)
    long = lax.axis_size("seq") > 8 or lax.axis_size("seq") % 2 == 1
    ring = Gathered if long else Ring
    table_of = plan(info, vertical_blocks, slash_offsets, not long, rows)

    twin = swap(own, "doc", 1)
    across = swap(own, "doc", 2)
    q_near, kv_near, gain_in, wq_in, wk_in, wv_in = project_near(
        own, twin, gain, w_query, key_weight, value_weight, table
    )
    near = ring(kv_near)
    near.advance()
    near.advance(table_of)
    near.advance()

    across = after(across, *near.latest)
    crossed = swap(across, "doc", 1)
    kv_across, across_in = project_keys_values(across, gain_in, wk_in, wv_in, table)
    kv_far, crossed_in = project_keys_values(crossed, gain_in, wk_in, wv_in, table, before=kv_across)
    far = ring(kv_far)
    far.advance()
    near.advance(kv_far)
    q_far = project_queries([across_in, after(crossed_in, kv_far)], wq_in, table)
    mixed_own, mixed_twin = attend(
        table_of,
        [(0, (0, 0), 0, rows), (1, (0, rows), rows, rows)],
        [after(q_near, *far.latest)],
        near.arrays,
        near.slots,
        near.chunks,
    )
    out_twin = swap(mixed_twin, "doc", 1)
    far.advance(q_far)
    far.advance(mixed_twin)
    q_far = after(q_far, out_twin)
    remote = [(2, (0, 0), 0, rows), (3, (0, rows), rows, rows)]
    if long:
        mixed = attend(table_of, remote, [q_far], far.arrays, far.slots, far.chunks)
        home = [swap(value, "doc", 2 + at) for at, value in enumerate(mixed)]
    else:
        ends = [far.last(far.front[1][at * rows:(at + 1) * rows]) for at in range(2)]
        count = len(far.slots)
        state = attend(table_of, remote[:1], [q_far], far.arrays, far.slots, end=False)
        (mixed,) = attend(
            table_of, remote[:1], [q_far], ends[:1], [lambda index: (0, 0)], first=count, states=[state]
        )
        home = [swap(mixed, "doc", 2)]
        (mixed,) = attend(
            table_of,
            remote[1:],
            [q_far],
            [*far.arrays, ends[1]],
            [*far.slots, lambda index: (count, -rows)],
        )
        home.append(swap(mixed, "doc", 3))
    count = lax.axis_size("doc")
    result = deliver(info, (0, 1), [mixed_own, out_twin], count)
    result = deliver(info, (2,), home[:1], count, before=result)
    return deliver(info, (3,), home[1:], count, before=result)


def solution(mesh):
    return jax.shard_map(
        local,
        mesh=mesh,
        in_specs=(
            P("doc", "seq", None),
            P(),
            P(None, "doc"),
            P(None, "doc"),
            P(None, "doc"),
            P(),
            P(),
        ),
        out_specs=P("doc", "seq", None),
        check_vma=False,
    )
```

```python
import functools
import math

import jax
import jax.numpy as jnp
from jax import lax
from jax.experimental import pallas as pl
from jax.experimental.pallas import tpu as pltpu
from jax.sharding import PartitionSpec as P

HEAD_WIDTH = 128
QUERY_HEADS = 16
KEY_VALUE_HEADS = 4
QUERY_GROUP = QUERY_HEADS // KEY_VALUE_HEADS
EPSILON = 1e-05
BAND = 16
MIB = 1024 * 1024
OUT_OF_REACH = 1 << 30

SMEM = pl.BlockSpec(memory_space=pltpu.SMEM)
VMEM = pl.BlockSpec(memory_space=pltpu.VMEM)
ANYWHERE = pl.BlockSpec(memory_space=pl.ANY)
HBM = pl.BlockSpec(memory_space=pltpu.HBM)


def swap(value, axis, mask):
    count = lax.axis_size(axis)
    return lax.ppermute(value, axis, [(source, source ^ mask) for source in range(count)])


def after(value, *others):
    return lax.optimization_barrier((value,) + others)[0]


def in_hbm(array):
    return pltpu.with_memory_space_constraint(array, pltpu.HBM)


def rope_table(positions, width):
    inverse = jnp.power(jnp.float32(500000.0), -jnp.arange(0, width, 2, dtype=jnp.float32) / width)
    angles = positions.astype(jnp.float32)[:, None] * inverse[None, :]
    return (jnp.cos(angles), jnp.sin(angles))


def normalize(token_ref, gain_ref, normed_ref, first):
    def norm_band(index, carry):
        at = pl.ds(pl.multiple_of(index * BAND, BAND), BAND)
        wide = token_ref[at, :].astype(jnp.float32)
        scale = lax.rsqrt(jnp.mean(wide * wide, axis=-1, keepdims=True) + EPSILON)
        normed_ref[pl.ds(pl.multiple_of(first + index * BAND, BAND), BAND), :] = (
            wide * scale * gain_ref[...]
        ).astype(jnp.bfloat16)
        return carry

    lax.fori_loop(0, token_ref.shape[0] // BAND, norm_band, 0, unroll=2)


def rotate(value, table_ref):
    half = HEAD_WIDTH // 2
    turned = jnp.concatenate([value[:, half:], value[:, :half]], axis=1)
    return (value * table_ref[:, :HEAD_WIDTH] + turned * table_ref[:, HEAD_WIDTH:]).astype(
        jnp.bfloat16
    )


def multiply(normed_ref, weight_of):
    width = normed_ref.shape[1]
    deep = min(1024, width)
    total = None
    for start in range(0, width, deep):
        part = jnp.dot(
            normed_ref[:, start:start + deep],
            weight_of(slice(start, start + deep)),
            preferred_element_type=jnp.float32,
        )
        total = part if total is None else total + part
    return total


def write_keys_values(normed_ref, wk_ref, wv_ref, table_ref, kv_ref, ahead):
    rows = table_ref.shape[0]
    for head in range(wk_ref.shape[1] // HEAD_WIDTH):
        at = slice(head * HEAD_WIDTH, (head + 1) * HEAD_WIDTH)
        both = multiply(
            normed_ref, lambda k: jnp.concatenate([wk_ref[k, at], wv_ref[k, at]], axis=1)
        )
        out = 2 * head * HEAD_WIDTH
        for first in range(0, normed_ref.shape[0], rows):
            mine = both[first:first + rows]
            band = slice(ahead + first, ahead + first + rows)
            kv_ref[band, out:out + HEAD_WIDTH] = rotate(mine[:, :HEAD_WIDTH], table_ref)
            kv_ref[band, out + HEAD_WIDTH:out + 2 * HEAD_WIDTH] = mine[:, HEAD_WIDTH:].astype(
                jnp.bfloat16
            )


def write_queries(normed_ref, wq_ref, table_ref, q_ref, ahead):
    rows, pair = table_ref.shape[0], 2 * HEAD_WIDTH
    for start in range(0, wq_ref.shape[1], pair):
        both = multiply(normed_ref, lambda k: wq_ref[k, start:start + pair])
        for first in range(0, normed_ref.shape[0], rows):
            band = slice(ahead + first, ahead + first + rows)
            for at in (0, HEAD_WIDTH):
                q_ref[band, start + at:start + at + HEAD_WIDTH] = rotate(
                    both[first:first + rows, at:at + HEAD_WIDTH], table_ref
                )


def near_kernel(
    own_hbm, twin_ref, gain_hbm, wq_hbm, wk_hbm, wv_hbm, table_ref,
    q_ref, kv_ref, gain_ref, wq_ref, wk_ref, wv_ref, own_ref, normed_ref, sems,
):
    copies = []
    for source, target in (
        (gain_hbm, gain_ref), (own_hbm, own_ref), (wk_hbm, wk_ref), (wv_hbm, wv_ref), (wq_hbm, wq_ref)
    ):
        copies.append(pltpu.make_async_copy(source, target, sems.at[len(copies)]))
        copies[-1].start()
    copies[0].wait()
    normalize(twin_ref, gain_ref, normed_ref, own_ref.shape[0])
    copies[1].wait()
    normalize(own_ref, gain_ref, normed_ref, 0)
    copies[2].wait()
    copies[3].wait()
    write_keys_values(normed_ref, wk_ref, wv_ref, table_ref, kv_ref, 0)
    copies[4].wait()
    write_queries(normed_ref, wq_ref, table_ref, q_ref, 0)


def keys_values_kernel(before, token_ref, gain_ref, wk_ref, wv_ref, table_ref, *refs):
    kv_ref, normed_ref = refs[-2:]
    ahead = 0
    if before:
        ahead = refs[0].shape[0]
        kv_ref[:ahead, :] = refs[0][...]
    normalize(token_ref, gain_ref, normed_ref, 0)
    write_keys_values(normed_ref, wk_ref, wv_ref, table_ref, kv_ref, ahead)


def queries_kernel(pieces, wq_ref, table_ref, *refs):
    for at, normed_ref in enumerate(refs[:pieces]):
        write_queries(normed_ref, wq_ref, table_ref, refs[pieces], at * normed_ref.shape[0])


def project_call(kernel, name, operands, kinds, shapes, scratch, rows, columns):
    width = max(array.shape[0] for array in operands)
    return pl.pallas_call(
        kernel,
        in_specs=kinds,
        out_specs=[VMEM] * len(shapes),
        out_shape=[jax.ShapeDtypeStruct(shape, dtype) for shape, dtype in shapes],
        scratch_shapes=scratch,
        compiler_params=pltpu.CompilerParams(vmem_limit_bytes=20 * MIB),
        cost_estimate=pl.CostEstimate(
            flops=2 * rows * width * columns,
            bytes_accessed=2 * width * (columns + rows),
            transcendentals=0,
        ),
        name=name,
    )(*operands)


def project_near(own, twin, gain, w_query, key_weight, value_weight, table):
    rows, width = own.shape
    q_cols, k_cols = w_query.shape[1], key_weight.shape[1]
    params = (gain, w_query, key_weight, value_weight)
    shapes = [((2 * rows, q_cols), jnp.bfloat16), ((2 * rows, 2 * k_cols), jnp.bfloat16)]
    shapes += [(array.shape, array.dtype) for array in params]
    return project_call(
        near_kernel,
        "project_near",
        (in_hbm(own), twin, *(in_hbm(array) for array in params), table),
        [HBM, VMEM] + [HBM] * 4 + [VMEM],
        shapes,
        [
            pltpu.VMEM(own.shape, own.dtype),
            pltpu.VMEM((2 * rows, width), jnp.bfloat16),
            pltpu.SemaphoreType.DMA((5,)),
        ],
        2 * rows,
        q_cols + 2 * k_cols,
    )


def project_keys_values(tokens, gain, key_weight, value_weight, table, before=None):
    held = () if before is None else (before,)
    rows, cols = tokens.shape[0], 2 * key_weight.shape[1]
    total = rows + sum(array.shape[0] for array in held)
    operands = (tokens, gain, key_weight, value_weight, table, *held)
    return project_call(
        functools.partial(keys_values_kernel, len(held)),
        "project_keys_values",
        operands,
        [VMEM] * len(operands),
        [((total, cols), jnp.bfloat16), (tokens.shape, jnp.bfloat16)],
        [],
        rows,
        cols,
    )


def project_queries(normed, w_query, table):
    operands = (w_query, table, *normed)
    rows = sum(array.shape[0] for array in normed)
    (queries,) = project_call(
        functools.partial(queries_kernel, len(normed)),
        "project_queries",
        operands,
        [VMEM] * len(operands),
        [((rows, w_query.shape[1]), jnp.bfloat16)],
        [],
        rows,
        w_query.shape[1],
    )
    return queries


def ring_order(count):
    return list(range(0, count, 2)) + list(range(count - 1, 0, -2))


class Gathered:
    def __init__(self, kv):
        count = lax.axis_size("seq")
        total = kv.shape[0]
        chunk = 8 if count % 8 == 0 else 1
        self.chunks, self.latest = count // chunk, ()
        self.arrays = [lax.all_gather(kv, "seq", axis=0, tiled=True)]
        self.slots = [
            lambda index, j=j: (0, pl.multiple_of((index * chunk + j) * total, BAND))
            for j in range(chunk)
        ]

    def advance(self, *others):
        pass


class Ring:
    def __init__(self, kv):
        self.count, self.chunks, self.stage = lax.axis_size("seq"), 1, 0
        self.order = ring_order(self.count)
        self.arrays, self.slots, self.latest = [], [], ()
        self.front = {1: kv, -1: kv}
        self.hold(kv)

    @staticmethod
    def sources(at, count):
        steps = [0]
        for stage in range(1, count // 2 + 1):
            steps += [stage, -stage] if 2 * stage < count else [stage]
        return [(at - step) % count for step in steps]

    def hold(self, array):
        self.slots.append(lambda index, r=len(self.arrays): (r, 0))
        self.arrays.append(array)

    def last(self, array):
        pairs = [(s, self.order[(at + 1) % self.count]) for at, s in enumerate(self.order)]
        return lax.ppermute(array, "seq", pairs)

    def advance(self, *others):
        if self.stage >= self.count // 2:
            return
        self.stage += 1
        fresh = []
        for way in (1, -1) if 2 * self.stage < self.count else (1,):
            value = after(self.front[way], *others) if others else self.front[way]
            pairs = [
                (source, self.order[(at + way) % self.count]) for at, source in enumerate(self.order)
            ]
            self.front[way] = lax.ppermute(value, "seq", pairs)
            fresh.append(self.front[way])
            self.hold(self.front[way])
        self.latest = tuple(fresh)


def plan_kernel(ring, lanes, heads, count, rows, info_ref, vertical_ref, slash_ref, plan_ref):
    place, me = info_ref[0], info_ref[1]
    plan_ref[0] = place

    def enter(number, block):
        for lane in range(lanes):
            doc = me ^ lane
            for head in range(heads):
                group = me * heads + head
                found = (block == place) | (block == place - 1)
                for s in range(slash_ref.shape[2]):
                    found = found | (block == place - slash_ref[doc, group, s])
                for s in range(vertical_ref.shape[2]):
                    found = found | ((block == vertical_ref[doc, group, s]) & (block < place - 1))
                at = 1 + (lane * heads + head) * count + number
                plan_ref[at] = jnp.where(found & (block >= 0), block * rows, OUT_OF_REACH)

    if ring:
        order = ring_order(count)
        lists = {order[at]: [order[r] for r in Ring.sources(at, count)] for at in range(count)}
        for number in range(count):
            block = jnp.int32(0)
            for here, blocks in lists.items():
                block = jnp.where(place == here, blocks[number], block)
            enter(number, block)
    else:

        def one(number, carry):
            enter(number, number)
            return carry

        lax.fori_loop(0, count, one, 0)


def plan(info, vertical, slash, ring, rows):
    count, lanes = lax.axis_size("seq"), lax.axis_size("doc")
    heads = vertical.shape[1] // lanes
    length = 1 + lanes * heads * count
    return pl.pallas_call(
        functools.partial(plan_kernel, ring, lanes, heads, count, rows),
        in_specs=[SMEM] * 3,
        out_specs=SMEM,
        out_shape=jax.ShapeDtypeStruct((length,), jnp.int32),
        compiler_params=pltpu.CompilerParams(vmem_limit_bytes=4 * MIB),
        name="plan",
    )(info, vertical, slash)


def attend_kernel(lanes, stride, slot_at, slots, chunks, q_count, kv_count, begin, end, plan_ref, *refs):
    q_refs, kv_refs, refs = refs[:q_count], refs[q_count:q_count + kv_count], refs[q_count + kv_count:]
    state_refs = refs[:0 if begin else 3 * len(lanes)]
    out_refs = refs[len(state_refs):]
    heads = kv_refs[0].shape[1] // (2 * HEAD_WIDTH)
    place = plan_ref[0]
    factor = HEAD_WIDTH ** (-0.5) * math.log2(math.e)

    for lane, (mask, q_at, kv_first, rows) in enumerate(lanes):
        rank = QUERY_GROUP * rows
        row_at = place * rows + lax.broadcasted_iota(jnp.int32, (1, rows), 1)
        query_at = jnp.concatenate([row_at] * QUERY_GROUP, axis=1)
        key_at = lax.broadcasted_iota(jnp.int32, (rows, rank), 0)
        for head in range(heads):
            table = 1 + (mask * heads + head) * stride + slot_at
            queries = jnp.concatenate(
                [
                    q_refs[q_at[0]][
                        q_at[1]:q_at[1] + rows,
                        (head * QUERY_GROUP + h) * HEAD_WIDTH:(head * QUERY_GROUP + h + 1) * HEAD_WIDTH,
                    ]
                    for h in range(QUERY_GROUP)
                ],
                axis=0,
            )

            def step(index, carry):
                found = [slot(index) for slot in slots]

                def column(at):
                    cols = slice(at * HEAD_WIDTH, (at + 1) * HEAD_WIDTH)
                    parts = []
                    for r, first in found:
                        if isinstance(first, int):
                            where = slice(first + kv_first, first + kv_first + rows)
                        else:
                            where = pl.ds(pl.multiple_of(first + kv_first, BAND), rows)
                        parts.append(kv_refs[r][where, cols])
                    return jnp.concatenate(parts, axis=0)

                keys, values = column(2 * head), column(2 * head + 1)
                scores = lax.dot_general(
                    keys, queries, (((1,), (1,)), ((), ())), preferred_element_type=jnp.float32
                )
                parts = []
                for j in range(len(slots)):
                    shift = plan_ref[table + index * len(slots) + j]
                    parts.append(
                        jnp.where(
                            key_at <= query_at - shift,
                            scores[j * rows:(j + 1) * rows],
                            -jnp.inf,
                        )
                    )
                scores = jnp.concatenate(parts, axis=0)
                top = jnp.max(scores, axis=0, keepdims=True)
                if carry is None:
                    fresh = safe = top
                else:
                    fresh = jnp.maximum(carry[0], top)
                    safe = jnp.where(fresh == -jnp.inf, jnp.float32(0), fresh)
                raised = jnp.exp2((scores - safe) * factor)
                total = jnp.sum(raised, axis=0, keepdims=True)
                mixed = lax.dot_general(
                    values,
                    raised.astype(jnp.bfloat16),
                    (((0,), (0,)), ((), ())),
                    preferred_element_type=jnp.float32,
                )
                if carry is not None:
                    fade = jnp.exp2((carry[0] - safe) * factor)
                    total, mixed = carry[1] * fade + total, carry[2] * fade + mixed
                return fresh, total, mixed

            carry = None
            if not begin:
                carry = tuple(ref[head] for ref in state_refs[3 * lane:3 * lane + 3])
            elif chunks > 1:
                carry = (
                    jnp.full((1, rank), -jnp.inf, jnp.float32),
                    jnp.zeros((1, rank), jnp.float32),
                    jnp.zeros((HEAD_WIDTH, rank), jnp.float32),
                )
            if chunks > 1:
                carry = lax.fori_loop(0, chunks, step, carry)
            else:
                carry = step(0, carry)
            if not end:
                for ref, value in zip(out_refs[3 * lane:3 * lane + 3], carry):
                    ref[head] = value
                continue
            result = carry[2] / carry[1]
            for h in range(QUERY_GROUP):
                cols = slice(
                    (head * QUERY_GROUP + h) * HEAD_WIDTH, (head * QUERY_GROUP + h + 1) * HEAD_WIDTH
                )
                out_refs[lane][:, cols] = result[:, h * rows:(h + 1) * rows].T.astype(jnp.bfloat16)


def attend(table, lanes, queries, arrays, slots, chunks=1, first=0, states=None, end=True):
    q_cols = queries[0].shape[1]
    rows = lanes[0][3]
    held = [array for state in states for array in state] if states else []
    if end:
        shapes = [jax.ShapeDtypeStruct((rows, q_cols), jnp.bfloat16)] * len(lanes)
    else:
        heads = q_cols // (QUERY_GROUP * HEAD_WIDTH)
        shapes = [
            jax.ShapeDtypeStruct((heads, deep, QUERY_GROUP * rows), jnp.float32)
            for deep in (1, 1, HEAD_WIDTH)
        ] * len(lanes)
    kernel = functools.partial(
        attend_kernel,
        lanes,
        lax.axis_size("seq"),
        first,
        slots,
        chunks,
        len(queries),
        len(arrays),
        not states,
        end,
    )
    return pl.pallas_call(
        kernel,
        in_specs=[SMEM] + [VMEM] * (len(queries) + len(arrays) + len(held)),
        out_specs=[VMEM] * len(shapes),
        out_shape=shapes,
        compiler_params=pltpu.CompilerParams(
            vmem_limit_bytes=10 * MIB + 4 * sum(a.size for a in (*queries, *arrays))
        ),
        cost_estimate=pl.CostEstimate(
            flops=4 * len(lanes) * rows * q_cols * len(slots) * chunks * rows,
            bytes_accessed=2 * sum(a.size for a in arrays) + 4 * len(lanes) * rows * q_cols,
            transcendentals=len(lanes) * rows * len(slots) * chunks * rows * QUERY_GROUP,
        ),
        name="attend",
    )(table, *queries, *arrays, *held)


def deliver_kernel(masks, *refs):
    pieces, (out_ref, sems) = refs[:len(masks)], refs[-2:]
    rows, cols = pieces[0].shape
    me, strips = lax.axis_index("doc"), sems.shape[1]
    copies = []
    for at, (mask, piece) in enumerate(zip(masks, pieces)):
        where = pl.ds(pl.multiple_of((me ^ mask) * cols, cols), cols)
        for strip in range(strips):
            band = pl.ds(strip * (rows // strips), rows // strips)
            copies.append(
                pltpu.make_async_copy(piece.at[band], out_ref.at[0, band, where], sems.at[at, strip])
            )
            copies[-1].start()
    for copy in copies:
        copy.wait()


def deliver(masks, pieces, count, before=None):
    rows, cols = pieces[0].shape
    begun = () if before is None else (before,)
    strips = 4 if rows % (4 * BAND) == 0 else 1
    return pl.pallas_call(
        functools.partial(deliver_kernel, masks),
        in_specs=[VMEM] * len(pieces) + [HBM] * len(begun),
        out_specs=HBM,
        out_shape=jax.ShapeDtypeStruct((1, rows, count * cols), jnp.bfloat16),
        input_output_aliases={len(pieces): 0} if begun else {},
        scratch_shapes=[pltpu.SemaphoreType.DMA((len(pieces), strips))],
        compiler_params=pltpu.CompilerParams(vmem_limit_bytes=4 * MIB),
        name="deliver",
    )(*pieces, *begun)


def local(tokens, norm_gain, w_query, key_weight, value_weight, vertical_blocks, slash_offsets):
    _, rows, width = tokens.shape
    assert lax.axis_size("doc") == 4
    place = lax.axis_index("seq")
    doc_place = lax.axis_index("doc")
    info = after(jnp.stack([place, doc_place, place * rows]).astype(jnp.int32))
    cosine, sine = rope_table(info[2:] + jnp.arange(rows, dtype=jnp.int32), HEAD_WIDTH)
    table = jnp.concatenate([cosine, cosine, -sine, sine], axis=1)
    own = after(tokens, info)[0]
    gain = norm_gain.reshape(1, width)
    long = lax.axis_size("seq") > 8 or lax.axis_size("seq") % 2 == 1
    ring = Gathered if long else Ring
    table_of = plan(info, vertical_blocks, slash_offsets, not long, rows)

    twin = swap(own, "doc", 1)
    across = swap(tokens[0], "doc", 2)
    q_near, kv_near, gain_in, wq_in, wk_in, wv_in = project_near(
        own, twin, gain, w_query, key_weight, value_weight, table
    )
    near = ring(kv_near)
    near.advance()
    near.advance(table_of)
    near.advance()

    across = after(across, *near.latest)
    near.advance()
    crossed = swap(across, "doc", 1)
    kv_across, across_in = project_keys_values(across, gain_in, wk_in, wv_in, table)
    kv_far, crossed_in = project_keys_values(crossed, gain_in, wk_in, wv_in, table, before=kv_across)
    far = ring(kv_far)
    far.advance()
    q_far = project_queries([across_in, after(crossed_in, kv_far, *near.latest)], wq_in, table)
    mixed_own, mixed_twin = attend(
        table_of,
        [(0, (0, 0), 0, rows), (1, (0, rows), rows, rows)],
        [after(q_near, *far.latest)],
        near.arrays,
        near.slots,
        near.chunks,
    )
    out_twin = swap(mixed_twin, "doc", 1)
    far.advance(q_far)
    far.advance(mixed_twin)
    q_far = after(q_far, out_twin)
    remote = [(2, (0, 0), 0, rows), (3, (0, rows), rows, rows)]
    if long:
        mixed = attend(table_of, remote, [q_far], far.arrays, far.slots, far.chunks)
        home = [swap(value, "doc", 2 + at) for at, value in enumerate(mixed)]
    else:
        ends = [far.last(far.front[1][at * rows:(at + 1) * rows]) for at in range(2)]
        count = len(far.slots)
        state = attend(table_of, remote[:1], [q_far], far.arrays, far.slots, end=False)
        (mixed,) = attend(
            table_of, remote[:1], [q_far], ends[:1], [lambda index: (0, 0)], first=count, states=[state]
        )
        home = [swap(mixed, "doc", 2)]
        (mixed,) = attend(
            table_of,
            remote[1:],
            [q_far],
            [*far.arrays, ends[1]],
            [*far.slots, lambda index: (count, -rows)],
        )
        home.append(swap(mixed, "doc", 3))
    count = lax.axis_size("doc")
    result = deliver((0, 1), [mixed_own, out_twin], count)
    result = deliver((2,), home[:1], count, before=result)
    return deliver((3,), home[1:], count, before=result)


def solution(mesh):
    return jax.shard_map(
        local,
        mesh=mesh,
        in_specs=(
            P("doc", "seq", None),
            P(),
            P(None, "doc"),
            P(None, "doc"),
            P(None, "doc"),
            P(),
            P(),
        ),
        out_specs=P("doc", "seq", None),
        check_vma=False,
    )
```

```python
import functools
import math

import jax
import jax.numpy as jnp
from jax import lax
from jax.experimental import pallas as pl
from jax.experimental.pallas import tpu as pltpu
from jax.sharding import PartitionSpec as P

HEAD_WIDTH = 128
QUERY_HEADS = 16
KEY_VALUE_HEADS = 4
QUERY_GROUP = QUERY_HEADS // KEY_VALUE_HEADS
EPSILON = 1e-05
BAND = 16
MIB = 1024 * 1024
OUT_OF_REACH = 1 << 30

SMEM = pl.BlockSpec(memory_space=pltpu.SMEM)
VMEM = pl.BlockSpec(memory_space=pltpu.VMEM)
ANYWHERE = pl.BlockSpec(memory_space=pl.ANY)
HBM = pl.BlockSpec(memory_space=pltpu.HBM)


def swap(value, axis, mask):
    count = lax.axis_size(axis)
    return lax.ppermute(value, axis, [(source, source ^ mask) for source in range(count)])


def after(value, *others):
    return lax.optimization_barrier((value,) + others)[0]


def in_hbm(array):
    return pltpu.with_memory_space_constraint(array, pltpu.HBM)


def rope_table(positions, width):
    inverse = jnp.power(jnp.float32(500000.0), -jnp.arange(0, width, 2, dtype=jnp.float32) / width)
    angles = positions.astype(jnp.float32)[:, None] * inverse[None, :]
    return (jnp.cos(angles), jnp.sin(angles))


def normalize(token_ref, gain_ref, normed_ref, first):
    def norm_band(index, carry):
        at = pl.ds(pl.multiple_of(index * BAND, BAND), BAND)
        wide = token_ref[at, :].astype(jnp.float32)
        scale = lax.rsqrt(jnp.mean(wide * wide, axis=-1, keepdims=True) + EPSILON)
        normed_ref[pl.ds(pl.multiple_of(first + index * BAND, BAND), BAND), :] = (
            wide * scale * gain_ref[...]
        ).astype(jnp.bfloat16)
        return carry

    lax.fori_loop(0, token_ref.shape[0] // BAND, norm_band, 0, unroll=4)


def rotate(value, table_ref):
    half = HEAD_WIDTH // 2
    turned = jnp.concatenate([value[:, half:], value[:, :half]], axis=1)
    return (value * table_ref[:, :HEAD_WIDTH] + turned * table_ref[:, HEAD_WIDTH:]).astype(
        jnp.bfloat16
    )


def multiply(normed_ref, weight_of):
    width = normed_ref.shape[1]
    deep = min(1024, width)
    total = None
    for start in range(0, width, deep):
        part = jnp.dot(
            normed_ref[:, start:start + deep],
            weight_of(slice(start, start + deep)),
            preferred_element_type=jnp.float32,
        )
        total = part if total is None else total + part
    return total


def write_keys_values(normed_ref, wk_ref, wv_ref, table_ref, kv_ref, ahead):
    rows = table_ref.shape[0]
    for head in range(wk_ref.shape[1] // HEAD_WIDTH):
        at = slice(head * HEAD_WIDTH, (head + 1) * HEAD_WIDTH)
        both = multiply(
            normed_ref, lambda k: jnp.concatenate([wk_ref[k, at], wv_ref[k, at]], axis=1)
        )
        out = 2 * head * HEAD_WIDTH
        for first in range(0, normed_ref.shape[0], rows):
            mine = both[first:first + rows]
            band = slice(ahead + first, ahead + first + rows)
            kv_ref[band, out:out + HEAD_WIDTH] = rotate(mine[:, :HEAD_WIDTH], table_ref)
            kv_ref[band, out + HEAD_WIDTH:out + 2 * HEAD_WIDTH] = mine[:, HEAD_WIDTH:].astype(
                jnp.bfloat16
            )


def write_queries(normed_ref, wq_ref, table_ref, q_ref, ahead):
    rows, pair = table_ref.shape[0], 2 * HEAD_WIDTH
    for start in range(0, wq_ref.shape[1], pair):
        both = multiply(normed_ref, lambda k: wq_ref[k, start:start + pair])
        for first in range(0, normed_ref.shape[0], rows):
            band = slice(ahead + first, ahead + first + rows)
            for at in (0, HEAD_WIDTH):
                q_ref[band, start + at:start + at + HEAD_WIDTH] = rotate(
                    both[first:first + rows, at:at + HEAD_WIDTH], table_ref
                )


def near_kernel(
    own_hbm, twin_ref, gain_hbm, wq_hbm, wk_hbm, wv_hbm, table_ref,
    q_ref, kv_ref, gain_ref, wq_ref, wk_ref, wv_ref, own_ref, normed_ref, sems,
):
    copies = []
    for source, target in (
        (gain_hbm, gain_ref), (own_hbm, own_ref), (wk_hbm, wk_ref), (wv_hbm, wv_ref), (wq_hbm, wq_ref)
    ):
        copies.append(pltpu.make_async_copy(source, target, sems.at[len(copies)]))
        copies[-1].start()
    copies[0].wait()
    normalize(twin_ref, gain_ref, normed_ref, own_ref.shape[0])
    copies[1].wait()
    normalize(own_ref, gain_ref, normed_ref, 0)
    copies[2].wait()
    copies[3].wait()
    write_keys_values(normed_ref, wk_ref, wv_ref, table_ref, kv_ref, 0)
    copies[4].wait()
    write_queries(normed_ref, wq_ref, table_ref, q_ref, 0)


def keys_values_kernel(before, token_ref, gain_ref, wk_ref, wv_ref, table_ref, *refs):
    kv_ref, normed_ref = refs[-2:]
    ahead = 0
    if before:
        ahead = refs[0].shape[0]
        kv_ref[:ahead, :] = refs[0][...]
    normalize(token_ref, gain_ref, normed_ref, 0)
    write_keys_values(normed_ref, wk_ref, wv_ref, table_ref, kv_ref, ahead)


def queries_kernel(pieces, wq_ref, table_ref, *refs):
    for at, normed_ref in enumerate(refs[:pieces]):
        write_queries(normed_ref, wq_ref, table_ref, refs[pieces], at * normed_ref.shape[0])


def project_call(kernel, name, operands, kinds, shapes, scratch, rows, columns):
    width = max(array.shape[0] for array in operands)
    return pl.pallas_call(
        kernel,
        in_specs=kinds,
        out_specs=[VMEM] * len(shapes),
        out_shape=[jax.ShapeDtypeStruct(shape, dtype) for shape, dtype in shapes],
        scratch_shapes=scratch,
        compiler_params=pltpu.CompilerParams(vmem_limit_bytes=20 * MIB),
        cost_estimate=pl.CostEstimate(
            flops=2 * rows * width * columns,
            bytes_accessed=2 * width * (columns + rows),
            transcendentals=0,
        ),
        name=name,
    )(*operands)


def project_near(own, twin, gain, w_query, key_weight, value_weight, table):
    rows, width = own.shape
    q_cols, k_cols = w_query.shape[1], key_weight.shape[1]
    params = (gain, w_query, key_weight, value_weight)
    shapes = [((2 * rows, q_cols), jnp.bfloat16), ((2 * rows, 2 * k_cols), jnp.bfloat16)]
    shapes += [(array.shape, array.dtype) for array in params]
    return project_call(
        near_kernel,
        "project_near",
        (in_hbm(own), twin, *(in_hbm(array) for array in params), table),
        [HBM, VMEM] + [HBM] * 4 + [VMEM],
        shapes,
        [
            pltpu.VMEM(own.shape, own.dtype),
            pltpu.VMEM((2 * rows, width), jnp.bfloat16),
            pltpu.SemaphoreType.DMA((5,)),
        ],
        2 * rows,
        q_cols + 2 * k_cols,
    )


def project_keys_values(tokens, gain, key_weight, value_weight, table, before=None):
    held = () if before is None else (before,)
    rows, cols = tokens.shape[0], 2 * key_weight.shape[1]
    total = rows + sum(array.shape[0] for array in held)
    operands = (tokens, gain, key_weight, value_weight, table, *held)
    return project_call(
        functools.partial(keys_values_kernel, len(held)),
        "project_keys_values",
        operands,
        [VMEM] * len(operands),
        [((total, cols), jnp.bfloat16), (tokens.shape, jnp.bfloat16)],
        [],
        rows,
        cols,
    )


def project_queries(normed, w_query, table):
    operands = (w_query, table, *normed)
    rows = sum(array.shape[0] for array in normed)
    (queries,) = project_call(
        functools.partial(queries_kernel, len(normed)),
        "project_queries",
        operands,
        [VMEM] * len(operands),
        [((rows, w_query.shape[1]), jnp.bfloat16)],
        [],
        rows,
        w_query.shape[1],
    )
    return queries


def ring_order(count):
    return list(range(0, count, 2)) + list(range(count - 1, 0, -2))


class Gathered:
    def __init__(self, kv):
        count = lax.axis_size("seq")
        total = kv.shape[0]
        chunk = 8 if count % 8 == 0 else 1
        self.chunks, self.latest = count // chunk, ()
        self.arrays = [lax.all_gather(kv, "seq", axis=0, tiled=True)]
        self.slots = [
            lambda index, j=j: (0, pl.multiple_of((index * chunk + j) * total, BAND))
            for j in range(chunk)
        ]

    def advance(self, *others):
        pass


class Ring:
    def __init__(self, kv):
        self.count, self.chunks, self.stage = lax.axis_size("seq"), 1, 0
        self.order = ring_order(self.count)
        self.arrays, self.slots, self.latest = [], [], ()
        self.front = {1: kv, -1: kv}
        self.hold(kv)

    @staticmethod
    def sources(at, count):
        steps = [0]
        for stage in range(1, count // 2 + 1):
            steps += [stage, -stage] if 2 * stage < count else [stage]
        return [(at - step) % count for step in steps]

    def hold(self, array):
        self.slots.append(lambda index, r=len(self.arrays): (r, 0))
        self.arrays.append(array)

    def last(self, array):
        pairs = [(s, self.order[(at + 1) % self.count]) for at, s in enumerate(self.order)]
        return lax.ppermute(array, "seq", pairs)

    def advance(self, *others):
        if self.stage >= self.count // 2:
            return
        self.stage += 1
        fresh = []
        for way in (1, -1) if 2 * self.stage < self.count else (1,):
            value = after(self.front[way], *others) if others else self.front[way]
            pairs = [
                (source, self.order[(at + way) % self.count]) for at, source in enumerate(self.order)
            ]
            self.front[way] = lax.ppermute(value, "seq", pairs)
            fresh.append(self.front[way])
            self.hold(self.front[way])
        self.latest = tuple(fresh)


def plan_kernel(ring, lanes, heads, count, rows, info_ref, vertical_ref, slash_ref, plan_ref):
    place, me = info_ref[0], info_ref[1]
    row_at = lax.broadcasted_iota(jnp.int32, (1, rows), 1)
    query_at = place * rows + jnp.concatenate([row_at] * QUERY_GROUP, axis=1)

    def enter(number, block):
        for lane in range(lanes):
            doc = me ^ lane
            for head in range(heads):
                group = me * heads + head
                found = (block == place) | (block == place - 1)
                for s in range(slash_ref.shape[2]):
                    found = found | (block == place - slash_ref[doc, group, s])
                for s in range(vertical_ref.shape[2]):
                    found = found | ((block == vertical_ref[doc, group, s]) & (block < place - 1))
                shift = jnp.where(found & (block >= 0), block * rows, OUT_OF_REACH)
                plan_ref[pl.ds((lane * heads + head) * count + number, 1), :] = query_at - shift

    if ring:
        order = ring_order(count)
        lists = {order[at]: [order[r] for r in Ring.sources(at, count)] for at in range(count)}
        for number in range(count):
            block = jnp.int32(0)
            for here, blocks in lists.items():
                block = jnp.where(place == here, blocks[number], block)
            enter(number, block)
    else:

        def one(number, carry):
            enter(number, number)
            return carry

        lax.fori_loop(0, count, one, 0)


def plan(info, vertical, slash, ring, rows):
    count, lanes = lax.axis_size("seq"), lax.axis_size("doc")
    heads = vertical.shape[1] // lanes
    return pl.pallas_call(
        functools.partial(plan_kernel, ring, lanes, heads, count, rows),
        in_specs=[SMEM] * 3,
        out_specs=VMEM,
        out_shape=jax.ShapeDtypeStruct((lanes * heads * count, QUERY_GROUP * rows), jnp.int32),
        compiler_params=pltpu.CompilerParams(vmem_limit_bytes=4 * MIB),
        name="plan",
    )(info, vertical, slash)


def attend_kernel(lanes, stride, slot_at, slots, chunks, q_count, kv_count, begin, end, plan_ref, *refs):
    q_refs, kv_refs, refs = refs[:q_count], refs[q_count:q_count + kv_count], refs[q_count + kv_count:]
    state_refs = refs[:0 if begin else 3 * len(lanes)]
    out_refs = refs[len(state_refs):]
    heads = kv_refs[0].shape[1] // (2 * HEAD_WIDTH)
    factor = HEAD_WIDTH ** (-0.5) * math.log2(math.e)

    for lane, (mask, q_at, kv_first, rows) in enumerate(lanes):
        rank = QUERY_GROUP * rows
        key_at = lax.broadcasted_iota(jnp.int32, (rows, rank), 0)
        for head in range(heads):
            table = (mask * heads + head) * stride + slot_at
            queries = jnp.concatenate(
                [
                    q_refs[q_at[0]][
                        q_at[1]:q_at[1] + rows,
                        (head * QUERY_GROUP + h) * HEAD_WIDTH:(head * QUERY_GROUP + h + 1) * HEAD_WIDTH,
                    ]
                    for h in range(QUERY_GROUP)
                ],
                axis=0,
            )

            def step(index, carry):
                found = [slot(index) for slot in slots]

                def column(at):
                    cols = slice(at * HEAD_WIDTH, (at + 1) * HEAD_WIDTH)
                    parts = []
                    for r, first in found:
                        if isinstance(first, int):
                            where = slice(first + kv_first, first + kv_first + rows)
                        else:
                            where = pl.ds(pl.multiple_of(first + kv_first, BAND), rows)
                        parts.append(kv_refs[r][where, cols])
                    return jnp.concatenate(parts, axis=0)

                keys, values = column(2 * head), column(2 * head + 1)
                scores = lax.dot_general(
                    keys, queries, (((1,), (1,)), ((), ())), preferred_element_type=jnp.float32
                )
                parts = []
                for j in range(len(slots)):
                    limit = plan_ref[pl.ds(table + index * len(slots) + j, 1), :]
                    parts.append(
                        jnp.where(
                            key_at <= limit,
                            scores[j * rows:(j + 1) * rows],
                            -jnp.inf,
                        )
                    )
                scores = jnp.concatenate(parts, axis=0)
                top = jnp.max(scores, axis=0, keepdims=True)
                if carry is None:
                    fresh = safe = top
                else:
                    fresh = jnp.maximum(carry[0], top)
                    safe = jnp.where(fresh == -jnp.inf, jnp.float32(0), fresh)
                raised = jnp.exp2((scores - safe) * factor)
                total = jnp.sum(raised, axis=0, keepdims=True)
                mixed = lax.dot_general(
                    values,
                    raised.astype(jnp.bfloat16),
                    (((0,), (0,)), ((), ())),
                    preferred_element_type=jnp.float32,
                )
                if carry is not None:
                    fade = jnp.exp2((carry[0] - safe) * factor)
                    total, mixed = carry[1] * fade + total, carry[2] * fade + mixed
                return fresh, total, mixed

            carry = None
            if not begin:
                carry = tuple(ref[head] for ref in state_refs[3 * lane:3 * lane + 3])
            elif chunks > 1:
                carry = (
                    jnp.full((1, rank), -jnp.inf, jnp.float32),
                    jnp.zeros((1, rank), jnp.float32),
                    jnp.zeros((HEAD_WIDTH, rank), jnp.float32),
                )
            if chunks > 1:
                carry = lax.fori_loop(0, chunks, step, carry)
            else:
                carry = step(0, carry)
            if not end:
                for ref, value in zip(out_refs[3 * lane:3 * lane + 3], carry):
                    ref[head] = value
                continue
            result = carry[2] / carry[1]
            for h in range(QUERY_GROUP):
                cols = slice(
                    (head * QUERY_GROUP + h) * HEAD_WIDTH, (head * QUERY_GROUP + h + 1) * HEAD_WIDTH
                )
                out_refs[lane][:, cols] = result[:, h * rows:(h + 1) * rows].T.astype(jnp.bfloat16)


def attend(table, lanes, queries, arrays, slots, chunks=1, first=0, states=None, end=True):
    q_cols = queries[0].shape[1]
    rows = lanes[0][3]
    held = [array for state in states for array in state] if states else []
    if end:
        shapes = [jax.ShapeDtypeStruct((rows, q_cols), jnp.bfloat16)] * len(lanes)
    else:
        heads = q_cols // (QUERY_GROUP * HEAD_WIDTH)
        shapes = [
            jax.ShapeDtypeStruct((heads, deep, QUERY_GROUP * rows), jnp.float32)
            for deep in (1, 1, HEAD_WIDTH)
        ] * len(lanes)
    kernel = functools.partial(
        attend_kernel,
        lanes,
        lax.axis_size("seq"),
        first,
        slots,
        chunks,
        len(queries),
        len(arrays),
        not states,
        end,
    )
    return pl.pallas_call(
        kernel,
        in_specs=[VMEM] * (1 + len(queries) + len(arrays) + len(held)),
        out_specs=[VMEM] * len(shapes),
        out_shape=shapes,
        compiler_params=pltpu.CompilerParams(
            vmem_limit_bytes=10 * MIB + 4 * sum(a.size for a in (*queries, *arrays))
        ),
        cost_estimate=pl.CostEstimate(
            flops=4 * len(lanes) * rows * q_cols * len(slots) * chunks * rows,
            bytes_accessed=2 * sum(a.size for a in arrays) + 4 * len(lanes) * rows * q_cols,
            transcendentals=len(lanes) * rows * len(slots) * chunks * rows * QUERY_GROUP,
        ),
        name="attend",
    )(table, *queries, *arrays, *held)


def deliver_kernel(masks, *refs):
    pieces, (out_ref, sems) = refs[:len(masks)], refs[-2:]
    rows, cols = pieces[0].shape
    me, strips = lax.axis_index("doc"), sems.shape[1]
    copies = []
    for at, (mask, piece) in enumerate(zip(masks, pieces)):
        where = pl.ds(pl.multiple_of((me ^ mask) * cols, cols), cols)
        for strip in range(strips):
            band = pl.ds(strip * (rows // strips), rows // strips)
            copies.append(
                pltpu.make_async_copy(piece.at[band], out_ref.at[0, band, where], sems.at[at, strip])
            )
            copies[-1].start()
    for copy in copies:
        copy.wait()


def deliver(masks, pieces, count, before=None):
    rows, cols = pieces[0].shape
    begun = () if before is None else (before,)
    strips = 4 if rows % (4 * BAND) == 0 else 1
    return pl.pallas_call(
        functools.partial(deliver_kernel, masks),
        in_specs=[VMEM] * len(pieces) + [HBM] * len(begun),
        out_specs=HBM,
        out_shape=jax.ShapeDtypeStruct((1, rows, count * cols), jnp.bfloat16),
        input_output_aliases={len(pieces): 0} if begun else {},
        scratch_shapes=[pltpu.SemaphoreType.DMA((len(pieces), strips))],
        compiler_params=pltpu.CompilerParams(vmem_limit_bytes=4 * MIB),
        name="deliver",
    )(*pieces, *begun)


def local(tokens, norm_gain, w_query, key_weight, value_weight, vertical_blocks, slash_offsets):
    _, rows, width = tokens.shape
    assert lax.axis_size("doc") == 4
    place = lax.axis_index("seq")
    doc_place = lax.axis_index("doc")
    info = after(jnp.stack([place, doc_place, place * rows]).astype(jnp.int32))
    cosine, sine = rope_table(info[2:] + jnp.arange(rows, dtype=jnp.int32), HEAD_WIDTH)
    table = jnp.concatenate([cosine, cosine, -sine, sine], axis=1)
    own = after(tokens, info)[0]
    gain = norm_gain.reshape(1, width)
    long = lax.axis_size("seq") > 8 or lax.axis_size("seq") % 2 == 1
    ring = Gathered if long else Ring
    table_of = plan(info, vertical_blocks, slash_offsets, not long, rows)

    twin = swap(own, "doc", 1)
    across = swap(tokens[0], "doc", 2)
    q_near, kv_near, gain_in, wq_in, wk_in, wv_in = project_near(
        own, twin, gain, w_query, key_weight, value_weight, table
    )
    near = ring(kv_near)
    near.advance()
    near.advance(table_of)
    near.advance()

    across = after(across, *near.latest)
    near.advance()
    crossed = swap(across, "doc", 1)
    kv_across, across_in = project_keys_values(across, gain_in, wk_in, wv_in, table)
    kv_far, crossed_in = project_keys_values(crossed, gain_in, wk_in, wv_in, table, before=kv_across)
    far = ring(kv_far)
    far.advance()
    q_far = project_queries([across_in, after(crossed_in, kv_far, *near.latest)], wq_in, table)
    mixed_own, mixed_twin = attend(
        table_of,
        [(0, (0, 0), 0, rows), (1, (0, rows), rows, rows)],
        [after(q_near, *far.latest)],
        near.arrays,
        near.slots,
        near.chunks,
    )
    far.advance(q_far)
    far.advance(mixed_twin)
    out_twin = swap(after(mixed_twin, *far.latest), "doc", 1)
    remote = [(2, (0, 0), 0, rows), (3, (0, rows), rows, rows)]
    if long:
        mixed = attend(table_of, remote, [q_far], far.arrays, far.slots, far.chunks)
        home = [swap(value, "doc", 2 + at) for at, value in enumerate(mixed)]
    else:
        ends = [far.last(far.front[1][at * rows:(at + 1) * rows]) for at in range(2)]
        count = len(far.slots)
        state = attend(table_of, remote[:1], [q_far], far.arrays, far.slots, end=False)
        (mixed,) = attend(
            table_of, remote[:1], [q_far], ends[:1], [lambda index: (0, 0)], first=count, states=[state]
        )
        home = [swap(mixed, "doc", 2)]
        mixed = attend(
            table_of,
            remote[1:],
            [q_far],
            [*far.arrays, ends[1]],
            [*far.slots, lambda index: (count, -rows)],
        )
        home.append(swap(mixed[0], "doc", 3))
    count = lax.axis_size("doc")
    result = deliver((0, 1), [mixed_own, out_twin], count)
    result = deliver((2,), home[:1], count, before=result)
    return deliver((3,), home[1:], count, before=result)


def solution(mesh):
    return jax.shard_map(
        local,
        mesh=mesh,
        in_specs=(
            P("doc", "seq", None),
            P(),
            P(None, "doc"),
            P(None, "doc"),
            P(None, "doc"),
            P(),
            P(),
        ),
        out_specs=P("doc", "seq", None),
        check_vma=False,
    )
```

```python
import functools
import math

import jax
import jax.numpy as jnp
from jax import lax
from jax.experimental import pallas as pl
from jax.experimental.pallas import tpu as pltpu
from jax.sharding import PartitionSpec as P

HEAD_WIDTH = 128
QUERY_HEADS = 16
KEY_VALUE_HEADS = 4
QUERY_GROUP = QUERY_HEADS // KEY_VALUE_HEADS
EPSILON = 1e-05
BAND = 16
MIB = 1024 * 1024
OUT_OF_REACH = 1 << 30

SMEM = pl.BlockSpec(memory_space=pltpu.SMEM)
VMEM = pl.BlockSpec(memory_space=pltpu.VMEM)
ANYWHERE = pl.BlockSpec(memory_space=pl.ANY)
HBM = pl.BlockSpec(memory_space=pltpu.HBM)


def swap(value, axis, mask):
    count = lax.axis_size(axis)
    return lax.ppermute(value, axis, [(source, source ^ mask) for source in range(count)])


def after(value, *others):
    return lax.optimization_barrier((value,) + others)[0]


def in_hbm(array):
    return pltpu.with_memory_space_constraint(array, pltpu.HBM)


def rope_table(positions, width):
    inverse = jnp.power(jnp.float32(500000.0), -jnp.arange(0, width, 2, dtype=jnp.float32) / width)
    angles = positions.astype(jnp.float32)[:, None] * inverse[None, :]
    return (jnp.cos(angles), jnp.sin(angles))


def normalize(token_ref, gain_ref, normed_ref, first):
    def norm_band(index, carry):
        at = pl.ds(pl.multiple_of(index * BAND, BAND), BAND)
        wide = token_ref[at, :].astype(jnp.float32)
        scale = lax.rsqrt(jnp.mean(wide * wide, axis=-1, keepdims=True) + EPSILON)
        normed_ref[pl.ds(pl.multiple_of(first + index * BAND, BAND), BAND), :] = (
            wide * scale * gain_ref[...]
        ).astype(jnp.bfloat16)
        return carry

    lax.fori_loop(0, token_ref.shape[0] // BAND, norm_band, 0, unroll=4)


def rotate(value, table_ref):
    half = HEAD_WIDTH // 2
    turned = jnp.concatenate([value[:, half:], value[:, :half]], axis=1)
    return (value * table_ref[:, :HEAD_WIDTH] + turned * table_ref[:, HEAD_WIDTH:]).astype(
        jnp.bfloat16
    )


def multiply(normed_ref, weight_of):
    width = normed_ref.shape[1]
    deep = min(1024, width)
    total = None
    for start in range(0, width, deep):
        part = jnp.dot(
            normed_ref[:, start:start + deep],
            weight_of(slice(start, start + deep)),
            preferred_element_type=jnp.float32,
        )
        total = part if total is None else total + part
    return total


def write_keys_values(normed_ref, wk_ref, wv_ref, table_ref, kv_ref):
    rows = table_ref.shape[0]
    for head in range(wk_ref.shape[1] // HEAD_WIDTH):
        at = slice(head * HEAD_WIDTH, (head + 1) * HEAD_WIDTH)
        both = multiply(
            normed_ref, lambda k: jnp.concatenate([wk_ref[k, at], wv_ref[k, at]], axis=1)
        )
        out = 2 * head * HEAD_WIDTH
        for first in range(0, normed_ref.shape[0], rows):
            mine = both[first:first + rows]
            band = slice(first, first + rows)
            kv_ref[band, out:out + HEAD_WIDTH] = rotate(mine[:, :HEAD_WIDTH], table_ref)
            kv_ref[band, out + HEAD_WIDTH:out + 2 * HEAD_WIDTH] = mine[:, HEAD_WIDTH:].astype(
                jnp.bfloat16
            )


def write_queries(normed_ref, wq_ref, table_ref, q_ref):
    rows, pair = table_ref.shape[0], 2 * HEAD_WIDTH
    for start in range(0, wq_ref.shape[1], pair):
        both = multiply(normed_ref, lambda k: wq_ref[k, start:start + pair])
        for first in range(0, normed_ref.shape[0], rows):
            band = slice(first, first + rows)
            for at in (0, HEAD_WIDTH):
                q_ref[band, start + at:start + at + HEAD_WIDTH] = rotate(
                    both[first:first + rows, at:at + HEAD_WIDTH], table_ref
                )


def near_kernel(
    own_hbm, twin_ref, gain_hbm, wq_hbm, wk_hbm, wv_hbm, table_ref,
    q_ref, kv_ref, gain_ref, wq_ref, wk_ref, wv_ref, own_ref, normed_ref, sems,
):
    copies = []
    for source, target in (
        (gain_hbm, gain_ref), (own_hbm, own_ref), (wk_hbm, wk_ref), (wv_hbm, wv_ref), (wq_hbm, wq_ref)
    ):
        copies.append(pltpu.make_async_copy(source, target, sems.at[len(copies)]))
        copies[-1].start()
    copies[0].wait()
    normalize(twin_ref, gain_ref, normed_ref, own_ref.shape[0])
    copies[1].wait()
    normalize(own_ref, gain_ref, normed_ref, 0)
    copies[2].wait()
    copies[3].wait()
    write_keys_values(normed_ref, wk_ref, wv_ref, table_ref, kv_ref)
    copies[4].wait()
    write_queries(normed_ref, wq_ref, table_ref, q_ref)


def keys_values_kernel(token_ref, gain_ref, wk_ref, wv_ref, table_ref, kv_ref, normed_ref):
    normalize(token_ref, gain_ref, normed_ref, 0)
    write_keys_values(normed_ref, wk_ref, wv_ref, table_ref, kv_ref)


def queries_kernel(pieces, wq_ref, table_ref, *refs):
    for normed_ref, q_ref in zip(refs[:pieces], refs[pieces:]):
        write_queries(normed_ref, wq_ref, table_ref, q_ref)


def project_call(kernel, name, operands, kinds, shapes, scratch, rows, columns):
    width = max(array.shape[0] for array in operands)
    return pl.pallas_call(
        kernel,
        in_specs=kinds,
        out_specs=[VMEM] * len(shapes),
        out_shape=[jax.ShapeDtypeStruct(shape, dtype) for shape, dtype in shapes],
        scratch_shapes=scratch,
        compiler_params=pltpu.CompilerParams(vmem_limit_bytes=20 * MIB),
        cost_estimate=pl.CostEstimate(
            flops=2 * rows * width * columns,
            bytes_accessed=2 * width * (columns + rows),
            transcendentals=0,
        ),
        name=name,
    )(*operands)


def project_near(own, twin, gain, w_query, key_weight, value_weight, table):
    rows, width = own.shape
    q_cols, k_cols = w_query.shape[1], key_weight.shape[1]
    params = (gain, w_query, key_weight, value_weight)
    shapes = [((2 * rows, q_cols), jnp.bfloat16), ((2 * rows, 2 * k_cols), jnp.bfloat16)]
    shapes += [(array.shape, array.dtype) for array in params]
    return project_call(
        near_kernel,
        "project_near",
        (in_hbm(own), twin, *(in_hbm(array) for array in params), table),
        [HBM, VMEM] + [HBM] * 4 + [VMEM],
        shapes,
        [
            pltpu.VMEM(own.shape, own.dtype),
            pltpu.VMEM((2 * rows, width), jnp.bfloat16),
            pltpu.SemaphoreType.DMA((5,)),
        ],
        2 * rows,
        q_cols + 2 * k_cols,
    )


def project_keys_values(tokens, gain, key_weight, value_weight, table):
    rows, cols = tokens.shape[0], 2 * key_weight.shape[1]
    operands = (tokens, gain, key_weight, value_weight, table)
    return project_call(
        keys_values_kernel,
        "project_keys_values",
        operands,
        [VMEM] * len(operands),
        [((rows, cols), jnp.bfloat16), (tokens.shape, jnp.bfloat16)],
        [],
        rows,
        cols,
    )


def project_queries(normed, w_query, table):
    operands = (w_query, table, *normed)
    q_cols = w_query.shape[1]
    return project_call(
        functools.partial(queries_kernel, len(normed)),
        "project_queries",
        operands,
        [VMEM] * len(operands),
        [((array.shape[0], q_cols), jnp.bfloat16) for array in normed],
        [],
        sum(array.shape[0] for array in normed),
        q_cols,
    )


def ring_order(count):
    return list(range(0, count, 2)) + list(range(count - 1, 0, -2))


class Gathered:
    def __init__(self, kv):
        count = lax.axis_size("seq")
        total = kv.shape[0]
        chunk = 8 if count % 8 == 0 else 1
        self.chunks, self.latest = count // chunk, ()
        self.arrays = [lax.all_gather(kv, "seq", axis=0, tiled=True)]
        self.slots = [
            lambda index, j=j: (0, pl.multiple_of((index * chunk + j) * total, BAND))
            for j in range(chunk)
        ]

    def advance(self, *others):
        pass


class Ring:
    def __init__(self, kv):
        self.count, self.chunks, self.stage = lax.axis_size("seq"), 1, 0
        self.order = ring_order(self.count)
        self.arrays, self.slots, self.latest = [], [], ()
        self.front = {1: kv, -1: kv}
        self.hold(kv)

    @staticmethod
    def sources(at, count):
        steps = [0]
        for stage in range(1, count // 2 + 1):
            steps += [stage, -stage] if 2 * stage < count else [stage]
        return [(at - step) % count for step in steps]

    def hold(self, array):
        self.slots.append(lambda index, r=len(self.arrays): (r, 0))
        self.arrays.append(array)

    def advance(self, *others):
        if self.stage >= self.count // 2:
            return
        self.stage += 1
        fresh = []
        for way in (1, -1) if 2 * self.stage < self.count else (1,):
            value = after(self.front[way], *others) if others else self.front[way]
            pairs = [
                (source, self.order[(at + way) % self.count]) for at, source in enumerate(self.order)
            ]
            self.front[way] = lax.ppermute(value, "seq", pairs)
            fresh.append(self.front[way])
            self.hold(self.front[way])
        self.latest = tuple(fresh)


def plan_kernel(ring, lanes, heads, count, rows, info_ref, vertical_ref, slash_ref, plan_ref):
    place, me = info_ref[0], info_ref[1]
    row_at = lax.broadcasted_iota(jnp.int32, (1, rows), 1)
    query_at = place * rows + jnp.concatenate([row_at] * QUERY_GROUP, axis=1)

    def enter(number, block):
        for lane in range(lanes):
            doc, holder = (me ^ lane, me) if lane < 2 else (me, me ^ lane)
            for head in range(heads):
                group = holder * heads + head
                found = (block == place) | (block == place - 1)
                for s in range(slash_ref.shape[2]):
                    found = found | (block == place - slash_ref[doc, group, s])
                for s in range(vertical_ref.shape[2]):
                    found = found | ((block == vertical_ref[doc, group, s]) & (block < place - 1))
                shift = jnp.where(found & (block >= 0), block * rows, OUT_OF_REACH)
                plan_ref[pl.ds((lane * heads + head) * count + number, 1), :] = query_at - shift

    if ring:
        order = ring_order(count)
        lists = {order[at]: [order[r] for r in Ring.sources(at, count)] for at in range(count)}
        for number in range(count):
            block = jnp.int32(0)
            for here, blocks in lists.items():
                block = jnp.where(place == here, blocks[number], block)
            enter(number, block)
    else:

        def one(number, carry):
            enter(number, number)
            return carry

        lax.fori_loop(0, count, one, 0)


def plan(info, vertical, slash, ring, rows):
    count, lanes = lax.axis_size("seq"), lax.axis_size("doc")
    heads = vertical.shape[1] // lanes
    return pl.pallas_call(
        functools.partial(plan_kernel, ring, lanes, heads, count, rows),
        in_specs=[SMEM] * 3,
        out_specs=VMEM,
        out_shape=jax.ShapeDtypeStruct((lanes * heads * count, QUERY_GROUP * rows), jnp.int32),
        compiler_params=pltpu.CompilerParams(vmem_limit_bytes=4 * MIB),
        name="plan",
    )(info, vertical, slash)


def attend_kernel(lanes, stride, slot_at, slots, chunks, q_count, kv_count, begin, end, plan_ref, *refs):
    q_refs, kv_refs, refs = refs[:q_count], refs[q_count:q_count + kv_count], refs[q_count + kv_count:]
    state_refs = refs[:0 if begin else 3 * len(lanes)]
    out_refs = refs[len(state_refs):]
    heads = kv_refs[0].shape[1] // (2 * HEAD_WIDTH)
    factor = HEAD_WIDTH ** (-0.5) * math.log2(math.e)

    for lane, (mask, q_at, kv_first, rows) in enumerate(lanes):
        rank = QUERY_GROUP * rows
        key_at = lax.broadcasted_iota(jnp.int32, (rows, rank), 0)
        for head in range(heads):
            table = (mask * heads + head) * stride + slot_at
            queries = jnp.concatenate(
                [
                    q_refs[q_at[0]][
                        q_at[1]:q_at[1] + rows,
                        (head * QUERY_GROUP + h) * HEAD_WIDTH:(head * QUERY_GROUP + h + 1) * HEAD_WIDTH,
                    ]
                    for h in range(QUERY_GROUP)
                ],
                axis=0,
            )

            def step(index, carry):
                found = [slot(index) for slot in slots]

                def column(at):
                    cols = slice(at * HEAD_WIDTH, (at + 1) * HEAD_WIDTH)
                    parts = []
                    for r, first in found:
                        if isinstance(first, int):
                            where = slice(first + kv_first, first + kv_first + rows)
                        else:
                            where = pl.ds(pl.multiple_of(first + kv_first, BAND), rows)
                        parts.append(kv_refs[r][where, cols])
                    return jnp.concatenate(parts, axis=0)

                keys, values = column(2 * head), column(2 * head + 1)
                scores = lax.dot_general(
                    keys, queries, (((1,), (1,)), ((), ())), preferred_element_type=jnp.float32
                )
                parts = []
                for j in range(len(slots)):
                    limit = plan_ref[pl.ds(table + index * len(slots) + j, 1), :]
                    parts.append(
                        jnp.where(
                            key_at <= limit,
                            scores[j * rows:(j + 1) * rows],
                            -jnp.inf,
                        )
                    )
                scores = jnp.concatenate(parts, axis=0)
                top = jnp.max(scores, axis=0, keepdims=True)
                if carry is None:
                    fresh = safe = top
                else:
                    fresh = jnp.maximum(carry[0], top)
                    safe = jnp.where(fresh == -jnp.inf, jnp.float32(0), fresh)
                raised = jnp.exp2((scores - safe) * factor)
                total = jnp.sum(raised, axis=0, keepdims=True)
                mixed = lax.dot_general(
                    values,
                    raised.astype(jnp.bfloat16),
                    (((0,), (0,)), ((), ())),
                    preferred_element_type=jnp.float32,
                )
                if carry is not None:
                    fade = jnp.exp2((carry[0] - safe) * factor)
                    total, mixed = carry[1] * fade + total, carry[2] * fade + mixed
                return fresh, total, mixed

            carry = None
            if not begin:
                carry = tuple(ref[head] for ref in state_refs[3 * lane:3 * lane + 3])
            elif chunks > 1:
                carry = (
                    jnp.full((1, rank), -jnp.inf, jnp.float32),
                    jnp.zeros((1, rank), jnp.float32),
                    jnp.zeros((HEAD_WIDTH, rank), jnp.float32),
                )
            if chunks > 1:
                carry = lax.fori_loop(0, chunks, step, carry)
            else:
                carry = step(0, carry)
            if not end:
                for ref, value in zip(out_refs[3 * lane:3 * lane + 3], carry):
                    ref[head] = value
                continue
            result = carry[2] / carry[1]
            for h in range(QUERY_GROUP):
                cols = slice(
                    (head * QUERY_GROUP + h) * HEAD_WIDTH, (head * QUERY_GROUP + h + 1) * HEAD_WIDTH
                )
                out_refs[lane][:, cols] = result[:, h * rows:(h + 1) * rows].T.astype(jnp.bfloat16)


def attend(table, lanes, queries, arrays, slots, chunks=1, first=0, states=None, end=True):
    q_cols = queries[0].shape[1]
    rows = lanes[0][3]
    held = [array for state in states for array in state] if states else []
    if end:
        shapes = [jax.ShapeDtypeStruct((rows, q_cols), jnp.bfloat16)] * len(lanes)
    else:
        heads = q_cols // (QUERY_GROUP * HEAD_WIDTH)
        shapes = [
            jax.ShapeDtypeStruct((heads, deep, QUERY_GROUP * rows), jnp.float32)
            for deep in (1, 1, HEAD_WIDTH)
        ] * len(lanes)
    kernel = functools.partial(
        attend_kernel,
        lanes,
        lax.axis_size("seq"),
        first,
        slots,
        chunks,
        len(queries),
        len(arrays),
        not states,
        end,
    )
    return pl.pallas_call(
        kernel,
        in_specs=[VMEM] * (1 + len(queries) + len(arrays) + len(held)),
        out_specs=[VMEM] * len(shapes),
        out_shape=shapes,
        compiler_params=pltpu.CompilerParams(
            vmem_limit_bytes=10 * MIB + 4 * sum(a.size for a in (*queries, *arrays))
        ),
        cost_estimate=pl.CostEstimate(
            flops=4 * len(lanes) * rows * q_cols * len(slots) * chunks * rows,
            bytes_accessed=2 * sum(a.size for a in arrays) + 4 * len(lanes) * rows * q_cols,
            transcendentals=len(lanes) * rows * len(slots) * chunks * rows * QUERY_GROUP,
        ),
        name="attend",
    )(table, *queries, *arrays, *held)


def deliver_kernel(masks, *refs):
    pieces, (out_ref, sems) = refs[:len(masks)], refs[-2:]
    rows, cols = pieces[0].shape
    me, strips = lax.axis_index("doc"), sems.shape[1]
    copies = []
    for at, (mask, piece) in enumerate(zip(masks, pieces)):
        where = pl.ds(pl.multiple_of((me ^ mask) * cols, cols), cols)
        for strip in range(strips):
            band = pl.ds(strip * (rows // strips), rows // strips)
            copies.append(
                pltpu.make_async_copy(piece.at[band], out_ref.at[0, band, where], sems.at[at, strip])
            )
            copies[-1].start()
    for copy in copies:
        copy.wait()


def deliver(masks, pieces, count, before=None):
    rows, cols = pieces[0].shape
    begun = () if before is None else (before,)
    strips = 4 if rows % (4 * BAND) == 0 else 1
    return pl.pallas_call(
        functools.partial(deliver_kernel, masks),
        in_specs=[VMEM] * len(pieces) + [HBM] * len(begun),
        out_specs=HBM,
        out_shape=jax.ShapeDtypeStruct((1, rows, count * cols), jnp.bfloat16),
        input_output_aliases={len(pieces): 0} if begun else {},
        scratch_shapes=[pltpu.SemaphoreType.DMA((len(pieces), strips))],
        compiler_params=pltpu.CompilerParams(vmem_limit_bytes=4 * MIB),
        name="deliver",
    )(*pieces, *begun)


def local(tokens, norm_gain, w_query, key_weight, value_weight, vertical_blocks, slash_offsets):
    _, rows, width = tokens.shape
    assert lax.axis_size("doc") == 4
    place = lax.axis_index("seq")
    doc_place = lax.axis_index("doc")
    info = after(jnp.stack([place, doc_place, place * rows]).astype(jnp.int32))
    cosine, sine = rope_table(info[2:] + jnp.arange(rows, dtype=jnp.int32), HEAD_WIDTH)
    table = jnp.concatenate([cosine, cosine, -sine, sine], axis=1)
    own = after(tokens, info)[0]
    gain = norm_gain.reshape(1, width)
    long = lax.axis_size("seq") > 8 or lax.axis_size("seq") % 2 == 1
    ring = Gathered if long else Ring
    table_of = plan(info, vertical_blocks, slash_offsets, not long, rows)

    twin = swap(own, "doc", 1)
    across = swap(tokens[0], "doc", 2)
    q_near, kv_near, gain_in, wq_in, wk_in, wv_in = project_near(
        own, twin, gain, w_query, key_weight, value_weight, table
    )
    near = ring(kv_near)
    near.advance()
    near.advance(table_of)
    near.advance()

    across = after(across, *near.latest)
    near.advance()
    crossed = swap(across, "doc", 1)
    kv_across, across_in = project_keys_values(across, gain_in, wk_in, wv_in, table)
    home_across = swap(kv_across, "doc", 2)
    kv_crossed, crossed_in = project_keys_values(crossed, gain_in, wk_in, wv_in, table)
    home_crossed = swap(kv_crossed, "doc", 3)
    q_across, q_crossed = project_queries(
        [across_in, after(crossed_in, kv_crossed)], wq_in, table
    )

    arrived = after((home_across, home_crossed), q_crossed, *near.latest)
    far = ring(jnp.concatenate(arrived, axis=0))
    far.advance()
    queries = [swap(after(q_across, home_crossed), "doc", 2), swap(q_crossed, "doc", 3)]
    mixed_own, mixed_twin = attend(
        table_of,
        [(0, (0, 0), 0, rows), (1, (0, rows), rows, rows)],
        [after(q_near, *far.latest)],
        near.arrays,
        near.slots,
        near.chunks,
    )
    far.advance()
    far.advance(mixed_twin, *queries)
    remote = [(2, (0, 0), 0, rows), (3, (1, 0), rows, rows)]
    if long:
        out_twin = swap(mixed_twin, "doc", 1)
        mixed = attend(table_of, remote, queries, far.arrays, far.slots, far.chunks)
    else:
        far.advance()
        last = len(far.slots) - 1
        states = attend(table_of, remote, queries, far.arrays[:last], far.slots[:last], end=False)
        out_twin = swap(after(mixed_twin, states[0]), "doc", 1)
        mixed = attend(
            table_of,
            remote,
            queries,
            far.arrays[last:],
            far.slots[:1],
            first=last,
            states=[states[:3], states[3:]],
        )
    count = lax.axis_size("doc")
    result = deliver((0, 1), [mixed_own, out_twin], count)
    return deliver((2, 3), mixed, count, before=result)


def solution(mesh):
    return jax.shard_map(
        local,
        mesh=mesh,
        in_specs=(
            P("doc", "seq", None),
            P(),
            P(None, "doc"),
            P(None, "doc"),
            P(None, "doc"),
            P(),
            P(),
        ),
        out_specs=P("doc", "seq", None),
        check_vma=False,
    )
```

```python
import functools
import math

import jax
import jax.numpy as jnp
from jax import lax
from jax.experimental import pallas as pl
from jax.experimental.pallas import tpu as pltpu
from jax.sharding import PartitionSpec as P

HEAD_WIDTH = 128
QUERY_HEADS = 16
KEY_VALUE_HEADS = 4
QUERY_GROUP = QUERY_HEADS // KEY_VALUE_HEADS
EPSILON = 1e-05
BAND = 16
MIB = 1024 * 1024
OUT_OF_REACH = 1 << 30

SMEM = pl.BlockSpec(memory_space=pltpu.SMEM)
VMEM = pl.BlockSpec(memory_space=pltpu.VMEM)
ANYWHERE = pl.BlockSpec(memory_space=pl.ANY)
HBM = pl.BlockSpec(memory_space=pltpu.HBM)


def swap(value, axis, mask):
    count = lax.axis_size(axis)
    return lax.ppermute(value, axis, [(source, source ^ mask) for source in range(count)])


def after(value, *others):
    return lax.optimization_barrier((value,) + others)[0]


def in_hbm(array):
    return pltpu.with_memory_space_constraint(array, pltpu.HBM)


def rope_table(positions, width):
    inverse = jnp.power(jnp.float32(500000.0), -jnp.arange(0, width, 2, dtype=jnp.float32) / width)
    angles = positions.astype(jnp.float32)[:, None] * inverse[None, :]
    return (jnp.cos(angles), jnp.sin(angles))


def normalize(token_ref, gain_ref, normed_ref, first):
    def norm_band(index, carry):
        at = pl.ds(pl.multiple_of(index * BAND, BAND), BAND)
        wide = token_ref[at, :].astype(jnp.float32)
        scale = lax.rsqrt(jnp.mean(wide * wide, axis=-1, keepdims=True) + EPSILON)
        normed_ref[pl.ds(pl.multiple_of(first + index * BAND, BAND), BAND), :] = (
            wide * scale * gain_ref[...]
        ).astype(jnp.bfloat16)
        return carry

    lax.fori_loop(0, token_ref.shape[0] // BAND, norm_band, 0, unroll=4)


def rotate(value, table_ref):
    half = HEAD_WIDTH // 2
    turned = jnp.concatenate([value[:, half:], value[:, :half]], axis=1)
    return (value * table_ref[:, :HEAD_WIDTH] + turned * table_ref[:, HEAD_WIDTH:]).astype(
        jnp.bfloat16
    )


def multiply(normed_ref, weight_of):
    width = normed_ref.shape[1]
    deep = min(1024, width)
    total = None
    for start in range(0, width, deep):
        part = jnp.dot(
            normed_ref[:, start:start + deep],
            weight_of(slice(start, start + deep)),
            preferred_element_type=jnp.float32,
        )
        total = part if total is None else total + part
    return total


def write_keys_values(normed_ref, wk_ref, wv_ref, table_ref, kv_ref):
    rows = table_ref.shape[0]
    for head in range(wk_ref.shape[1] // HEAD_WIDTH):
        at = slice(head * HEAD_WIDTH, (head + 1) * HEAD_WIDTH)
        both = multiply(
            normed_ref, lambda k: jnp.concatenate([wk_ref[k, at], wv_ref[k, at]], axis=1)
        )
        out = 2 * head * HEAD_WIDTH
        for first in range(0, normed_ref.shape[0], rows):
            mine = both[first:first + rows]
            band = slice(first, first + rows)
            kv_ref[band, out:out + HEAD_WIDTH] = rotate(mine[:, :HEAD_WIDTH], table_ref)
            kv_ref[band, out + HEAD_WIDTH:out + 2 * HEAD_WIDTH] = mine[:, HEAD_WIDTH:].astype(
                jnp.bfloat16
            )


def write_queries(normed_ref, wq_ref, table_ref, q_ref):
    rows, pair = table_ref.shape[0], 2 * HEAD_WIDTH
    for start in range(0, wq_ref.shape[1], pair):
        both = multiply(normed_ref, lambda k: wq_ref[k, start:start + pair])
        for first in range(0, normed_ref.shape[0], rows):
            band = slice(first, first + rows)
            for at in (0, HEAD_WIDTH):
                q_ref[band, start + at:start + at + HEAD_WIDTH] = rotate(
                    both[first:first + rows, at:at + HEAD_WIDTH], table_ref
                )


def near_kernel(
    own_hbm, twin_ref, gain_hbm, wq_hbm, wk_hbm, wv_hbm, table_ref,
    q_ref, kv_ref, gain_ref, wq_ref, wk_ref, wv_ref, own_ref, normed_ref, sems,
):
    copies = []
    for source, target in (
        (gain_hbm, gain_ref), (own_hbm, own_ref), (wk_hbm, wk_ref), (wv_hbm, wv_ref), (wq_hbm, wq_ref)
    ):
        copies.append(pltpu.make_async_copy(source, target, sems.at[len(copies)]))
        copies[-1].start()
    copies[0].wait()
    normalize(twin_ref, gain_ref, normed_ref, own_ref.shape[0])
    copies[1].wait()
    normalize(own_ref, gain_ref, normed_ref, 0)
    copies[2].wait()
    copies[3].wait()
    write_keys_values(normed_ref, wk_ref, wv_ref, table_ref, kv_ref)
    copies[4].wait()
    write_queries(normed_ref, wq_ref, table_ref, q_ref)


def keys_values_kernel(token_ref, gain_ref, wk_ref, wv_ref, table_ref, kv_ref, normed_ref):
    normalize(token_ref, gain_ref, normed_ref, 0)
    write_keys_values(normed_ref, wk_ref, wv_ref, table_ref, kv_ref)


def queries_kernel(pieces, wq_ref, table_ref, *refs):
    for normed_ref, q_ref in zip(refs[:pieces], refs[pieces:]):
        write_queries(normed_ref, wq_ref, table_ref, q_ref)


def project_call(kernel, name, operands, kinds, shapes, scratch, rows, columns):
    width = max(array.shape[0] for array in operands)
    return pl.pallas_call(
        kernel,
        in_specs=kinds,
        out_specs=[VMEM] * len(shapes),
        out_shape=[jax.ShapeDtypeStruct(shape, dtype) for shape, dtype in shapes],
        scratch_shapes=scratch,
        compiler_params=pltpu.CompilerParams(vmem_limit_bytes=20 * MIB),
        cost_estimate=pl.CostEstimate(
            flops=2 * rows * width * columns,
            bytes_accessed=2 * width * (columns + rows),
            transcendentals=0,
        ),
        name=name,
    )(*operands)


def project_near(own, twin, gain, w_query, key_weight, value_weight, table):
    rows, width = own.shape
    q_cols, k_cols = w_query.shape[1], key_weight.shape[1]
    params = (gain, w_query, key_weight, value_weight)
    shapes = [((2 * rows, q_cols), jnp.bfloat16), ((2 * rows, 2 * k_cols), jnp.bfloat16)]
    shapes += [(array.shape, array.dtype) for array in params]
    return project_call(
        near_kernel,
        "project_near",
        (in_hbm(own), twin, *(in_hbm(array) for array in params), table),
        [HBM, VMEM] + [HBM] * 4 + [VMEM],
        shapes,
        [
            pltpu.VMEM(own.shape, own.dtype),
            pltpu.VMEM((2 * rows, width), jnp.bfloat16),
            pltpu.SemaphoreType.DMA((5,)),
        ],
        2 * rows,
        q_cols + 2 * k_cols,
    )


def project_keys_values(tokens, gain, key_weight, value_weight, table):
    rows, cols = tokens.shape[0], 2 * key_weight.shape[1]
    operands = (tokens, gain, key_weight, value_weight, table)
    return project_call(
        keys_values_kernel,
        "project_keys_values",
        operands,
        [VMEM] * len(operands),
        [((rows, cols), jnp.bfloat16), (tokens.shape, jnp.bfloat16)],
        [],
        rows,
        cols,
    )


def project_queries(normed, w_query, table):
    operands = (w_query, table, *normed)
    q_cols = w_query.shape[1]
    return project_call(
        functools.partial(queries_kernel, len(normed)),
        "project_queries",
        operands,
        [VMEM] * len(operands),
        [((array.shape[0], q_cols), jnp.bfloat16) for array in normed],
        [],
        sum(array.shape[0] for array in normed),
        q_cols,
    )


def ring_order(count):
    return list(range(0, count, 2)) + list(range(count - 1, 0, -2))


class Gathered:
    def __init__(self, kv):
        count = lax.axis_size("seq")
        total = kv.shape[0]
        chunk = 8 if count % 8 == 0 else 1
        self.chunks, self.latest = count // chunk, ()
        self.arrays = [lax.all_gather(kv, "seq", axis=0, tiled=True)]
        self.slots = [
            lambda index, j=j: (0, pl.multiple_of((index * chunk + j) * total, BAND))
            for j in range(chunk)
        ]

    def advance(self, *others):
        pass


class Ring:
    def __init__(self, kv):
        self.count, self.chunks, self.stage = lax.axis_size("seq"), 1, 0
        self.order = ring_order(self.count)
        self.arrays, self.slots, self.latest = [], [], ()
        self.front = {1: kv, -1: kv}
        self.hold(kv)

    @staticmethod
    def sources(at, count):
        steps = [0]
        for stage in range(1, count // 2 + 1):
            steps += [stage, -stage] if 2 * stage < count else [stage]
        return [(at - step) % count for step in steps]

    def hold(self, array):
        self.slots.append(lambda index, r=len(self.arrays): (r, 0))
        self.arrays.append(array)

    def advance(self, *others):
        if self.stage >= self.count // 2:
            return
        self.stage += 1
        fresh = []
        for way in (1, -1) if 2 * self.stage < self.count else (1,):
            value = after(self.front[way], *others) if others else self.front[way]
            pairs = [
                (source, self.order[(at + way) % self.count]) for at, source in enumerate(self.order)
            ]
            self.front[way] = lax.ppermute(value, "seq", pairs)
            fresh.append(self.front[way])
            self.hold(self.front[way])
        self.latest = tuple(fresh)


def plan_kernel(ring, lanes, heads, count, rows, info_ref, vertical_ref, slash_ref, plan_ref):
    place, me = info_ref[0], info_ref[1]
    row_at = lax.broadcasted_iota(jnp.int32, (1, rows), 1)
    query_at = place * rows + jnp.concatenate([row_at] * QUERY_GROUP, axis=1)

    def enter(number, block):
        for lane in range(lanes):
            doc, holder = (me ^ lane, me) if lane < 2 else (me, me ^ lane)
            for head in range(heads):
                group = holder * heads + head
                found = (block == place) | (block == place - 1)
                for s in range(slash_ref.shape[2]):
                    found = found | (block == place - slash_ref[doc, group, s])
                for s in range(vertical_ref.shape[2]):
                    found = found | ((block == vertical_ref[doc, group, s]) & (block < place - 1))
                shift = jnp.where(found & (block >= 0), block * rows, OUT_OF_REACH)
                plan_ref[pl.ds((lane * heads + head) * count + number, 1), :] = query_at - shift

    if ring:
        order = ring_order(count)
        lists = {order[at]: [order[r] for r in Ring.sources(at, count)] for at in range(count)}
        for number in range(count):
            block = jnp.int32(0)
            for here, blocks in lists.items():
                block = jnp.where(place == here, blocks[number], block)
            enter(number, block)
    else:

        def one(number, carry):
            enter(number, number)
            return carry

        lax.fori_loop(0, count, one, 0)


def plan(info, vertical, slash, ring, rows):
    count, lanes = lax.axis_size("seq"), lax.axis_size("doc")
    heads = vertical.shape[1] // lanes
    return pl.pallas_call(
        functools.partial(plan_kernel, ring, lanes, heads, count, rows),
        in_specs=[SMEM] * 3,
        out_specs=VMEM,
        out_shape=jax.ShapeDtypeStruct((lanes * heads * count, QUERY_GROUP * rows), jnp.int32),
        compiler_params=pltpu.CompilerParams(vmem_limit_bytes=4 * MIB),
        name="plan",
    )(info, vertical, slash)


def attend_kernel(lanes, stride, slot_at, slots, chunks, q_count, kv_count, begin, end, plan_ref, *refs):
    q_refs, kv_refs, refs = refs[:q_count], refs[q_count:q_count + kv_count], refs[q_count + kv_count:]
    state_refs = refs[:0 if begin else 3 * len(lanes)]
    out_refs = refs[len(state_refs):]
    heads = kv_refs[0].shape[1] // (2 * HEAD_WIDTH)
    factor = HEAD_WIDTH ** (-0.5) * math.log2(math.e)

    for lane, (mask, q_at, kv_first, rows) in enumerate(lanes):
        rank = QUERY_GROUP * rows
        key_at = lax.broadcasted_iota(jnp.int32, (rows, rank), 0)
        for head in range(heads):
            table = (mask * heads + head) * stride + slot_at
            queries = jnp.concatenate(
                [
                    q_refs[q_at[0]][
                        q_at[1]:q_at[1] + rows,
                        (head * QUERY_GROUP + h) * HEAD_WIDTH:(head * QUERY_GROUP + h + 1) * HEAD_WIDTH,
                    ]
                    for h in range(QUERY_GROUP)
                ],
                axis=0,
            )

            def step(index, carry):
                found = [slot(index) for slot in slots]

                def column(at):
                    cols = slice(at * HEAD_WIDTH, (at + 1) * HEAD_WIDTH)
                    parts = []
                    for r, first in found:
                        if isinstance(first, int):
                            where = slice(first + kv_first, first + kv_first + rows)
                        else:
                            where = pl.ds(pl.multiple_of(first + kv_first, BAND), rows)
                        parts.append(kv_refs[r][where, cols])
                    return jnp.concatenate(parts, axis=0)

                keys, values = column(2 * head), column(2 * head + 1)
                scores = lax.dot_general(
                    keys, queries, (((1,), (1,)), ((), ())), preferred_element_type=jnp.float32
                )
                parts = []
                for j in range(len(slots)):
                    limit = plan_ref[pl.ds(table + index * len(slots) + j, 1), :]
                    parts.append(
                        jnp.where(
                            key_at <= limit,
                            scores[j * rows:(j + 1) * rows],
                            -jnp.inf,
                        )
                    )
                scores = jnp.concatenate(parts, axis=0)
                top = jnp.max(scores, axis=0, keepdims=True)
                if carry is None:
                    fresh = safe = top
                else:
                    fresh = jnp.maximum(carry[0], top)
                    safe = jnp.where(fresh == -jnp.inf, jnp.float32(0), fresh)
                raised = jnp.exp2((scores - safe) * factor)
                total = jnp.sum(raised, axis=0, keepdims=True)
                mixed = lax.dot_general(
                    values,
                    raised.astype(jnp.bfloat16),
                    (((0,), (0,)), ((), ())),
                    preferred_element_type=jnp.float32,
                )
                if carry is not None:
                    fade = jnp.exp2((carry[0] - safe) * factor)
                    total, mixed = carry[1] * fade + total, carry[2] * fade + mixed
                return fresh, total, mixed

            carry = None
            if not begin:
                carry = tuple(ref[head] for ref in state_refs[3 * lane:3 * lane + 3])
            elif chunks > 1:
                carry = (
                    jnp.full((1, rank), -jnp.inf, jnp.float32),
                    jnp.zeros((1, rank), jnp.float32),
                    jnp.zeros((HEAD_WIDTH, rank), jnp.float32),
                )
            if chunks > 1:
                carry = lax.fori_loop(0, chunks, step, carry)
            else:
                carry = step(0, carry)
            if not end:
                for ref, value in zip(out_refs[3 * lane:3 * lane + 3], carry):
                    ref[head] = value
                continue
            result = carry[2] / carry[1]
            for h in range(QUERY_GROUP):
                cols = slice(
                    (head * QUERY_GROUP + h) * HEAD_WIDTH, (head * QUERY_GROUP + h + 1) * HEAD_WIDTH
                )
                out_refs[lane][:, cols] = result[:, h * rows:(h + 1) * rows].T.astype(jnp.bfloat16)


def attend(table, lanes, queries, arrays, slots, chunks=1, first=0, states=None, end=True):
    q_cols = queries[0].shape[1]
    rows = lanes[0][3]
    held = [array for state in states for array in state] if states else []
    if end:
        shapes = [jax.ShapeDtypeStruct((rows, q_cols), jnp.bfloat16)] * len(lanes)
    else:
        heads = q_cols // (QUERY_GROUP * HEAD_WIDTH)
        shapes = [
            jax.ShapeDtypeStruct((heads, deep, QUERY_GROUP * rows), jnp.float32)
            for deep in (1, 1, HEAD_WIDTH)
        ] * len(lanes)
    kernel = functools.partial(
        attend_kernel,
        lanes,
        lax.axis_size("seq"),
        first,
        slots,
        chunks,
        len(queries),
        len(arrays),
        not states,
        end,
    )
    return pl.pallas_call(
        kernel,
        in_specs=[VMEM] * (1 + len(queries) + len(arrays) + len(held)),
        out_specs=[VMEM] * len(shapes),
        out_shape=shapes,
        compiler_params=pltpu.CompilerParams(
            vmem_limit_bytes=10 * MIB + 4 * sum(a.size for a in (*queries, *arrays))
        ),
        cost_estimate=pl.CostEstimate(
            flops=4 * len(lanes) * rows * q_cols * len(slots) * chunks * rows,
            bytes_accessed=2 * sum(a.size for a in arrays) + 4 * len(lanes) * rows * q_cols,
            transcendentals=len(lanes) * rows * len(slots) * chunks * rows * QUERY_GROUP,
        ),
        name="attend",
    )(table, *queries, *arrays, *held)


def deliver_kernel(masks, *refs):
    pieces, (out_ref, sems) = refs[:len(masks)], refs[-2:]
    rows, cols = pieces[0].shape
    me, strips = lax.axis_index("doc"), sems.shape[1]
    copies = []
    for at, (mask, piece) in enumerate(zip(masks, pieces)):
        where = pl.ds(pl.multiple_of((me ^ mask) * cols, cols), cols)
        for strip in range(strips):
            band = pl.ds(strip * (rows // strips), rows // strips)
            copies.append(
                pltpu.make_async_copy(piece.at[band], out_ref.at[0, band, where], sems.at[at, strip])
            )
            copies[-1].start()
    for copy in copies:
        copy.wait()


def deliver(masks, pieces, count, before=None):
    rows, cols = pieces[0].shape
    begun = () if before is None else (before,)
    strips = 4 if rows % (4 * BAND) == 0 else 1
    return pl.pallas_call(
        functools.partial(deliver_kernel, masks),
        in_specs=[VMEM] * len(pieces) + [HBM] * len(begun),
        out_specs=HBM,
        out_shape=jax.ShapeDtypeStruct((1, rows, count * cols), jnp.bfloat16),
        input_output_aliases={len(pieces): 0} if begun else {},
        scratch_shapes=[pltpu.SemaphoreType.DMA((len(pieces), strips))],
        compiler_params=pltpu.CompilerParams(vmem_limit_bytes=4 * MIB),
        name="deliver",
    )(*pieces, *begun)


def local(tokens, norm_gain, w_query, key_weight, value_weight, vertical_blocks, slash_offsets):
    _, rows, width = tokens.shape
    assert lax.axis_size("doc") == 4
    place = lax.axis_index("seq")
    doc_place = lax.axis_index("doc")
    info = after(jnp.stack([place, doc_place, place * rows]).astype(jnp.int32))
    cosine, sine = rope_table(info[2:] + jnp.arange(rows, dtype=jnp.int32), HEAD_WIDTH)
    table = jnp.concatenate([cosine, cosine, -sine, sine], axis=1)
    own = after(tokens, info)[0]
    gain = norm_gain.reshape(1, width)
    long = lax.axis_size("seq") > 8 or lax.axis_size("seq") % 2 == 1
    ring = Gathered if long else Ring
    table_of = plan(info, vertical_blocks, slash_offsets, not long, rows)

    twin = swap(own, "doc", 1)
    across = swap(tokens[0], "doc", 2)
    q_near, kv_near, gain_in, wq_in, wk_in, wv_in = project_near(
        own, twin, gain, w_query, key_weight, value_weight, table
    )
    near = ring(kv_near)
    near.advance()
    near.advance(table_of)
    near.advance()

    across = after(across, *near.latest)
    near.advance()
    crossed = swap(across, "doc", 1)
    kv_across, across_in = project_keys_values(across, gain_in, wk_in, wv_in, table)
    home_across = swap(kv_across, "doc", 2)
    kv_crossed, crossed_in = project_keys_values(crossed, gain_in, wk_in, wv_in, table)
    home_crossed = swap(kv_crossed, "doc", 3)
    q_across, q_crossed = project_queries(
        [across_in, after(crossed_in, kv_crossed)], wq_in, table
    )

    arrived = after((home_across, home_crossed), q_crossed, *near.latest)
    far = ring(jnp.concatenate(arrived, axis=0))
    far.advance()
    queries = [swap(after(q_across, home_crossed), "doc", 2), swap(q_crossed, "doc", 3)]
    mixed_own, mixed_twin = attend(
        table_of,
        [(0, (0, 0), 0, rows), (1, (0, rows), rows, rows)],
        [after(q_near, *far.latest)],
        near.arrays,
        near.slots,
        near.chunks,
    )
    far.advance()
    far.advance(mixed_twin, *queries)
    out_twin = swap(after(mixed_twin, *far.latest), "doc", 1)
    remote = [(2, (0, 0), 0, rows), (3, (1, 0), rows, rows)]
    if long:
        mixed = attend(table_of, remote, queries, far.arrays, far.slots, far.chunks)
    else:
        far.advance()
        last = len(far.slots) - 1
        states = attend(table_of, remote, queries, far.arrays[:last], far.slots[:last], end=False)
        mixed = attend(
            table_of,
            remote,
            queries,
            far.arrays[last:],
            far.slots[:1],
            first=last,
            states=[states[:3], states[3:]],
        )
    count = lax.axis_size("doc")
    result = deliver((0, 1), [mixed_own, out_twin], count)
    return deliver((2, 3), mixed, count, before=result)


def solution(mesh):
    return jax.shard_map(
        local,
        mesh=mesh,
        in_specs=(
            P("doc", "seq", None),
            P(),
            P(None, "doc"),
            P(None, "doc"),
            P(None, "doc"),
            P(),
            P(),
        ),
        out_specs=P("doc", "seq", None),
        check_vma=False,
    )
```

```python
import functools
import math

import jax
import jax.numpy as jnp
from jax import lax
from jax.experimental import pallas as pl
from jax.experimental.pallas import tpu as pltpu
from jax.sharding import PartitionSpec as P

HEAD_WIDTH = 128
QUERY_HEADS = 16
KEY_VALUE_HEADS = 4
QUERY_GROUP = QUERY_HEADS // KEY_VALUE_HEADS
EPSILON = 1e-05
BAND = 16
MIB = 1024 * 1024
OUT_OF_REACH = 1 << 30

SMEM = pl.BlockSpec(memory_space=pltpu.SMEM)
VMEM = pl.BlockSpec(memory_space=pltpu.VMEM)
ANYWHERE = pl.BlockSpec(memory_space=pl.ANY)
HBM = pl.BlockSpec(memory_space=pltpu.HBM)


def swap(value, axis, mask):
    count = lax.axis_size(axis)
    return lax.ppermute(value, axis, [(source, source ^ mask) for source in range(count)])


def after(value, *others):
    return lax.optimization_barrier((value,) + others)[0]


def in_hbm(array):
    return pltpu.with_memory_space_constraint(array, pltpu.HBM)


def rope_table(positions, width):
    inverse = jnp.power(jnp.float32(500000.0), -jnp.arange(0, width, 2, dtype=jnp.float32) / width)
    angles = positions.astype(jnp.float32)[:, None] * inverse[None, :]
    return (jnp.cos(angles), jnp.sin(angles))


def normalize(token_ref, gain_ref, normed_ref, first):
    def norm_band(index, carry):
        at = pl.ds(pl.multiple_of(index * BAND, BAND), BAND)
        wide = token_ref[at, :].astype(jnp.float32)
        scale = lax.rsqrt(jnp.mean(wide * wide, axis=-1, keepdims=True) + EPSILON)
        normed_ref[pl.ds(pl.multiple_of(first + index * BAND, BAND), BAND), :] = (
            wide * scale * gain_ref[...]
        ).astype(jnp.bfloat16)
        return carry

    lax.fori_loop(0, token_ref.shape[0] // BAND, norm_band, 0, unroll=8)


def rotate(value, table_ref):
    half = HEAD_WIDTH // 2
    turned = jnp.concatenate([value[:, half:], value[:, :half]], axis=1)
    return (value * table_ref[:, :HEAD_WIDTH] + turned * table_ref[:, HEAD_WIDTH:]).astype(
        jnp.bfloat16
    )


def multiply(normed_ref, weight_of):
    width = normed_ref.shape[1]
    deep = min(1024, width)
    total = None
    for start in range(0, width, deep):
        part = jnp.dot(
            normed_ref[:, start:start + deep],
            weight_of(slice(start, start + deep)),
            preferred_element_type=jnp.float32,
        )
        total = part if total is None else total + part
    return total


def write_keys_values(normed_ref, wk_ref, wv_ref, table_ref, kv_ref):
    rows = table_ref.shape[0]
    for head in range(wk_ref.shape[1] // HEAD_WIDTH):
        at = slice(head * HEAD_WIDTH, (head + 1) * HEAD_WIDTH)
        both = multiply(
            normed_ref, lambda k: jnp.concatenate([wk_ref[k, at], wv_ref[k, at]], axis=1)
        )
        out = 2 * head * HEAD_WIDTH
        for first in range(0, normed_ref.shape[0], rows):
            mine = both[first:first + rows]
            band = slice(first, first + rows)
            kv_ref[band, out:out + HEAD_WIDTH] = rotate(mine[:, :HEAD_WIDTH], table_ref)
            kv_ref[band, out + HEAD_WIDTH:out + 2 * HEAD_WIDTH] = mine[:, HEAD_WIDTH:].astype(
                jnp.bfloat16
            )


def write_queries(normed_ref, wq_ref, table_ref, q_ref):
    rows, pair = table_ref.shape[0], 2 * HEAD_WIDTH
    for start in range(0, wq_ref.shape[1], pair):
        both = multiply(normed_ref, lambda k: wq_ref[k, start:start + pair])
        for first in range(0, normed_ref.shape[0], rows):
            band = slice(first, first + rows)
            for at in (0, HEAD_WIDTH):
                q_ref[band, start + at:start + at + HEAD_WIDTH] = rotate(
                    both[first:first + rows, at:at + HEAD_WIDTH], table_ref
                )


def near_kernel(
    own_hbm, twin_ref, gain_hbm, wq_hbm, wk_hbm, wv_hbm, table_ref,
    q_ref, kv_ref, gain_ref, wq_ref, wk_ref, wv_ref, own_ref, normed_ref, sems,
):
    copies = []
    for source, target in (
        (gain_hbm, gain_ref), (own_hbm, own_ref), (wk_hbm, wk_ref), (wv_hbm, wv_ref), (wq_hbm, wq_ref)
    ):
        copies.append(pltpu.make_async_copy(source, target, sems.at[len(copies)]))
        copies[-1].start()
    copies[0].wait()
    normalize(twin_ref, gain_ref, normed_ref, own_ref.shape[0])
    copies[1].wait()
    normalize(own_ref, gain_ref, normed_ref, 0)
    copies[2].wait()
    copies[3].wait()
    write_keys_values(normed_ref, wk_ref, wv_ref, table_ref, kv_ref)
    copies[4].wait()
    write_queries(normed_ref, wq_ref, table_ref, q_ref)


def keys_values_kernel(token_ref, gain_ref, wk_ref, wv_ref, table_ref, kv_ref, normed_ref):
    normalize(token_ref, gain_ref, normed_ref, 0)
    write_keys_values(normed_ref, wk_ref, wv_ref, table_ref, kv_ref)


def queries_kernel(pieces, wq_ref, table_ref, *refs):
    for normed_ref, q_ref in zip(refs[:pieces], refs[pieces:]):
        write_queries(normed_ref, wq_ref, table_ref, q_ref)


def project_call(kernel, name, operands, kinds, shapes, scratch, rows, columns):
    width = max(array.shape[0] for array in operands)
    return pl.pallas_call(
        kernel,
        in_specs=kinds,
        out_specs=[VMEM] * len(shapes),
        out_shape=[jax.ShapeDtypeStruct(shape, dtype) for shape, dtype in shapes],
        scratch_shapes=scratch,
        compiler_params=pltpu.CompilerParams(vmem_limit_bytes=20 * MIB),
        cost_estimate=pl.CostEstimate(
            flops=2 * rows * width * columns,
            bytes_accessed=2 * width * (columns + rows),
            transcendentals=0,
        ),
        name=name,
    )(*operands)


def project_near(own, twin, gain, w_query, key_weight, value_weight, table):
    rows, width = own.shape
    q_cols, k_cols = w_query.shape[1], key_weight.shape[1]
    params = (gain, w_query, key_weight, value_weight)
    shapes = [((2 * rows, q_cols), jnp.bfloat16), ((2 * rows, 2 * k_cols), jnp.bfloat16)]
    shapes += [(array.shape, array.dtype) for array in params]
    return project_call(
        near_kernel,
        "project_near",
        (in_hbm(own), twin, *(in_hbm(array) for array in params), table),
        [HBM, VMEM] + [HBM] * 4 + [VMEM],
        shapes,
        [
            pltpu.VMEM(own.shape, own.dtype),
            pltpu.VMEM((2 * rows, width), jnp.bfloat16),
            pltpu.SemaphoreType.DMA((5,)),
        ],
        2 * rows,
        q_cols + 2 * k_cols,
    )


def project_keys_values(tokens, gain, key_weight, value_weight, table):
    rows, cols = tokens.shape[0], 2 * key_weight.shape[1]
    operands = (tokens, gain, key_weight, value_weight, table)
    return project_call(
        keys_values_kernel,
        "project_keys_values",
        operands,
        [VMEM] * len(operands),
        [((rows, cols), jnp.bfloat16), (tokens.shape, jnp.bfloat16)],
        [],
        rows,
        cols,
    )


def project_queries(normed, w_query, table):
    operands = (w_query, table, *normed)
    q_cols = w_query.shape[1]
    return project_call(
        functools.partial(queries_kernel, len(normed)),
        "project_queries",
        operands,
        [VMEM] * len(operands),
        [((array.shape[0], q_cols), jnp.bfloat16) for array in normed],
        [],
        sum(array.shape[0] for array in normed),
        q_cols,
    )


def ring_order(count):
    return list(range(0, count, 2)) + list(range(count - 1, 0, -2))


class Gathered:
    def __init__(self, kv):
        count = lax.axis_size("seq")
        total = kv.shape[0]
        chunk = 8 if count % 8 == 0 else 1
        self.chunks, self.latest = count // chunk, ()
        self.arrays = [lax.all_gather(kv, "seq", axis=0, tiled=True)]
        self.slots = [
            lambda index, j=j: (0, pl.multiple_of((index * chunk + j) * total, BAND))
            for j in range(chunk)
        ]

    def advance(self, *others):
        pass


class Ring:
    def __init__(self, kv):
        self.count, self.chunks, self.stage = lax.axis_size("seq"), 1, 0
        self.order = ring_order(self.count)
        self.arrays, self.slots, self.latest = [], [], ()
        self.front = {1: kv, -1: kv}
        self.hold(kv)

    @staticmethod
    def sources(at, count):
        steps = [0]
        for stage in range(1, count // 2 + 1):
            steps += [stage, -stage] if 2 * stage < count else [stage]
        return [(at - step) % count for step in steps]

    def hold(self, array):
        self.slots.append(lambda index, r=len(self.arrays): (r, 0))
        self.arrays.append(array)

    def advance(self, *others):
        if self.stage >= self.count // 2:
            return
        self.stage += 1
        fresh = []
        for way in (1, -1) if 2 * self.stage < self.count else (1,):
            value = after(self.front[way], *others) if others else self.front[way]
            pairs = [
                (source, self.order[(at + way) % self.count]) for at, source in enumerate(self.order)
            ]
            self.front[way] = lax.ppermute(value, "seq", pairs)
            fresh.append(self.front[way])
            self.hold(self.front[way])
        self.latest = tuple(fresh)


def plan_kernel(ring, lanes, heads, count, rows, info_ref, vertical_ref, slash_ref, plan_ref):
    place, me = info_ref[0], info_ref[1]
    row_at = lax.broadcasted_iota(jnp.int32, (1, rows), 1)
    query_at = place * rows + jnp.concatenate([row_at] * QUERY_GROUP, axis=1)

    def enter(number, block):
        for lane in range(lanes):
            doc, holder = (me ^ lane, me) if lane < 2 else (me, me ^ lane)
            for head in range(heads):
                group = holder * heads + head
                found = (block == place) | (block == place - 1)
                for s in range(slash_ref.shape[2]):
                    found = found | (block == place - slash_ref[doc, group, s])
                for s in range(vertical_ref.shape[2]):
                    found = found | ((block == vertical_ref[doc, group, s]) & (block < place - 1))
                shift = jnp.where(found & (block >= 0), block * rows, OUT_OF_REACH)
                plan_ref[pl.ds((lane * heads + head) * count + number, 1), :] = query_at - shift

    if ring:
        order = ring_order(count)
        lists = {order[at]: [order[r] for r in Ring.sources(at, count)] for at in range(count)}
        for number in range(count):
            block = jnp.int32(0)
            for here, blocks in lists.items():
                block = jnp.where(place == here, blocks[number], block)
            enter(number, block)
    else:

        def one(number, carry):
            enter(number, number)
            return carry

        lax.fori_loop(0, count, one, 0)


def plan(info, vertical, slash, ring, rows):
    count, lanes = lax.axis_size("seq"), lax.axis_size("doc")
    heads = vertical.shape[1] // lanes
    return pl.pallas_call(
        functools.partial(plan_kernel, ring, lanes, heads, count, rows),
        in_specs=[SMEM] * 3,
        out_specs=VMEM,
        out_shape=jax.ShapeDtypeStruct((lanes * heads * count, QUERY_GROUP * rows), jnp.int32),
        compiler_params=pltpu.CompilerParams(vmem_limit_bytes=4 * MIB),
        name="plan",
    )(info, vertical, slash)


def attend_kernel(lanes, stride, slot_at, slots, chunks, q_count, kv_count, begin, end, plan_ref, *refs):
    q_refs, kv_refs, refs = refs[:q_count], refs[q_count:q_count + kv_count], refs[q_count + kv_count:]
    state_refs = refs[:0 if begin else 3 * len(lanes)]
    out_refs = refs[len(state_refs):]
    heads = kv_refs[0].shape[1] // (2 * HEAD_WIDTH)
    factor = HEAD_WIDTH ** (-0.5) * math.log2(math.e)

    for lane, (mask, q_at, kv_first, rows) in enumerate(lanes):
        rank = QUERY_GROUP * rows
        key_at = lax.broadcasted_iota(jnp.int32, (rows, rank), 0)
        for head in range(heads):
            table = (mask * heads + head) * stride + slot_at
            queries = jnp.concatenate(
                [
                    q_refs[q_at[0]][
                        q_at[1]:q_at[1] + rows,
                        (head * QUERY_GROUP + h) * HEAD_WIDTH:(head * QUERY_GROUP + h + 1) * HEAD_WIDTH,
                    ]
                    for h in range(QUERY_GROUP)
                ],
                axis=0,
            )

            def step(index, carry):
                found = [slot(index) for slot in slots]

                def column(at):
                    cols = slice(at * HEAD_WIDTH, (at + 1) * HEAD_WIDTH)
                    parts = []
                    for r, first in found:
                        if isinstance(first, int):
                            where = slice(first + kv_first, first + kv_first + rows)
                        else:
                            where = pl.ds(pl.multiple_of(first + kv_first, BAND), rows)
                        parts.append(kv_refs[r][where, cols])
                    return jnp.concatenate(parts, axis=0)

                keys, values = column(2 * head), column(2 * head + 1)
                scores = lax.dot_general(
                    keys, queries, (((1,), (1,)), ((), ())), preferred_element_type=jnp.float32
                )
                parts = []
                for j in range(len(slots)):
                    limit = plan_ref[pl.ds(table + index * len(slots) + j, 1), :]
                    parts.append(
                        jnp.where(
                            key_at <= limit,
                            scores[j * rows:(j + 1) * rows],
                            -jnp.inf,
                        )
                    )
                scores = jnp.concatenate(parts, axis=0)
                top = jnp.max(scores, axis=0, keepdims=True)
                if carry is None:
                    fresh = safe = top
                else:
                    fresh = jnp.maximum(carry[0], top)
                    safe = jnp.where(fresh == -jnp.inf, jnp.float32(0), fresh)
                raised = jnp.exp2((scores - safe) * factor)
                total = jnp.sum(raised, axis=0, keepdims=True)
                mixed = lax.dot_general(
                    values,
                    raised.astype(jnp.bfloat16),
                    (((0,), (0,)), ((), ())),
                    preferred_element_type=jnp.float32,
                )
                if carry is not None:
                    fade = jnp.exp2((carry[0] - safe) * factor)
                    total, mixed = carry[1] * fade + total, carry[2] * fade + mixed
                return fresh, total, mixed

            carry = None
            if not begin:
                carry = tuple(ref[head] for ref in state_refs[3 * lane:3 * lane + 3])
            elif chunks > 1:
                carry = (
                    jnp.full((1, rank), -jnp.inf, jnp.float32),
                    jnp.zeros((1, rank), jnp.float32),
                    jnp.zeros((HEAD_WIDTH, rank), jnp.float32),
                )
            if chunks > 1:
                carry = lax.fori_loop(0, chunks, step, carry)
            else:
                carry = step(0, carry)
            if not end:
                for ref, value in zip(out_refs[3 * lane:3 * lane + 3], carry):
                    ref[head] = value
                continue
            result = carry[2] / carry[1]
            for h in range(QUERY_GROUP):
                cols = slice(
                    (head * QUERY_GROUP + h) * HEAD_WIDTH, (head * QUERY_GROUP + h + 1) * HEAD_WIDTH
                )
                out_refs[lane][:, cols] = result[:, h * rows:(h + 1) * rows].T.astype(jnp.bfloat16)


def attend(table, lanes, queries, arrays, slots, chunks=1, first=0, states=None, end=True):
    q_cols = queries[0].shape[1]
    rows = lanes[0][3]
    held = [array for state in states for array in state] if states else []
    if end:
        shapes = [jax.ShapeDtypeStruct((rows, q_cols), jnp.bfloat16)] * len(lanes)
    else:
        heads = q_cols // (QUERY_GROUP * HEAD_WIDTH)
        shapes = [
            jax.ShapeDtypeStruct((heads, deep, QUERY_GROUP * rows), jnp.float32)
            for deep in (1, 1, HEAD_WIDTH)
        ] * len(lanes)
    kernel = functools.partial(
        attend_kernel,
        lanes,
        lax.axis_size("seq"),
        first,
        slots,
        chunks,
        len(queries),
        len(arrays),
        not states,
        end,
    )
    return pl.pallas_call(
        kernel,
        in_specs=[VMEM] * (1 + len(queries) + len(arrays) + len(held)),
        out_specs=[VMEM] * len(shapes),
        out_shape=shapes,
        compiler_params=pltpu.CompilerParams(
            vmem_limit_bytes=10 * MIB + 4 * sum(a.size for a in (*queries, *arrays))
        ),
        cost_estimate=pl.CostEstimate(
            flops=4 * len(lanes) * rows * q_cols * len(slots) * chunks * rows,
            bytes_accessed=2 * sum(a.size for a in arrays) + 4 * len(lanes) * rows * q_cols,
            transcendentals=len(lanes) * rows * len(slots) * chunks * rows * QUERY_GROUP,
        ),
        name="attend",
    )(table, *queries, *arrays, *held)


def deliver_kernel(masks, *refs):
    pieces, (out_ref, sems) = refs[:len(masks)], refs[-2:]
    rows, cols = pieces[0].shape
    me, strips = lax.axis_index("doc"), sems.shape[1]
    copies = []
    for at, (mask, piece) in enumerate(zip(masks, pieces)):
        where = pl.ds(pl.multiple_of((me ^ mask) * cols, cols), cols)
        for strip in range(strips):
            band = pl.ds(strip * (rows // strips), rows // strips)
            copies.append(
                pltpu.make_async_copy(piece.at[band], out_ref.at[0, band, where], sems.at[at, strip])
            )
            copies[-1].start()
    for copy in copies:
        copy.wait()


def deliver(masks, pieces, count, before=None):
    rows, cols = pieces[0].shape
    begun = () if before is None else (before,)
    strips = 4 if rows % (4 * BAND) == 0 else 1
    return pl.pallas_call(
        functools.partial(deliver_kernel, masks),
        in_specs=[VMEM] * len(pieces) + [HBM] * len(begun),
        out_specs=HBM,
        out_shape=jax.ShapeDtypeStruct((1, rows, count * cols), jnp.bfloat16),
        input_output_aliases={len(pieces): 0} if begun else {},
        scratch_shapes=[pltpu.SemaphoreType.DMA((len(pieces), strips))],
        compiler_params=pltpu.CompilerParams(vmem_limit_bytes=4 * MIB),
        name="deliver",
    )(*pieces, *begun)


def local(tokens, norm_gain, w_query, key_weight, value_weight, vertical_blocks, slash_offsets):
    _, rows, width = tokens.shape
    assert lax.axis_size("doc") == 4
    place = lax.axis_index("seq")
    doc_place = lax.axis_index("doc")
    info = after(jnp.stack([place, doc_place, place * rows]).astype(jnp.int32))
    cosine, sine = rope_table(info[2:] + jnp.arange(rows, dtype=jnp.int32), HEAD_WIDTH)
    table = jnp.concatenate([cosine, cosine, -sine, sine], axis=1)
    own = after(tokens, info)[0]
    gain = norm_gain.reshape(1, width)
    long = lax.axis_size("seq") > 8 or lax.axis_size("seq") % 2 == 1
    ring = Gathered if long else Ring
    table_of = plan(info, vertical_blocks, slash_offsets, not long, rows)

    twin = swap(own, "doc", 1)
    across = swap(tokens[0], "doc", 2)
    q_near, kv_near, gain_in, wq_in, wk_in, wv_in = project_near(
        own, twin, gain, w_query, key_weight, value_weight, table
    )
    near = ring(kv_near)
    near.advance()
    near.advance(table_of)
    near.advance()

    across = after(across, *near.latest)
    crossed = swap(across, "doc", 1)
    kv_across, across_in = project_keys_values(across, gain_in, wk_in, wv_in, table)
    home_across = swap(kv_across, "doc", 2)
    kv_crossed, crossed_in = project_keys_values(after(crossed, kv_across), gain_in, wk_in, wv_in, table)
    home_crossed = swap(kv_crossed, "doc", 3)
    near.advance(kv_crossed)
    q_across, q_crossed = project_queries(
        [across_in, after(crossed_in, kv_crossed)], wq_in, table
    )

    arrived = after((home_across, home_crossed), q_crossed, *near.latest)
    far = ring(jnp.concatenate(arrived, axis=0))
    far.advance()
    queries = [swap(after(q_across, home_crossed), "doc", 2), swap(q_crossed, "doc", 3)]
    mixed_own, mixed_twin = attend(
        table_of,
        [(0, (0, 0), 0, rows), (1, (0, rows), rows, rows)],
        [after(q_near, *far.latest)],
        near.arrays,
        near.slots,
        near.chunks,
    )
    far.advance()
    far.advance(mixed_twin, *queries)
    out_twin = swap(after(mixed_twin, *far.latest), "doc", 1)
    remote = [(2, (0, 0), 0, rows), (3, (1, 0), rows, rows)]
    if long:
        mixed = attend(table_of, remote, queries, far.arrays, far.slots, far.chunks)
    else:
        far.advance()
        last = len(far.slots) - 1
        states = attend(table_of, remote, queries, far.arrays[:last], far.slots[:last], end=False)
        mixed = attend(
            table_of,
            remote,
            queries,
            far.arrays[last:],
            far.slots[:1],
            first=last,
            states=[states[:3], states[3:]],
        )
    count = lax.axis_size("doc")
    result = deliver((0, 1), [mixed_own, out_twin], count)
    return deliver((2, 3), mixed, count, before=result)


def solution(mesh):
    return jax.shard_map(
        local,
        mesh=mesh,
        in_specs=(
            P("doc", "seq", None),
            P(),
            P(None, "doc"),
            P(None, "doc"),
            P(None, "doc"),
            P(),
            P(),
        ),
        out_specs=P("doc", "seq", None),
        check_vma=False,
    )
```
